32 devices in a mesh: dp: 8 (over z, y), mp: 4 (over x, core).
Axes of the slice: x: 2, y: 2, z: 4, core: 2. Of those that a mesh axis runs over, the one named last changes fastest.
Arguments:
- tokens: bfloat16 [24576, 768], P('dp'), may hold values from -6 to 6
- seg_ids: int32 [24576], P('dp'), may hold values from 0 to 180, as said below
- labels: int32 [1440], P('dp'), may hold values from 0 to 999
- w_qkv: float32 [3, 768, 768], P(None, 'dp', 'mp'), may hold values from -0.21875 to 0.21875
- m_qkv: float32 [3, 768, 768], P(None, 'dp', 'mp'), may hold values from -0.0009765625 to 0.0009765625
- v_qkv: float32 [3, 768, 768], P(None, 'dp', 'mp'), may hold values from 1.890432e-09 to 7.561728e-09
- w_out: float32 [768, 768], P('mp', 'dp'), may hold values from -0.4375 to 0.4375
- m_out: float32 [768, 768], P('mp', 'dp'), may hold values from -0.0009765625 to 0.0009765625
- v_out: float32 [768, 768], P('mp', 'dp'), may hold values from 1.890432e-09 to 7.561728e-09
- w_up: float32 [768, 3072], P('dp', 'mp'), may hold values from -0.21875 to 0.21875
- m_up: float32 [768, 3072], P('dp', 'mp'), may hold values from -0.0004272461 to 0.0004272461
- v_up: float32 [768, 3072], P('dp', 'mp'), may hold values from 4.72608e-10 to 1.890432e-09
- w_down: float32 [3072, 768], P('mp', 'dp'), may hold values from -0.109375 to 0.109375
- m_down: float32 [3072, 768], P('mp', 'dp'), may hold values from -0.0004272461 to 0.0004272461
- v_down: float32 [3072, 768], P('mp', 'dp'), may hold values from 4.72608e-10 to 1.890432e-09
- w_cls: float32 [768, 1000], P('dp', 'mp')
- m_cls: float32 [768, 1000], P('dp', 'mp'), may hold values from -0.00030517578 to 0.00030517578
- v_cls: float32 [768, 1000], P('dp', 'mp'), may hold values from 2.5e-10 to 1e-09
- norm_params: float32 [7, 768], P(None, 'dp')
- m_norm: float32 [7, 768], P(None, 'dp'), may hold values from -0.0009765625 to 0.0009765625
- v_norm: float32 [7, 768], P(None, 'dp'), may hold values from 1.890432e-09 to 7.561728e-09
- qk_gain: float32 [2, 12, 64], P(None, 'mp', 'dp'), may hold values from 1.2 to 1.6
- m_qk: float32 [2, 12, 64], P(None, 'mp', 'dp'), may hold values from -0.0009765625 to 0.0009765625
- v_qk: float32 [2, 12, 64], P(None, 'mp', 'dp'), may hold values from 1.890432e-09 to 7.561728e-09
Outputs:
- block_out: bfloat16 [24576, 768], P('dp')
- input_grad: float32 [24576, 768], P('dp')
- mean_loss: float32 [], replicated
- m_qkv_new: float32 [3, 768, 768], P(None, 'dp', 'mp')
- v_qkv_new: float32 [3, 768, 768], P(None, 'dp', 'mp')
- w_qkv_new: float32 [3, 768, 768], P(None, 'dp', 'mp')
- m_out_new: float32 [768, 768], P('mp', 'dp')
- v_out_new: float32 [768, 768], P('mp', 'dp')
- w_out_new: float32 [768, 768], P('mp', 'dp')
- m_up_new: float32 [768, 3072], P('dp', 'mp')
- v_up_new: float32 [768, 3072], P('dp', 'mp')
- w_up_new: float32 [768, 3072], P('dp', 'mp')
- m_down_new: float32 [3072, 768], P('mp', 'dp')
- v_down_new: float32 [3072, 768], P('mp', 'dp')
- w_down_new: float32 [3072, 768], P('mp', 'dp')
- m_cls_new: float32 [768, 1000], P('dp', 'mp')
- v_cls_new: float32 [768, 1000], P('dp', 'mp')
- w_cls_new: float32 [768, 1000], P('dp', 'mp')
- m_norm_new: float32 [7, 768], P(None, 'dp')
- v_norm_new: float32 [6, 768], P(None, 'dp')
- v_probe_new: float32 [768], P('dp')
- norm_new: float32 [7, 768], P(None, 'dp')
- m_qk_new: float32 [2, 12, 64], P(None, 'mp', 'dp')
- v_qk_new: float32 [2, 12, 64], P(None, 'mp', 'dp')
- qk_new: float32 [2, 12, 64], P(None, 'mp', 'dp')
The draws below stay inside these ranges and needn't reach their ends.
Inputs may be any that keep to these rules, and one draw needn't show every extreme that they name: `seg_ids`: each of the 3 sequences of 1024 positions on a data device holds, from its start, images one after another numbered k * 60 + j for its number k on the device and j = 0, 1, ..., each of one position or more, at least 512 positions in all; the rest, one position or more at its end, holds 180.
All inputs are finite; a program needn't handle non-finite values.
Results may differ from the reference program's by a relative error of at most 0.017.
The reference program's roundings to bfloat16 on the way count: a program that leaves them out, or rounds other values in their place, can miss the bound.
Values may be sent and summed in bfloat16 or wider, within the bound.
A program may use at most 256 MiB of HBM per device.

```python
import math
import jax
import jax.numpy as jnp
from jax import lax

D = 768
HEADS = 12
HD = 64
FF = 3072
CLASSES = 1000
LEN = 1024
IMG_SEQ = 60
STEP = 10
SEQ_DEV = 3
ROWS = 3072
IMG_DEV = 180
TOKENS = 24576
IMAGES = 1440
N_DP = 8


def packing(key):
    key = jax.random.fold_in(key, 11)
    count_key, length_key, share_key = jax.random.split(key, 3)
    slot_count = TOKENS // LEN
    device_count = slot_count // SEQ_DEV
    device_of = jnp.arange(slot_count, dtype=jnp.int32) // SEQ_DEV
    rising = IMG_SEQ * (device_count + 2 * device_of) // (3 * device_count)
    images = jnp.clip(rising + jax.random.randint(count_key, (slot_count,), -2, 3), 1, IMG_SEQ)
    images = images.at[slot_count - 1].set(IMG_SEQ)
    used_len = jax.random.randint(length_key, (slot_count,), LEN // 2, LEN)
    image_order = jnp.arange(IMG_SEQ, dtype=jnp.int32)
    live_mask = (image_order[None, :] < images[:, None]).astype(jnp.int32)
    shares = jax.random.randint(share_key, (slot_count, IMG_SEQ), 1, 1000) * live_mask
    spare_len = used_len - images
    extra_len = spare_len[:, None] * shares // jnp.sum(shares, axis=1, keepdims=True)
    extra_len = extra_len.at[:, 0].add(spare_len - jnp.sum(extra_len, axis=1))
    lengths = (1 + extra_len) * live_mask
    image_ends = jnp.cumsum(lengths, axis=1)
    position = jnp.arange(LEN, dtype=jnp.int32)
    within = jnp.sum((position[None, :, None] >= image_ends[:, None, :]).astype(jnp.int32), axis=2)
    slot_local = jnp.arange(slot_count, dtype=jnp.int32) % SEQ_DEV
    numbered = slot_local[:, None] * IMG_SEQ + within
    filled = jnp.where(position[None, :] < used_len[:, None], numbered, IMG_DEV)
    return filled.reshape(TOKENS).astype(jnp.int32)


def draw_seg_ids(key, part):
    filled = packing(key)
    return filled


def draw_tokens(key, part):
    image_ids = packing(key)
    key = jax.random.fold_in(key, 17)
    common_key, noise_key = jax.random.split(key, 2)
    device_total = TOKENS // ROWS
    slot_of = jnp.arange(TOKENS, dtype=jnp.int32) // ROWS * (IMG_DEV + 1) + image_ids
    common = jax.random.normal(common_key, (device_total * (IMG_DEV + 1), D), jnp.float32)
    noise = jax.random.normal(noise_key, (TOKENS, D), jnp.float32)
    values = 0.7 * jnp.take(common, slot_of, axis=0) + 0.714 * noise
    return jnp.clip(values, -6.0, 6.0).astype(jnp.bfloat16)


def draw_w_cls(key, part):
    key = jax.random.fold_in(key, 23)
    column = jnp.arange(CLASSES, dtype=jnp.float32) / CLASSES
    rising = 1.0 + 2.0 * column
    entries = jax.random.normal(key, (D, CLASSES), jnp.float32)
    return (entries * rising[None, :] * (2.5 * D ** (-0.5))).astype(jnp.float32)


def draw_norm_params(key, part):
    key = jax.random.fold_in(key, 31)
    gain_key, shift_key, probe_key = jax.random.split(key, 3)
    gain_rows = 1.0 + 0.2 * jax.random.uniform(gain_key, (3, D), jnp.float32, -1.0, 1.0)
    shift_rows = 0.25 * jax.random.normal(shift_key, (3, D), jnp.float32)
    probe_row = jax.random.normal(probe_key, (D,), jnp.float32) * D ** (-0.5)
    return jnp.stack([gain_rows[0], shift_rows[0], gain_rows[1], shift_rows[1], gain_rows[2], shift_rows[2], probe_row]).astype(jnp.float32)


def with_ends(values, key, smallest, high):
    spot = [jax.random.randint(jax.random.fold_in(key, axis), (), 0, length) for axis, length in enumerate(values.shape)]
    main_axis = values.shape.index(max(values.shape))
    neighbour = spot[:main_axis] + [(spot[main_axis] + 1) % values.shape[main_axis]] + spot[main_axis + 1:]
    return values.at[tuple(spot)].set(smallest).at[tuple(neighbour)].set(high)


def steps_of(rng, dims, shards, smallest, top_value):
    loudness, own = 1.0, jax.random.fold_in(rng, 6)
    for dim, shards_of in shards:
        steps = jnp.exp(jax.random.uniform(jax.random.fold_in(own, dim), (shards_of,), jnp.float32, smallest / len(shards), top_value / len(shards)))
        loudness = loudness * jnp.repeat(steps, dims[dim] // shards_of).reshape([-1 if axis == dim else 1 for axis in range(len(dims))])
    return loudness


def gaussian(stream_key, dims, scale, limit, cuts=(), kind=jnp.bfloat16):
    loudness = steps_of(stream_key, dims, cuts, -0.22, 0.18) if cuts else 1.0
    values = jax.random.normal(stream_key, dims, jnp.float32) * scale * loudness
    return jnp.minimum(jnp.maximum(values, -limit), limit).astype(kind)


def setup_inputs(seed: int = 0) -> dict:
    seeds = jax.random.split(jax.random.key(seed), 25)
    return {
        "tokens": draw_tokens(jax.random.fold_in(seeds[24], 71), 0),
        "seg_ids": draw_seg_ids(jax.random.fold_in(seeds[24], 71), 0),
        "labels": with_ends(jax.random.randint(seeds[2], (IMAGES,), 0, CLASSES), jax.random.fold_in(seeds[2], 1), 0, CLASSES - 1).astype(jnp.int32),
        "w_qkv": gaussian(seeds[3], (3, D, D), D ** -0.5, 0.21875, ((1, 8), (2, 4)), jnp.float32),
        "m_qkv": gaussian(seeds[4], (3, D, D), (0.0385 * D ** -0.5 * IMAGES ** -1.0 * TOKENS ** 0.5), 0.0009765625, ((1, 8), (2, 4)), jnp.float32),
        "v_qkv": jnp.clip(jnp.exp(math.log(7.561728132543521e-09) - 1.3862944 * jax.random.uniform(seeds[5], (3, D, D), jnp.float32) ** steps_of(seeds[5], (3, D, D), ((1, 8), (2, 4)), -0.2, 0.2)), 1.8904320331358804e-09, 7.561728132543521e-09),
        "w_out": gaussian(seeds[6], (D, D), (D // 4) ** -0.5, 0.4375, ((0, 4), (1, 8)), jnp.float32),
        "m_out": gaussian(seeds[7], (D, D), (0.0385 * D ** -0.5 * IMAGES ** -1.0 * TOKENS ** 0.5), 0.0009765625, ((0, 4), (1, 8)), jnp.float32),
        "v_out": jnp.clip(jnp.exp(math.log(7.561728132543521e-09) - 1.3862944 * jax.random.uniform(seeds[8], (D, D), jnp.float32) ** steps_of(seeds[8], (D, D), ((0, 4), (1, 8)), -0.2, 0.2)), 1.8904320331358804e-09, 7.561728132543521e-09),
        "w_up": gaussian(seeds[9], (D, FF), D ** -0.5, 0.21875, ((0, 8), (1, 4)), jnp.float32),
        "m_up": gaussian(seeds[10], (D, FF), (0.019 * D ** -0.5 * IMAGES ** -1.0 * TOKENS ** 0.5), 0.0004272461, ((0, 8), (1, 4)), jnp.float32),
        "v_up": jnp.clip(jnp.exp(math.log(1.8904320331358804e-09) - 1.3862944 * jax.random.uniform(seeds[11], (D, FF), jnp.float32) ** steps_of(seeds[11], (D, FF), ((0, 8), (1, 4)), -0.2, 0.2)), 4.726080082839701e-10, 1.8904320331358804e-09),
        "w_down": gaussian(seeds[12], (FF, D), FF ** -0.5, 0.109375, ((0, 4), (1, 8)), jnp.float32),
        "m_down": gaussian(seeds[13], (FF, D), (0.019 * D ** -0.5 * IMAGES ** -1.0 * TOKENS ** 0.5), 0.0004272461, ((0, 4), (1, 8)), jnp.float32),
        "v_down": jnp.clip(jnp.exp(math.log(1.8904320331358804e-09) - 1.3862944 * jax.random.uniform(seeds[14], (FF, D), jnp.float32) ** steps_of(seeds[14], (FF, D), ((0, 4), (1, 8)), -0.2, 0.2)), 4.726080082839701e-10, 1.8904320331358804e-09),
        "w_cls": draw_w_cls(jax.random.fold_in(seeds[24], 71), 0),
        "m_cls": gaussian(seeds[16], (D, CLASSES), (0.066 * (IMAGES * CLASSES) ** -0.5), 0.00030517578, ((0, 8), (1, 4)), jnp.float32),
        "v_cls": jnp.clip(jnp.exp(math.log(9.999999717180685e-10) - 1.3862944 * jax.random.uniform(seeds[17], (D, CLASSES), jnp.float32) ** steps_of(seeds[17], (D, CLASSES), ((0, 8), (1, 4)), -0.2, 0.2)), 2.4999999292951713e-10, 9.999999717180685e-10),
        "norm_params": draw_norm_params(jax.random.fold_in(seeds[24], 71), 0),
        "m_norm": gaussian(seeds[19], (7, D), (0.0385 * D ** -0.5 * IMAGES ** -1.0 * TOKENS ** 0.5), 0.0009765625, ((1, 8),), jnp.float32),
        "v_norm": jnp.clip(jnp.exp(math.log(7.561728132543521e-09) - 1.3862944 * jax.random.uniform(seeds[20], (7, D), jnp.float32) ** steps_of(seeds[20], (7, D), ((1, 8),), -0.2, 0.2)), 1.8904320331358804e-09, 7.561728132543521e-09),
        "qk_gain": jnp.clip(1.2 + 0.39999998 * jax.random.uniform(seeds[21], (2, HEADS, HD), jnp.float32) ** steps_of(seeds[21], (2, HEADS, HD), ((1, 4), (2, 8)), -0.2, 0.2), 1.2, 1.6),
        "m_qk": gaussian(seeds[22], (2, HEADS, HD), (0.0385 * D ** -0.5 * IMAGES ** -1.0 * TOKENS ** 0.5), 0.0009765625, ((1, 4), (2, 8)), jnp.float32),
        "v_qk": jnp.clip(jnp.exp(math.log(7.561728132543521e-09) - 1.3862944 * jax.random.uniform(seeds[23], (2, HEADS, HD), jnp.float32) ** steps_of(seeds[23], (2, HEADS, HD), ((1, 4), (2, 8)), -0.2, 0.2)), 1.8904320331358804e-09, 7.561728132543521e-09),
    }


NORM_EPS = 1e-06
MASK_FILL = -1000000000.0
BETA_ONE = 0.9
BETA_TWO = 0.999
ADAM_EPS = 1e-08
MATRIX_RATE = 0.1
MATRIX_DECAY = 0.1
GAIN_RATE = 0.8

@jax.custom_vjp
def low(v):
    return lax.optimization_barrier(v.astype(jnp.bfloat16)).astype(jnp.float32)

@jax.custom_vjp
def low_back(v):
    return v

def low_keep(v):
    return (low(v), None)

def low_pass(kept, grad):
    return (grad,)

def back_keep(v):
    return (v, None)

def back_low(kept, grad):
    return (low(grad),)
low.defvjp(low_keep, low_pass)
low_back.defvjp(back_keep, back_low)

def layer_norm(values, gain_row, shift_row):
    centre = values - lax.optimization_barrier(jnp.mean(values, axis=-1, keepdims=True))
    spread = lax.optimization_barrier(jnp.mean(centre * centre, axis=-1, keepdims=True))
    return centre * lax.rsqrt(spread + NORM_EPS) * gain_row + shift_row

def head_norm(values, gain_row):
    centre = values - lax.optimization_barrier(jnp.mean(values, axis=-1, keepdims=True))
    spread = lax.optimization_barrier(jnp.mean(centre * centre, axis=-1, keepdims=True))
    return centre * lax.rsqrt(spread + NORM_EPS) * gain_row

def pool_weights(normed, probe_row, image_ids, images):
    pool_score = jnp.dot(normed, probe_row, precision=lax.Precision.HIGHEST)
    member = image_ids[None, :] == jnp.arange(images, dtype=jnp.int32)[:, None]
    image_top = lax.optimization_barrier(jnp.max(jnp.where(member, pool_score[None, :], MASK_FILL), axis=1))
    shifted = jnp.where(member, pool_score[None, :] - image_top[:, None], MASK_FILL)
    weight = jnp.exp(shifted)
    non_empty = jnp.any(member, axis=1)
    image_sum = lax.optimization_barrier(jnp.sum(weight, axis=1)) + jnp.where(non_empty, 0.0, 1.0)
    return weight / image_sum[:, None]

def attend(pieces):
    query_slot, key_slot, value_slot, seg_slot = pieces
    raw_scores = low_back(jnp.einsum('qhe,khe->hqk', query_slot, key_slot, precision=lax.Precision.HIGHEST) * HD ** (-0.5))
    same_image = seg_slot[:, None] == seg_slot[None, :]
    masked = jnp.where(same_image[None], raw_scores, MASK_FILL)
    row_top = lax.optimization_barrier(jnp.max(masked, axis=-1, keepdims=True))
    exp_scores = jnp.exp(masked - row_top)
    soft_probs = exp_scores / lax.optimization_barrier(jnp.sum(exp_scores, axis=-1, keepdims=True))
    return jnp.einsum('hqk,khe->qhe', low(soft_probs), value_slot, precision=lax.Precision.HIGHEST)

def adam_update(weight, moment_one, moment_two, gradient, step_rate, decay_rate):
    fresh_one = BETA_ONE * moment_one + (1.0 - BETA_ONE) * gradient
    fresh_two = BETA_TWO * moment_two + (1.0 - BETA_TWO) * gradient * gradient
    one_hat = fresh_one / (1.0 - BETA_ONE ** STEP)
    two_hat = fresh_two / (1.0 - BETA_TWO ** STEP)
    updated = weight - step_rate * (one_hat / (jnp.sqrt(two_hat) + ADAM_EPS) + decay_rate * weight)
    return (fresh_one, fresh_two, updated)

def reference(tokens, seg_ids, labels, w_qkv, m_qkv, v_qkv, w_out, m_out, v_out, w_up, m_up, v_up, w_down, m_down, v_down, w_cls, m_cls, v_cls, norm_params, m_norm, v_norm, qk_gain, m_qk, v_qk):
    highest = lax.Precision.HIGHEST
    inputs = tokens.astype(jnp.float32)
    slot_count = TOKENS // LEN
    local_ids = seg_ids.reshape(N_DP, ROWS)
    member_count = lax.optimization_barrier(jnp.sum((local_ids[:, None, :] == jnp.arange(IMG_DEV, dtype=jnp.int32)[None, :, None]).astype(jnp.float32), axis=2)).reshape(IMAGES)
    present = jnp.where(member_count > 0, 1.0, 0.0).astype(jnp.float32)
    chosen = labels[:, None] == jnp.arange(CLASSES, dtype=jnp.int32)[None, :]

    def forward(inputs, qkv_raw, out_raw, up_raw, down_raw, cls_raw, norm_raw, qk_raw):
        qkv_w = low(qkv_raw)
        out_w = low(out_raw)
        up_w = low(up_raw)
        down_w = low(down_raw)
        cls_w = low(cls_raw)
        params = low(norm_raw)
        qk_low = low(qk_raw)
        normed_one = low(layer_norm(inputs, params[0], params[1]))
        projected = jnp.einsum('rd,pde->pre', normed_one, qkv_w, precision=highest)
        query = low(head_norm(low_back(projected[0]).reshape(TOKENS, HEADS, HD), qk_low[0]))
        key_norm = low(head_norm(low_back(projected[1]).reshape(TOKENS, HEADS, HD), qk_low[1]))
        value = low(low_back(projected[2])).reshape(TOKENS, HEADS, HD)
        slot_shape = (slot_count, LEN, HEADS, HD)
        attended = lax.map(jax.checkpoint(attend), (query.reshape(slot_shape), key_norm.reshape(slot_shape), value.reshape(slot_shape), seg_ids.reshape(slot_count, LEN)))
        attended = low(low_back(attended.reshape(TOKENS, D)))
        middle = inputs + low_back(jnp.dot(attended, out_w, precision=highest))
        normed_two = low(layer_norm(middle, params[2], params[3]))
        hidden = low_back(jnp.dot(normed_two, up_w, precision=highest))
        active = low(jax.nn.gelu(hidden, approximate=False))
        result = middle + low_back(jnp.dot(active, down_w, precision=highest))

        def pool_device(pieces):
            values, image_ids = pieces
            final_norm = layer_norm(values, params[4], params[5])
            pool_share = pool_weights(final_norm, params[6], image_ids, IMG_DEV)
            return jnp.dot(low(pool_share), low(final_norm), precision=highest)
        pooled = lax.map(jax.checkpoint(pool_device), (result.reshape(N_DP, ROWS, D), local_ids))
        pooled = low(low_back(pooled.reshape(IMAGES, D)))
        logits = low_back(jnp.dot(pooled, cls_w, precision=highest))
        row_top = lax.optimization_barrier(jnp.max(logits, axis=1, keepdims=True))
        log_total = row_top[:, 0] + jnp.log(lax.optimization_barrier(jnp.sum(jnp.exp(logits - row_top), axis=1)))
        label_logit = lax.optimization_barrier(jnp.sum(jnp.where(chosen, logits, 0.0), axis=1))
        mean_loss = jnp.sum(present * (log_total - label_logit)) / jnp.sum(present)
        return (mean_loss, result)
    (mean_loss, result), backward = jax.vjp(forward, inputs, w_qkv, w_out, w_up, w_down, w_cls, norm_params, qk_gain)
    grads = backward((jnp.ones((), jnp.float32), jnp.zeros_like(result)))
    outs = [result.astype(jnp.bfloat16), grads[0], mean_loss]
    groups = ((w_qkv, m_qkv, v_qkv, MATRIX_RATE, MATRIX_DECAY), (w_out, m_out, v_out, MATRIX_RATE, MATRIX_DECAY), (w_up, m_up, v_up, MATRIX_RATE, MATRIX_DECAY), (w_down, m_down, v_down, MATRIX_RATE, MATRIX_DECAY), (w_cls, m_cls, v_cls, MATRIX_RATE, MATRIX_DECAY), (norm_params, m_norm, v_norm, GAIN_RATE, 0.0), (qk_gain, m_qk, v_qk, GAIN_RATE, 0.0))
    for number, group in enumerate(groups):
        fresh_one, fresh_two, updated = adam_update(group[0], group[1], group[2], grads[number + 1], group[3], group[4])
        if number == 5:
            outs = outs + [fresh_one, fresh_two[:6], fresh_two[6], updated]
        else:
            outs = outs + [fresh_one, fresh_two, updated]
    return tuple(outs)
```

```python
import functools

import jax
import jax.numpy as jnp
from jax import lax
from jax.experimental import pallas as pl
from jax.experimental.pallas import tpu as pltpu
from jax.sharding import PartitionSpec as P

LEN = 1024
STEP = 10
SEQ_DEV = 3
IMG_DEV = 180
PAD_ID = 180

NORM_EPS = 1e-06
MASK_FILL = -1000000000.0
BETA_ONE = 0.9
BETA_TWO = 0.999
ADAM_EPS = 1e-08
MATRIX_RATE = 0.1
MATRIX_DECAY = 0.1
GAIN_RATE = 0.8

HEAD = 64
QB = 128
QBLOCKS = LEN // QB
WINDOWS = (384, 640, 1024)
F32 = jnp.float32
BF16 = jnp.bfloat16
VMEM_LIMIT = 56 * 1024 * 1024
IMG_SEQ = 60
SLOTS = 64
ANY = pl.BlockSpec(memory_space=pl.ANY)
PARAMS = pltpu.CompilerParams(vmem_limit_bytes=VMEM_LIMIT)


def dot(a, b, ca, cb):
    return lax.dot_general(a, b, (((ca,), (cb,)), ((), ())), preferred_element_type=F32)


def head_mean(values, ones_block):
    high = values.astype(BF16)
    rest = (values - high.astype(F32)).astype(BF16)
    return dot(high, ones_block, 1, 0) + dot(rest, ones_block, 1, 0)


def norm_parts(values):
    centre = values - jnp.mean(values, axis=-1, keepdims=True)
    spread = jnp.mean(centre * centre, axis=-1, keepdims=True)
    scale = lax.rsqrt(spread + NORM_EPS)
    return centre * scale, scale


def norm_back(grad, normed, scale, gain):
    scaled = grad * gain
    first = jnp.mean(scaled, axis=-1, keepdims=True)
    second = jnp.mean(scaled * normed, axis=-1, keepdims=True)
    return (scaled - first - normed * second) * scale


def head_parts(values, ones_block):
    centre = values - head_mean(values, ones_block)
    scale = lax.rsqrt(head_mean(centre * centre, ones_block) + NORM_EPS)
    return centre * scale, scale


def cost(flops, read, exps=0):
    return pl.CostEstimate(flops=int(flops), bytes_accessed=int(read), transcendentals=int(exps))


def whole(shape):
    return pl.BlockSpec(tuple(shape), lambda *_: (0,) * len(shape))


class Plan:
    def __init__(self, n_dp, n_mp, dim):
        self.n_dp, self.n_mp = n_dp, n_mp
        self.merge = 1 if dim // n_dp % 16 == 0 else 2
        self.groups = n_dp // self.merge
        self.block = dim // self.groups
        self.far = [2 * k for k in range(1, self.groups // 2)]

    def swap(self, value, axis, bits):
        size = self.n_dp if axis == "dp" else self.n_mp
        return lax.ppermute(value, axis, [(i, i ^ bits) for i in range(size)])

    def group_swap(self, value, bits):
        return self.swap(value, "dp", bits * self.merge)

    def merged(self, value, dim):
        if self.merge == 1:
            return value
        other = self.swap(value, "dp", 1)
        even = lax.axis_index("dp") % 2 == 0
        first, second = jnp.where(even, value, other), jnp.where(even, other, value)
        return jnp.concatenate([first, second], axis=dim)

    def unmerged(self, value, dim):
        if self.merge == 1:
            return value
        half = value.shape[dim] // 2
        me = lax.axis_index("dp") % 2
        mine = lax.dynamic_slice_in_dim(value, me * half, half, dim)
        theirs = lax.dynamic_slice_in_dim(value, (1 - me) * half, half, dim)
        return mine + self.swap(theirs, "dp", 1)

    def gather(self, block, order, after=None):
        value, places = block[None], [(0, 0)]
        for step in order:
            if step == "x":
                got = [(self.swap(value, "mp", 2), 0, 2)]
            elif step == "y":
                got = [(self.group_swap(value, 1), 1, 0)]
            else:
                got = [(self.group_swap(value, k), k, 0) for k in self.far]
            value = jnp.concatenate([value] + [g for g, _, _ in got], axis=0)
            places = places + [(a ^ i, b ^ j) for _, i, j in got for a, b in places]
        return value, places

    def both_cores(self, gathered):
        value, places = gathered
        return [gathered, (self.swap(value, "mp", 1), [(a, b ^ 1) for a, b in places])]

    def scatter(self, keep, send, order):
        value = keep.astype(F32) + self.swap(send, "mp", 1).astype(F32)
        return self.scatter_rest(value, "xyz", order, 0)

    def scatter_rest(self, value, axes, order, row_dim):
        for step in order:
            at = axes.index(step)
            axes = axes[:at] + axes[at + 1 :]
            low = value.astype(BF16)
            count = value.shape[at]
            parts = [lax.index_in_dim(low, k, at, keepdims=False) for k in range(1, count)]
            value = lax.index_in_dim(value, 0, at, keepdims=False)
            for k, part in enumerate(parts, start=1):
                if step == "x":
                    got = self.swap(part, "mp", 2)
                else:
                    got = self.group_swap(part, k if step == "y" else 2 * k)
                value = value + got.astype(F32)
        return self.unmerged(value, row_dim)

    def total(self, value, axis):
        size = self.n_dp if axis == "dp" else self.n_mp
        bits = 1
        while bits < size:
            value = value + self.swap(value, axis, bits)
            bits *= 2
        return value


def copy_blocks(pieces, target, sems, first):
    copies = []
    for ref, places in pieces:
        for i, (group, other) in enumerate(places):
            source, dest = target(ref, i, group, other)
            copies.append(pltpu.make_async_copy(source, dest, sems.at[first + len(copies)]))
    return copies


def start_all(copies):
    for c in copies:
        c.start()


def wait_all(copies):
    for c in copies:
        c.wait()


def project(plan, ids, tokens, qk_pieces, v_pieces, params, gains, ones):
    rows, dim = tokens.shape
    cols = ones.shape[0]
    block = 512
    size = plan.block

    def kernel(ids_ref, x_ref, norm_ref, gain_ref, ones_ref, qk_ref, v_in_ref, low_ref, pq_ref, pk_ref, q_ref, k_ref, v_ref, w_ref, sems):
        me = ids_ref[0]

        def place(slot, count):
            def target(ref, i, group, other):
                rows_at = pl.ds(pl.multiple_of((me ^ group) * size, 16), size)
                return ref.at[i], w_ref.at[pl.ds(slot, count), rows_at, :]

            return target

        copies = copy_blocks([(qk_ref, qk_pieces[1])], place(0, 2), sems, 0)
        copies += copy_blocks([(v_in_ref, v_pieces[1])], place(2, 1), sems, len(copies))
        pl.when(pl.program_id(0) == 0)(lambda: start_all(copies))
        normed, _ = norm_parts(x_ref[...].astype(F32))
        low = (normed * norm_ref[0:1, :] + norm_ref[1:2, :]).astype(BF16)
        low_ref[...] = low
        pl.when(pl.program_id(0) == 0)(lambda: wait_all(copies))
        ones_block = ones_ref[...]
        pq = dot(low, w_ref[0], 1, 0)
        pk = dot(low, w_ref[1], 1, 0)
        pq_ref[...] = pq
        pk_ref[...] = pk
        v_ref[...] = dot(low, w_ref[2], 1, 0).astype(BF16)
        nq, _ = head_parts(pq, ones_block)
        nk, _ = head_parts(pk, ones_block)
        q_ref[...] = (nq * gain_ref[0:1, :]).astype(BF16)
        k_ref[...] = (nk * gain_ref[1:2, :]).astype(BF16)

    row = lambda c: pl.BlockSpec((block, c), lambda i, *_: (i, 0))
    shape = lambda c, t: jax.ShapeDtypeStruct((rows, c), t)
    return pl.pallas_call(
        kernel,
        grid_spec=pltpu.PrefetchScalarGridSpec(
            num_scalar_prefetch=1,
            grid=(rows // block,),
            in_specs=[row(dim), whole(params.shape), whole(gains.shape), whole(ones.shape), ANY, ANY],
            out_specs=[row(dim), row(cols), row(cols), row(cols), row(cols), row(cols)],
            scratch_shapes=[pltpu.VMEM((3, dim, cols), BF16), pltpu.SemaphoreType.DMA((2 * plan.groups,))],
        ),
        out_shape=[shape(dim, BF16), shape(cols, F32), shape(cols, F32), shape(cols, BF16), shape(cols, BF16), shape(cols, BF16)],
        compiler_params=PARAMS,
        cost_estimate=cost(6 * rows * dim * cols, rows * dim * 8),
        name="project",
    )(ids, tokens, params, gains, ones, qk_pieces[0], v_pieces[0])


def head_masks(cols):
    lane = lax.broadcasted_iota(jnp.int32, (1, cols), 1)
    return [(lane >= h * HEAD) & (lane < (h + 1) * HEAD) for h in range(cols // HEAD)]


def spread_heads(block, masks):
    zero = jnp.zeros_like(block)
    return jnp.concatenate([jnp.where(m, block, zero) for m in masks], axis=0)


def join_heads(stacked, masks):
    total = stacked[0:QB]
    for h in range(1, len(masks)):
        total = jnp.where(masks[h], stacked[h * QB : (h + 1) * QB], total)
    return total


def by_window(width_ref, step, body):
    width = width_ref[step]
    for number, window in enumerate(WINDOWS):
        pl.when(width == number)(functools.partial(body, window))


def seq_specs(seq, cols):
    block = lambda c: pl.BlockSpec((QB, c), lambda b, *_: (seq * QBLOCKS + b, 0))
    all_keys = lambda c: pl.BlockSpec((LEN, c), lambda b, *_: (seq, 0))
    seg_row = pl.BlockSpec((1, 1, LEN), lambda b, *_: (seq, 0, 0))
    return block, all_keys, seg_row


def attend(plan, seq, ids, starts, widths, q, k, v, seg_col, seg_row):
    rows, cols = q.shape
    n_mp = plan.n_mp
    share = LEN // n_mp
    per = share // QB

    def kernel(ids_ref, start_ref, width_ref, q_ref, k_ref, v_ref, col_ref, row_ref, *outs):
        out_refs, log_ref = outs[:n_mp], outs[n_mp]
        block = pl.program_id(0)
        step = seq * QBLOCKS + block
        masks = head_masks(cols)
        heads = len(masks)

        def body(window):
            start = pl.multiple_of(start_ref[step], QB)
            keys = k_ref[pl.ds(start, window), :]
            values = v_ref[pl.ds(start, window), :]
            q3 = spread_heads(q_ref[...], masks)
            s = (dot(q3, keys, 1, 1) * HEAD**-0.5).reshape(heads, QB, window)
            same = col_ref[...] == row_ref[0, :, pl.ds(start, window)]
            s = jnp.where(same[None], s, MASK_FILL)
            top = jnp.max(s, axis=-1, keepdims=True)
            e = jnp.exp(s - top)
            total = jnp.sum(e, axis=-1, keepdims=True)
            p = (e * (1.0 / total)).astype(BF16).reshape(heads * QB, window)
            out = join_heads(dot(p, values, 1, 0), masks).astype(BF16)
            other = (block // per) ^ ids_ref[1]
            at = pl.ds(pl.multiple_of(block % per * QB, QB), QB)
            for r in range(n_mp):

                @pl.when(other == r)
                def _():
                    out_refs[r][at, :] = out

            log = top + jnp.log(total)
            lane = lax.broadcasted_iota(jnp.int32, (QB, 128), 1)
            logs = jnp.zeros((QB, 128), F32)
            for h in range(heads):
                logs = jnp.where(lane == h, log[h], logs)
            log_ref[...] = logs

        by_window(width_ref, step, body)

    block, all_keys, row_spec = seq_specs(seq, cols)
    return pl.pallas_call(
        kernel,
        grid_spec=pltpu.PrefetchScalarGridSpec(
            num_scalar_prefetch=3,
            grid=(QBLOCKS,),
            in_specs=[block(cols), all_keys(cols), all_keys(cols), block(1), row_spec],
            out_specs=[whole((share, cols))] * n_mp + [pl.BlockSpec((QB, 128), lambda b, *_: (b, 0))],
        ),
        out_shape=[jax.ShapeDtypeStruct((share, cols), BF16)] * n_mp + [jax.ShapeDtypeStruct((LEN, 128), F32)],
        compiler_params=PARAMS,
        cost_estimate=cost(4 * LEN * LEN * cols, LEN * cols * 8, LEN * LEN),
        name="attend",
    )(ids, starts, widths, q, k, v, seg_col, seg_row)


def attend_back(plan, seq, ids, starts, widths, live, q, k, v, grads, logs, seg_col, seg_row):
    rows, cols = q.shape
    n_mp = plan.n_mp
    share = LEN // n_mp
    per = share // QB

    def kernel(ids_ref, start_ref, width_ref, live_ref, q_ref, k_ref, v_ref, col_ref, row_ref, log_ref, *refs):
        grad_refs, (dq_ref, dk_ref, dv_ref) = refs[:n_mp], refs[n_mp:]
        block = pl.program_id(0)
        step = seq * QBLOCKS + block
        masks = head_masks(cols)
        heads = len(masks)

        @pl.when(block == 0)
        def _():
            dk_ref[...] = jnp.zeros_like(dk_ref)
            dv_ref[...] = jnp.zeros_like(dv_ref)

        def body(window):
            start = pl.multiple_of(start_ref[step], QB)
            keys = pl.ds(start, window)
            k_win = k_ref[keys, :]
            v_win = v_ref[keys, :]
            other = (block // per) ^ ids_ref[1]
            at = pl.ds(pl.multiple_of(block % per * QB, QB), QB)
            g = grad_refs[0][at, :]
            for r in range(1, n_mp):
                g = jnp.where(other == r, grad_refs[r][at, :], g)
            q3 = spread_heads(q_ref[...], masks)
            g3 = spread_heads(g, masks)
            s = (dot(q3, k_win, 1, 1) * HEAD**-0.5).reshape(heads, QB, window)
            same = col_ref[...] == row_ref[0, :, keys]
            all_logs = log_ref[...]
            log = jnp.stack([all_logs[:, h : h + 1] for h in range(heads)])
            p = jnp.exp(jnp.where(same[None], s - log, MASK_FILL))
            dp = dot(g3, v_win, 1, 1).reshape(heads, QB, window)
            inner = jnp.sum(p * dp, axis=-1, keepdims=True)
            ds = (p * (dp - inner)).astype(BF16).reshape(heads * QB, window)
            p_low = p.astype(BF16).reshape(heads * QB, window)
            dv_ref[keys, :] += dot(p_low, g3, 0, 0)
            dk_ref[keys, :] += dot(ds, q3, 0, 0) * HEAD**-0.5
            dq_ref[...] = join_heads(dot(ds, k_win, 1, 0), masks) * HEAD**-0.5

        alive = live_ref[step]

        @pl.when(alive == 0)
        def _():
            dq_ref[...] = jnp.zeros_like(dq_ref)

        @pl.when(alive != 0)
        def _():
            by_window(width_ref, step, body)

    block, all_keys, row_spec = seq_specs(seq, cols)
    grad_spec = pl.BlockSpec((share, cols), lambda b, *_: (seq, 0))
    shape = jax.ShapeDtypeStruct((LEN, cols), F32)
    return pl.pallas_call(
        kernel,
        grid_spec=pltpu.PrefetchScalarGridSpec(
            num_scalar_prefetch=4,
            grid=(QBLOCKS,),
            in_specs=[block(cols), all_keys(cols), all_keys(cols), block(1), row_spec, pl.BlockSpec((QB, 128), lambda b, *_: (b, 0))]
            + [grad_spec] * n_mp,
            out_specs=[pl.BlockSpec((QB, cols), lambda b, *_: (b, 0)), whole((LEN, cols)), whole((LEN, cols))],
        ),
        out_shape=[shape, shape, shape],
        compiler_params=PARAMS,
        cost_estimate=cost(10 * LEN * LEN * cols, LEN * cols * 24, LEN * LEN),
        name="attend_back",
    )(ids, starts, widths, live, q, k, v, seg_col, seg_row, logs, *grads)


def key_windows(seg_ids):
    seg = seg_ids.reshape(-1, LEN)
    first = seg[:, ::QB]
    last = seg[:, QB - 1 :: QB]
    low = jnp.sum((seg[:, None, :] < first[:, :, None]).astype(jnp.int32), axis=2)
    high = jnp.sum((seg[:, None, :] <= last[:, :, None]).astype(jnp.int32), axis=2)
    base = low // QB * QB
    number = jnp.full(base.shape, len(WINDOWS) - 1, jnp.int32)
    start = jnp.zeros_like(base)
    for choice in range(len(WINDOWS) - 2, -1, -1):
        at = jnp.minimum(base, LEN - WINDOWS[choice])
        fits = high <= at + WINDOWS[choice]
        number = jnp.where(fits, choice, number)
        start = jnp.where(fits, at, start)
    live = (first != PAD_ID).astype(jnp.int32)
    return start.reshape(-1), number.reshape(-1), live.reshape(-1)


def project_back(plan, seq, ids, low, pq, pk, dq, dk, dv, w_grad, qk_pieces, v_pieces, gains, ones):
    rows, dim = low.shape
    cols = ones.shape[0]
    n_mp = plan.n_mp
    share = LEN // n_mp
    size = plan.block
    half = n_mp // 2

    def kernel(ids_ref, low_ref, pq_ref, pk_ref, dq_ref, dk_ref, dv_ref, gain_ref, ones_ref, qk_ref, v_in_ref, *rest):
        if w_grad is not None:
            base_ref, base_gain_ref = rest[:2]
            rest = rest[2:]
        keep_ref, send_ref, grad_ref, gains_ref, w_ref, sems = rest
        me = ids_ref[0]
        step = pl.program_id(0)

        def place(slot, count):
            def target(ref, i, group, other):
                rows_at = pl.ds(pl.multiple_of((me ^ group) * size, 16), size)
                return ref.at[i], w_ref.at[pl.ds(slot, count), rows_at, :]

            return target

        copies = copy_blocks([(qk_ref, qk_pieces[1])], place(0, 2), sems, 0)
        copies += copy_blocks([(v_in_ref, v_pieces[1])], place(2, 1), sems, len(copies))

        @pl.when(step == 0)
        def _():
            start_all(copies)
            if w_grad is None:
                grad_ref[...] = jnp.zeros_like(grad_ref)
                gains_ref[...] = jnp.zeros_like(gains_ref)
            else:
                grad_ref[...] = base_ref[...]
                gains_ref[...] = base_gain_ref[...]

        ones_block = ones_ref[...]

        def back(values, grad, gain, slot):
            normed, scale = head_parts(values, ones_block)
            gains_ref[slot, :, :] += jnp.sum((grad * normed).reshape(-1, 8, cols), axis=0)
            scaled = grad * gain
            first = head_mean(scaled, ones_block)
            second = head_mean(scaled * normed, ones_block)
            return ((scaled - first - normed * second) * scale).astype(BF16)

        gq = back(pq_ref[...], dq_ref[...], gain_ref[0:1, :], 0)
        gk = back(pk_ref[...], dk_ref[...], gain_ref[1:2, :], 1)
        gv = dv_ref[...].astype(BF16)
        x = low_ref[...]
        pl.when(step == 0)(lambda: wait_all(copies))
        terms = dot(gq, w_ref[0], 1, 1) + dot(gk, w_ref[1], 1, 1) + dot(gv, w_ref[2], 1, 1)
        terms = terms.astype(BF16)

        @pl.when(step < half)
        def _():
            keep_ref[...] = terms

        @pl.when(step >= half)
        def _():
            send_ref[...] = terms

        for p, g in enumerate((gq, gk, gv)):
            grad_ref[p] += dot(x, g, 0, 0)

    at = lambda i, ids_ref: ids_ref[1] ^ (i % half * 2 + i // half)
    far = lambda c: pl.BlockSpec((share, c), lambda i, ids_ref: (seq * n_mp + at(i, ids_ref), 0))
    near = lambda c: pl.BlockSpec((share, c), lambda i, ids_ref: (at(i, ids_ref), 0))
    w_shape, g_shape = (3, dim, cols), (2, 8, cols)
    base = [] if w_grad is None else list(w_grad)
    return pl.pallas_call(
        kernel,
        grid_spec=pltpu.PrefetchScalarGridSpec(
            num_scalar_prefetch=1,
            grid=(n_mp,),
            in_specs=[far(dim), far(cols), far(cols), near(cols), near(cols), near(cols), whole(gains.shape), whole(ones.shape), ANY, ANY]
            + [whole(b.shape) for b in base],
            out_specs=[
                pl.BlockSpec((None, share, dim), lambda i, *_: (jnp.minimum(i, half - 1), 0, 0)),
                pl.BlockSpec((None, share, dim), lambda i, *_: (jnp.maximum(i - half, 0), 0, 0)),
                whole(w_shape),
                whole(g_shape),
            ],
            scratch_shapes=[pltpu.VMEM(w_shape, BF16), pltpu.SemaphoreType.DMA((2 * plan.groups,))],
        ),
        out_shape=[
            jax.ShapeDtypeStruct((half, share, dim), BF16),
            jax.ShapeDtypeStruct((half, share, dim), BF16),
            jax.ShapeDtypeStruct(w_shape, F32),
            jax.ShapeDtypeStruct(g_shape, F32),
        ],
        compiler_params=PARAMS,
        cost_estimate=cost(12 * LEN * dim * cols, LEN * dim * 12),
        name="project_back",
    )(ids, low, pq, pk, dq, dk, dv, gains, ones, qk_pieces[0], v_pieces[0], *base)


def out_target(plan, me, out_ref):
    def target(ref, i, group, other):
        rows_at = pl.ds(pl.multiple_of((me ^ group) * plan.block, 16), plan.block)
        return ref.at[i, :, pl.ds(0, out_ref.shape[2])], out_ref.at[other, rows_at, :]

    return target


def wide_target(plan, me, mp, w_ref, source_col=None):
    width = w_ref.shape[1] // plan.n_mp

    def target(ref, i, group, other):
        rows_at = pl.ds(pl.multiple_of((me ^ group) * plan.block, 16), plan.block)
        cols_at = pl.ds(pl.multiple_of((mp ^ other) * width, 128), width)
        source = ref.at[i] if source_col is None else ref.at[i, :, pl.ds(source_col, width)]
        return source, w_ref.at[rows_at, cols_at]

    return target


def blocks_of(pieces):
    return sum(len(places) for _, places in pieces)


def feed_up(plan, ids, x, attended, params, oc, up, out_cols):
    rows, dim = x.shape
    cols = attended[0].shape[1]
    n_mp = plan.n_mp
    width = up[0][0].shape[2]
    hidden_size = n_mp * width
    block = 256

    def kernel(ids_ref, x_ref, *refs):
        a_refs, refs = refs[:n_mp], refs[n_mp:]
        norm_ref, oc_a, oc_b, up_a, up_b, mid_ref, low_ref, act_ref, der_ref, o_ref, u_ref, sems = refs
        me, mp = ids_ref[0], ids_ref[1]
        first = pl.program_id(0) == 0
        o_copies = copy_blocks([(oc_a, oc[0][1]), (oc_b, oc[1][1])], out_target(plan, me, o_ref), sems, 0)
        u_copies = copy_blocks([(up_a, up[0][1]), (up_b, up[1][1])], wide_target(plan, me, mp, u_ref), sems, len(o_copies))

        @pl.when(first)
        def _():
            start_all(o_copies)
            start_all(u_copies)
            wait_all(o_copies)

        middle = x_ref[...].astype(F32)
        for r in range(n_mp):
            middle = middle + dot(a_refs[r][...], o_ref[r, :, :cols], 1, 1)
        mid_ref[...] = middle
        normed, _ = norm_parts(middle)
        low = (normed * norm_ref[2:3, :] + norm_ref[3:4, :]).astype(BF16)
        low_ref[...] = low
        pl.when(first)(lambda: wait_all(u_copies))
        for c in range(n_mp):
            at = slice(c * width, (c + 1) * width)
            hidden = dot(low, u_ref[:, at], 1, 0)
            phi = 0.5 * (1.0 + lax.erf(hidden * (0.5**0.5)))
            act_ref[:, at] = (hidden * phi).astype(BF16)
            der_ref[:, at] = phi + hidden * (jnp.exp(-0.5 * hidden * hidden) * 0.3989422804014327)

    row = lambda c: pl.BlockSpec((block, c), lambda i, *_: (i, 0))
    shape = lambda c, t: jax.ShapeDtypeStruct((rows, c), t)
    return pl.pallas_call(
        kernel,
        grid_spec=pltpu.PrefetchScalarGridSpec(
            num_scalar_prefetch=1,
            grid=(rows // block,),
            in_specs=[row(dim)] + [row(cols)] * n_mp + [whole(params.shape)] + [ANY] * 4,
            out_specs=[row(dim), row(dim), row(hidden_size), row(hidden_size)],
            scratch_shapes=[
                pltpu.VMEM((n_mp, dim, out_cols), BF16),
                pltpu.VMEM((dim, hidden_size), BF16),
                pltpu.SemaphoreType.DMA((blocks_of(oc) + blocks_of(up),)),
            ],
        ),
        out_shape=[shape(dim, F32), shape(dim, BF16), shape(hidden_size, BF16), shape(hidden_size, F32)],
        compiler_params=PARAMS,
        cost_estimate=cost(2 * rows * dim * (hidden_size + dim), rows * hidden_size * 8, rows * hidden_size * 2),
        name="feed_up",
    )(ids, x, *attended, params, oc[0][0], oc[1][0], up[0][0], up[1][0])


def image_rows(seq_block, shape, axis):
    slot = lax.broadcasted_iota(jnp.int32, shape, axis)
    return slot, seq_block * IMG_SEQ


def feed_down(plan, ids, middle, active, seg_row, params, down):
    rows, dim = middle.shape
    n_mp = plan.n_mp
    hidden_size = active.shape[1]
    block = 256
    seqs = rows // block

    def kernel(ids_ref, mid_ref, act_ref, seg_ref, norm_ref, d_a, d_b, res_ref, block_ref, pool_ref, d_ref, sems):
        me, mp = ids_ref[0], ids_ref[1]
        seq = pl.program_id(0)
        copies = copy_blocks([(d_a, down[0][1]), (d_b, down[1][1])], wide_target(plan, me, mp, d_ref), sems, 0)

        @pl.when(seq == 0)
        def _():
            start_all(copies)
            wait_all(copies)

        result = mid_ref[...] + dot(act_ref[...], d_ref[...], 1, 1)
        res_ref[...] = result
        block_ref[...] = result.astype(BF16)
        normed, _ = norm_parts(result)
        final = normed * norm_ref[4:5, :] + norm_ref[5:6, :]
        probe = jnp.broadcast_to(norm_ref[6:7, :], (8, dim))
        score = lax.dot_general(
            probe, final, (((1,), (1,)), ((), ())), precision=lax.Precision.HIGHEST, preferred_element_type=F32
        )[0:1]
        slot = lax.broadcasted_iota(jnp.int32, (SLOTS, block), 0)
        member = (seg_ref[0] - seq * IMG_SEQ == slot) & (slot < IMG_SEQ)
        top = jnp.max(jnp.where(member, score, MASK_FILL), axis=1, keepdims=True)
        e = jnp.exp(jnp.where(member, score - top, MASK_FILL))
        e = jnp.where(member, e, 0.0)
        total = jnp.sum(e, axis=1, keepdims=True)
        low = final.astype(BF16)
        high = e.astype(BF16)
        rest = (e - high.astype(F32)).astype(BF16)
        pool_ref[:, :dim] = dot(high, low, 1, 0) + dot(rest, low, 1, 0)
        lane = lax.broadcasted_iota(jnp.int32, (SLOTS, 128), 1)
        pool_ref[:, dim:] = jnp.where(lane == 0, top, jnp.where(lane == 1, total, 0.0))

    row = lambda c: pl.BlockSpec((block, c), lambda i, *_: (i, 0))
    return pl.pallas_call(
        kernel,
        grid_spec=pltpu.PrefetchScalarGridSpec(
            num_scalar_prefetch=1,
            grid=(seqs,),
            in_specs=[row(dim), row(hidden_size), pl.BlockSpec((1, 1, block), lambda i, *_: (i, 0, 0)), whole(params.shape), ANY, ANY],
            out_specs=[row(dim), row(dim), pl.BlockSpec((SLOTS, dim + 128), lambda i, *_: (i, 0))],
            scratch_shapes=[pltpu.VMEM((dim, hidden_size), BF16), pltpu.SemaphoreType.DMA((blocks_of(down),))],
        ),
        out_shape=[
            jax.ShapeDtypeStruct((rows, dim), F32),
            jax.ShapeDtypeStruct((rows, dim), BF16),
            jax.ShapeDtypeStruct((seqs * SLOTS, dim + 128), F32),
        ],
        compiler_params=PARAMS,
        cost_estimate=cost(2 * rows * dim * hidden_size, rows * hidden_size * 4),
        name="feed_down",
    )(ids, middle, active, seg_row, params, down[0][0], down[1][0])


def combine_pools(plan, pool, bits, dim):
    other = plan.swap(pool, "mp", bits)
    lower = lax.axis_index("mp") & bits == 0
    first, second = jnp.where(lower, pool, other), jnp.where(lower, other, pool)
    top_a, top_b = first[:, dim : dim + 1], second[:, dim : dim + 1]
    top = jnp.maximum(top_a, top_b)
    weight_a, weight_b = jnp.exp(top_a - top), jnp.exp(top_b - top)
    rows = first[:, :dim] * weight_a + second[:, :dim] * weight_b
    total = first[:, dim + 1 : dim + 2] * weight_a + second[:, dim + 1 : dim + 2] * weight_b
    pad = jnp.zeros((pool.shape[0], pool.shape[1] - dim - 2), F32)
    return jnp.concatenate([rows, top, total, pad], axis=1)


def classify(plan, ids, pool, labels, images, oc, class_count, class_cols, source_col):
    slots, full = pool.shape
    dim = full - 128
    n_mp = plan.n_mp
    wide = n_mp * class_cols

    def kernel(ids_ref, pool_ref, label_ref, images_ref, c_a, c_b, grad_ref, stat_ref, loss_ref, cls_ref, c_ref, l_ref, sems):
        me, mp = ids_ref[0], ids_ref[1]
        copies = copy_blocks([(c_a, oc[0][1]), (c_b, oc[1][1])], wide_target(plan, me, mp, c_ref, source_col), sems, 0)
        start_all(copies)
        top = pool_ref[:, dim : dim + 1]
        total = pool_ref[:, dim + 1 : dim + 2]
        present = jnp.where(total > 0, 1.0, 0.0)
        safe = total + (1.0 - present)
        pooled = pool_ref[:, :dim] / safe
        low = pooled.astype(BF16)
        wait_all(copies)
        logits = dot(low, c_ref[...], 1, 0)
        column = lax.broadcasted_iota(jnp.int32, (slots, wide), 1)
        logits = jnp.where(column % class_cols < class_count, logits, MASK_FILL)
        row_top = jnp.max(logits, axis=1, keepdims=True)
        log_total = row_top + jnp.log(jnp.sum(jnp.exp(logits - row_top), axis=1, keepdims=True))
        chosen = jnp.where(column == label_ref[...], 1.0, 0.0)
        label_logit = jnp.sum(chosen * logits, axis=1, keepdims=True)
        loss = jnp.sum(present * (log_total - label_logit), axis=0, keepdims=True)
        loss_ref[...] = jnp.broadcast_to(loss, loss_ref.shape)
        scale = present / images_ref[0:1, 0:1]
        grad = ((jnp.exp(logits - log_total) - chosen) * scale).astype(BF16)
        l_ref[...] = grad
        row_grad = dot(grad, c_ref[...], 1, 1).astype(BF16)
        grad_ref[...] = row_grad
        inner = jnp.sum(row_grad.astype(F32) * pooled, axis=1, keepdims=True)
        lane = lax.broadcasted_iota(jnp.int32, (slots, 128), 1)
        stat_ref[...] = jnp.where(lane == 0, top, jnp.where(lane == 1, 1.0 / safe, jnp.where(lane == 2, inner, 0.0)))
        own = l_ref[:, pl.ds(pl.multiple_of(mp * class_cols, 128), class_cols)]
        grad_cls = dot(low, own, 0, 0)
        for g in range(plan.groups):
            r = g ^ me
            at = (r & 1) * (plan.groups // 2) + (r >> 1)
            cls_ref[at] = grad_cls[g * plan.block : (g + 1) * plan.block].astype(BF16)

    vmem = pl.BlockSpec(memory_space=pltpu.VMEM)
    return pl.pallas_call(
        kernel,
        in_specs=[pl.BlockSpec(memory_space=pltpu.SMEM), vmem, vmem, vmem, ANY, ANY],
        out_specs=[vmem] * 4,
        out_shape=[
            jax.ShapeDtypeStruct((slots, dim), BF16),
            jax.ShapeDtypeStruct((slots, 128), F32),
            jax.ShapeDtypeStruct((8, 128), F32),
            jax.ShapeDtypeStruct((plan.groups, plan.block, class_cols), BF16),
        ],
        scratch_shapes=[
            pltpu.VMEM((dim, wide), BF16),
            pltpu.VMEM((slots, wide), BF16),
            pltpu.SemaphoreType.DMA((blocks_of(oc),)),
        ],
        compiler_params=PARAMS,
        cost_estimate=cost(6 * slots * dim * wide, dim * wide * 2),
        name="classify",
    )(ids, pool, labels, images, oc[0][0], oc[1][0])


def split_three(values):
    high = values.astype(BF16)
    rest = values - high.astype(F32)
    middle = rest.astype(BF16)
    low = (rest - middle.astype(F32)).astype(BF16)
    return high, middle, low


def feed_back(plan, ids, result, middle, slope, row_grads, stats, seg_col, params, oc, up, down, out_cols, cols):
    rows, dim = result.shape
    n_mp = plan.n_mp
    width = up[0][0].shape[2]
    hidden_size = n_mp * width
    block = 256

    def kernel(ids_ref, res_ref, mid_ref, der_ref, pg_ref, stat_ref, seg_ref, norm_ref, oc_a, oc_b, u_a, u_b, d_a, d_b, *refs):
        rlow_ref, hlow_ref, mlow_ref, mgrad_ref, *refs = refs
        ag_refs, (sums_ref, o_ref, u_ref, d_ref, sems) = refs[:n_mp], refs[n_mp:]
        me, mp = ids_ref[0], ids_ref[1]
        seq = pl.program_id(0)
        d_copies = copy_blocks([(d_a, down[0][1]), (d_b, down[1][1])], wide_target(plan, me, mp, d_ref), sems, 0)
        u_copies = copy_blocks([(u_a, up[0][1]), (u_b, up[1][1])], wide_target(plan, me, mp, u_ref), sems, len(d_copies))
        o_copies = copy_blocks(
            [(oc_a, oc[0][1]), (oc_b, oc[1][1])], out_target(plan, me, o_ref), sems, len(d_copies) + len(u_copies)
        )

        @pl.when(seq == 0)
        def _():
            start_all(d_copies)
            start_all(u_copies)
            start_all(o_copies)
            sums_ref[...] = jnp.zeros_like(sums_ref)

        normed, scale = norm_parts(res_ref[...])
        gain, probe = norm_ref[4:5, :], norm_ref[6:7, :]
        final = normed * gain + norm_ref[5:6, :]
        score = jnp.sum(final * probe, axis=1, keepdims=True)
        slot = lax.broadcasted_iota(jnp.int32, (block, SLOTS), 1)
        member = (seg_ref[...] - seq * IMG_SEQ == slot) & (slot < IMG_SEQ)
        held = jnp.max(jnp.where(member, 1.0, 0.0), axis=1, keepdims=True)
        one = jnp.where(member, 1.0, 0.0).astype(BF16)
        row_stat = sum(dot(one, part, 1, 0) for part in split_three(stat_ref[...]))
        top, inverse, inner = row_stat[:, 0:1], row_stat[:, 1:2], row_stat[:, 2:3]
        share = jnp.exp(jnp.where(held > 0, score - top, 0.0)) * inverse * held
        row_grad = dot(one, pg_ref[...], 1, 0)
        share_low = share.astype(BF16).astype(F32)
        share_grad = jnp.sum(row_grad * final.astype(BF16).astype(F32), axis=1, keepdims=True)
        score_grad = share * (share_grad - inner)
        final_grad = share_low * row_grad + score_grad * probe
        add = lambda slot, value: sums_ref.at[slot].__setitem__(
            ..., sums_ref[slot] + jnp.sum(value.reshape(-1, 8, dim), axis=0)
        )
        add(4, score_grad * final)
        add(2, final_grad * normed)
        add(3, final_grad)
        result_grad = norm_back(final_grad, normed, scale, gain)
        result_low = result_grad.astype(BF16)
        rlow_ref[...] = result_low
        pl.when(seq == 0)(lambda: (wait_all(d_copies), wait_all(u_copies), wait_all(o_copies)) and None)
        second = jnp.zeros((block, dim), F32)
        for c in range(n_mp):
            at = slice(c * width, (c + 1) * width)
            hidden_low = (der_ref[:, at] * dot(result_low, d_ref[:, at], 1, 0)).astype(BF16)
            hlow_ref[:, at] = hidden_low
            second = second + dot(hidden_low, u_ref[:, at], 1, 1)
        normed_two, scale_two = norm_parts(mid_ref[...])
        add(0, second * normed_two)
        add(1, second)
        middle_grad = result_grad + norm_back(second, normed_two, scale_two, norm_ref[2:3, :])
        mgrad_ref[...] = middle_grad
        middle_low = middle_grad.astype(BF16)
        mlow_ref[...] = middle_low
        for r in range(n_mp):
            ag_refs[r][...] = dot(middle_low, o_ref[r, :, :cols], 1, 0).astype(BF16)

    row = lambda c: pl.BlockSpec((block, c), lambda i, *_: (i, 0))
    shape = lambda c, t: jax.ShapeDtypeStruct((rows, c), t)
    slots = lambda c: pl.BlockSpec((SLOTS, c), lambda i, *_: (i, 0))
    return pl.pallas_call(
        kernel,
        grid_spec=pltpu.PrefetchScalarGridSpec(
            num_scalar_prefetch=1,
            grid=(rows // block,),
            in_specs=[row(dim), row(dim), row(hidden_size), slots(dim), slots(128), row(1), whole(params.shape)] + [ANY] * 6,
            out_specs=[row(dim), row(hidden_size), row(dim), row(dim)] + [row(cols)] * n_mp + [whole((5, 8, dim))],
            scratch_shapes=[
                pltpu.VMEM((n_mp, dim, out_cols), BF16),
                pltpu.VMEM((dim, hidden_size), BF16),
                pltpu.VMEM((dim, hidden_size), BF16),
                pltpu.SemaphoreType.DMA((blocks_of(oc) + blocks_of(up) + blocks_of(down),)),
            ],
        ),
        out_shape=[shape(dim, BF16), shape(hidden_size, BF16), shape(dim, BF16), shape(dim, F32)]
        + [shape(cols, BF16)] * n_mp
        + [jax.ShapeDtypeStruct((5, 8, dim), F32)],
        compiler_params=PARAMS,
        cost_estimate=cost(2 * rows * dim * (2 * hidden_size + dim), rows * hidden_size * 8),
        name="feed_back",
    )(ids, result, middle, slope, row_grads, stats, seg_col, params, oc[0][0], oc[1][0], up[0][0], up[1][0], down[0][0], down[1][0])


def weight_grad(plan, ids, left, right, name):
    rows, dim = left.shape
    n_mp = plan.n_mp
    parts = right if isinstance(right, list) else None
    width = parts[0].shape[1] if parts else right.shape[1] // n_mp
    out_width = -(-width // 128) * 128
    half = n_mp // 2
    far = plan.groups // 2

    def kernel(ids_ref, left_ref, *refs):
        right_refs, (keep_ref, send_ref) = refs[:-2], refs[-2:]
        me = ids_ref[0]
        step = pl.program_id(0)

        def body(rhs_ref, out_ref):
            grad = dot(left_ref[...], rhs_ref[...], 0, 0).astype(BF16)
            if out_width != width:
                grad = jnp.concatenate([grad, jnp.zeros((dim, out_width - width), BF16)], axis=1)
            for g in range(plan.groups):
                r = g ^ me
                out_ref[r & 1, r >> 1] = grad[g * plan.block : (g + 1) * plan.block]

        for i in range(n_mp):
            out_ref = keep_ref if i < half else send_ref
            if parts:
                rhs_ref = right_refs[i % half * 2 + i // half]
                pl.when(step == i)(functools.partial(body, rhs_ref, out_ref))
        if not parts:
            pl.when(step < half)(lambda: body(right_refs[0], keep_ref))
            pl.when(step >= half)(lambda: body(right_refs[0], send_ref))

    at = lambda i, ids_ref: ids_ref[1] ^ (i % half * 2 + i // half)
    rights = parts or [right]
    if parts:
        right_specs = [whole((rows, width))] * n_mp
    else:
        right_specs = [pl.BlockSpec((rows, width), lambda i, ids_ref: (0, at(i, ids_ref)))]
    out_block = (None, 2, far, plan.block, out_width)
    out = jax.ShapeDtypeStruct((half, 2, far, plan.block, out_width), BF16)
    return pl.pallas_call(
        kernel,
        grid_spec=pltpu.PrefetchScalarGridSpec(
            num_scalar_prefetch=1,
            grid=(n_mp,),
            in_specs=[whole((rows, dim))] + right_specs,
            out_specs=[
                pl.BlockSpec(out_block, lambda i, *_: (jnp.minimum(i, half - 1), 0, 0, 0, 0)),
                pl.BlockSpec(out_block, lambda i, *_: (jnp.maximum(i - half, 0), 0, 0, 0, 0)),
            ],
        ),
        out_shape=[out, out],
        compiler_params=PARAMS,
        cost_estimate=cost(2 * rows * dim * width * n_mp, 2 * dim * width * n_mp),
        name=name,
    )(ids, left, *rights)


def assemble(plan, ids, own, across, mates, dtype, name):
    seqs, share, dim = own.shape
    n_mp = plan.n_mp

    def kernel(ids_ref, own_ref, across_ref, mate_ref, out_ref):
        r = pl.program_id(1)
        value = jnp.where(r == 0, own_ref[...], jnp.where(r == 2, across_ref[...], mate_ref[...]))
        out_ref[...] = value.astype(dtype)

    same = pl.BlockSpec((None, share, dim), lambda s, r, *_: (s, 0, 0))
    return pl.pallas_call(
        kernel,
        grid_spec=pltpu.PrefetchScalarGridSpec(
            num_scalar_prefetch=1,
            grid=(seqs, n_mp),
            in_specs=[same, same, pl.BlockSpec((None, None, share, dim), lambda s, r, *_: (r // 2, s, 0, 0))],
            out_specs=pl.BlockSpec((share, dim), lambda s, r, ids_ref: (s * n_mp + (ids_ref[1] ^ r), 0)),
        ),
        out_shape=jax.ShapeDtypeStruct((seqs * n_mp * share, dim), dtype),
        compiler_params=PARAMS,
        cost_estimate=cost(0, seqs * n_mp * share * dim * 8),
        name=name,
    )(ids, own, across, mates)


def adam_update(weight, moment_one, moment_two, gradient, step_rate, decay_rate):
    fresh_one = BETA_ONE * moment_one + (1.0 - BETA_ONE) * gradient
    fresh_two = BETA_TWO * moment_two + (1.0 - BETA_TWO) * gradient * gradient
    one_hat = fresh_one / (1.0 - BETA_ONE**STEP)
    two_hat = fresh_two / (1.0 - BETA_TWO**STEP)
    updated = weight - step_rate * (one_hat / (jnp.sqrt(two_hat) + ADAM_EPS) + decay_rate * weight)
    return (fresh_one, fresh_two, updated)


def shards(
    tokens,
    seg_ids,
    labels,
    w_qkv,
    m_qkv,
    v_qkv,
    w_out,
    m_out,
    v_out,
    w_up,
    m_up,
    v_up,
    w_down,
    m_down,
    v_down,
    w_cls,
    m_cls,
    v_cls,
    norm_params,
    m_norm,
    v_norm,
    qk_gain,
    m_qk,
    v_qk,
    *,
    n_dp,
    n_mp,
):
    dp, mp = lax.axis_index("dp"), lax.axis_index("mp")
    group_rows, dim = tokens.shape
    plan = Plan(n_dp, n_mp, dim)
    seqs = group_rows // LEN
    share = LEN // n_mp
    rows = seqs * share
    cols = w_qkv.shape[2]
    classes = w_cls.shape[1]
    class_cols = -(-classes // 128) * 128
    out_cols = -(-cols // 128) * 128
    ids = jnp.stack([dp // plan.merge, mp]).astype(jnp.int32)

    qkv_low = plan.merged(w_qkv.astype(BF16), 1)
    qk_pieces = plan.gather(qkv_low[:2], "zy")
    v_pieces = plan.gather(qkv_low[2:], "yz")

    new_image = seg_ids != jnp.concatenate([jnp.full((1,), -1, jnp.int32), seg_ids[:-1]])
    count = jnp.sum((new_image & (seg_ids != PAD_ID)).astype(F32))
    dim_part, head_part = norm_params.shape[1], qk_gain.shape[2]
    small = jnp.zeros((16, dim), F32)
    small = lax.dynamic_update_slice(small, lax.reduce_precision(norm_params, 8, 7), (0, dp * dim_part))
    gain_row = jnp.zeros((2, cols // HEAD, HEAD), F32)
    gain_row = lax.dynamic_update_slice(gain_row, lax.reduce_precision(qk_gain, 8, 7), (0, 0, dp * head_part))
    small = lax.dynamic_update_slice(small, gain_row.reshape(2, cols), (8, 0))
    small = lax.dynamic_update_slice(small, jnp.broadcast_to(count, (1, 1)), (10, 0))
    small = plan.total(small, "dp")
    params, gains, image_total = small[:8], small[8:10, :cols], small[10, 0]

    low_up = plan.merged(w_up.astype(BF16), 0)
    low_down = plan.merged(w_down.T.astype(BF16), 0)
    low_oc = plan.merged(
        jnp.concatenate(
            [
                jnp.pad(w_out.T.astype(BF16), ((0, 0), (0, out_cols - cols))),
                jnp.pad(w_cls.astype(BF16), ((0, 0), (0, class_cols - classes))),
            ],
            axis=1,
        ),
        0,
    )
    oc = plan.both_cores(plan.gather(low_oc, "xyz"))
    up = plan.both_cores(plan.gather(low_up, "zyx"))
    down = plan.both_cores(plan.gather(low_down, "zxy"))

    head_of = jnp.arange(cols) // HEAD
    ones = jnp.where(head_of[:, None] == head_of[None, :], 1.0 / HEAD, 0.0).astype(BF16)
    starts, widths, live = key_windows(seg_ids)
    seg_col = seg_ids.reshape(group_rows, 1)
    seg_row = seg_ids.reshape(-1, 1, LEN)
    normed_low, pq, pk, q, k, v = project(plan, ids, tokens, qk_pieces, v_pieces, params, gains, ones)
    logs, received = [], []
    for s in range(seqs):
        *parts, log = attend(plan, s, ids, starts, widths, q, k, v, seg_col, seg_row)
        logs.append(log)
        received.append([parts[0]] + [plan.swap(parts[r], "mp", r) for r in range(1, n_mp)])
    attended = [jnp.concatenate([received[s][r] for s in range(seqs)], axis=0) for r in range(n_mp)]

    own = lambda a: lax.dynamic_slice_in_dim(a.reshape((seqs, n_mp, share) + a.shape[1:]), mp, 1, 1)
    x = own(tokens).reshape(rows, dim)
    seg = own(seg_ids).reshape(rows)
    middle, second_low, active, slope = feed_up(plan, ids, x, attended, params, oc, up, out_cols)
    result, block_rows, pool = feed_down(plan, ids, middle, active, seg.reshape(seqs, 1, share), params, down)

    def spread(part):
        across = plan.swap(part, "mp", 2)
        return across, plan.swap(jnp.stack([part, across]), "mp", 1)

    block_rows = block_rows.reshape(seqs, share, dim)
    block_across, block_mates = spread(block_rows)
    block_out = assemble(plan, ids, block_rows, block_across, block_mates, BF16, "block_out")

    pool = combine_pools(plan, combine_pools(plan, pool, 1, dim), 2, dim)
    slot_label = labels.reshape(seqs, IMG_SEQ)
    slot_label = slot_label // classes * class_cols + slot_label % classes
    slot_label = jnp.pad(slot_label, ((0, 0), (0, SLOTS - IMG_SEQ)), constant_values=-1).reshape(seqs * SLOTS, 1)
    images = jnp.broadcast_to(image_total, (8, 128))
    row_grads, stats, loss, cls_blocks = classify(plan, ids, pool, slot_label, images, oc, classes, class_cols, out_cols)
    mean_loss = plan.total(loss, "dp")[0, 0] / image_total

    result_low, hidden_low, middle_low, middle_grad, *rest = feed_back(
        plan, ids, result, middle, slope, row_grads, stats, seg.reshape(rows, 1), params, oc, up, down, out_cols, cols
    )
    grads, sums = rest[:n_mp], rest[n_mp]
    grad_parts = [grads[0]] + [plan.swap(grads[r], "mp", r) for r in range(1, n_mp)]
    down_keep, down_send = weight_grad(plan, ids, result_low, active, "grad_down")
    grad_down = plan.scatter(down_keep, down_send, "yxz").T
    up_keep, up_send = weight_grad(plan, ids, second_low, hidden_low, "grad_up")
    grad_up = plan.scatter(up_keep, up_send, "xyz")
    out_keep, out_send = weight_grad(plan, ids, middle_low, attended, "grad_out")
    out_sum = out_keep.astype(F32) + plan.swap(out_send, "mp", 1).astype(F32)
    out_sum = out_sum[0] + plan.swap(out_sum[1].astype(BF16), "mp", 2).astype(F32)
    cls_blocks = cls_blocks.reshape(out_sum.shape[:3] + (class_cols,)).astype(F32)
    both = plan.scatter_rest(jnp.concatenate([out_sum, cls_blocks], axis=3), "yz", "yz", 0)
    grad_out, grad_cls = both[:, :cols].T, both[:, out_cols : out_cols + classes]

    w_grad = None
    norm_one = norm_parts(x.astype(F32))
    first_sums = []
    input_rows, input_across, input_mates = [], [], []
    for s in range(seqs):
        dq, dk, dv = attend_back(plan, s, ids, starts, widths, live, q, k, v, grad_parts, logs[s], seg_col, seg_row)
        keep, send, *w_grad = project_back(
            plan, s, ids, normed_low, pq, pk, dq, dk, dv, w_grad, qk_pieces, v_pieces, gains, ones
        )
        joint = keep.astype(F32) + plan.swap(send, "mp", 1).astype(F32)
        first = joint[0] + plan.swap(joint[1].astype(BF16), "mp", 2).astype(F32)
        at = slice(s * share, (s + 1) * share)
        normed, scale = norm_one[0][at], norm_one[1][at]
        first_sums.append(jnp.stack([jnp.sum(first * normed, axis=0), jnp.sum(first, axis=0)]))
        part = (middle_grad[at] + norm_back(first, normed, scale, params[0:1])).astype(BF16)
        across, mates = spread(part)
        input_rows.append(part)
        input_across.append(across)
        input_mates.append(mates)
    input_grad = assemble(
        plan, ids, jnp.stack(input_rows), jnp.stack(input_across), jnp.stack(input_mates, axis=1), F32, "input_grad"
    )

    grad_w, gain_parts = w_grad
    order = jnp.arange(plan.groups, dtype=jnp.int32)
    order = (order % (plan.groups // 2) * 2 + order // (plan.groups // 2)) ^ ids[0]
    qkv_blocks = jnp.take(grad_w.reshape(3, plan.groups, plan.block, cols), order, axis=1)
    qkv_blocks = qkv_blocks.transpose(1, 0, 2, 3).reshape(2, plan.groups // 2, 3, plan.block, cols)
    grad_qkv = plan.scatter_rest(qkv_blocks, "yz", "yz", 1)

    sums = jnp.sum(sums, axis=1)
    first_sum = sum(first_sums)
    norm_grads = plan.total(jnp.concatenate([first_sum, sums, jnp.zeros((1, dim), F32)], axis=0), "mp")
    qk_grads = jnp.sum(gain_parts, axis=1)
    qk_grads = jnp.pad(qk_grads, ((0, 6), (0, dim - cols)))
    small_grads = plan.total(jnp.concatenate([norm_grads, qk_grads], axis=0), "dp")
    norm_part = lax.dynamic_slice(small_grads, (0, dp * dim_part), (7, dim_part))
    qk_part = lax.dynamic_slice_in_dim(small_grads[8:10, :cols].reshape(2, cols // HEAD, HEAD), dp * head_part, head_part, 2)
    reduced = (grad_qkv, grad_out, grad_up, grad_down, grad_cls, norm_part, qk_part)
    groups = (
        (w_qkv, m_qkv, v_qkv, MATRIX_RATE, MATRIX_DECAY),
        (w_out, m_out, v_out, MATRIX_RATE, MATRIX_DECAY),
        (w_up, m_up, v_up, MATRIX_RATE, MATRIX_DECAY),
        (w_down, m_down, v_down, MATRIX_RATE, MATRIX_DECAY),
        (w_cls, m_cls, v_cls, MATRIX_RATE, MATRIX_DECAY),
        (norm_params, m_norm, v_norm, GAIN_RATE, 0.0),
        (qk_gain, m_qk, v_qk, GAIN_RATE, 0.0),
    )
    outputs = [block_out, input_grad, mean_loss]
    for number, group in enumerate(groups):
        fresh_one, fresh_two, updated = adam_update(group[0], group[1], group[2], reduced[number], group[3], group[4])
        if number == 5:
            outputs = outputs + [fresh_one, fresh_two[:6], fresh_two[6], updated]
        else:
            outputs = outputs + [fresh_one, fresh_two, updated]
    return tuple(outputs)


def solution(mesh):
    rows_cols = (P("mp", "dp"),) * 3
    cols_rows = (P("dp", "mp"),) * 3
    qkv_spec = (P(None, "dp", "mp"),) * 3
    qk_spec = (P(None, "mp", "dp"),) * 3
    norm_spec = P(None, "dp")
    in_specs = (
        (P("dp", None), P("dp"), P("dp")) + qkv_spec + rows_cols + cols_rows + rows_cols + cols_rows + (norm_spec,) * 3 + qk_spec
    )
    out_specs = (
        (P("dp", None), P("dp", None), P())
        + qkv_spec
        + rows_cols
        + cols_rows
        + rows_cols
        + cols_rows
        + (norm_spec, norm_spec, P("dp"), norm_spec)
        + qk_spec
    )
    body = functools.partial(shards, n_dp=mesh.shape["dp"], n_mp=mesh.shape["mp"])
    return jax.shard_map(body, mesh=mesh, in_specs=in_specs, out_specs=out_specs, check_vma=False)
```

```python
import functools

import jax
import jax.numpy as jnp
from jax import lax
from jax.experimental import pallas as pl
from jax.experimental.pallas import tpu as pltpu
from jax.sharding import PartitionSpec as P

LEN = 1024
STEP = 10
SEQ_DEV = 3
IMG_DEV = 180
PAD_ID = 180

NORM_EPS = 1e-06
MASK_FILL = -1000000000.0
BETA_ONE = 0.9
BETA_TWO = 0.999
ADAM_EPS = 1e-08
MATRIX_RATE = 0.1
MATRIX_DECAY = 0.1
GAIN_RATE = 0.8

HEAD = 64
QB = 128
QBLOCKS = LEN // QB
WINDOWS = (384, 640, 1024)
F32 = jnp.float32
BF16 = jnp.bfloat16
VMEM_LIMIT = 56 * 1024 * 1024
IMG_SEQ = 60
SLOTS = 64
ANY = pl.BlockSpec(memory_space=pl.ANY)
PARAMS = pltpu.CompilerParams(vmem_limit_bytes=VMEM_LIMIT)


def dot(a, b, ca, cb):
    return lax.dot_general(a, b, (((ca,), (cb,)), ((), ())), preferred_element_type=F32)


def head_mean(values, ones_block):
    high = values.astype(BF16)
    rest = (values - high.astype(F32)).astype(BF16)
    return dot(high, ones_block, 1, 0) + dot(rest, ones_block, 1, 0)


def norm_parts(values):
    centre = values - jnp.mean(values, axis=-1, keepdims=True)
    spread = jnp.mean(centre * centre, axis=-1, keepdims=True)
    scale = lax.rsqrt(spread + NORM_EPS)
    return centre * scale, scale


def norm_back(grad, normed, scale, gain):
    scaled = grad * gain
    first = jnp.mean(scaled, axis=-1, keepdims=True)
    second = jnp.mean(scaled * normed, axis=-1, keepdims=True)
    return (scaled - first - normed * second) * scale


def head_parts(values, ones_block):
    centre = values - head_mean(values, ones_block)
    scale = lax.rsqrt(head_mean(centre * centre, ones_block) + NORM_EPS)
    return centre * scale, scale


def cost(flops, read, exps=0):
    return pl.CostEstimate(flops=int(flops), bytes_accessed=int(read), transcendentals=int(exps))


def whole(shape):
    return pl.BlockSpec(tuple(shape), lambda *_: (0,) * len(shape))


class Plan:
    def __init__(self, n_dp, n_mp, dim):
        self.n_dp, self.n_mp = n_dp, n_mp
        self.merge = 1 if dim // n_dp % 16 == 0 else 2
        self.groups = n_dp // self.merge
        self.block = dim // self.groups
        self.far = [2 * k for k in range(1, self.groups // 2)]

    def swap(self, value, axis, bits):
        size = self.n_dp if axis == "dp" else self.n_mp
        return lax.ppermute(value, axis, [(i, i ^ bits) for i in range(size)])

    def group_swap(self, value, bits):
        return self.swap(value, "dp", bits * self.merge)

    def merged(self, value, dim):
        if self.merge == 1:
            return value
        other = self.swap(value, "dp", 1)
        even = lax.axis_index("dp") % 2 == 0
        first, second = jnp.where(even, value, other), jnp.where(even, other, value)
        return jnp.concatenate([first, second], axis=dim)

    def unmerged(self, value, dim):
        if self.merge == 1:
            return value
        half = value.shape[dim] // 2
        me = lax.axis_index("dp") % 2
        mine = lax.dynamic_slice_in_dim(value, me * half, half, dim)
        theirs = lax.dynamic_slice_in_dim(value, (1 - me) * half, half, dim)
        return mine + self.swap(theirs, "dp", 1)

    def core_sum(self, keep, send):
        return keep.astype(F32) + self.swap(send, "mp", 1).astype(F32)

    def scatter_step(self, value, step, at):
        low = value.astype(BF16)
        total = lax.index_in_dim(value, 0, at, keepdims=False)
        for k in range(1, value.shape[at]):
            part = lax.index_in_dim(low, k, at, keepdims=False)
            if step == "x":
                got = self.swap(part, "mp", 2)
            else:
                got = self.group_swap(part, k if step == "y" else 2 * k)
            total = total + got.astype(F32)
        return total

    def total(self, value, axis):
        size = self.n_dp if axis == "dp" else self.n_mp
        bits = 1
        while bits < size:
            value = value + self.swap(value, axis, bits)
            bits *= 2
        return value


MESH = pl.DeviceIdType.MESH


class Chain:
    def __init__(self, region, order, lines):
        self.region, self.order, self.lines = region, order, lines
        self.steps = [s for step in order for s in ([("z", t) for t in range(1, lines)] if step == "z" else [(step, 0)])]
        self.copies = sum({"z": 2, "c": 2}.get(s[0], 1) for s in self.steps)


class Gatherer:
    def __init__(self, plan, send_sems, recv_sems):
        self.plan, self.send_sems, self.recv_sems = plan, send_sems, recv_sems
        self.dp, self.mp = lax.axis_index("dp"), lax.axis_index("mp")
        self.pair = self.dp % plan.merge
        group = self.dp // plan.merge
        self.z, self.y = group // 2, group % 2
        self.x, self.core = self.mp // 2, self.mp % 2
        self.lines = plan.groups // 2
        self.used = 0
        self.pending = []

    def device(self, z, y, x, core):
        return ((z * 2 + y) * self.plan.merge + self.pair, x * 2 + core)

    def here(self):
        return self.z, self.y, self.x, self.core

    def meet(self, barrier):
        z, y, x, core = self.here()
        for other in ((z, 1 - y, x, core), (z, y, 1 - x, core), (z, y, x, 1 - core)):
            pl.semaphore_signal(barrier, inc=1, device_id=self.device(*other), device_id_type=MESH)

        @pl.when(z > 0)
        def _():
            pl.semaphore_signal(barrier, inc=1, device_id=self.device(z - 1, y, x, core), device_id_type=MESH)

        @pl.when(z < self.lines - 1)
        def _():
            pl.semaphore_signal(barrier, inc=1, device_id=self.device(z + 1, y, x, core), device_id_type=MESH)

        pl.semaphore_wait(barrier, 3 + jnp.where(z > 0, 1, 0) + jnp.where(z < self.lines - 1, 1, 0))

    def plan_step(self, chain, number):
        step, hop = chain.steps[number]
        z, y, x, core = self.here()
        done = [s for s in chain.order[: chain.order.index(step)]]
        span = lambda axis, at: None if axis in done else at
        spot = dict(z=span("z", z), y=span("y", y), x=span("x", x), core=core)
        if step == "z":
            lines = self.lines
            out = []
            for sign in (1, -1):
                from_z = z - sign * (hop - 1)
                to_z = z + sign
                got_z = z - sign * hop
                inside = lambda v: (v >= 0) & (v < lines)
                clip = lambda v: jnp.clip(v, 0, lines - 1)
                out.append(
                    (
                        inside(from_z) & inside(to_z),
                        chain.region(**{**spot, "z": clip(from_z)}),
                        self.device(clip(to_z), y, x, core),
                        inside(got_z),
                    )
                )
            return out
        if step == "c":
            return [
                (None, chain.region(**{**spot, "x": side}), self.device(z, y, x, 1 - core), None) for side in (0, 1)
            ]
        other = dict(y=(z, 1 - y, x, core), x=(z, y, 1 - x, core))[step]
        return [(None, chain.region(**spot), self.device(*other), None)]

    def start(self, chain, number, source=None):
        records = []
        for send_if, region, device, recv_if in self.plan_step(chain, number):
            sems = dict(send_sem=self.send_sems.at[self.used], recv_sem=self.recv_sems.at[self.used])
            self.used += 1
            src = region if source is None else source
            out = pltpu.make_async_remote_copy(src_ref=src, dst_ref=region, device_id=device, device_id_type=MESH, **sems)
            if send_if is None:
                out.start()
            else:
                pl.when(send_if)(out.start)
            records.append((send_if, out, recv_if))
        self.pending += [(c, o) for c, o, _ in records]
        return records

    @staticmethod
    def arrive(records):
        for _, out, recv_if in records:
            if recv_if is None:
                out.wait_recv()
            else:
                pl.when(recv_if)(out.wait_recv)

    def finish(self):
        for send_if, out in self.pending:
            if send_if is None:
                out.wait_send()
            else:
                pl.when(send_if)(out.wait_send)


def gather_project(plan, tokens, qkv_block, up_block, down_block, out_block, cls_block, small_block, ones):
    rows, dim = tokens.shape
    cols = ones.shape[0]
    n_mp, merge, size = plan.n_mp, plan.merge, plan.block
    lines = plan.groups // 2
    width = up_block.shape[1]
    out_cols, class_cols = out_block.shape[1], cls_block.shape[1]
    half = width // 2
    block = 512
    blocks = rows // block
    dim_part = dim // plan.n_dp
    head_part = HEAD // plan.n_dp

    orders = [("w_qk", "zy"), ("w_v", "yz"), ("small", "zy"), ("up0", "zyxc"), ("up1", "zxyc"), ("out", "zyxc")]
    orders += [("down0", "zyxc"), ("down1", "zxyc"), ("cls", "xyzc")]
    sizes = {name: Chain(None, order, lines).copies for name, order in orders}
    n_sems = sum(sizes.values())

    def kernel(x_ref, qkv_in, up_in, down_in, out_in, cls_in, small_in, ones_ref, *refs):
        low_ref, pq_ref, pk_ref, q_ref, k_ref, v_ref, w_ref, up_ref, down_ref, o_ref, c_ref, norm_ref, gain_ref, image_ref = refs[:14]
        w_buf, small_buf, low_buf, pq_buf, pk_buf, q_buf, k_buf, v_buf, send_sems, recv_sems, own_sems, out_sems = refs[14:]
        g = Gatherer(plan, send_sems, recv_sems)
        z, y, x, core = g.here()
        everything = slice(None)

        def at(v):
            return everything if v is None else v

        def wide(ref, first, count):
            columns = pl.ds(first, count)
            return lambda z, y, x, core: ref.at[at(x), core, at(z), at(y), :, columns]

        regions = dict(
            w_qk=lambda z, y, x, core: w_buf.at[pl.ds(0, 2), at(z), at(y)],
            w_v=lambda z, y, x, core: w_buf.at[pl.ds(2, 1), at(z), at(y)],
            small=lambda z, y, x, core: small_buf.at[at(z), at(y)],
            up0=wide(up_ref, 0, half),
            up1=wide(up_ref, half, half),
            down0=wide(down_ref, 0, half),
            down1=wide(down_ref, half, half),
            out=wide(o_ref, 0, out_cols),
            cls=wide(c_ref, 0, class_cols),
        )
        chains = {name: Chain(regions[name], order, lines) for name, order in orders}
        sources = dict(
            w_qk=qkv_in.at[pl.ds(0, 2)],
            w_v=qkv_in.at[pl.ds(2, 1)],
            small=small_in,
            up0=up_in.at[:, pl.ds(0, half)],
            up1=up_in.at[:, pl.ds(half, half)],
            down0=down_in.at[:, pl.ds(0, half)],
            down1=down_in.at[:, pl.ds(half, half)],
            out=out_in,
            cls=cls_in,
        )
        own = {}
        for i, (name, _) in enumerate(orders):
            own[name] = pltpu.make_async_copy(sources[name], regions[name](z, y, x, core), own_sems.at[i])
            own[name].start()
        live, reached = {}, {}

        def begin(name):
            live[name] = g.start(chains[name], 0, source=sources[name])
            reached[name] = 0

        def advance(*names):
            for name in names:
                if reached[name] == len(chains[name].steps):
                    continue
                if reached[name] == 0:
                    own[name].wait()
                g.arrive(live[name])
                reached[name] += 1
                if reached[name] < len(chains[name].steps):
                    live[name] = g.start(chains[name], reached[name])

        g.meet(pltpu.get_barrier_semaphore())
        for name in ("small", "w_qk", "w_v", "cls"):
            begin(name)
        hops = len(chains["small"].steps)
        for _ in range(hops - 1):
            advance("small", "w_qk", "w_v")
        advance("small", "cls")
        begin("up0")
        begin("up1")
        begin("out")

        lane = lax.broadcasted_iota(jnp.int32, (128, dim), 0)
        column = lax.broadcasted_iota(jnp.int32, (128, dim), 1)
        head_lane = lax.broadcasted_iota(jnp.int32, (128, cols), 0)
        head_column = lax.broadcasted_iota(jnp.int32, (128, cols), 1)
        norm = jnp.zeros((8, dim), F32)
        gain = jnp.zeros((8, cols), F32)
        image = jnp.zeros((8, 128), F32)
        for d in range(plan.n_dp):
            part = small_buf[d // merge // 2, d // merge % 2, d % merge]
            spread = jnp.where((column == d * dim_part + lane) & (lane < dim_part), 1.0, 0.0).astype(BF16)
            norm = norm + dot(part[0:8].astype(BF16), spread, 1, 0)
            same = (head_column // HEAD == head_lane // head_part) & (head_column % HEAD == d * head_part + head_lane % head_part)
            gain = gain + dot(part[8:16].astype(BF16), jnp.where(same, 1.0, 0.0).astype(BF16), 1, 0)
            image = image + part[16:24]
        norm_ref[...] = norm
        gain_ref[...] = gain
        image_ref[...] = image

        def first_norm(i, carry):
            at_rows = pl.ds(pl.multiple_of(i * block, block), block)
            normed, _ = norm_parts(x_ref[at_rows, :].astype(F32))
            low_buf[at_rows, :] = (normed * norm[0:1, :] + norm[1:2, :]).astype(BF16)
            return carry

        lax.fori_loop(0, blocks, first_norm, 0)
        outs = [pltpu.make_async_copy(low_buf, low_ref, out_sems.at[0])]
        outs[0].start()
        advance("w_v", "w_qk", "w_v", "w_qk")
        outs.append(pltpu.make_async_copy(w_buf, w_ref, out_sems.at[1]))
        outs[1].start()
        begin("down0")
        begin("down1")

        def project(i, carry):
            at_rows = pl.ds(pl.multiple_of(i * block, block), block)
            low = low_buf[at_rows, :]
            pq = dot(low, w_buf[0].reshape(dim, cols), 1, 0)
            pk = dot(low, w_buf[1].reshape(dim, cols), 1, 0)
            pq_buf[at_rows, :] = pq
            pk_buf[at_rows, :] = pk
            v_buf[at_rows, :] = dot(low, w_buf[2].reshape(dim, cols), 1, 0).astype(BF16)
            nq, _ = head_parts(pq, ones_ref[...])
            nk, _ = head_parts(pk, ones_ref[...])
            q_buf[at_rows, :] = (nq * gain[0:1, :]).astype(BF16)
            k_buf[at_rows, :] = (nk * gain[1:2, :]).astype(BF16)
            return carry

        third = blocks // 3
        advance("up0", "up1", "out", "cls")
        lax.fori_loop(0, third, project, 0)
        for _ in range(lines - 3):
            advance("up0", "up1", "out")
        advance("down0", "down1")
        lax.fori_loop(third, 2 * third, project, 0)
        advance("up0", "up1", "out", "down0", "down1", "cls")
        lax.fori_loop(2 * third, blocks, project, 0)
        pairs = ((pq_buf, pq_ref), (pk_buf, pk_ref), (q_buf, q_ref), (k_buf, k_ref), (v_buf, v_ref))
        for i, (a, b) in enumerate(pairs):
            outs.append(pltpu.make_async_copy(a, b, out_sems.at[2 + i]))
            outs[-1].start()
        for _ in range(lines - 3):
            advance("down0", "down1")
        advance("up0", "up1", "out", "cls", "down0", "down1", "cls", "up0", "up1", "out", "cls", "down0", "down1")
        for _ in range(lines):
            advance("up0", "up1", "out", "cls", "down0", "down1")
        g.finish()
        for c in outs:
            c.wait()

    vmem = pl.BlockSpec(memory_space=pltpu.VMEM)
    shape = jax.ShapeDtypeStruct
    wide_shape = lambda c: (n_mp // 2, 2, lines, 2, size, c)
    n_rows = lambda c, t: shape((rows, c), t)
    return pl.pallas_call(
        kernel,
        in_specs=[vmem] + [ANY] * 6 + [vmem],
        out_specs=[ANY] * 11 + [vmem] * 3,
        out_shape=[n_rows(dim, BF16), n_rows(cols, F32), n_rows(cols, F32), n_rows(cols, BF16), n_rows(cols, BF16), n_rows(cols, BF16)]
        + [
            shape((3, lines, 2, size, cols), BF16),
            shape(wide_shape(width), BF16),
            shape(wide_shape(width), BF16),
            shape(wide_shape(out_cols), BF16),
            shape(wide_shape(class_cols), BF16),
            shape((8, dim), F32),
            shape((8, cols), F32),
            shape((8, 128), F32),
        ],
        scratch_shapes=[
            pltpu.VMEM((3, lines, 2, size, cols), BF16),
            pltpu.VMEM((lines, 2, merge, 24, 128), F32),
            pltpu.VMEM((rows, dim), BF16),
            pltpu.VMEM((rows, cols), F32),
            pltpu.VMEM((rows, cols), F32),
            pltpu.VMEM((rows, cols), BF16),
            pltpu.VMEM((rows, cols), BF16),
            pltpu.VMEM((rows, cols), BF16),
            pltpu.SemaphoreType.DMA((n_sems,)),
            pltpu.SemaphoreType.DMA((n_sems,)),
            pltpu.SemaphoreType.DMA((len(orders),)),
            pltpu.SemaphoreType.DMA((7,)),
        ],
        compiler_params=pltpu.CompilerParams(vmem_limit_bytes=VMEM_LIMIT, collective_id=0, has_side_effects=True),
        cost_estimate=cost(6 * rows * dim * cols, rows * dim * 8),
        name="gather_project",
    )(tokens, qkv_block, up_block, down_block, out_block, cls_block, small_block, ones)


def head_masks(cols):
    lane = lax.broadcasted_iota(jnp.int32, (1, cols), 1)
    return [(lane >= h * HEAD) & (lane < (h + 1) * HEAD) for h in range(cols // HEAD)]


def spread_heads(block, masks):
    zero = jnp.zeros_like(block)
    return jnp.concatenate([jnp.where(m, block, zero) for m in masks], axis=0)


def join_heads(stacked, masks):
    total = stacked[0:QB]
    for h in range(1, len(masks)):
        total = jnp.where(masks[h], stacked[h * QB : (h + 1) * QB], total)
    return total


def by_window(width_ref, step, body):
    width = width_ref[step]
    for number, window in enumerate(WINDOWS):
        pl.when(width == number)(functools.partial(body, window))


def seq_specs(seq, cols):
    block = lambda c: pl.BlockSpec((QB, c), lambda b, *_: (seq * QBLOCKS + b, 0))
    all_keys = lambda c: pl.BlockSpec((LEN, c), lambda b, *_: (seq, 0))
    seg_row = pl.BlockSpec((1, 1, LEN), lambda b, *_: (seq, 0, 0))
    return block, all_keys, seg_row


def attend(plan, seq, ids, starts, widths, q, k, v, seg_col, seg_row):
    rows, cols = q.shape
    n_mp = plan.n_mp
    share = LEN // n_mp
    per = share // QB

    def kernel(ids_ref, start_ref, width_ref, q_ref, k_ref, v_ref, col_ref, row_ref, *outs):
        out_refs, log_ref = outs[:n_mp], outs[n_mp]
        block = pl.program_id(0)
        step = seq * QBLOCKS + block
        masks = head_masks(cols)
        heads = len(masks)

        def body(window):
            start = pl.multiple_of(start_ref[step], QB)
            keys = k_ref[pl.ds(start, window), :]
            values = v_ref[pl.ds(start, window), :]
            q3 = spread_heads(q_ref[...], masks)
            s = (dot(q3, keys, 1, 1) * HEAD**-0.5).reshape(heads, QB, window)
            same = col_ref[...] == row_ref[0, :, pl.ds(start, window)]
            s = jnp.where(same[None], s, MASK_FILL)
            top = jnp.max(s, axis=-1, keepdims=True)
            e = jnp.exp(s - top)
            total = jnp.sum(e, axis=-1, keepdims=True)
            p = (e * (1.0 / total)).astype(BF16).reshape(heads * QB, window)
            out = join_heads(dot(p, values, 1, 0), masks).astype(BF16)
            other = (block // per) ^ ids_ref[1]
            at = pl.ds(pl.multiple_of(block % per * QB, QB), QB)
            for r in range(n_mp):

                @pl.when(other == r)
                def _():
                    out_refs[r][at, :] = out

            log = top + jnp.log(total)
            lane = lax.broadcasted_iota(jnp.int32, (QB, 128), 1)
            logs = jnp.zeros((QB, 128), F32)
            for h in range(heads):
                logs = jnp.where(lane == h, log[h], logs)
            log_ref[...] = logs

        by_window(width_ref, step, body)

    block, all_keys, row_spec = seq_specs(seq, cols)
    return pl.pallas_call(
        kernel,
        grid_spec=pltpu.PrefetchScalarGridSpec(
            num_scalar_prefetch=3,
            grid=(QBLOCKS,),
            in_specs=[block(cols), all_keys(cols), all_keys(cols), block(1), row_spec],
            out_specs=[whole((share, cols))] * n_mp + [pl.BlockSpec((QB, 128), lambda b, *_: (b, 0))],
        ),
        out_shape=[jax.ShapeDtypeStruct((share, cols), BF16)] * n_mp + [jax.ShapeDtypeStruct((LEN, 128), F32)],
        compiler_params=PARAMS,
        cost_estimate=cost(4 * LEN * LEN * cols, LEN * cols * 8, LEN * LEN),
        name="attend",
    )(ids, starts, widths, q, k, v, seg_col, seg_row)


def attend_back(plan, seq, ids, starts, widths, live, q, k, v, grads, logs, seg_col, seg_row):
    rows, cols = q.shape
    n_mp = plan.n_mp
    share = LEN // n_mp
    per = share // QB

    def kernel(ids_ref, start_ref, width_ref, live_ref, q_ref, k_ref, v_ref, col_ref, row_ref, log_ref, *refs):
        grad_refs, (dq_ref, dk_ref, dv_ref) = refs[:n_mp], refs[n_mp:]
        block = pl.program_id(0)
        step = seq * QBLOCKS + block
        masks = head_masks(cols)
        heads = len(masks)

        @pl.when(block == 0)
        def _():
            dk_ref[...] = jnp.zeros_like(dk_ref)
            dv_ref[...] = jnp.zeros_like(dv_ref)

        def body(window):
            start = pl.multiple_of(start_ref[step], QB)
            keys = pl.ds(start, window)
            k_win = k_ref[keys, :]
            v_win = v_ref[keys, :]
            other = (block // per) ^ ids_ref[1]
            at = pl.ds(pl.multiple_of(block % per * QB, QB), QB)
            g = grad_refs[0][at, :]
            for r in range(1, n_mp):
                g = jnp.where(other == r, grad_refs[r][at, :], g)
            q3 = spread_heads(q_ref[...], masks)
            g3 = spread_heads(g, masks)
            s = (dot(q3, k_win, 1, 1) * HEAD**-0.5).reshape(heads, QB, window)
            same = col_ref[...] == row_ref[0, :, keys]
            all_logs = log_ref[...]
            log = jnp.stack([all_logs[:, h : h + 1] for h in range(heads)])
            p = jnp.exp(jnp.where(same[None], s - log, MASK_FILL))
            dp = dot(g3, v_win, 1, 1).reshape(heads, QB, window)
            inner = jnp.sum(p * dp, axis=-1, keepdims=True)
            ds = (p * (dp - inner)).astype(BF16).reshape(heads * QB, window)
            p_low = p.astype(BF16).reshape(heads * QB, window)
            dv_ref[keys, :] += dot(p_low, g3, 0, 0)
            dk_ref[keys, :] += dot(ds, q3, 0, 0) * HEAD**-0.5
            dq_ref[...] = join_heads(dot(ds, k_win, 1, 0), masks) * HEAD**-0.5

        alive = live_ref[step]

        @pl.when(alive == 0)
        def _():
            dq_ref[...] = jnp.zeros_like(dq_ref)

        @pl.when(alive != 0)
        def _():
            by_window(width_ref, step, body)

    block, all_keys, row_spec = seq_specs(seq, cols)
    grad_spec = pl.BlockSpec((share, cols), lambda b, *_: (seq, 0))
    shape = jax.ShapeDtypeStruct((LEN, cols), F32)
    return pl.pallas_call(
        kernel,
        grid_spec=pltpu.PrefetchScalarGridSpec(
            num_scalar_prefetch=4,
            grid=(QBLOCKS,),
            in_specs=[block(cols), all_keys(cols), all_keys(cols), block(1), row_spec, pl.BlockSpec((QB, 128), lambda b, *_: (b, 0))]
            + [grad_spec] * n_mp,
            out_specs=[pl.BlockSpec((QB, cols), lambda b, *_: (b, 0)), whole((LEN, cols)), whole((LEN, cols))],
        ),
        out_shape=[shape, shape, shape],
        compiler_params=PARAMS,
        cost_estimate=cost(10 * LEN * LEN * cols, LEN * cols * 24, LEN * LEN),
        name="attend_back",
    )(ids, starts, widths, live, q, k, v, seg_col, seg_row, logs, *grads)


def key_windows(seg_ids):
    seg = seg_ids.reshape(-1, LEN)
    first = seg[:, ::QB]
    last = seg[:, QB - 1 :: QB]
    low = jnp.sum((seg[:, None, :] < first[:, :, None]).astype(jnp.int32), axis=2)
    high = jnp.sum((seg[:, None, :] <= last[:, :, None]).astype(jnp.int32), axis=2)
    base = low // QB * QB
    number = jnp.full(base.shape, len(WINDOWS) - 1, jnp.int32)
    start = jnp.zeros_like(base)
    for choice in range(len(WINDOWS) - 2, -1, -1):
        at = jnp.minimum(base, LEN - WINDOWS[choice])
        fits = high <= at + WINDOWS[choice]
        number = jnp.where(fits, choice, number)
        start = jnp.where(fits, at, start)
    live = (first != PAD_ID).astype(jnp.int32)
    return start.reshape(-1), number.reshape(-1), live.reshape(-1)


def project_back(plan, seq, ids, low, pq, pk, dq, dk, dv, w_grad, w, gains, ones, last):
    rows, dim = low.shape
    cols = ones.shape[0]
    n_mp = plan.n_mp
    share = LEN // n_mp
    size = plan.block
    half = n_mp // 2

    def kernel(ids_ref, low_ref, pq_ref, pk_ref, dq_ref, dk_ref, dv_ref, gain_ref, ones_ref, w_ref, *rest):
        if w_grad is not None:
            base_ref, base_gain_ref = rest[:2]
            rest = rest[2:]
        keep_ref, send_ref, total_ref, gains_ref = rest[:4]
        grad_ref = rest[4] if last else total_ref
        me = ids_ref[0]
        step = pl.program_id(0)

        @pl.when(step == 0)
        def _():
            if w_grad is None:
                grad_ref[...] = jnp.zeros_like(grad_ref)
                gains_ref[...] = jnp.zeros_like(gains_ref)
            else:
                grad_ref[...] = base_ref[...]
                gains_ref[...] = base_gain_ref[...]

        ones_block = ones_ref[...]

        def back(values, grad, gain, slot):
            normed, scale = head_parts(values, ones_block)
            gains_ref[slot, :, :] += jnp.sum((grad * normed).reshape(-1, 8, cols), axis=0)
            scaled = grad * gain
            first = head_mean(scaled, ones_block)
            second = head_mean(scaled * normed, ones_block)
            return ((scaled - first - normed * second) * scale).astype(BF16)

        gq = back(pq_ref[...], dq_ref[...], gain_ref[0:1, :], 0)
        gk = back(pk_ref[...], dk_ref[...], gain_ref[1:2, :], 1)
        gv = dv_ref[...].astype(BF16)
        x = low_ref[...]
        terms = dot(gq, w_ref[0], 1, 1) + dot(gk, w_ref[1], 1, 1) + dot(gv, w_ref[2], 1, 1)
        terms = terms.astype(BF16)

        @pl.when(step < half)
        def _():
            keep_ref[...] = terms

        @pl.when(step >= half)
        def _():
            send_ref[...] = terms

        for p, g in enumerate((gq, gk, gv)):
            grad_ref[p] += dot(x, g, 0, 0)
        if last:

            @pl.when(step == n_mp - 1)
            def _():
                for group in range(plan.groups):
                    r = group ^ me
                    for p in range(3):
                        part = grad_ref[p, group * size : (group + 1) * size, :]
                        total_ref[(r & 1) * (plan.groups // 2) + (r >> 1), p] = part.astype(BF16)

    at = lambda i, ids_ref: ids_ref[1] ^ (i % half * 2 + i // half)
    far = lambda c: pl.BlockSpec((share, c), lambda i, ids_ref: (seq * n_mp + at(i, ids_ref), 0))
    near = lambda c: pl.BlockSpec((share, c), lambda i, ids_ref: (at(i, ids_ref), 0))
    w_shape, g_shape = (3, dim, cols), (2, 8, cols)
    base = [] if w_grad is None else list(w_grad)
    total = jax.ShapeDtypeStruct((plan.groups, 3, size, cols), BF16) if last else jax.ShapeDtypeStruct(w_shape, F32)
    return pl.pallas_call(
        kernel,
        grid_spec=pltpu.PrefetchScalarGridSpec(
            num_scalar_prefetch=1,
            grid=(n_mp,),
            in_specs=[far(dim), far(cols), far(cols), near(cols), near(cols), near(cols), whole(gains.shape), whole(ones.shape), whole(w.shape)]
            + [whole(b.shape) for b in base],
            out_specs=[
                pl.BlockSpec((None, share, dim), lambda i, *_: (jnp.minimum(i, half - 1), 0, 0)),
                pl.BlockSpec((None, share, dim), lambda i, *_: (jnp.maximum(i - half, 0), 0, 0)),
                whole(total.shape),
                whole(g_shape),
            ],
            scratch_shapes=[pltpu.VMEM(w_shape, F32)] if last else [],
        ),
        out_shape=[
            jax.ShapeDtypeStruct((half, share, dim), BF16),
            jax.ShapeDtypeStruct((half, share, dim), BF16),
            total,
            jax.ShapeDtypeStruct(g_shape, F32),
        ],
        compiler_params=PARAMS,
        cost_estimate=cost(12 * LEN * dim * cols, LEN * dim * 12),
        name="project_back",
    )(ids, low, pq, pk, dq, dk, dv, gains, ones, w, *base)


def feed_up(plan, ids, x, attended, params, out_w, up):
    rows, dim = x.shape
    cols = attended[0].shape[1]
    n_mp = plan.n_mp
    width = up.shape[2]
    hidden_size = n_mp * width
    block = 256

    def kernel(ids_ref, x_ref, *refs):
        a_refs, refs = refs[:n_mp], refs[n_mp:]
        norm_ref, o_ref, u_ref, mid_ref, low_ref, act_ref, der_ref = refs
        mp = ids_ref[1]
        middle = x_ref[...].astype(F32)
        for r in range(n_mp):
            middle = middle + dot(a_refs[r][...], o_ref[mp ^ r, :, :cols], 1, 1)
        mid_ref[...] = middle
        normed, _ = norm_parts(middle)
        low = (normed * norm_ref[2:3, :] + norm_ref[3:4, :]).astype(BF16)
        low_ref[...] = low
        for c in range(n_mp):
            at = slice(c * width, (c + 1) * width)
            hidden = dot(low, u_ref[c], 1, 0)
            phi = 0.5 * (1.0 + lax.erf(hidden * (0.5**0.5)))
            act_ref[:, at] = (hidden * phi).astype(BF16)
            der_ref[:, at] = phi + hidden * (jnp.exp(-0.5 * hidden * hidden) * 0.3989422804014327)

    row = lambda c: pl.BlockSpec((block, c), lambda i, *_: (i, 0))
    shape = lambda c, t: jax.ShapeDtypeStruct((rows, c), t)
    return pl.pallas_call(
        kernel,
        grid_spec=pltpu.PrefetchScalarGridSpec(
            num_scalar_prefetch=1,
            grid=(rows // block,),
            in_specs=[row(dim)] + [row(cols)] * n_mp + [whole(params.shape), whole(out_w.shape), whole(up.shape)],
            out_specs=[row(dim), row(dim), row(hidden_size), row(hidden_size)],
        ),
        out_shape=[shape(dim, F32), shape(dim, BF16), shape(hidden_size, BF16), shape(hidden_size, F32)],
        compiler_params=PARAMS,
        cost_estimate=cost(2 * rows * dim * (hidden_size + dim), rows * hidden_size * 8, rows * hidden_size * 2),
        name="feed_up",
    )(ids, x, *attended, params, out_w, up)


def feed_down(plan, ids, middle, active, seg_row, params, down):
    rows, dim = middle.shape
    n_mp = plan.n_mp
    hidden_size = active.shape[1]
    width = hidden_size // n_mp
    block = 256
    seqs = rows // block

    def kernel(ids_ref, mid_ref, act_ref, seg_ref, norm_ref, d_ref, res_ref, block_ref, pool_ref):
        seq = pl.program_id(0)
        result = mid_ref[...]
        for c in range(n_mp):
            result = result + dot(act_ref[:, c * width : (c + 1) * width], d_ref[c], 1, 1)
        res_ref[...] = result
        block_ref[...] = result.astype(BF16)
        normed, _ = norm_parts(result)
        final = normed * norm_ref[4:5, :] + norm_ref[5:6, :]
        probe = jnp.broadcast_to(norm_ref[6:7, :], (8, dim))
        score = lax.dot_general(
            probe, final, (((1,), (1,)), ((), ())), precision=lax.Precision.HIGHEST, preferred_element_type=F32
        )[0:1]
        slot = lax.broadcasted_iota(jnp.int32, (SLOTS, block), 0)
        member = (seg_ref[0] - seq * IMG_SEQ == slot) & (slot < IMG_SEQ)
        top = jnp.max(jnp.where(member, score, MASK_FILL), axis=1, keepdims=True)
        e = jnp.exp(jnp.where(member, score - top, MASK_FILL))
        e = jnp.where(member, e, 0.0)
        total = jnp.sum(e, axis=1, keepdims=True)
        low = final.astype(BF16)
        high = e.astype(BF16)
        rest = (e - high.astype(F32)).astype(BF16)
        pool_ref[:, :dim] = dot(high, low, 1, 0) + dot(rest, low, 1, 0)
        lane = lax.broadcasted_iota(jnp.int32, (SLOTS, 128), 1)
        pool_ref[:, dim:] = jnp.where(lane == 0, top, jnp.where(lane == 1, total, 0.0))

    row = lambda c: pl.BlockSpec((block, c), lambda i, *_: (i, 0))
    return pl.pallas_call(
        kernel,
        grid_spec=pltpu.PrefetchScalarGridSpec(
            num_scalar_prefetch=1,
            grid=(seqs,),
            in_specs=[row(dim), row(hidden_size), pl.BlockSpec((1, 1, block), lambda i, *_: (i, 0, 0)), whole(params.shape), whole(down.shape)],
            out_specs=[row(dim), row(dim), pl.BlockSpec((SLOTS, dim + 128), lambda i, *_: (i, 0))],
        ),
        out_shape=[
            jax.ShapeDtypeStruct((rows, dim), F32),
            jax.ShapeDtypeStruct((rows, dim), BF16),
            jax.ShapeDtypeStruct((seqs * SLOTS, dim + 128), F32),
        ],
        compiler_params=PARAMS,
        cost_estimate=cost(2 * rows * dim * hidden_size, rows * hidden_size * 4),
        name="feed_down",
    )(ids, middle, active, seg_row, params, down)


def combine_pools(plan, pool, bits, dim):
    other = plan.swap(pool, "mp", bits)
    lower = lax.axis_index("mp") & bits == 0
    first, second = jnp.where(lower, pool, other), jnp.where(lower, other, pool)
    top_a, top_b = first[:, dim : dim + 1], second[:, dim : dim + 1]
    top = jnp.maximum(top_a, top_b)
    weight_a, weight_b = jnp.exp(top_a - top), jnp.exp(top_b - top)
    rows = first[:, :dim] * weight_a + second[:, :dim] * weight_b
    total = first[:, dim + 1 : dim + 2] * weight_a + second[:, dim + 1 : dim + 2] * weight_b
    pad = jnp.zeros((pool.shape[0], pool.shape[1] - dim - 2), F32)
    return jnp.concatenate([rows, top, total, pad], axis=1)


def classify(plan, ids, pool, labels, images, cls, class_count):
    slots, full = pool.shape
    dim = full - 128
    n_mp = plan.n_mp
    class_cols = cls.shape[2]
    wide = n_mp * class_cols

    def kernel(ids_ref, pool_ref, label_ref, images_ref, c_ref, grad_ref, stat_ref, loss_ref, cls_ref, l_ref):
        me, mp = ids_ref[0], ids_ref[1]
        top = pool_ref[:, dim : dim + 1]
        total = pool_ref[:, dim + 1 : dim + 2]
        present = jnp.where(total > 0, 1.0, 0.0)
        safe = total + (1.0 - present)
        pooled = pool_ref[:, :dim] / safe
        low = pooled.astype(BF16)
        logits = jnp.concatenate([dot(low, c_ref[c], 1, 0) for c in range(n_mp)], axis=1)
        column = lax.broadcasted_iota(jnp.int32, (slots, wide), 1)
        logits = jnp.where(column % class_cols < class_count, logits, MASK_FILL)
        row_top = jnp.max(logits, axis=1, keepdims=True)
        log_total = row_top + jnp.log(jnp.sum(jnp.exp(logits - row_top), axis=1, keepdims=True))
        chosen = jnp.where(column == label_ref[...], 1.0, 0.0)
        label_logit = jnp.sum(chosen * logits, axis=1, keepdims=True)
        loss = jnp.sum(present * (log_total - label_logit), axis=0, keepdims=True)
        loss_ref[...] = jnp.broadcast_to(loss, loss_ref.shape)
        scale = present / images_ref[0:1, 0:1]
        grad = ((jnp.exp(logits - log_total) - chosen) * scale).astype(BF16)
        l_ref[...] = grad
        row_grad = sum(dot(grad[:, c * class_cols : (c + 1) * class_cols], c_ref[c], 1, 1) for c in range(n_mp)).astype(BF16)
        grad_ref[...] = row_grad
        inner = jnp.sum(row_grad.astype(F32) * pooled, axis=1, keepdims=True)
        lane = lax.broadcasted_iota(jnp.int32, (slots, 128), 1)
        stat_ref[...] = jnp.where(lane == 0, top, jnp.where(lane == 1, 1.0 / safe, jnp.where(lane == 2, inner, 0.0)))
        own = l_ref[:, pl.ds(pl.multiple_of(mp * class_cols, 128), class_cols)]
        grad_cls = dot(low, own, 0, 0)
        for g in range(plan.groups):
            r = g ^ me
            at = (r & 1) * (plan.groups // 2) + (r >> 1)
            cls_ref[at] = grad_cls[g * plan.block : (g + 1) * plan.block].astype(BF16)

    vmem = pl.BlockSpec(memory_space=pltpu.VMEM)
    return pl.pallas_call(
        kernel,
        in_specs=[pl.BlockSpec(memory_space=pltpu.SMEM), vmem, vmem, vmem, vmem],
        out_specs=[vmem] * 4,
        out_shape=[
            jax.ShapeDtypeStruct((slots, dim), BF16),
            jax.ShapeDtypeStruct((slots, 128), F32),
            jax.ShapeDtypeStruct((8, 128), F32),
            jax.ShapeDtypeStruct((plan.groups, plan.block, class_cols), BF16),
        ],
        scratch_shapes=[pltpu.VMEM((slots, wide), BF16)],
        compiler_params=PARAMS,
        cost_estimate=cost(6 * slots * dim * wide, dim * wide * 2),
        name="classify",
    )(ids, pool, labels, images, cls)


def split_three(values):
    high = values.astype(BF16)
    rest = values - high.astype(F32)
    middle = rest.astype(BF16)
    low = (rest - middle.astype(F32)).astype(BF16)
    return high, middle, low


def feed_back(plan, ids, result, middle, slope, row_grads, stats, seg_col, params, out_w, up, down, cols):
    rows, dim = result.shape
    n_mp = plan.n_mp
    width = up.shape[2]
    hidden_size = n_mp * width
    block = 256

    def kernel(ids_ref, res_ref, mid_ref, der_ref, pg_ref, stat_ref, seg_ref, norm_ref, o_ref, u_ref, d_ref, *refs):
        rlow_ref, hlow_ref, mlow_ref, mgrad_ref, *refs = refs
        ag_refs, sums_ref = refs[:n_mp], refs[n_mp]
        mp = ids_ref[1]
        seq = pl.program_id(0)

        @pl.when(seq == 0)
        def _():
            sums_ref[...] = jnp.zeros_like(sums_ref)

        normed, scale = norm_parts(res_ref[...])
        gain, probe = norm_ref[4:5, :], norm_ref[6:7, :]
        final = normed * gain + norm_ref[5:6, :]
        score = jnp.sum(final * probe, axis=1, keepdims=True)
        slot = lax.broadcasted_iota(jnp.int32, (block, SLOTS), 1)
        member = (seg_ref[...] - seq * IMG_SEQ == slot) & (slot < IMG_SEQ)
        held = jnp.max(jnp.where(member, 1.0, 0.0), axis=1, keepdims=True)
        one = jnp.where(member, 1.0, 0.0).astype(BF16)
        row_stat = sum(dot(one, part, 1, 0) for part in split_three(stat_ref[...]))
        top, inverse, inner = row_stat[:, 0:1], row_stat[:, 1:2], row_stat[:, 2:3]
        share = jnp.exp(jnp.where(held > 0, score - top, 0.0)) * inverse * held
        row_grad = dot(one, pg_ref[...], 1, 0)
        share_low = share.astype(BF16).astype(F32)
        share_grad = jnp.sum(row_grad * final.astype(BF16).astype(F32), axis=1, keepdims=True)
        score_grad = share * (share_grad - inner)
        final_grad = share_low * row_grad + score_grad * probe
        add = lambda slot, value: sums_ref.at[slot].__setitem__(
            ..., sums_ref[slot] + jnp.sum(value.reshape(-1, 8, dim), axis=0)
        )
        add(4, score_grad * final)
        add(2, final_grad * normed)
        add(3, final_grad)
        result_grad = norm_back(final_grad, normed, scale, gain)
        result_low = result_grad.astype(BF16)
        rlow_ref[...] = result_low
        second = jnp.zeros((block, dim), F32)
        for c in range(n_mp):
            at = slice(c * width, (c + 1) * width)
            hidden_low = (der_ref[:, at] * dot(result_low, d_ref[c], 1, 0)).astype(BF16)
            hlow_ref[:, at] = hidden_low
            second = second + dot(hidden_low, u_ref[c], 1, 1)
        normed_two, scale_two = norm_parts(mid_ref[...])
        add(0, second * normed_two)
        add(1, second)
        middle_grad = result_grad + norm_back(second, normed_two, scale_two, norm_ref[2:3, :])
        mgrad_ref[...] = middle_grad
        middle_low = middle_grad.astype(BF16)
        mlow_ref[...] = middle_low
        for r in range(n_mp):
            ag_refs[r][...] = dot(middle_low, o_ref[mp ^ r, :, :cols], 1, 0).astype(BF16)

    row = lambda c: pl.BlockSpec((block, c), lambda i, *_: (i, 0))
    shape = lambda c, t: jax.ShapeDtypeStruct((rows, c), t)
    slots = lambda c: pl.BlockSpec((SLOTS, c), lambda i, *_: (i, 0))
    return pl.pallas_call(
        kernel,
        grid_spec=pltpu.PrefetchScalarGridSpec(
            num_scalar_prefetch=1,
            grid=(rows // block,),
            in_specs=[row(dim), row(dim), row(hidden_size), slots(dim), slots(128), row(1), whole(params.shape)] + [whole(a.shape) for a in (out_w, up, down)],
            out_specs=[row(dim), row(hidden_size), row(dim), row(dim)] + [row(cols)] * n_mp + [whole((5, 8, dim))],
        ),
        out_shape=[shape(dim, BF16), shape(hidden_size, BF16), shape(dim, BF16), shape(dim, F32)]
        + [shape(cols, BF16)] * n_mp
        + [jax.ShapeDtypeStruct((5, 8, dim), F32)],
        compiler_params=PARAMS,
        cost_estimate=cost(2 * rows * dim * (2 * hidden_size + dim), rows * hidden_size * 8),
        name="feed_back",
    )(ids, result, middle, slope, row_grads, stats, seg_col, params, out_w, up, down)


def weight_grad(plan, ids, left, right, name):
    rows, dim = left.shape
    n_mp = plan.n_mp
    parts = right if isinstance(right, list) else None
    width = parts[0].shape[1] if parts else right.shape[1] // n_mp
    out_width = -(-width // 128) * 128
    half = n_mp // 2
    far = plan.groups // 2

    def kernel(ids_ref, left_ref, *refs):
        right_refs, (keep_ref, send_ref) = refs[:-2], refs[-2:]
        me = ids_ref[0]
        step = pl.program_id(0)

        def body(rhs_ref, out_ref):
            grad = dot(left_ref[...], rhs_ref[...], 0, 0).astype(BF16)
            if out_width != width:
                grad = jnp.concatenate([grad, jnp.zeros((dim, out_width - width), BF16)], axis=1)
            for g in range(plan.groups):
                r = g ^ me
                out_ref[r & 1, r >> 1] = grad[g * plan.block : (g + 1) * plan.block]

        for i in range(n_mp):
            out_ref = keep_ref if i < half else send_ref
            if parts:
                rhs_ref = right_refs[i % half * 2 + i // half]
                pl.when(step == i)(functools.partial(body, rhs_ref, out_ref))
        if not parts:
            pl.when(step < half)(lambda: body(right_refs[0], keep_ref))
            pl.when(step >= half)(lambda: body(right_refs[0], send_ref))

    at = lambda i, ids_ref: ids_ref[1] ^ (i % half * 2 + i // half)
    rights = parts or [right]
    if parts:
        right_specs = [whole((rows, width))] * n_mp
    else:
        right_specs = [pl.BlockSpec((rows, width), lambda i, ids_ref: (0, at(i, ids_ref)))]
    out_block = (None, 2, far, plan.block, out_width)
    out = jax.ShapeDtypeStruct((half, 2, far, plan.block, out_width), BF16)
    return pl.pallas_call(
        kernel,
        grid_spec=pltpu.PrefetchScalarGridSpec(
            num_scalar_prefetch=1,
            grid=(n_mp,),
            in_specs=[whole((rows, dim))] + right_specs,
            out_specs=[
                pl.BlockSpec(out_block, lambda i, *_: (jnp.minimum(i, half - 1), 0, 0, 0, 0)),
                pl.BlockSpec(out_block, lambda i, *_: (jnp.maximum(i - half, 0), 0, 0, 0, 0)),
            ],
        ),
        out_shape=[out, out],
        compiler_params=PARAMS,
        cost_estimate=cost(2 * rows * dim * width * n_mp, 2 * dim * width * n_mp),
        name=name,
    )(ids, left, *rights)


def assemble(plan, ids, own, across, mates, dtype, name):
    seqs, share, dim = own.shape
    n_mp = plan.n_mp

    def kernel(ids_ref, own_ref, across_ref, mate_ref, out_ref):
        r = pl.program_id(1)
        value = jnp.where(r == 0, own_ref[...], jnp.where(r == 2, across_ref[...], mate_ref[...]))
        out_ref[...] = value.astype(dtype)

    same = pl.BlockSpec((None, share, dim), lambda s, r, *_: (s, 0, 0))
    return pl.pallas_call(
        kernel,
        grid_spec=pltpu.PrefetchScalarGridSpec(
            num_scalar_prefetch=1,
            grid=(seqs, n_mp),
            in_specs=[same, same, pl.BlockSpec((None, None, share, dim), lambda s, r, *_: (r // 2, s, 0, 0))],
            out_specs=pl.BlockSpec((share, dim), lambda s, r, ids_ref: (s * n_mp + (ids_ref[1] ^ r), 0)),
        ),
        out_shape=jax.ShapeDtypeStruct((seqs * n_mp * share, dim), dtype),
        compiler_params=PARAMS,
        cost_estimate=cost(0, seqs * n_mp * share * dim * 8),
        name=name,
    )(ids, own, across, mates)


def adam_update(weight, moment_one, moment_two, gradient, step_rate, decay_rate):
    fresh_one = BETA_ONE * moment_one + (1.0 - BETA_ONE) * gradient
    fresh_two = BETA_TWO * moment_two + (1.0 - BETA_TWO) * gradient * gradient
    one_hat = fresh_one / (1.0 - BETA_ONE**STEP)
    two_hat = fresh_two / (1.0 - BETA_TWO**STEP)
    updated = weight - step_rate * (one_hat / (jnp.sqrt(two_hat) + ADAM_EPS) + decay_rate * weight)
    return (fresh_one, fresh_two, updated)


def shards(
    tokens,
    seg_ids,
    labels,
    w_qkv,
    m_qkv,
    v_qkv,
    w_out,
    m_out,
    v_out,
    w_up,
    m_up,
    v_up,
    w_down,
    m_down,
    v_down,
    w_cls,
    m_cls,
    v_cls,
    norm_params,
    m_norm,
    v_norm,
    qk_gain,
    m_qk,
    v_qk,
    *,
    n_dp,
    n_mp,
):
    dp, mp = lax.axis_index("dp"), lax.axis_index("mp")
    group_rows, dim = tokens.shape
    plan = Plan(n_dp, n_mp, dim)
    seqs = group_rows // LEN
    share = LEN // n_mp
    rows = seqs * share
    cols = w_qkv.shape[2]
    classes = w_cls.shape[1]
    class_cols = -(-classes // 128) * 128
    out_cols = -(-cols // 128) * 128
    ids = jnp.stack([dp // plan.merge, mp]).astype(jnp.int32)

    new_image = seg_ids != jnp.concatenate([jnp.full((1,), -1, jnp.int32), seg_ids[:-1]])
    count = jnp.sum((new_image & (seg_ids != PAD_ID)).astype(F32))
    dim_part, head_part = norm_params.shape[1], qk_gain.shape[2]
    pad = lambda a, r, c: jnp.pad(a, ((0, r - a.shape[0]), (0, c - a.shape[1])))
    low_param = lambda a: lax.reduce_precision(a, 8, 7)
    small = jnp.concatenate(
        [
            pad(low_param(norm_params), 8, 128),
            pad(low_param(qk_gain).reshape(2, cols // HEAD * head_part), 8, 128),
            pad(count.reshape(1, 1), 8, 128),
        ]
    )
    qkv_block = plan.merged(w_qkv.astype(BF16), 1)
    up_block = plan.merged(w_up.astype(BF16), 0)
    down_block = plan.merged(w_down.T.astype(BF16), 0)
    out_block = plan.merged(pad(w_out.T.astype(BF16), dim_part, out_cols), 0)
    cls_block = plan.merged(pad(w_cls.astype(BF16), dim_part, class_cols), 0)
    small_block = plan.merged(small[None], 0)

    head_of = jnp.arange(cols) // HEAD
    ones = jnp.where(head_of[:, None] == head_of[None, :], 1.0 / HEAD, 0.0).astype(BF16)
    starts, widths, live = key_windows(seg_ids)
    seg_col = seg_ids.reshape(group_rows, 1)
    seg_row = seg_ids.reshape(-1, 1, LEN)
    normed_low, pq, pk, q, k, v, w, up, down, out_w, cls, params, gains, images = gather_project(
        plan, tokens, qkv_block, up_block, down_block, out_block, cls_block, small_block, ones
    )
    w = w.reshape(3, dim, cols)
    up, down, out_w, cls = (a.reshape(n_mp, dim, a.shape[-1]) for a in (up, down, out_w, cls))
    image_total = images[0, 0]
    logs, received = [], []
    for s in range(seqs):
        *parts, log = attend(plan, s, ids, starts, widths, q, k, v, seg_col, seg_row)
        logs.append(log)
        received.append([parts[0]] + [plan.swap(parts[r], "mp", r) for r in range(1, n_mp)])
    attended = [jnp.concatenate([received[s][r] for s in range(seqs)], axis=0) for r in range(n_mp)]

    own = lambda a: lax.dynamic_slice_in_dim(a.reshape((seqs, n_mp, share) + a.shape[1:]), mp, 1, 1)
    x = own(tokens).reshape(rows, dim)
    seg = own(seg_ids).reshape(rows)
    middle, second_low, active, slope = feed_up(plan, ids, x, attended, params, out_w, up)
    result, block_rows, pool = feed_down(plan, ids, middle, active, seg.reshape(seqs, 1, share), params, down)

    def spread(part):
        across = plan.swap(part, "mp", 2)
        return across, plan.swap(jnp.stack([part, across]), "mp", 1)

    block_rows = block_rows.reshape(seqs, share, dim)
    block_across, block_mates = spread(block_rows)
    block_out = assemble(plan, ids, block_rows, block_across, block_mates, BF16, "block_out")

    pool = combine_pools(plan, combine_pools(plan, pool, 1, dim), 2, dim)
    slot_label = labels.reshape(seqs, IMG_SEQ)
    slot_label = slot_label // classes * class_cols + slot_label % classes
    slot_label = jnp.pad(slot_label, ((0, 0), (0, SLOTS - IMG_SEQ)), constant_values=-1).reshape(seqs * SLOTS, 1)
    row_grads, stats, loss, cls_blocks = classify(plan, ids, pool, slot_label, images, cls, classes)
    mean_loss = plan.total(loss, "dp")[0, 0] / image_total

    result_low, hidden_low, middle_low, middle_grad, *rest = feed_back(
        plan, ids, result, middle, slope, row_grads, stats, seg.reshape(rows, 1), params, out_w, up, down, cols
    )
    grads, sums = rest[:n_mp], rest[n_mp]
    grad_parts = [grads[0]] + [plan.swap(grads[r], "mp", r) for r in range(1, n_mp)]
    down_keep, down_send = weight_grad(plan, ids, result_low, active, "grad_down")
    up_keep, up_send = weight_grad(plan, ids, second_low, hidden_low, "grad_up")
    out_keep, out_send = weight_grad(plan, ids, middle_low, attended, "grad_out")

    after = lambda *values: lax.optimization_barrier((ids,) + values)[0]
    down_sum = plan.core_sum(down_keep, down_send)
    up_sum = plan.core_sum(up_keep, up_send)
    rest_sum = plan.core_sum(out_keep, out_send)
    cls_blocks = cls_blocks.reshape(rest_sum.shape[1:4] + (class_cols,)).astype(F32)
    norm_one = norm_parts(x.astype(F32))
    w_grad = None
    first_sums = []
    input_rows, input_across, input_mates = [], [], []
    for s in range(seqs):
        if s == 0:
            ids_now = after(down_sum, up_sum, rest_sum, block_out)
            down_sum = plan.scatter_step(down_sum, "y", 1)
            up_sum = plan.scatter_step(up_sum, "x", 0)
            rest_sum = plan.scatter_step(rest_sum, "x", 0)
            rest_sum = jnp.concatenate([rest_sum, cls_blocks], axis=3)
        elif s == 1:
            ids_now = after(down_sum, up_sum, rest_sum)
            down_sum = plan.scatter_step(down_sum, "x", 0)
            up_sum = plan.scatter_step(up_sum, "y", 0)
            rest_sum = plan.scatter_step(rest_sum, "y", 0)
        elif s == 2:
            ids_now = after(down_sum, up_sum, rest_sum)
            down_sum = plan.unmerged(plan.scatter_step(down_sum, "z", 0), 0)
            up_sum = plan.unmerged(plan.scatter_step(up_sum, "z", 0), 0)
            rest_sum = plan.unmerged(plan.scatter_step(rest_sum, "z", 0), 0)
        dq, dk, dv = attend_back(plan, s, ids_now, starts, widths, live, q, k, v, grad_parts, logs[s], seg_col, seg_row)
        keep, send, *w_grad = project_back(
            plan, s, ids_now, normed_low, pq, pk, dq, dk, dv, w_grad, w, gains, ones, s == seqs - 1
        )
        first = plan.scatter_step(plan.core_sum(keep, send), "x", 0)
        at = slice(s * share, (s + 1) * share)
        normed, scale = norm_one[0][at], norm_one[1][at]
        first_sums.append(jnp.stack([jnp.sum(first * normed, axis=0), jnp.sum(first, axis=0)]))
        part = (middle_grad[at] + norm_back(first, normed, scale, params[0:1])).astype(BF16)
        across, mates = spread(part)
        input_rows.append(part)
        input_across.append(across)
        input_mates.append(mates)
    input_grad = assemble(
        plan, ids, jnp.stack(input_rows), jnp.stack(input_across), jnp.stack(input_mates, axis=1), F32, "input_grad"
    )
    grad_down, grad_up = down_sum.T, up_sum
    grad_out, grad_cls = rest_sum[:, :cols].T, rest_sum[:, out_cols : out_cols + classes]

    qkv_blocks, gain_parts = w_grad
    qkv_sum = qkv_blocks.astype(F32).reshape(2, plan.groups // 2, 3, plan.block, cols)
    qkv_sum = plan.scatter_step(qkv_sum, "y", 0)
    grad_qkv = plan.unmerged(plan.scatter_step(qkv_sum, "z", 0), 1)

    sums = jnp.sum(sums, axis=1)
    first_sum = sum(first_sums)
    norm_grads = plan.total(jnp.concatenate([first_sum, sums, jnp.zeros((1, dim), F32)], axis=0), "mp")
    qk_grads = jnp.sum(gain_parts, axis=1)
    qk_grads = jnp.pad(qk_grads, ((0, 6), (0, dim - cols)))
    small_grads = plan.total(jnp.concatenate([norm_grads, qk_grads], axis=0), "dp")
    norm_part = lax.dynamic_slice(small_grads, (0, dp * dim_part), (7, dim_part))
    qk_part = lax.dynamic_slice_in_dim(small_grads[8:10, :cols].reshape(2, cols // HEAD, HEAD), dp * head_part, head_part, 2)
    reduced = (grad_qkv, grad_out, grad_up, grad_down, grad_cls, norm_part, qk_part)
    groups = (
        (w_qkv, m_qkv, v_qkv, MATRIX_RATE, MATRIX_DECAY),
        (w_out, m_out, v_out, MATRIX_RATE, MATRIX_DECAY),
        (w_up, m_up, v_up, MATRIX_RATE, MATRIX_DECAY),
        (w_down, m_down, v_down, MATRIX_RATE, MATRIX_DECAY),
        (w_cls, m_cls, v_cls, MATRIX_RATE, MATRIX_DECAY),
        (norm_params, m_norm, v_norm, GAIN_RATE, 0.0),
        (qk_gain, m_qk, v_qk, GAIN_RATE, 0.0),
    )
    outputs = [block_out, input_grad, mean_loss]
    for number, group in enumerate(groups):
        fresh_one, fresh_two, updated = adam_update(group[0], group[1], group[2], reduced[number], group[3], group[4])
        if number == 5:
            outputs = outputs + [fresh_one, fresh_two[:6], fresh_two[6], updated]
        else:
            outputs = outputs + [fresh_one, fresh_two, updated]
    return tuple(outputs)


def solution(mesh):
    rows_cols = (P("mp", "dp"),) * 3
    cols_rows = (P("dp", "mp"),) * 3
    qkv_spec = (P(None, "dp", "mp"),) * 3
    qk_spec = (P(None, "mp", "dp"),) * 3
    norm_spec = P(None, "dp")
    in_specs = (
        (P("dp", None), P("dp"), P("dp")) + qkv_spec + rows_cols + cols_rows + rows_cols + cols_rows + (norm_spec,) * 3 + qk_spec
    )
    out_specs = (
        (P("dp", None), P("dp", None), P())
        + qkv_spec
        + rows_cols
        + cols_rows
        + rows_cols
        + cols_rows
        + (norm_spec, norm_spec, P("dp"), norm_spec)
        + qk_spec
    )
    body = functools.partial(shards, n_dp=mesh.shape["dp"], n_mp=mesh.shape["mp"])
    return jax.shard_map(body, mesh=mesh, in_specs=in_specs, out_specs=out_specs, check_vma=False)
```

```python
import functools

import jax
import jax.numpy as jnp
from jax import lax
from jax.experimental import pallas as pl
from jax.experimental.pallas import tpu as pltpu
from jax.sharding import PartitionSpec as P

LEN = 1024
STEP = 10
SEQ_DEV = 3
IMG_DEV = 180
PAD_ID = 180

NORM_EPS = 1e-06
MASK_FILL = -1000000000.0
BETA_ONE = 0.9
BETA_TWO = 0.999
ADAM_EPS = 1e-08
MATRIX_RATE = 0.1
MATRIX_DECAY = 0.1
GAIN_RATE = 0.8

HEAD = 64
QB = 128
QBLOCKS = LEN // QB
WINDOWS = (384, 640, 1024)
F32 = jnp.float32
BF16 = jnp.bfloat16
VMEM_LIMIT = 56 * 1024 * 1024
IMG_SEQ = 60
SLOTS = 64
ANY = pl.BlockSpec(memory_space=pl.ANY)
PARAMS = pltpu.CompilerParams(vmem_limit_bytes=VMEM_LIMIT)


def dot(a, b, ca, cb):
    return lax.dot_general(a, b, (((ca,), (cb,)), ((), ())), preferred_element_type=F32)


def head_mean(values, ones_block):
    high = values.astype(BF16)
    rest = (values - high.astype(F32)).astype(BF16)
    return dot(high, ones_block, 1, 0) + dot(rest, ones_block, 1, 0)


def norm_parts(values):
    centre = values - jnp.mean(values, axis=-1, keepdims=True)
    spread = jnp.mean(centre * centre, axis=-1, keepdims=True)
    scale = lax.rsqrt(spread + NORM_EPS)
    return centre * scale, scale


def norm_back(grad, normed, scale, gain):
    scaled = grad * gain
    first = jnp.mean(scaled, axis=-1, keepdims=True)
    second = jnp.mean(scaled * normed, axis=-1, keepdims=True)
    return (scaled - first - normed * second) * scale


def head_parts(values, ones_block):
    centre = values - head_mean(values, ones_block)
    scale = lax.rsqrt(head_mean(centre * centre, ones_block) + NORM_EPS)
    return centre * scale, scale


def cost(flops, read, exps=0):
    return pl.CostEstimate(flops=int(flops), bytes_accessed=int(read), transcendentals=int(exps))


def whole(shape):
    return pl.BlockSpec(tuple(shape), lambda *_: (0,) * len(shape))


class Plan:
    def __init__(self, n_dp, n_mp, dim):
        self.n_dp, self.n_mp = n_dp, n_mp
        self.merge = 1 if dim // n_dp % 16 == 0 else 2
        self.groups = n_dp // self.merge
        self.block = dim // self.groups
        self.far = [2 * k for k in range(1, self.groups // 2)]

    def swap(self, value, axis, bits):
        size = self.n_dp if axis == "dp" else self.n_mp
        return lax.ppermute(value, axis, [(i, i ^ bits) for i in range(size)])

    def group_swap(self, value, bits):
        return self.swap(value, "dp", bits * self.merge)

    def merged(self, value, dim):
        if self.merge == 1:
            return value
        other = self.swap(value, "dp", 1)
        even = lax.axis_index("dp") % 2 == 0
        first, second = jnp.where(even, value, other), jnp.where(even, other, value)
        return jnp.concatenate([first, second], axis=dim)

    def unmerged(self, value, dim):
        if self.merge == 1:
            return value
        half = value.shape[dim] // 2
        me = lax.axis_index("dp") % 2
        mine = lax.dynamic_slice_in_dim(value, me * half, half, dim)
        theirs = lax.dynamic_slice_in_dim(value, (1 - me) * half, half, dim)
        return mine + self.swap(theirs, "dp", 1)

    def total(self, value, axis):
        size = self.n_dp if axis == "dp" else self.n_mp
        bits = 1
        while bits < size:
            value = value + self.swap(value, axis, bits)
            bits *= 2
        return value


MESH = pl.DeviceIdType.MESH


def flip(index, bits):
    bit = 1
    while bit <= bits:
        if bits & bit:
            index = index + bit * (1 - 2 * (index // bit % 2))
        bit *= 2
    return index


class Chain:
    def __init__(self, region, order, lines):
        self.region, self.steps = region, order
        self.copies = sum({"z": lines - 1, "c": 2}.get(step, 1) for step in order)


class Gatherer:
    def __init__(self, plan, send_sems, recv_sems):
        self.plan, self.send_sems, self.recv_sems = plan, send_sems, recv_sems
        self.dp, self.mp = lax.axis_index("dp"), lax.axis_index("mp")
        self.pair = self.dp % plan.merge
        group = self.dp // plan.merge
        self.z, self.y = group // 2, group % 2
        self.x, self.core = self.mp // 2, self.mp % 2
        self.lines = plan.groups // 2
        self.used = 0
        self.pending = []

    def device(self, z, y, x, core):
        return ((z * 2 + y) * self.plan.merge + self.pair, x * 2 + core)

    def here(self):
        return self.z, self.y, self.x, self.core

    def meet(self, barrier):
        z, y, x, core = self.here()
        others = [(z, 1 - y, x, core), (z, y, 1 - x, core), (z, y, x, 1 - core)]
        others += [(flip(z, k), y, x, core) for k in range(1, self.lines)]
        for other in others:
            pl.semaphore_signal(barrier, inc=1, device_id=self.device(*other), device_id_type=MESH)
        pl.semaphore_wait(barrier, len(others))

    def start(self, chain, number, source=None):
        step, done = chain.steps[number], chain.steps[:number]
        z, y, x, core = self.here()
        spot = dict(z=None if "z" in done else z, y=None if "y" in done else y, x=None if "x" in done else x, core=core)
        if step == "z":
            copies = [(spot, (flip(z, k), y, x, core)) for k in range(1, self.lines)]
        elif step == "c":
            copies = [({**spot, "x": side}, (z, y, x, 1 - core)) for side in (0, 1)]
        else:
            copies = [(spot, dict(y=(z, 1 - y, x, core), x=(z, y, 1 - x, core))[step])]
        started = []
        for place, other in copies:
            region = chain.region(**place)
            out = pltpu.make_async_remote_copy(
                src_ref=region if source is None else source,
                dst_ref=region,
                send_sem=self.send_sems.at[self.used],
                recv_sem=self.recv_sems.at[self.used],
                device_id=self.device(*other),
                device_id_type=MESH,
            )
            self.used += 1
            out.start()
            started.append(out)
        self.pending += started
        return started

    @staticmethod
    def arrive(copies):
        for out in copies:
            out.wait_recv()

    def finish(self):
        for out in self.pending:
            out.wait_send()


def gather_project(plan, tokens, qkv_block, up_block, down_block, out_block, cls_block, small_block, ones):
    rows, dim = tokens.shape
    cols = ones.shape[0]
    n_mp, merge, size = plan.n_mp, plan.merge, plan.block
    lines = plan.groups // 2
    width = up_block.shape[1]
    out_cols, class_cols = out_block.shape[1], cls_block.shape[1]
    block = 512
    blocks = rows // block
    dim_part = dim // plan.n_dp
    head_part = HEAD // plan.n_dp

    orders = [("small", "zy"), ("w_qk", "zy"), ("w_v", "zy"), ("out", "zyxc"), ("cls", "zyxc"), ("up", "zy"), ("down", "zx")]
    sizes = {name: Chain(None, order, lines).copies for name, order in orders}
    n_sems = sum(sizes.values())

    def kernel(x_ref, qkv_in, up_in, down_in, out_in, cls_in, small_in, ones_ref, *refs):
        low_ref, pq_ref, pk_ref, q_ref, k_ref, v_ref, w_ref, up_ref, down_ref, o_ref, c_ref, norm_ref, gain_ref, image_ref = refs[:14]
        w_buf, small_buf, low_buf, pq_buf, pk_buf, q_buf, k_buf, v_buf, send_sems, recv_sems, own_sems, out_sems = refs[14:]
        g = Gatherer(plan, send_sems, recv_sems)
        z, y, x, core = g.here()
        everything = slice(None)

        def at(v):
            return everything if v is None else v

        def wide(ref, first, count):
            columns = pl.ds(first, count)
            return lambda z, y, x, core: ref.at[at(x), core, at(z), at(y), :, columns]

        regions = dict(
            w_qk=lambda z, y, x, core: w_buf.at[pl.ds(0, 2), at(z), at(y)],
            w_v=lambda z, y, x, core: w_buf.at[pl.ds(2, 1), at(z), at(y)],
            small=lambda z, y, x, core: small_buf.at[at(z), at(y)],
            up=lambda z, y, x, core: up_ref.at[at(z), at(y)],
            down=lambda z, y, x, core: down_ref.at[at(x), at(z)],
            out=wide(o_ref, 0, out_cols),
            cls=wide(c_ref, 0, class_cols),
        )
        chains = {name: Chain(regions[name], order, lines) for name, order in orders}
        sources = dict(
            w_qk=qkv_in.at[pl.ds(0, 2)],
            w_v=qkv_in.at[pl.ds(2, 1)],
            small=small_in,
            up=up_in,
            down=down_in,
            out=out_in,
            cls=cls_in,
        )
        own = {}
        for i, (name, _) in enumerate(orders):
            own[name] = pltpu.make_async_copy(sources[name], regions[name](z, y, x, core), own_sems.at[i])
            own[name].start()
        live, reached = {}, {}

        def begin(name):
            live[name] = g.start(chains[name], 0, source=sources[name])
            reached[name] = 0

        def advance(*names):
            for name in names:
                if reached[name] == len(chains[name].steps):
                    continue
                if reached[name] == 0:
                    own[name].wait()
                g.arrive(live[name])
                reached[name] += 1
                if reached[name] < len(chains[name].steps):
                    live[name] = g.start(chains[name], reached[name])

        g.meet(pltpu.get_barrier_semaphore())
        for name in ("small", "w_qk", "w_v", "out", "cls"):
            begin(name)
        advance("small", "small")

        lane = lax.broadcasted_iota(jnp.int32, (128, dim), 0)
        column = lax.broadcasted_iota(jnp.int32, (128, dim), 1)
        head_lane = lax.broadcasted_iota(jnp.int32, (128, cols), 0)
        head_column = lax.broadcasted_iota(jnp.int32, (128, cols), 1)
        norm = jnp.zeros((8, dim), F32)
        gain = jnp.zeros((8, cols), F32)
        image = jnp.zeros((8, 128), F32)
        for d in range(plan.n_dp):
            part = small_buf[d // merge // 2, d // merge % 2, d % merge]
            spread = jnp.where((column == d * dim_part + lane) & (lane < dim_part), 1.0, 0.0).astype(BF16)
            norm = norm + dot(part[0:8].astype(BF16), spread, 1, 0)
            same = (head_column // HEAD == head_lane // head_part) & (head_column % HEAD == d * head_part + head_lane % head_part)
            gain = gain + dot(part[8:16].astype(BF16), jnp.where(same, 1.0, 0.0).astype(BF16), 1, 0)
            image = image + part[16:24]
        norm_ref[...] = norm
        gain_ref[...] = gain
        image_ref[...] = image

        def first_norm(i, carry):
            at_rows = pl.ds(pl.multiple_of(i * block, block), block)
            normed, _ = norm_parts(x_ref[at_rows, :].astype(F32))
            low_buf[at_rows, :] = (normed * norm[0:1, :] + norm[1:2, :]).astype(BF16)
            return carry

        third = blocks // 3
        lax.fori_loop(0, third, first_norm, 0)
        advance("w_qk", "w_v", "out", "cls")
        begin("up")
        begin("down")
        lax.fori_loop(third, blocks, first_norm, 0)
        outs = [pltpu.make_async_copy(low_buf, low_ref, out_sems.at[0])]
        outs[0].start()
        advance("w_qk", "w_v", "out", "cls")
        outs.append(pltpu.make_async_copy(w_buf, w_ref, out_sems.at[1]))
        outs[1].start()

        def project(i, carry):
            at_rows = pl.ds(pl.multiple_of(i * block, block), block)
            low = low_buf[at_rows, :]
            pq = dot(low, w_buf[0].reshape(dim, cols), 1, 0)
            pk = dot(low, w_buf[1].reshape(dim, cols), 1, 0)
            pq_buf[at_rows, :] = pq
            pk_buf[at_rows, :] = pk
            v_buf[at_rows, :] = dot(low, w_buf[2].reshape(dim, cols), 1, 0).astype(BF16)
            nq, _ = head_parts(pq, ones_ref[...])
            nk, _ = head_parts(pk, ones_ref[...])
            q_buf[at_rows, :] = (nq * gain[0:1, :]).astype(BF16)
            k_buf[at_rows, :] = (nk * gain[1:2, :]).astype(BF16)
            return carry

        lax.fori_loop(0, third, project, 0)
        advance("up", "down")
        lax.fori_loop(third, 2 * third, project, 0)
        advance("out", "cls")
        lax.fori_loop(2 * third, blocks, project, 0)
        pairs = ((pq_buf, pq_ref), (pk_buf, pk_ref), (q_buf, q_ref), (k_buf, k_ref), (v_buf, v_ref))
        for i, (a, b) in enumerate(pairs):
            outs.append(pltpu.make_async_copy(a, b, out_sems.at[2 + i]))
            outs[-1].start()
        advance("out", "cls", "up", "down")
        g.finish()
        for c in outs:
            c.wait()

    vmem = pl.BlockSpec(memory_space=pltpu.VMEM)
    shape = jax.ShapeDtypeStruct
    wide_shape = lambda c: (n_mp // 2, 2, lines, 2, size, c)
    n_rows = lambda c, t: shape((rows, c), t)
    return pl.pallas_call(
        kernel,
        in_specs=[vmem] + [ANY] * 6 + [vmem],
        out_specs=[ANY] * 11 + [vmem] * 3,
        out_shape=[n_rows(dim, BF16), n_rows(cols, F32), n_rows(cols, F32), n_rows(cols, BF16), n_rows(cols, BF16), n_rows(cols, BF16)]
        + [
            shape((3, lines, 2, size, cols), BF16),
            shape((lines, 2, size, width), BF16),
            shape((n_mp // 2, lines, size, width), BF16),
            shape(wide_shape(out_cols), BF16),
            shape(wide_shape(class_cols), BF16),
            shape((8, dim), F32),
            shape((8, cols), F32),
            shape((8, 128), F32),
        ],
        scratch_shapes=[
            pltpu.VMEM((3, lines, 2, size, cols), BF16),
            pltpu.VMEM((lines, 2, merge, 24, 128), F32),
            pltpu.VMEM((rows, dim), BF16),
            pltpu.VMEM((rows, cols), F32),
            pltpu.VMEM((rows, cols), F32),
            pltpu.VMEM((rows, cols), BF16),
            pltpu.VMEM((rows, cols), BF16),
            pltpu.VMEM((rows, cols), BF16),
            pltpu.SemaphoreType.DMA((n_sems,)),
            pltpu.SemaphoreType.DMA((n_sems,)),
            pltpu.SemaphoreType.DMA((len(orders),)),
            pltpu.SemaphoreType.DMA((7,)),
        ],
        compiler_params=pltpu.CompilerParams(vmem_limit_bytes=VMEM_LIMIT, collective_id=0, has_side_effects=True),
        cost_estimate=cost(6 * rows * dim * cols, rows * dim * 8),
        name="gather_project",
    )(tokens, qkv_block, up_block, down_block, out_block, cls_block, small_block, ones)


def head_masks(cols):
    lane = lax.broadcasted_iota(jnp.int32, (1, cols), 1)
    return [(lane >= h * HEAD) & (lane < (h + 1) * HEAD) for h in range(cols // HEAD)]


def spread_heads(block, masks):
    zero = jnp.zeros_like(block)
    return jnp.concatenate([jnp.where(m, block, zero) for m in masks], axis=0)


def join_heads(stacked, masks):
    total = stacked[0:QB]
    for h in range(1, len(masks)):
        total = jnp.where(masks[h], stacked[h * QB : (h + 1) * QB], total)
    return total


def by_window(width_ref, step, body):
    width = width_ref[step]
    for number, window in enumerate(WINDOWS):
        pl.when(width == number)(functools.partial(body, window))


def seq_specs(seq, cols):
    block = lambda c: pl.BlockSpec((QB, c), lambda b, *_: (seq * QBLOCKS + b, 0))
    all_keys = lambda c: pl.BlockSpec((LEN, c), lambda b, *_: (seq, 0))
    seg_row = pl.BlockSpec((1, 1, LEN), lambda b, *_: (seq, 0, 0))
    return block, all_keys, seg_row


def attend(plan, seq, ids, starts, widths, q, k, v, seg_col, seg_row):
    rows, cols = q.shape
    n_mp = plan.n_mp
    share = LEN // n_mp
    per = share // QB

    def kernel(ids_ref, start_ref, width_ref, q_ref, k_ref, v_ref, col_ref, row_ref, *outs):
        out_refs, log_ref = outs[:n_mp], outs[n_mp]
        block = pl.program_id(0)
        step = seq * QBLOCKS + block
        masks = head_masks(cols)
        heads = len(masks)

        def body(window):
            start = pl.multiple_of(start_ref[step], QB)
            keys = k_ref[pl.ds(start, window), :]
            values = v_ref[pl.ds(start, window), :]
            q3 = spread_heads(q_ref[...], masks)
            s = (dot(q3, keys, 1, 1) * HEAD**-0.5).reshape(heads, QB, window)
            same = col_ref[...] == row_ref[0, :, pl.ds(start, window)]
            s = jnp.where(same[None], s, MASK_FILL)
            top = jnp.max(s, axis=-1, keepdims=True)
            e = jnp.exp(s - top)
            total = jnp.sum(e, axis=-1, keepdims=True)
            p = (e * (1.0 / total)).astype(BF16).reshape(heads * QB, window)
            out = join_heads(dot(p, values, 1, 0), masks).astype(BF16)
            other = (block // per) ^ ids_ref[1]
            at = pl.ds(pl.multiple_of(block % per * QB, QB), QB)
            for r in range(n_mp):

                @pl.when(other == r)
                def _():
                    out_refs[r][at, :] = out

            log = top + jnp.log(total)
            lane = lax.broadcasted_iota(jnp.int32, (QB, 128), 1)
            logs = jnp.zeros((QB, 128), F32)
            for h in range(heads):
                logs = jnp.where(lane == h, log[h], logs)
            log_ref[...] = logs

        by_window(width_ref, step, body)

    block, all_keys, row_spec = seq_specs(seq, cols)
    return pl.pallas_call(
        kernel,
        grid_spec=pltpu.PrefetchScalarGridSpec(
            num_scalar_prefetch=3,
            grid=(QBLOCKS,),
            in_specs=[block(cols), all_keys(cols), all_keys(cols), block(1), row_spec],
            out_specs=[whole((share, cols))] * n_mp + [pl.BlockSpec((QB, 128), lambda b, *_: (b, 0))],
        ),
        out_shape=[jax.ShapeDtypeStruct((share, cols), BF16)] * n_mp + [jax.ShapeDtypeStruct((LEN, 128), F32)],
        compiler_params=PARAMS,
        cost_estimate=cost(4 * LEN * LEN * cols, LEN * cols * 8, LEN * LEN),
        name="attend",
    )(ids, starts, widths, q, k, v, seg_col, seg_row)


def attend_back(plan, seq, ids, starts, widths, live, q, k, v, pq, pk, gains, ones, grads, logs, seg_col, seg_row):
    rows, cols = q.shape
    n_mp = plan.n_mp
    share = LEN // n_mp
    per = share // QB

    def kernel(ids_ref, start_ref, width_ref, live_ref, q_ref, k_ref, v_ref, pq_ref, pk_ref, gain_ref, ones_ref, col_ref, row_ref, log_ref, *refs):
        grad_refs, (gq_ref, gk_ref, gv_ref, sum_ref, dk_ref, dv_ref) = refs[:n_mp], refs[n_mp:]
        block = pl.program_id(0)
        step = seq * QBLOCKS + block
        masks = head_masks(cols)
        heads = len(masks)

        @pl.when(block == 0)
        def _():
            dk_ref[...] = jnp.zeros_like(dk_ref)
            dv_ref[...] = jnp.zeros_like(dv_ref)
            sum_ref[...] = jnp.zeros_like(sum_ref)

        def back(values, grad, slot):
            ones_block = ones_ref[...]
            normed, scale = head_parts(values, ones_block)
            sum_ref[slot] += jnp.sum((grad * normed).reshape(-1, 8, cols), axis=0)
            scaled = grad * gain_ref[slot : slot + 1, :]
            first = head_mean(scaled, ones_block)
            second = head_mean(scaled * normed, ones_block)
            return ((scaled - first - normed * second) * scale).astype(BF16)

        def body(window):
            start = pl.multiple_of(start_ref[step], QB)
            keys = pl.ds(start, window)
            k_win = k_ref[keys, :]
            v_win = v_ref[keys, :]
            other = (block // per) ^ ids_ref[1]
            at = pl.ds(pl.multiple_of(block % per * QB, QB), QB)
            g = grad_refs[0][at, :]
            for r in range(1, n_mp):
                g = jnp.where(other == r, grad_refs[r][at, :], g)
            q3 = spread_heads(q_ref[...], masks)
            g3 = spread_heads(g, masks)
            s = (dot(q3, k_win, 1, 1) * HEAD**-0.5).reshape(heads, QB, window)
            same = col_ref[...] == row_ref[0, :, keys]
            all_logs = log_ref[...]
            log = jnp.stack([all_logs[:, h : h + 1] for h in range(heads)])
            p = jnp.exp(jnp.where(same[None], s - log, MASK_FILL))
            dp = dot(g3, v_win, 1, 1).reshape(heads, QB, window)
            inner = jnp.sum(p * dp, axis=-1, keepdims=True)
            ds = (p * (dp - inner)).astype(BF16).reshape(heads * QB, window)
            p_low = p.astype(BF16).reshape(heads * QB, window)
            dv_ref[keys, :] += dot(p_low, g3, 0, 0)
            dk_ref[keys, :] += dot(ds, q3, 0, 0) * HEAD**-0.5
            dq = join_heads(dot(ds, k_win, 1, 0), masks) * HEAD**-0.5
            gq_ref[...] = back(pq_ref[...], dq, 0)

        alive = live_ref[step]

        @pl.when(alive == 0)
        def _():
            gq_ref[...] = jnp.zeros_like(gq_ref)

        @pl.when(alive != 0)
        def _():
            by_window(width_ref, step, body)

        @pl.when(block == QBLOCKS - 1)
        def _():
            gv_ref[...] = dv_ref[...].astype(BF16)

            def keys_back(i, carry):
                at = pl.ds(pl.multiple_of(i * share, share), share)
                gk_ref[at, :] = back(pk_ref[at, :], dk_ref[at, :], 1)
                return carry

            lax.fori_loop(0, n_mp, keys_back, 0)

    block, all_keys, row_spec = seq_specs(seq, cols)
    grad_spec = pl.BlockSpec((share, cols), lambda b, *_: (seq, 0))
    shape = jax.ShapeDtypeStruct((LEN, cols), BF16)
    return pl.pallas_call(
        kernel,
        grid_spec=pltpu.PrefetchScalarGridSpec(
            num_scalar_prefetch=4,
            grid=(QBLOCKS,),
            in_specs=[block(cols), all_keys(cols), all_keys(cols), block(cols), all_keys(cols), whole(gains.shape), whole(ones.shape)]
            + [block(1), row_spec, pl.BlockSpec((QB, 128), lambda b, *_: (b, 0))]
            + [grad_spec] * n_mp,
            out_specs=[pl.BlockSpec((QB, cols), lambda b, *_: (b, 0)), whole((LEN, cols)), whole((LEN, cols)), whole((2, 8, cols))],
            scratch_shapes=[pltpu.VMEM((LEN, cols), F32), pltpu.VMEM((LEN, cols), F32)],
        ),
        out_shape=[shape, shape, shape, jax.ShapeDtypeStruct((2, 8, cols), F32)],
        compiler_params=PARAMS,
        cost_estimate=cost(60 * LEN * LEN * cols, LEN * cols * 24, LEN * LEN),
        name="attend_back",
    )(ids, starts, widths, live, q, k, v, pq, pk, gains, ones, seg_col, seg_row, logs, *grads)


def key_windows(seg_ids):
    seg = seg_ids.reshape(-1, LEN)
    first = seg[:, ::QB]
    last = seg[:, QB - 1 :: QB]
    low = jnp.sum((seg[:, None, :] < first[:, :, None]).astype(jnp.int32), axis=2)
    high = jnp.sum((seg[:, None, :] <= last[:, :, None]).astype(jnp.int32), axis=2)
    base = low // QB * QB
    number = jnp.full(base.shape, len(WINDOWS) - 1, jnp.int32)
    start = jnp.zeros_like(base)
    for choice in range(len(WINDOWS) - 2, -1, -1):
        at = jnp.minimum(base, LEN - WINDOWS[choice])
        fits = high <= at + WINDOWS[choice]
        number = jnp.where(fits, choice, number)
        start = jnp.where(fits, at, start)
    live = (first != PAD_ID).astype(jnp.int32)
    return start.reshape(-1), number.reshape(-1), live.reshape(-1)


RELATIVE = (0, 2, 1, 3)


def down_copies(plan, ids_ref, parts, target, sems):
    y = ids_ref[0] % 2
    core = ids_ref[1] % 2
    copies = []
    for i, part in enumerate(parts):
        for side in range(2):
            place = target.at[side * 2 + (core ^ (i // 2)), :, y ^ (i % 2)]
            copies.append(pltpu.make_async_copy(part.at[side], place, sems.at[len(copies)]))
    return copies


def feed_up(plan, ids, x, attended, params, out_w, up):
    rows, dim = x.shape
    cols = attended[0].shape[1]
    n_mp = plan.n_mp
    width = up[0].shape[1]
    hidden_size = n_mp * width
    block = 256

    def kernel(ids_ref, x_ref, *refs):
        a_refs, refs = refs[:n_mp], refs[n_mp:]
        norm_ref, o_ref, *refs = refs
        u_refs, (mid_ref, low_ref, act_ref, der_ref) = refs[:n_mp], refs[n_mp:]
        mp = ids_ref[1]
        middle = x_ref[...].astype(F32)
        for r in range(n_mp):
            middle = middle + dot(a_refs[r][...], o_ref[mp ^ r, :, :cols], 1, 1)
        mid_ref[...] = middle
        normed, _ = norm_parts(middle)
        low = (normed * norm_ref[2:3, :] + norm_ref[3:4, :]).astype(BF16)
        low_ref[...] = low
        for c in range(n_mp):
            at = pl.ds(pl.multiple_of((mp ^ RELATIVE[c]) * width, 128), width)
            hidden = dot(low, u_refs[c][...], 1, 0)
            phi = 0.5 * (1.0 + lax.erf(hidden * (0.5**0.5)))
            act_ref[:, at] = (hidden * phi).astype(BF16)
            der_ref[:, at] = phi + hidden * (jnp.exp(-0.5 * hidden * hidden) * 0.3989422804014327)

    row = lambda c: pl.BlockSpec((block, c), lambda i, *_: (i, 0))
    shape = lambda c, t: jax.ShapeDtypeStruct((rows, c), t)
    return pl.pallas_call(
        kernel,
        grid_spec=pltpu.PrefetchScalarGridSpec(
            num_scalar_prefetch=1,
            grid=(rows // block,),
            in_specs=[row(dim)] + [row(cols)] * n_mp + [whole(params.shape), whole(out_w.shape)] + [whole(up[0].shape)] * n_mp,
            out_specs=[row(dim), row(dim), row(hidden_size), row(hidden_size)],
        ),
        out_shape=[shape(dim, F32), shape(dim, BF16), shape(hidden_size, BF16), shape(hidden_size, F32)],
        compiler_params=PARAMS,
        cost_estimate=cost(2 * rows * dim * (hidden_size + dim), rows * hidden_size * 8, rows * hidden_size * 2),
        name="feed_up",
    )(ids, x, *attended, params, out_w, *up)


def start_all(copies):
    for c in copies:
        c.start()


def wait_all(copies):
    for c in copies:
        c.wait()


def feed_down(plan, ids, middle, active, seg_row, params, down):
    rows, dim = middle.shape
    n_mp = plan.n_mp
    hidden_size = active.shape[1]
    width = hidden_size // n_mp
    block = 256
    seqs = rows // block

    def kernel(ids_ref, mid_ref, act_ref, seg_ref, norm_ref, *refs):
        d_parts, (res_ref, block_ref, pool_ref, d_ref, sems) = refs[:4], refs[4:]
        seq = pl.program_id(0)
        copies = down_copies(plan, ids_ref, d_parts, d_ref, sems)

        @pl.when(seq == 0)
        def _():
            start_all(copies)
            wait_all(copies)

        result = mid_ref[...]
        for c in range(n_mp):
            result = result + dot(act_ref[:, c * width : (c + 1) * width], d_ref[c].reshape(dim, width), 1, 1)
        res_ref[...] = result
        block_ref[...] = result.astype(BF16)
        normed, _ = norm_parts(result)
        final = normed * norm_ref[4:5, :] + norm_ref[5:6, :]
        probe = jnp.broadcast_to(norm_ref[6:7, :], (8, dim))
        score = lax.dot_general(
            probe, final, (((1,), (1,)), ((), ())), precision=lax.Precision.HIGHEST, preferred_element_type=F32
        )[0:1]
        slot = lax.broadcasted_iota(jnp.int32, (SLOTS, block), 0)
        member = (seg_ref[0] - seq * IMG_SEQ == slot) & (slot < IMG_SEQ)
        top = jnp.max(jnp.where(member, score, MASK_FILL), axis=1, keepdims=True)
        e = jnp.exp(jnp.where(member, score - top, MASK_FILL))
        e = jnp.where(member, e, 0.0)
        total = jnp.sum(e, axis=1, keepdims=True)
        low = final.astype(BF16)
        high = e.astype(BF16)
        rest = (e - high.astype(F32)).astype(BF16)
        pool_ref[:, :dim] = dot(high, low, 1, 0) + dot(rest, low, 1, 0)
        lane = lax.broadcasted_iota(jnp.int32, (SLOTS, 128), 1)
        pool_ref[:, dim:] = jnp.where(lane == 0, top, jnp.where(lane == 1, total, 0.0))

    row = lambda c: pl.BlockSpec((block, c), lambda i, *_: (i, 0))
    return pl.pallas_call(
        kernel,
        grid_spec=pltpu.PrefetchScalarGridSpec(
            num_scalar_prefetch=1,
            grid=(seqs,),
            in_specs=[row(dim), row(hidden_size), pl.BlockSpec((1, 1, block), lambda i, *_: (i, 0, 0)), whole(params.shape)] + [ANY] * 4,
            out_specs=[row(dim), row(dim), pl.BlockSpec((SLOTS, dim + 128), lambda i, *_: (i, 0))],
            scratch_shapes=[pltpu.VMEM((n_mp, plan.groups // 2, 2, plan.block, width), BF16), pltpu.SemaphoreType.DMA((8,))],
        ),
        out_shape=[
            jax.ShapeDtypeStruct((rows, dim), F32),
            jax.ShapeDtypeStruct((rows, dim), BF16),
            jax.ShapeDtypeStruct((seqs * SLOTS, dim + 128), F32),
        ],
        compiler_params=PARAMS,
        cost_estimate=cost(2 * rows * dim * hidden_size, rows * hidden_size * 4),
        name="feed_down",
    )(ids, middle, active, seg_row, params, *down)


def combine_pools(plan, pool, bits, dim):
    other = plan.swap(pool, "mp", bits)
    lower = lax.axis_index("mp") & bits == 0
    first, second = jnp.where(lower, pool, other), jnp.where(lower, other, pool)
    top_a, top_b = first[:, dim : dim + 1], second[:, dim : dim + 1]
    top = jnp.maximum(top_a, top_b)
    weight_a, weight_b = jnp.exp(top_a - top), jnp.exp(top_b - top)
    rows = first[:, :dim] * weight_a + second[:, :dim] * weight_b
    total = first[:, dim + 1 : dim + 2] * weight_a + second[:, dim + 1 : dim + 2] * weight_b
    pad = jnp.zeros((pool.shape[0], pool.shape[1] - dim - 2), F32)
    return jnp.concatenate([rows, top, total, pad], axis=1)


def classify(plan, ids, pool, labels, images, cls, class_count):
    slots, full = pool.shape
    dim = full - 128
    n_mp = plan.n_mp
    class_cols = cls.shape[2]
    wide = n_mp * class_cols

    def kernel(ids_ref, pool_ref, label_ref, images_ref, c_ref, grad_ref, stat_ref, loss_ref, cls_ref, l_ref):
        me, mp = ids_ref[0], ids_ref[1]
        top = pool_ref[:, dim : dim + 1]
        total = pool_ref[:, dim + 1 : dim + 2]
        present = jnp.where(total > 0, 1.0, 0.0)
        safe = total + (1.0 - present)
        pooled = pool_ref[:, :dim] / safe
        low = pooled.astype(BF16)
        logits = jnp.concatenate([dot(low, c_ref[c], 1, 0) for c in range(n_mp)], axis=1)
        column = lax.broadcasted_iota(jnp.int32, (slots, wide), 1)
        logits = jnp.where(column % class_cols < class_count, logits, MASK_FILL)
        row_top = jnp.max(logits, axis=1, keepdims=True)
        log_total = row_top + jnp.log(jnp.sum(jnp.exp(logits - row_top), axis=1, keepdims=True))
        chosen = jnp.where(column == label_ref[...], 1.0, 0.0)
        label_logit = jnp.sum(chosen * logits, axis=1, keepdims=True)
        loss = jnp.sum(present * (log_total - label_logit), axis=0, keepdims=True)
        loss_ref[...] = jnp.broadcast_to(loss, loss_ref.shape)
        scale = present / images_ref[0:1, 0:1]
        grad = ((jnp.exp(logits - log_total) - chosen) * scale).astype(BF16)
        l_ref[...] = grad
        row_grad = sum(dot(grad[:, c * class_cols : (c + 1) * class_cols], c_ref[c], 1, 1) for c in range(n_mp)).astype(BF16)
        grad_ref[...] = row_grad
        inner = jnp.sum(row_grad.astype(F32) * pooled, axis=1, keepdims=True)
        lane = lax.broadcasted_iota(jnp.int32, (slots, 128), 1)
        stat_ref[...] = jnp.where(lane == 0, top, jnp.where(lane == 1, 1.0 / safe, jnp.where(lane == 2, inner, 0.0)))
        own = l_ref[:, pl.ds(pl.multiple_of(mp * class_cols, 128), class_cols)]
        grad_cls = dot(low, own, 0, 0)
        for g in range(plan.groups):
            at = (g ^ me) % 2 * (plan.groups // 2) + g // 2
            cls_ref[at] = grad_cls[g * plan.block : (g + 1) * plan.block].astype(BF16)

    vmem = pl.BlockSpec(memory_space=pltpu.VMEM)
    return pl.pallas_call(
        kernel,
        in_specs=[pl.BlockSpec(memory_space=pltpu.SMEM), vmem, vmem, vmem, vmem],
        out_specs=[vmem] * 4,
        out_shape=[
            jax.ShapeDtypeStruct((slots, dim), BF16),
            jax.ShapeDtypeStruct((slots, 128), F32),
            jax.ShapeDtypeStruct((8, 128), F32),
            jax.ShapeDtypeStruct((plan.groups, plan.block, class_cols), BF16),
        ],
        scratch_shapes=[pltpu.VMEM((slots, wide), BF16)],
        compiler_params=PARAMS,
        cost_estimate=cost(6 * slots * dim * wide, dim * wide * 2),
        name="classify",
    )(ids, pool, labels, images, cls)


def split_three(values):
    high = values.astype(BF16)
    rest = values - high.astype(F32)
    middle = rest.astype(BF16)
    low = (rest - middle.astype(F32)).astype(BF16)
    return high, middle, low


def feed_back(plan, ids, result, middle, slope, row_grads, stats, seg_col, params, out_w, up, down, cols):
    rows, dim = result.shape
    n_mp = plan.n_mp
    width = up[0].shape[1]
    hidden_size = n_mp * width
    block = 256

    def kernel(ids_ref, res_ref, mid_ref, der_ref, pg_ref, stat_ref, seg_ref, norm_ref, o_ref, *refs):
        u_refs, d_parts, refs = refs[:n_mp], refs[n_mp : n_mp + 4], refs[n_mp + 4 :]
        rlow_ref, hlow_ref, mlow_ref, mgrad_ref, *refs = refs
        ag_refs, (sums_ref, d_ref, sems) = refs[:n_mp], refs[n_mp:]
        mp = ids_ref[1]
        seq = pl.program_id(0)
        copies = down_copies(plan, ids_ref, d_parts, d_ref, sems)

        @pl.when(seq == 0)
        def _():
            start_all(copies)
            sums_ref[...] = jnp.zeros_like(sums_ref)

        normed, scale = norm_parts(res_ref[...])
        gain, probe = norm_ref[4:5, :], norm_ref[6:7, :]
        final = normed * gain + norm_ref[5:6, :]
        score = jnp.sum(final * probe, axis=1, keepdims=True)
        slot = lax.broadcasted_iota(jnp.int32, (block, SLOTS), 1)
        member = (seg_ref[...] - seq * IMG_SEQ == slot) & (slot < IMG_SEQ)
        held = jnp.max(jnp.where(member, 1.0, 0.0), axis=1, keepdims=True)
        one = jnp.where(member, 1.0, 0.0).astype(BF16)
        row_stat = sum(dot(one, part, 1, 0) for part in split_three(stat_ref[...]))
        top, inverse, inner = row_stat[:, 0:1], row_stat[:, 1:2], row_stat[:, 2:3]
        share = jnp.exp(jnp.where(held > 0, score - top, 0.0)) * inverse * held
        row_grad = dot(one, pg_ref[...], 1, 0)
        share_low = share.astype(BF16).astype(F32)
        share_grad = jnp.sum(row_grad * final.astype(BF16).astype(F32), axis=1, keepdims=True)
        score_grad = share * (share_grad - inner)
        final_grad = share_low * row_grad + score_grad * probe
        add = lambda slot, value: sums_ref.at[slot].__setitem__(
            ..., sums_ref[slot] + jnp.sum(value.reshape(-1, 8, dim), axis=0)
        )
        add(4, score_grad * final)
        add(2, final_grad * normed)
        add(3, final_grad)
        result_grad = norm_back(final_grad, normed, scale, gain)
        result_low = result_grad.astype(BF16)
        rlow_ref[...] = result_low
        pl.when(seq == 0)(lambda: wait_all(copies))
        second = jnp.zeros((block, dim), F32)
        for c in range(n_mp):
            other = mp ^ RELATIVE[c]
            at = pl.ds(pl.multiple_of(other * width, 128), width)
            hidden_low = (der_ref[:, at] * dot(result_low, d_ref[other].reshape(dim, width), 1, 0)).astype(BF16)
            hlow_ref[:, at] = hidden_low
            second = second + dot(hidden_low, u_refs[c][...], 1, 1)
        normed_two, scale_two = norm_parts(mid_ref[...])
        add(0, second * normed_two)
        add(1, second)
        middle_grad = result_grad + norm_back(second, normed_two, scale_two, norm_ref[2:3, :])
        mgrad_ref[...] = middle_grad
        middle_low = middle_grad.astype(BF16)
        mlow_ref[...] = middle_low
        for r in range(n_mp):
            ag_refs[r][...] = dot(middle_low, o_ref[mp ^ r, :, :cols], 1, 0).astype(BF16)

    row = lambda c: pl.BlockSpec((block, c), lambda i, *_: (i, 0))
    shape = lambda c, t: jax.ShapeDtypeStruct((rows, c), t)
    slots = lambda c: pl.BlockSpec((SLOTS, c), lambda i, *_: (i, 0))
    return pl.pallas_call(
        kernel,
        grid_spec=pltpu.PrefetchScalarGridSpec(
            num_scalar_prefetch=1,
            grid=(rows // block,),
            in_specs=[row(dim), row(dim), row(hidden_size), slots(dim), slots(128), row(1), whole(params.shape), whole(out_w.shape)]
            + [whole(up[0].shape)] * n_mp
            + [ANY] * 4,
            out_specs=[row(dim), row(hidden_size), row(dim), row(dim)] + [row(cols)] * n_mp + [whole((5, 8, dim))],
            scratch_shapes=[pltpu.VMEM((n_mp, plan.groups // 2, 2, plan.block, width), BF16), pltpu.SemaphoreType.DMA((8,))],
        ),
        out_shape=[shape(dim, BF16), shape(hidden_size, BF16), shape(dim, BF16), shape(dim, F32)]
        + [shape(cols, BF16)] * n_mp
        + [jax.ShapeDtypeStruct((5, 8, dim), F32)],
        compiler_params=PARAMS,
        cost_estimate=cost(2 * rows * dim * (2 * hidden_size + dim), rows * hidden_size * 8),
        name="feed_back",
    )(ids, result, middle, slope, row_grads, stats, seg_col, params, out_w, *up, *down)


class Loads:
    def __init__(self, sources, targets, sems):
        self.targets = targets
        self.copies = [pltpu.make_async_copy(a, b, sems.at[i]) for i, (a, b) in enumerate(zip(sources, targets))]
        self.done = [False] * len(self.copies)
        for c in self.copies:
            c.start()

    def __getitem__(self, i):
        if not self.done[i]:
            self.copies[i].wait()
            self.done[i] = True
        return self.targets[i]


class Sender:
    def __init__(self, send_sems, recv_sems):
        self.dp, self.mp = lax.axis_index("dp"), lax.axis_index("mp")
        self.send_sems, self.recv_sems = send_sems, recv_sems
        self.started, self.used = [], 0

    def device(self, axis, bits):
        return (flip(self.dp, bits), self.mp) if axis == "dp" else (self.dp, flip(self.mp, bits))

    def meet(self, partners):
        barrier = pltpu.get_barrier_semaphore()
        for axis, bits in partners:
            pl.semaphore_signal(barrier, inc=1, device_id=self.device(axis, bits), device_id_type=MESH)
        pl.semaphore_wait(barrier, len(partners))

    def copy(self, src, dst, axis, bits):
        n = self.used
        self.used += 1
        c = pltpu.make_async_remote_copy(
            src_ref=src,
            dst_ref=dst,
            send_sem=self.send_sems.at[n],
            recv_sem=self.recv_sems.at[n],
            device_id=self.device(axis, bits),
            device_id_type=MESH,
        )
        self.started.append(c)
        c.start()
        return c

    def finish(self):
        for c in self.started:
            c.wait_send()


def weight_grads(plan, pairs, out_pair, cls_blocks, sends):
    dim = pairs[0][0].shape[1]
    rows = pairs[0][0].shape[0]
    n_mp, size, merge = plan.n_mp, plan.block, plan.merge
    lines = plan.groups // 2
    width = pairs[0][1].shape[1] // n_mp
    cols = out_pair[1][0].shape[1]
    out_cols = -(-cols // 128) * 128
    inputs = [a for pair in pairs for a in pair] + [out_pair[0]] + list(out_pair[1]) + [cls_blocks]
    n_load = len(inputs)
    widths = [width] * len(pairs) + [out_cols]
    n = len(widths)

    def kernel(*refs):
        sources, ag_in, refs = refs[:n_load], refs[n_load : n_load + n_mp - 1], refs[n_load + n_mp - 1 :]
        keep_out, send_out, cls_out, ag_out, refs = refs[:n], refs[n : 2 * n], refs[2 * n], refs[2 * n + 1 : 2 * n + n_mp], refs[2 * n + n_mp :]
        targets, refs = refs[:n_load], refs[n_load:]
        send_buf, got_buf, own_buf, keep_buf, low_buf = (refs[i * n : (i + 1) * n] for i in range(5))
        cls_got, load_sems, store_sems, send_sems, recv_sems = refs[5 * n :]
        loads = Loads(sources, targets, load_sems)
        net = Sender(send_sems, recv_sems)
        y = net.dp // merge % 2
        side, core = net.mp // 2, net.mp % 2
        net.meet([("mp", 1), ("mp", 2), ("mp", 3), ("dp", merge)])
        ag = [net.copy(a, b, "mp", r) for r, (a, b) in enumerate(zip(ag_in, ag_out), start=1)]
        cls_ref = loads[n_load - 1]
        cls_copy = net.copy(cls_ref.at[1], cls_got, "dp", merge)
        stores = []

        def grad(number, other_side, other_core):
            if number < len(pairs):
                left, right = loads[2 * number], loads[2 * number + 1]
                at = flip(side, other_side) * 2 + flip(core, other_core)
                return dot(left[...], right[:, pl.ds(pl.multiple_of(at * width, 128), width)], 0, 0)
            left = loads[2 * len(pairs)]
            right = loads[2 * len(pairs) + 1 + other_side * 2 + other_core]
            value = dot(left[...], right[...], 0, 0)
            return jnp.concatenate([value, jnp.zeros((dim, out_cols - cols), F32)], axis=1) if out_cols != cols else value

        split = lambda value: value.reshape(lines, 2, size, value.shape[1])
        cores = []
        for i in range(n):
            for other_side in (0, 1):
                send_buf[i][flip(side, other_side)] = split(grad(i, other_side, 1).astype(BF16))
            cores.append(net.copy(send_buf[i], got_buf[i], "mp", 1))
            for other_side in (0, 1):
                own_buf[i][flip(side, other_side)] = split(grad(i, other_side, 0))
        for i in range(n):
            cores[i].wait_recv()
            for x in (0, 1):
                for half in (0, 1):
                    at = flip(y, half)
                    total = own_buf[i][x, :, at] + got_buf[i][x, :, at].astype(F32)
                    if half:
                        low_buf[i][x] = total.astype(BF16)
                    else:
                        keep_buf[i][x] = total
            for a, b in ((low_buf[i], send_out[i]), (keep_buf[i], keep_out[i])):
                stores.append(pltpu.make_async_copy(a, b, store_sems.at[len(stores)]))
                stores[-1].start()
        cls_copy.wait_recv()
        cls_out[...] = cls_ref[0].astype(F32) + cls_got[...].astype(F32)
        for c in ag:
            c.wait_recv()
        net.finish()
        for c in stores:
            c.wait()

    shape = jax.ShapeDtypeStruct
    vmem = pl.BlockSpec(memory_space=pltpu.VMEM)
    full = [(2, lines, 2, size, w) for w in widths]
    half = [(2, lines, size, w) for w in widths]
    n_sems = n + n_mp
    out = pl.pallas_call(
        kernel,
        in_specs=[ANY] * (n_load + n_mp - 1),
        out_specs=[ANY] * (2 * n) + [vmem] + [ANY] * (n_mp - 1),
        out_shape=[shape(h, F32) for h in half]
        + [shape(h, BF16) for h in half]
        + [shape(cls_blocks.shape[1:], F32)]
        + [shape(a.shape, a.dtype) for a in sends],
        scratch_shapes=[pltpu.VMEM(a.shape, a.dtype) for a in inputs]
        + [pltpu.VMEM(f, BF16) for f in full]
        + [pltpu.VMEM(f, BF16) for f in full]
        + [pltpu.VMEM(f, F32) for f in full]
        + [pltpu.VMEM(h, F32) for h in half]
        + [pltpu.VMEM(h, BF16) for h in half]
        + [
            pltpu.VMEM(cls_blocks.shape[1:], BF16),
            pltpu.SemaphoreType.DMA((n_load,)),
            pltpu.SemaphoreType.DMA((2 * n,)),
            pltpu.SemaphoreType.DMA((n_sems,)),
            pltpu.SemaphoreType.DMA((n_sems,)),
        ],
        compiler_params=pltpu.CompilerParams(vmem_limit_bytes=60 * 1024 * 1024, collective_id=2, has_side_effects=True),
        cost_estimate=cost(2 * rows * dim * n_mp * sum(widths), rows * width * n_mp * 8),
        name="grads",
    )(*inputs, *sends)
    return out[:n], out[n : 2 * n], out[2 * n], out[2 * n + 1 :]


def assemble(plan, ids, parts, dtype, name):
    n_mp, seqs, share, dim = parts.shape

    def kernel(ids_ref, part_ref, out_ref):
        out_ref[...] = part_ref[...].astype(dtype)

    relative = lambda i: i % 2 * 2 + i // 2
    return pl.pallas_call(
        kernel,
        grid_spec=pltpu.PrefetchScalarGridSpec(
            num_scalar_prefetch=1,
            grid=(n_mp,),
            in_specs=[pl.BlockSpec((None, seqs, share, dim), lambda i, *_: (i, 0, 0, 0))],
            out_specs=pl.BlockSpec((seqs, None, share, dim), lambda i, ids_ref: (0, ids_ref[1] ^ relative(i), 0, 0)),
        ),
        out_shape=jax.ShapeDtypeStruct((seqs, n_mp, share, dim), dtype),
        compiler_params=PARAMS,
        cost_estimate=cost(0, seqs * n_mp * share * dim * 8),
        name=name,
    )(ids, parts).reshape(seqs * n_mp * share, dim)


def finish(plan, low, proj_grads, w, middle_grad, x, params, sums, zx, xz, z_only):
    seqs = len(proj_grads)
    dim = low.shape[1]
    cols = w.shape[2]
    n_mp = plan.n_mp
    share = LEN // n_mp
    lines, size, merge = plan.groups // 2, plan.block, plan.merge
    dp_bits = [1 << i for i in range(plan.n_dp.bit_length() - 1)]
    far = [2 * k * merge for k in range(1, lines)]
    partners = [("mp", 1), ("mp", 2)] + [("dp", b) for b in sorted(set(dp_bits + far + [merge]))]
    stages = [("mp", 1), ("mp", 2)] + [("dp", b) for b in dp_bits]
    inputs = [a for pair in zx + xz for a in pair] + list(z_only) + [w] + [g for seq in proj_grads for g in seq]
    inputs += [low, x, middle_grad]
    n_in = len(inputs)
    n_zx, n_xz, n_z = len(zx), len(xz), len(z_only)
    n_sems = (lines - 1) * (n_zx + n_xz + n_z + 1) + n_zx + n_xz + 1 + 4 * seqs + len(stages)
    n_out = 3 + n_zx + n_xz + n_z

    def kernel(*refs):
        sources, (norm_ref, sums_ref), refs = refs[:n_in], refs[n_in : n_in + 2], refs[n_in + 2 :]
        rows_ref, qkv_out, total_ref, *owned = refs[:n_out]
        zx_out, xz_out, z_out = owned[:n_zx], owned[n_zx : n_zx + n_xz], owned[n_zx + n_xz :]
        scratch = list(refs[n_out:])
        take = lambda n: [scratch.pop(0) for _ in range(n)]
        targets = take(n_in)
        t_keep, t_send, t_got, t_mine, x_send, x_got, acc, q_low, q_y, q_send, q_z, got_sums, load_sems, send_sems, recv_sems = take(15)
        zx_low, zx_got, zx_send, zx_last = take(n_zx), take(n_zx), take(n_zx), take(n_zx)
        xz_low, xz_got, xz_send, xz_last = take(n_xz), take(n_xz), take(n_xz), take(n_xz)
        z_low, z_got = take(n_z), take(n_z)
        loads = Loads(sources, targets, load_sems)
        net = Sender(send_sems, recv_sems)
        copy = net.copy
        group = net.dp // merge
        z, y = group // 2, group % 2
        side, core = net.mp // 2, net.mp % 2
        net.meet(partners)
        others = range(1, lines)
        to_z = lambda src, dst, k: copy(src, dst, "dp", 2 * k * merge)
        pair = lambda i: (loads[2 * i], loads[2 * i + 1])
        both = lambda a, b, *at: a[at].astype(F32) + b[at].astype(F32)

        xz_copies = []
        for i in range(n_xz):
            a, b = pair(n_zx + i)
            xz_low[i][...] = both(a, b, 1 - side).astype(BF16)
            xz_copies.append(copy(xz_low[i], xz_got[i], "mp", 2))
        z_copies = []
        for i in range(n_zx):
            a, b = pair(i)
            for k in others:
                for s in (0, 1):
                    zx_low[i][k - 1, s] = both(a, b, s, flip(z, k)).astype(BF16)
                z_copies.append(to_z(zx_low[i].at[k - 1], zx_got[i].at[k - 1], k))
        z_from = 2 * (n_zx + n_xz)
        for i in range(n_z):
            for k in others:
                z_low[i][k - 1] = loads[z_from + i][flip(z, k)].astype(BF16)
                z_copies.append(to_z(z_low[i].at[k - 1], z_got[i].at[k - 1], k))

        w_at = z_from + n_z
        w_ref = loads[w_at]
        pg = [[loads[w_at + 1 + 3 * s + p] for p in range(3)] for s in range(seqs)]
        core_copies = []
        x_copies = []

        def over_x(s):
            core_copies[s].wait_recv()
            x_send[s] = (t_keep[s, 1].astype(F32) + t_got[s, 1].astype(F32)).astype(BF16)
            x_copies.append(copy(x_send.at[s], x_got.at[s], "mp", 2))
            t_mine[s] = t_keep[s, 0].astype(F32) + t_got[s, 0].astype(F32)

        for s in range(seqs):

            def terms(target, i, carry):
                to_other = i // 2
                row_side = side + i % 2 * (1 - 2 * side)
                row_core = core + (1 - to_other) * (1 - 2 * core)
                at = pl.ds(pl.multiple_of((row_side * 2 + row_core) * share, share), share)
                gq, gk, gv = (ref[at, :] for ref in pg[s])
                total = dot(gq, w_ref[0], 1, 1) + dot(gk, w_ref[1], 1, 1) + dot(gv, w_ref[2], 1, 1)
                target[s, i % 2] = total.astype(BF16)
                return carry

            lax.fori_loop(0, 2, functools.partial(terms, t_send), 0)
            core_copies.append(copy(t_send.at[s], t_got.at[s], "mp", 1))
            lax.fori_loop(2, 4, functools.partial(terms, t_keep), 0)
            over_x(s)

        low_ref = loads[n_in - 3]
        for s in range(seqs):
            for p in range(3):
                part = dot(low_ref[s * LEN : (s + 1) * LEN, :], pg[s][p][...], 0, 0)
                acc[p] = part if s == 0 else acc[p] + part
        for p in range(3):
            q_low[p] = acc[p].reshape(lines, 2, size, cols).astype(BF16)
        y_copy = copy(q_low.at[:, :, 1 - y], q_y, "dp", merge)

        x_ref, mid_ref = loads[n_in - 2], loads[n_in - 1]
        total_ref[...] = sums_ref[...]
        row_copies = []
        q_copies = []
        for s in range(seqs):
            at = slice(s * share, (s + 1) * share)
            normed, scale = norm_parts(x_ref[at, :].astype(F32))
            x_copies[s].wait_recv()
            first = t_mine[s] + x_got[s].astype(F32)
            total_ref[0:1, :] += jnp.sum(first * normed, axis=0, keepdims=True)
            total_ref[1:2, :] += jnp.sum(first, axis=0, keepdims=True)
            rows_ref[0, s] = (mid_ref[at, :] + norm_back(first, normed, scale, norm_ref[0:1, :])).astype(BF16)
            row_copies.append(copy(rows_ref.at[0, s], rows_ref.at[1, s], "mp", 2))
            if s == 0:
                y_copy.wait_recv()
                for line in range(lines):
                    for p in range(3):
                        rows_at = pl.ds(pl.multiple_of((line * 2 + y) * size, 8), size)
                        q_send[line, p] = (acc[p, rows_at, :] + q_y[p, line].astype(F32)).astype(BF16)
                q_copies = [to_z(q_send.at[flip(z, k)], q_z.at[k - 1], k) for k in others]
            if s == seqs - 2:
                for i in range(n_xz):
                    a, b = pair(n_zx + i)
                    xz_copies[i].wait_recv()
                    for k in others:
                        at_z = flip(z, k)
                        total = both(a, b, side, at_z) + xz_got[i][at_z].astype(F32)
                        xz_send[i][k - 1] = total.astype(BF16)
                        z_copies.append(to_z(xz_send[i].at[k - 1], xz_last[i].at[k - 1], k))
        mate_copies = []
        for n, (axis, bits) in enumerate(stages):
            count = 8 if axis == "mp" else 16
            stage = copy(total_ref.at[pl.ds(0, count)], got_sums.at[n, pl.ds(0, count)], axis, bits)
            net.started.pop()
            stage.wait()
            total_ref[0:count, :] += got_sums[n, 0:count, :]
            if 1 <= n < 1 + seqs:
                row_copies[n - 1].wait_recv()
                mate_copies.append(copy(rows_ref.at[pl.ds(0, 2), n - 1], rows_ref.at[pl.ds(2, 2), n - 1], "mp", 1))
        for c in z_copies:
            c.wait_recv()
        last_copies = []
        for i in range(n_zx):
            a, b = pair(i)
            other = both(a, b, 1 - side, z) + sum(zx_got[i][k - 1, 1 - side].astype(F32) for k in others)
            zx_send[i][...] = other.astype(BF16)
            last_copies.append(copy(zx_send[i], zx_last[i], "mp", 2))
            zx_out[i][...] = both(a, b, side, z) + sum(zx_got[i][k - 1, side].astype(F32) for k in others)
        for i in range(n_xz):
            a, b = pair(n_zx + i)
            own = both(a, b, side, z) + xz_got[i][z].astype(F32)
            xz_out[i][...] = own + sum(xz_last[i][k - 1].astype(F32) for k in others)
        for i in range(n_z):
            z_out[i][...] = loads[z_from + i][z] + sum(z_got[i][k - 1].astype(F32) for k in others)
        for c in q_copies:
            c.wait_recv()
        for p in range(3):
            rows_at = pl.ds(pl.multiple_of((z * 2 + y) * size, 8), size)
            own = acc[p, rows_at, :] + q_y[p, z].astype(F32)
            qkv_out[p] = own + sum(q_z[k - 1, p].astype(F32) for k in others)
        for i, c in enumerate(last_copies):
            c.wait_recv()
            zx_out[i][...] += zx_last[i][...].astype(F32)
        for c in mate_copies:
            c.wait_recv()
        net.finish()

    vmem = pl.BlockSpec(memory_space=pltpu.VMEM)
    shape = jax.ShapeDtypeStruct
    blk = (3, size, cols)
    piece = lambda a: a.shape[-2:]
    buf = lambda a, lead, t=BF16: pltpu.VMEM(tuple(lead) + piece(a), t)
    three = lines - 1
    scratch = [pltpu.VMEM(a.shape, a.dtype) for a in inputs]
    scratch += [
        pltpu.VMEM((seqs, 2, share, dim), BF16),
        pltpu.VMEM((seqs, 2, share, dim), BF16),
        pltpu.VMEM((seqs, 2, share, dim), BF16),
        pltpu.VMEM((seqs, share, dim), F32),
        pltpu.VMEM((seqs, share, dim), BF16),
        pltpu.VMEM((seqs, share, dim), BF16),
        pltpu.VMEM((3, dim, cols), F32),
        pltpu.VMEM((3, lines, 2, size, cols), BF16),
        pltpu.VMEM((3, lines, size, cols), BF16),
        pltpu.VMEM((lines,) + blk, BF16),
        pltpu.VMEM((three,) + blk, BF16),
        pltpu.VMEM((len(stages), 16, dim), F32),
        pltpu.SemaphoreType.DMA((n_in,)),
        pltpu.SemaphoreType.DMA((n_sems,)),
        pltpu.SemaphoreType.DMA((n_sems,)),
    ]
    firsts, seconds = [a for a, _ in zx], [a for a, _ in xz]
    for lead in ((three, 2), (three, 2), (), ()):
        scratch += [buf(a, lead) for a in firsts]
    for lead in ((lines,), (lines,), (three,), (three,)):
        scratch += [buf(a, lead) for a in seconds]
    scratch += [buf(a, (three,)) for a in z_only] + [buf(a, (three,)) for a in z_only]
    out = pl.pallas_call(
        kernel,
        in_specs=[ANY] * n_in + [vmem] * 2,
        out_specs=[vmem] * n_out,
        out_shape=[shape((4, seqs, share, dim), BF16), shape(blk, F32), shape(sums.shape, F32)]
        + [shape(piece(a), F32) for a in firsts + seconds + list(z_only)],
        scratch_shapes=scratch,
        compiler_params=pltpu.CompilerParams(vmem_limit_bytes=60 * 1024 * 1024, collective_id=1, has_side_effects=True),
        cost_estimate=cost(12 * seqs * LEN * dim * cols, seqs * LEN * dim * 8),
        name="finish",
    )(*inputs, params, sums)
    return out[0], out[1], out[2], out[3:]


def adam_update(weight, moment_one, moment_two, gradient, step_rate, decay_rate):
    fresh_one = BETA_ONE * moment_one + (1.0 - BETA_ONE) * gradient
    fresh_two = BETA_TWO * moment_two + (1.0 - BETA_TWO) * gradient * gradient
    one_hat = fresh_one / (1.0 - BETA_ONE**STEP)
    two_hat = fresh_two / (1.0 - BETA_TWO**STEP)
    updated = weight - step_rate * (one_hat / (jnp.sqrt(two_hat) + ADAM_EPS) + decay_rate * weight)
    return (fresh_one, fresh_two, updated)


def shards(
    tokens,
    seg_ids,
    labels,
    w_qkv,
    m_qkv,
    v_qkv,
    w_out,
    m_out,
    v_out,
    w_up,
    m_up,
    v_up,
    w_down,
    m_down,
    v_down,
    w_cls,
    m_cls,
    v_cls,
    norm_params,
    m_norm,
    v_norm,
    qk_gain,
    m_qk,
    v_qk,
    *,
    n_dp,
    n_mp,
):
    dp, mp = lax.axis_index("dp"), lax.axis_index("mp")
    group_rows, dim = tokens.shape
    plan = Plan(n_dp, n_mp, dim)
    seqs = group_rows // LEN
    share = LEN // n_mp
    rows = seqs * share
    cols = w_qkv.shape[2]
    classes = w_cls.shape[1]
    class_cols = -(-classes // 128) * 128
    out_cols = -(-cols // 128) * 128
    ids = jnp.stack([dp // plan.merge, mp]).astype(jnp.int32)

    new_image = seg_ids != jnp.concatenate([jnp.full((1,), -1, jnp.int32), seg_ids[:-1]])
    count = jnp.sum((new_image & (seg_ids != PAD_ID)).astype(F32))
    dim_part, head_part = norm_params.shape[1], qk_gain.shape[2]
    pad = lambda a, r, c: jnp.pad(a, ((0, r - a.shape[0]), (0, c - a.shape[1])))
    low_param = lambda a: lax.reduce_precision(a, 8, 7)
    small = jnp.concatenate(
        [
            pad(low_param(norm_params), 8, 128),
            pad(low_param(qk_gain).reshape(2, cols // HEAD * head_part), 8, 128),
            pad(count.reshape(1, 1), 8, 128),
        ]
    )
    qkv_block = plan.merged(w_qkv.astype(BF16), 1)
    up_block = plan.merged(w_up.astype(BF16), 0)
    down_block = plan.merged(w_down.T.astype(BF16), 0)
    out_block = plan.merged(pad(w_out.T.astype(BF16), dim_part, out_cols), 0)
    cls_block = plan.merged(pad(w_cls.astype(BF16), dim_part, class_cols), 0)
    small_block = plan.merged(small[None], 0)

    head_of = jnp.arange(cols) // HEAD
    ones = jnp.where(head_of[:, None] == head_of[None, :], 1.0 / HEAD, 0.0).astype(BF16)
    starts, widths, live = key_windows(seg_ids)
    seg_col = seg_ids.reshape(group_rows, 1)
    seg_row = seg_ids.reshape(-1, 1, LEN)
    normed_low, pq, pk, q, k, v, w, up, down, out_w, cls, params, gains, images = gather_project(
        plan, tokens, qkv_block, up_block, down_block, out_block, cls_block, small_block, ones
    )
    w = w.reshape(3, dim, cols)
    out_w, cls = (a.reshape(n_mp, dim, a.shape[-1]) for a in (out_w, cls))
    up_across, down_across = plan.swap(up, "mp", 2), plan.group_swap(down, 1)
    up_mate, down_mate = plan.swap(up, "mp", 1), plan.swap(down, "mp", 1)
    up = [a.reshape(dim, a.shape[-1]) for a in (up, up_across, up_mate, plan.swap(up_across, "mp", 1))]
    down = [down, down_across, down_mate, plan.swap(down_across, "mp", 1)]
    image_total = images[0, 0]
    logs, received = [], []
    for s in range(seqs):
        ids_now = ids
        if s == 1:
            ids_now = lax.optimization_barrier((ids, up_mate, down_mate, logs[0]))[0]
        elif s == 2:
            ids_now = lax.optimization_barrier((ids, up_across, down_across, logs[1]))[0]
        *parts, log = attend(plan, s, ids_now, starts, widths, q, k, v, seg_col, seg_row)
        logs.append(log)
        received.append([parts[0]] + [plan.swap(parts[r], "mp", r) for r in range(1, n_mp)])
    attended = [jnp.concatenate([received[s][r] for s in range(seqs)], axis=0) for r in range(n_mp)]

    own = lambda a: lax.dynamic_slice_in_dim(a.reshape((seqs, n_mp, share) + a.shape[1:]), mp, 1, 1)
    x = own(tokens).reshape(rows, dim)
    seg = own(seg_ids).reshape(rows)
    middle, second_low, active, slope = feed_up(plan, ids, x, attended, params, out_w, up)
    result, block_rows, pool = feed_down(plan, ids, middle, active, seg.reshape(seqs, 1, share), params, down)

    pool = combine_pools(plan, combine_pools(plan, pool, 1, dim), 2, dim)
    block_rows, pool = lax.optimization_barrier((block_rows, pool))
    block_rows = block_rows.reshape(seqs, share, dim)
    block_pair = jnp.stack([block_rows, plan.swap(block_rows, "mp", 2)])
    block_parts = jnp.concatenate([block_pair, plan.swap(block_pair, "mp", 1)])
    block_out = assemble(plan, ids, block_parts, BF16, "block_out")
    slot_label = labels.reshape(seqs, IMG_SEQ)
    slot_label = slot_label // classes * class_cols + slot_label % classes
    slot_label = jnp.pad(slot_label, ((0, 0), (0, SLOTS - IMG_SEQ)), constant_values=-1).reshape(seqs * SLOTS, 1)
    row_grads, stats, loss, cls_blocks = classify(plan, ids, pool, slot_label, images, cls, classes)
    mean_loss = plan.total(loss, "dp")[0, 0] / image_total

    result_low, hidden_low, middle_low, middle_grad, *rest = feed_back(
        plan, ids, result, middle, slope, row_grads, stats, seg.reshape(rows, 1), params, out_w, up, down, cols
    )
    attended_grads, sums = rest[:n_mp], rest[n_mp]
    cls_blocks = cls_blocks.reshape(2, plan.groups // 2, plan.block, class_cols)
    kept, sent, cls_sum, arrived = weight_grads(
        plan, [(result_low, active), (second_low, hidden_low)], (middle_low, attended), cls_blocks, attended_grads[1:]
    )
    grad_parts = [attended_grads[0]] + list(arrived)
    got = [plan.group_swap(part, 1) for part in sent]

    proj_grads, gain_sums = [], []
    for s in range(seqs):
        *grad, gain_sum = attend_back(
            plan, s, ids, starts, widths, live, q, k, v, pq, pk, gains, ones, grad_parts, logs[s], seg_col, seg_row
        )
        proj_grads.append(grad)
        gain_sums.append(gain_sum)
    *got, block_out, _ = lax.optimization_barrier((*got, block_out, proj_grads[-1][0]))

    sums = jnp.concatenate(
        [jnp.zeros((2, dim), F32), jnp.sum(sums, axis=1), jnp.zeros((1, dim), F32), pad(jnp.sum(sum(gain_sums), axis=1), 8, dim)]
    )
    down_pair, up_pair, out_pair = zip(kept, got)
    last_rows, grad_qkv, small_grads, owned = finish(
        plan, normed_low, proj_grads, w, middle_grad, x, params, sums, [up_pair, out_pair], [down_pair], [cls_sum]
    )
    grad_qkv = plan.unmerged(grad_qkv, 1)
    grad_up, grad_out, grad_down, grad_cls = (plan.unmerged(a, 0) for a in owned)
    grad_out, grad_down, grad_cls = grad_out[:, :cols].T, grad_down.T, grad_cls[:, :classes]
    input_grad = assemble(plan, ids, last_rows, F32, "input_grad")
    norm_part = lax.dynamic_slice(small_grads, (0, dp * dim_part), (7, dim_part))
    qk_part = lax.dynamic_slice_in_dim(small_grads[8:10, :cols].reshape(2, cols // HEAD, HEAD), dp * head_part, head_part, 2)
    reduced = (grad_qkv, grad_out, grad_up, grad_down, grad_cls, norm_part, qk_part)
    groups = (
        (w_qkv, m_qkv, v_qkv, MATRIX_RATE, MATRIX_DECAY),
        (w_out, m_out, v_out, MATRIX_RATE, MATRIX_DECAY),
        (w_up, m_up, v_up, MATRIX_RATE, MATRIX_DECAY),
        (w_down, m_down, v_down, MATRIX_RATE, MATRIX_DECAY),
        (w_cls, m_cls, v_cls, MATRIX_RATE, MATRIX_DECAY),
        (norm_params, m_norm, v_norm, GAIN_RATE, 0.0),
        (qk_gain, m_qk, v_qk, GAIN_RATE, 0.0),
    )
    outputs = [block_out, input_grad, mean_loss]
    for number, group in enumerate(groups):
        fresh_one, fresh_two, updated = adam_update(group[0], group[1], group[2], reduced[number], group[3], group[4])
        if number == 5:
            outputs = outputs + [fresh_one, fresh_two[:6], fresh_two[6], updated]
        else:
            outputs = outputs + [fresh_one, fresh_two, updated]
    return tuple(outputs)


def solution(mesh):
    rows_cols = (P("mp", "dp"),) * 3
    cols_rows = (P("dp", "mp"),) * 3
    qkv_spec = (P(None, "dp", "mp"),) * 3
    qk_spec = (P(None, "mp", "dp"),) * 3
    norm_spec = P(None, "dp")
    in_specs = (
        (P("dp", None), P("dp"), P("dp")) + qkv_spec + rows_cols + cols_rows + rows_cols + cols_rows + (norm_spec,) * 3 + qk_spec
    )
    out_specs = (
        (P("dp", None), P("dp", None), P())
        + qkv_spec
        + rows_cols
        + cols_rows
        + rows_cols
        + cols_rows
        + (norm_spec, norm_spec, P("dp"), norm_spec)
        + qk_spec
    )
    body = functools.partial(shards, n_dp=mesh.shape["dp"], n_mp=mesh.shape["mp"])
    return jax.shard_map(body, mesh=mesh, in_specs=in_specs, out_specs=out_specs, check_vma=False)
```

```python
import functools

import jax
import jax.numpy as jnp
from jax import lax
from jax.experimental import pallas as pl
from jax.experimental.pallas import tpu as pltpu
from jax.sharding import PartitionSpec as P

LEN = 1024
STEP = 10
SEQ_DEV = 3
IMG_DEV = 180
PAD_ID = 180

NORM_EPS = 1e-06
MASK_FILL = -1000000000.0
BETA_ONE = 0.9
BETA_TWO = 0.999
ADAM_EPS = 1e-08
MATRIX_RATE = 0.1
MATRIX_DECAY = 0.1
GAIN_RATE = 0.8

HEAD = 64
QB = 256
QBLOCKS = LEN // QB
WINDOWS = (384, 512, 768, 1024)
ALIGN = 64
LANES = 128
F32 = jnp.float32
BF16 = jnp.bfloat16
VMEM_LIMIT = 56 * 1024 * 1024
IMG_SEQ = 60
SLOTS = 64
ANY = pl.BlockSpec(memory_space=pl.ANY)
PARAMS = pltpu.CompilerParams(vmem_limit_bytes=VMEM_LIMIT)


def dot(a, b, ca, cb):
    return lax.dot_general(a, b, (((ca,), (cb,)), ((), ())), preferred_element_type=F32)


def head_mean(values, ones_block):
    high = values.astype(BF16)
    rest = (values - high.astype(F32)).astype(BF16)
    return dot(high, ones_block, 1, 0) + dot(rest, ones_block, 1, 0)


def norm_parts(values):
    centre = values - jnp.mean(values, axis=-1, keepdims=True)
    spread = jnp.mean(centre * centre, axis=-1, keepdims=True)
    scale = lax.rsqrt(spread + NORM_EPS)
    return centre * scale, scale


def norm_back(grad, normed, scale, gain):
    scaled = grad * gain
    first = jnp.mean(scaled, axis=-1, keepdims=True)
    second = jnp.mean(scaled * normed, axis=-1, keepdims=True)
    return (scaled - first - normed * second) * scale


def head_parts(values, ones_block):
    centre = values - head_mean(values, ones_block)
    scale = lax.rsqrt(head_mean(centre * centre, ones_block) + NORM_EPS)
    return centre * scale, scale


def cost(flops, read, exps=0):
    return pl.CostEstimate(flops=int(flops), bytes_accessed=int(read), transcendentals=int(exps))


def whole(shape):
    return pl.BlockSpec(tuple(shape), lambda *_: (0,) * len(shape))


class Plan:
    def __init__(self, n_dp, n_mp, dim):
        self.n_dp, self.n_mp = n_dp, n_mp
        self.merge = 1 if dim // n_dp % 16 == 0 else 2
        self.groups = n_dp // self.merge
        self.block = dim // self.groups
        self.far = [2 * k for k in range(1, self.groups // 2)]

    def swap(self, value, axis, bits):
        size = self.n_dp if axis == "dp" else self.n_mp
        return lax.ppermute(value, axis, [(i, i ^ bits) for i in range(size)])

    def group_swap(self, value, bits):
        return self.swap(value, "dp", bits * self.merge)

    def merged(self, value, dim):
        if self.merge == 1:
            return value
        other = self.swap(value, "dp", 1)
        even = lax.axis_index("dp") % 2 == 0
        first, second = jnp.where(even, value, other), jnp.where(even, other, value)
        return jnp.concatenate([first, second], axis=dim)

    def unmerged(self, value, dim):
        if self.merge == 1:
            return value
        half = value.shape[dim] // 2
        me = lax.axis_index("dp") % 2
        mine = lax.dynamic_slice_in_dim(value, me * half, half, dim)
        theirs = lax.dynamic_slice_in_dim(value, (1 - me) * half, half, dim)
        return mine + self.swap(theirs, "dp", 1)

    def total(self, value, axis):
        size = self.n_dp if axis == "dp" else self.n_mp
        bits = 1
        while bits < size:
            value = value + self.swap(value, axis, bits)
            bits *= 2
        return value


MESH = pl.DeviceIdType.MESH


def flip(index, bits):
    bit = 1
    while bit <= bits:
        if bits & bit:
            index = index + bit * (1 - 2 * (index // bit % 2))
        bit *= 2
    return index


class Chain:
    def __init__(self, region, order, lines):
        self.region, self.steps = region, order
        self.copies = sum({"z": lines - 1, "c": 2}.get(step, 1) for step in order)


class Gatherer:
    def __init__(self, plan, send_sems, recv_sems):
        self.plan, self.send_sems, self.recv_sems = plan, send_sems, recv_sems
        self.dp, self.mp = lax.axis_index("dp"), lax.axis_index("mp")
        self.pair = self.dp % plan.merge
        group = self.dp // plan.merge
        self.z, self.y = group // 2, group % 2
        self.x, self.core = self.mp // 2, self.mp % 2
        self.lines = plan.groups // 2
        self.used = 0
        self.pending = []

    def device(self, z, y, x, core):
        return ((z * 2 + y) * self.plan.merge + self.pair, x * 2 + core)

    def here(self):
        return self.z, self.y, self.x, self.core

    def meet(self, barrier):
        z, y, x, core = self.here()
        others = [(z, 1 - y, x, core), (z, y, 1 - x, core), (z, y, x, 1 - core)]
        others += [(flip(z, k), y, x, core) for k in range(1, self.lines)]
        for other in others:
            pl.semaphore_signal(barrier, inc=1, device_id=self.device(*other), device_id_type=MESH)
        pl.semaphore_wait(barrier, len(others))

    def start(self, chain, number, source=None):
        step, done = chain.steps[number], chain.steps[:number]
        z, y, x, core = self.here()
        spot = dict(z=None if "z" in done else z, y=None if "y" in done else y, x=None if "x" in done else x, core=core)
        if step == "z":
            copies = [(spot, (flip(z, k), y, x, core)) for k in range(1, self.lines)]
        elif step == "c":
            copies = [({**spot, "x": side}, (z, y, x, 1 - core)) for side in (0, 1)]
        else:
            copies = [(spot, dict(y=(z, 1 - y, x, core), x=(z, y, 1 - x, core))[step])]
        started = []
        for place, other in copies:
            region = chain.region(**place)
            out = pltpu.make_async_remote_copy(
                src_ref=region if source is None else source,
                dst_ref=region,
                send_sem=self.send_sems.at[self.used],
                recv_sem=self.recv_sems.at[self.used],
                device_id=self.device(*other),
                device_id_type=MESH,
            )
            self.used += 1
            out.start()
            started.append(out)
        self.pending += started
        return started

    @staticmethod
    def arrive(copies):
        for out in copies:
            out.wait_recv()

    def finish(self):
        for out in self.pending:
            out.wait_send()


class Loads:
    def __init__(self, sources, targets, sems):
        self.targets = targets
        self.copies = [pltpu.make_async_copy(a, b, sems.at[i]) for i, (a, b) in enumerate(zip(sources, targets))]
        self.done = [False] * len(self.copies)
        for c in self.copies:
            c.start()

    def __getitem__(self, i):
        if not self.done[i]:
            self.copies[i].wait()
            self.done[i] = True
        return self.targets[i]


class Sender:
    def __init__(self, send_sems, recv_sems):
        self.dp, self.mp = lax.axis_index("dp"), lax.axis_index("mp")
        self.send_sems, self.recv_sems = send_sems, recv_sems
        self.started, self.used = [], 0

    def device(self, axis, bits):
        return (flip(self.dp, bits), self.mp) if axis == "dp" else (self.dp, flip(self.mp, bits))

    def meet(self, partners):
        barrier = pltpu.get_barrier_semaphore()
        for axis, bits in partners:
            pl.semaphore_signal(barrier, inc=1, device_id=self.device(axis, bits), device_id_type=MESH)
        pl.semaphore_wait(barrier, len(partners))

    def copy(self, src, dst, axis, bits):
        n = self.used
        self.used += 1
        c = pltpu.make_async_remote_copy(
            src_ref=src,
            dst_ref=dst,
            send_sem=self.send_sems.at[n],
            recv_sem=self.recv_sems.at[n],
            device_id=self.device(axis, bits),
            device_id_type=MESH,
        )
        self.started.append(c)
        c.start()
        return c

    def finish(self):
        for c in self.started:
            c.wait_send()


def gather_project(plan, tokens, qkv_block, up_block, down_block, out_block, cls_block, small_block, ones):
    rows, dim = tokens.shape
    cols = ones.shape[0]
    n_mp, merge, size = plan.n_mp, plan.merge, plan.block
    lines = plan.groups // 2
    width = up_block.shape[1]
    out_cols, class_cols = out_block.shape[1], cls_block.shape[1]
    block = 512
    blocks = rows // block
    dim_part = dim // plan.n_dp
    head_part = HEAD // plan.n_dp

    orders = [("small", "zy"), ("w_qk", "zy"), ("w_v", "zy"), ("out", "zyxc"), ("cls", "zy"), ("up", "zy"), ("down", "zx")]
    sizes = {name: Chain(None, order, lines).copies for name, order in orders}
    n_sems = sum(sizes.values())

    def kernel(x_ref, qkv_in, up_in, down_in, out_in, cls_in, small_in, ones_ref, *refs):
        low_ref, pq_ref, pk_ref, q_ref, k_ref, v_ref, w_ref, up_ref, down_ref, o_ref, c_ref, norm_ref, gain_ref, image_ref = refs[:14]
        w_buf, small_buf, low_buf, pq_buf, pk_buf, q_buf, k_buf, v_buf, send_sems, recv_sems, own_sems, out_sems = refs[14:]
        g = Gatherer(plan, send_sems, recv_sems)
        z, y, x, core = g.here()
        everything = slice(None)

        def at(v):
            return everything if v is None else v

        def wide(ref, first, count):
            columns = pl.ds(first, count)
            return lambda z, y, x, core: ref.at[at(x), core, at(z), at(y), :, columns]

        regions = dict(
            w_qk=lambda z, y, x, core: w_buf.at[pl.ds(0, 2), at(z), at(y)],
            w_v=lambda z, y, x, core: w_buf.at[pl.ds(2, 1), at(z), at(y)],
            small=lambda z, y, x, core: small_buf.at[at(z), at(y)],
            up=lambda z, y, x, core: up_ref.at[at(z), at(y)],
            down=lambda z, y, x, core: down_ref.at[at(x), at(z)],
            out=wide(o_ref, 0, out_cols),
            cls=lambda z, y, x, core: c_ref.at[at(z), at(y)],
        )
        chains = {name: Chain(regions[name], order, lines) for name, order in orders}
        sources = dict(
            w_qk=qkv_in.at[pl.ds(0, 2)],
            w_v=qkv_in.at[pl.ds(2, 1)],
            small=small_in,
            up=up_in,
            down=down_in,
            out=out_in,
            cls=cls_in,
        )
        own = {}
        for i, (name, _) in enumerate(orders):
            own[name] = pltpu.make_async_copy(sources[name], regions[name](z, y, x, core), own_sems.at[i])
            own[name].start()
        live, reached = {}, {}

        def begin(name):
            live[name] = g.start(chains[name], 0, source=sources[name])
            reached[name] = 0

        def advance(*names):
            for name in names:
                if reached[name] == len(chains[name].steps):
                    continue
                if reached[name] == 0:
                    own[name].wait()
                g.arrive(live[name])
                reached[name] += 1
                if reached[name] < len(chains[name].steps):
                    live[name] = g.start(chains[name], reached[name])

        g.meet(pltpu.get_barrier_semaphore())
        for name in ("small", "w_qk", "w_v", "out", "cls"):
            begin(name)
        advance("small", "small")

        lane = lax.broadcasted_iota(jnp.int32, (128, dim), 0)
        column = lax.broadcasted_iota(jnp.int32, (128, dim), 1)
        head_lane = lax.broadcasted_iota(jnp.int32, (128, cols), 0)
        head_column = lax.broadcasted_iota(jnp.int32, (128, cols), 1)
        norm = jnp.zeros((8, dim), F32)
        gain = jnp.zeros((8, cols), F32)
        image = jnp.zeros((8, 128), F32)
        for d in range(plan.n_dp):
            part = small_buf[d // merge // 2, d // merge % 2, d % merge]
            spread = jnp.where((column == d * dim_part + lane) & (lane < dim_part), 1.0, 0.0).astype(BF16)
            norm = norm + dot(part[0:8].astype(BF16), spread, 1, 0)
            same = (head_column // HEAD == head_lane // head_part) & (head_column % HEAD == d * head_part + head_lane % head_part)
            gain = gain + dot(part[8:16].astype(BF16), jnp.where(same, 1.0, 0.0).astype(BF16), 1, 0)
            image = image + part[16:24]
        norm_ref[...] = norm
        gain_ref[...] = gain
        image_ref[...] = image

        def first_norm(i, carry):
            at_rows = pl.ds(pl.multiple_of(i * block, block), block)
            normed, _ = norm_parts(x_ref[at_rows, :].astype(F32))
            low_buf[at_rows, :] = (normed * norm[0:1, :] + norm[1:2, :]).astype(BF16)
            return carry

        third = blocks // 3
        lax.fori_loop(0, third, first_norm, 0)
        advance("w_qk", "w_v")
        begin("up")
        begin("down")
        lax.fori_loop(third, blocks, first_norm, 0)
        outs = [pltpu.make_async_copy(low_buf, low_ref, out_sems.at[0])]
        outs[0].start()
        advance("out", "cls", "w_qk", "w_v")
        outs.append(pltpu.make_async_copy(w_buf, w_ref, out_sems.at[1]))
        outs[1].start()

        def project(i, carry):
            at_rows = pl.ds(pl.multiple_of(i * block, block), block)
            low = low_buf[at_rows, :]
            pq = dot(low, w_buf[0].reshape(dim, cols), 1, 0)
            pk = dot(low, w_buf[1].reshape(dim, cols), 1, 0)
            pq_buf[at_rows, :] = pq
            pk_buf[at_rows, :] = pk
            v_buf[at_rows, :] = dot(low, w_buf[2].reshape(dim, cols), 1, 0).astype(BF16)
            nq, _ = head_parts(pq, ones_ref[...])
            nk, _ = head_parts(pk, ones_ref[...])
            q_buf[at_rows, :] = (nq * gain[0:1, :]).astype(BF16)
            k_buf[at_rows, :] = (nk * gain[1:2, :]).astype(BF16)
            return carry

        lax.fori_loop(0, third, project, 0)
        advance("out", "up", "down")
        lax.fori_loop(third, 2 * third, project, 0)
        lax.fori_loop(2 * third, blocks, project, 0)
        pairs = ((pq_buf, pq_ref), (pk_buf, pk_ref), (q_buf, q_ref), (k_buf, k_ref), (v_buf, v_ref))
        for i, (a, b) in enumerate(pairs):
            outs.append(pltpu.make_async_copy(a, b, out_sems.at[2 + i]))
            outs[-1].start()
        advance("out", "cls", "up", "down", "out")
        g.finish()
        for c in outs:
            c.wait()

    vmem = pl.BlockSpec(memory_space=pltpu.VMEM)
    shape = jax.ShapeDtypeStruct
    wide_shape = lambda c: (n_mp // 2, 2, lines, 2, size, c)
    n_rows = lambda c, t: shape((rows, c), t)
    return pl.pallas_call(
        kernel,
        in_specs=[vmem] + [ANY] * 6 + [vmem],
        out_specs=[ANY] * 11 + [vmem] * 3,
        out_shape=[n_rows(dim, BF16), n_rows(cols, F32), n_rows(cols, F32), n_rows(cols, BF16), n_rows(cols, BF16), n_rows(cols, BF16)]
        + [
            shape((3, lines, 2, size, cols), BF16),
            shape((lines, 2, size, width), BF16),
            shape((n_mp // 2, lines, size, width), BF16),
            shape(wide_shape(out_cols), BF16),
            shape((lines, 2, size, class_cols), BF16),
            shape((8, dim), F32),
            shape((8, cols), F32),
            shape((8, 128), F32),
        ],
        scratch_shapes=[
            pltpu.VMEM((3, lines, 2, size, cols), BF16),
            pltpu.VMEM((lines, 2, merge, 24, 128), F32),
            pltpu.VMEM((rows, dim), BF16),
            pltpu.VMEM((rows, cols), F32),
            pltpu.VMEM((rows, cols), F32),
            pltpu.VMEM((rows, cols), BF16),
            pltpu.VMEM((rows, cols), BF16),
            pltpu.VMEM((rows, cols), BF16),
            pltpu.SemaphoreType.DMA((n_sems,)),
            pltpu.SemaphoreType.DMA((n_sems,)),
            pltpu.SemaphoreType.DMA((len(orders),)),
            pltpu.SemaphoreType.DMA((7,)),
        ],
        compiler_params=pltpu.CompilerParams(vmem_limit_bytes=VMEM_LIMIT, collective_id=0, has_side_effects=True),
        cost_estimate=cost(6 * rows * dim * cols, rows * dim * 8),
        name="gather_project",
    )(tokens, qkv_block, up_block, down_block, out_block, cls_block, small_block, ones)


def head_masks(cols):
    lane = lax.broadcasted_iota(jnp.int32, (1, cols), 1)
    return [(lane >= h * HEAD) & (lane < (h + 1) * HEAD) for h in range(cols // HEAD)]


def spread_heads(block, masks):
    zero = jnp.zeros_like(block)
    return jnp.concatenate([jnp.where(m, block, zero) for m in masks], axis=0)


def join_heads(stacked, masks):
    total = stacked[0:QB]
    for h in range(1, len(masks)):
        total = jnp.where(masks[h], stacked[h * QB : (h + 1) * QB], total)
    return total


def by_window(width_ref, step, body):
    width = width_ref[step]
    for number, window in enumerate(WINDOWS):
        pl.when(width == number)(functools.partial(body, window))


def key_segments(row_ref, start, window):
    at = pl.ds(pl.multiple_of(start // LANES * LANES, LANES), window)
    return jnp.where(start % LANES == 0, row_ref[0, 0:1, at], row_ref[0, 1:2, at])


def seq_specs(seq, cols):
    block = lambda c: pl.BlockSpec((QB, c), lambda b, *_: (seq * QBLOCKS + b, 0))
    all_keys = lambda c: pl.BlockSpec((LEN, c), lambda b, *_: (seq, 0))
    seg_row = pl.BlockSpec((1, 2, LEN), lambda b, *_: (seq, 0, 0))
    return block, all_keys, seg_row


def attend(plan, ids, starts, widths, q, k, v, seg_col, seg_row):
    rows, cols = q.shape
    n_mp = plan.n_mp
    share = LEN // n_mp
    per = share // QB
    seqs = rows // LEN

    def kernel(ids_ref, start_ref, width_ref, q_ref, k_ref, v_ref, col_ref, row_ref, *outs):
        out_refs, log_ref = outs[:n_mp], outs[n_mp]
        seq, block = pl.program_id(0), pl.program_id(1)
        step = seq * QBLOCKS + block
        masks = head_masks(cols)
        heads = len(masks)

        def body(window):
            start = pl.multiple_of(start_ref[step], ALIGN)
            keys = k_ref[pl.ds(start, window), :]
            values = v_ref[pl.ds(start, window), :]
            q3 = spread_heads(q_ref[...], masks)
            s = (dot(q3, keys, 1, 1) * HEAD**-0.5).reshape(heads, QB, window)
            same = col_ref[...] == key_segments(row_ref, start, window)
            s = jnp.where(same[None], s, MASK_FILL)
            top = jnp.max(s, axis=-1, keepdims=True)
            e = jnp.exp(s - top)
            total = jnp.sum(e, axis=-1, keepdims=True)
            p = (e * (1.0 / total)).astype(BF16).reshape(heads * QB, window)
            out = join_heads(dot(p, values, 1, 0), masks).astype(BF16)
            other = (block // per) ^ ids_ref[1]
            at = pl.ds(pl.multiple_of(seq * share + block % per * QB, QB), QB)
            for r in range(n_mp):

                @pl.when(other == r)
                def _():
                    out_refs[r][at, :] = out

            log = top + jnp.log(total)
            lane = lax.broadcasted_iota(jnp.int32, (QB, 128), 1)
            logs = jnp.zeros((QB, 128), F32)
            for h in range(heads):
                logs = jnp.where(lane == h, log[h], logs)
            log_ref[...] = logs

        by_window(width_ref, step, body)

    block = lambda c: pl.BlockSpec((QB, c), lambda s, b, *_: (s * QBLOCKS + b, 0))
    all_keys = lambda c: pl.BlockSpec((LEN, c), lambda s, b, *_: (s, 0))
    return pl.pallas_call(
        kernel,
        grid_spec=pltpu.PrefetchScalarGridSpec(
            num_scalar_prefetch=3,
            grid=(seqs, QBLOCKS),
            in_specs=[block(cols), all_keys(cols), all_keys(cols), block(1), pl.BlockSpec((1, 2, LEN), lambda s, b, *_: (s, 0, 0))],
            out_specs=[whole((seqs * share, cols))] * n_mp + [block(128)],
        ),
        out_shape=[jax.ShapeDtypeStruct((seqs * share, cols), BF16)] * n_mp + [jax.ShapeDtypeStruct((rows, 128), F32)],
        compiler_params=PARAMS,
        cost_estimate=cost(60 * rows * LEN * cols, rows * cols * 8, rows * LEN),
        name="attend",
    )(ids, starts, widths, q, k, v, seg_col, seg_row)


def attend_back(plan, seq, ids, starts, widths, live, q, k, v, pq, pk, gains, ones, grads, logs, seg_col, seg_row):
    rows, cols = q.shape
    n_mp = plan.n_mp
    share = LEN // n_mp
    per = share // QB

    def kernel(ids_ref, start_ref, width_ref, live_ref, q_ref, k_ref, v_ref, pq_ref, pk_ref, gain_ref, ones_ref, col_ref, row_ref, log_ref, *refs):
        grad_refs, (gq_ref, gk_ref, gv_ref, sum_ref, dk_ref, dv_ref) = refs[:n_mp], refs[n_mp:]
        block = pl.program_id(0)
        step = seq * QBLOCKS + block
        masks = head_masks(cols)
        heads = len(masks)

        @pl.when(block == 0)
        def _():
            dk_ref[...] = jnp.zeros_like(dk_ref)
            dv_ref[...] = jnp.zeros_like(dv_ref)
            sum_ref[...] = jnp.zeros_like(sum_ref)

        def back(values, grad, slot):
            ones_block = ones_ref[...]
            normed, scale = head_parts(values, ones_block)
            sum_ref[slot] += jnp.sum((grad * normed).reshape(-1, 8, cols), axis=0)
            scaled = grad * gain_ref[slot : slot + 1, :]
            first = head_mean(scaled, ones_block)
            second = head_mean(scaled * normed, ones_block)
            return ((scaled - first - normed * second) * scale).astype(BF16)

        def body(window):
            start = pl.multiple_of(start_ref[step], ALIGN)
            keys = pl.ds(start, window)
            k_win = k_ref[keys, :]
            v_win = v_ref[keys, :]
            other = (block // per) ^ ids_ref[1]
            at = pl.ds(pl.multiple_of(block % per * QB, QB), QB)
            g = grad_refs[0][at, :]
            for r in range(1, n_mp):
                g = jnp.where(other == r, grad_refs[r][at, :], g)
            q3 = spread_heads(q_ref[...], masks)
            g3 = spread_heads(g, masks)
            s = (dot(q3, k_win, 1, 1) * HEAD**-0.5).reshape(heads, QB, window)
            same = col_ref[...] == key_segments(row_ref, start, window)
            all_logs = log_ref[...]
            log = jnp.stack([all_logs[:, h : h + 1] for h in range(heads)])
            p = jnp.exp(jnp.where(same[None], s - log, MASK_FILL))
            dp = dot(g3, v_win, 1, 1).reshape(heads, QB, window)
            inner = jnp.sum(p * dp, axis=-1, keepdims=True)
            ds = (p * (dp - inner)).astype(BF16).reshape(heads * QB, window)
            p_low = p.astype(BF16).reshape(heads * QB, window)
            dv_ref[keys, :] += dot(p_low, g3, 0, 0)
            dk_ref[keys, :] += dot(ds, q3, 0, 0) * HEAD**-0.5
            dq = join_heads(dot(ds, k_win, 1, 0), masks) * HEAD**-0.5
            gq_ref[...] = back(pq_ref[...], dq, 0)

        alive = live_ref[step]

        @pl.when(alive == 0)
        def _():
            gq_ref[...] = jnp.zeros_like(gq_ref)

        @pl.when(alive != 0)
        def _():
            by_window(width_ref, step, body)

        @pl.when(block == QBLOCKS - 1)
        def _():
            gv_ref[...] = dv_ref[...].astype(BF16)

            def keys_back(i, carry):
                at = pl.ds(pl.multiple_of(i * share, share), share)
                gk_ref[at, :] = back(pk_ref[at, :], dk_ref[at, :], 1)
                return carry

            lax.fori_loop(0, n_mp, keys_back, 0)

    block, all_keys, row_spec = seq_specs(seq, cols)
    grad_spec = pl.BlockSpec((share, cols), lambda b, *_: (seq, 0))
    shape = jax.ShapeDtypeStruct((LEN, cols), BF16)
    return pl.pallas_call(
        kernel,
        grid_spec=pltpu.PrefetchScalarGridSpec(
            num_scalar_prefetch=4,
            grid=(QBLOCKS,),
            in_specs=[block(cols), all_keys(cols), all_keys(cols), block(cols), all_keys(cols), whole(gains.shape), whole(ones.shape)]
            + [block(1), row_spec, block(128)]
            + [grad_spec] * n_mp,
            out_specs=[pl.BlockSpec((QB, cols), lambda b, *_: (b, 0)), whole((LEN, cols)), whole((LEN, cols)), whole((2, 8, cols))],
            scratch_shapes=[pltpu.VMEM((LEN, cols), F32), pltpu.VMEM((LEN, cols), F32)],
        ),
        out_shape=[shape, shape, shape, jax.ShapeDtypeStruct((2, 8, cols), F32)],
        compiler_params=PARAMS,
        cost_estimate=cost(60 * LEN * LEN * cols, LEN * cols * 24, LEN * LEN),
        name="attend_back",
    )(ids, starts, widths, live, q, k, v, pq, pk, gains, ones, seg_col, seg_row, logs, *grads)


def key_windows(seg_ids):
    seg = seg_ids.reshape(-1, LEN)
    first = seg[:, ::QB]
    last = seg[:, QB - 1 :: QB]
    low = jnp.sum((seg[:, None, :] < first[:, :, None]).astype(jnp.int32), axis=2)
    high = jnp.sum((seg[:, None, :] <= last[:, :, None]).astype(jnp.int32), axis=2)
    base = low // ALIGN * ALIGN
    number = jnp.full(base.shape, len(WINDOWS) - 1, jnp.int32)
    start = jnp.zeros_like(base)
    for choice in range(len(WINDOWS) - 2, -1, -1):
        at = jnp.minimum(base, LEN - WINDOWS[choice])
        fits = high <= at + WINDOWS[choice]
        number = jnp.where(fits, choice, number)
        start = jnp.where(fits, at, start)
    live = (first != PAD_ID).astype(jnp.int32)
    return start.reshape(-1), number.reshape(-1), live.reshape(-1)


RELATIVE = (0, 2, 1, 3)


def down_copies(plan, ids_ref, parts, target, sems):
    y = ids_ref[0] % 2
    core = ids_ref[1] % 2
    copies = []
    for i, part in enumerate(parts):
        for side in range(2):
            place = target.at[side * 2 + (core ^ (i // 2)), :, y ^ (i % 2)]
            copies.append(pltpu.make_async_copy(part.at[side], place, sems.at[len(copies)]))
    return copies


def own_rows(source, target, share, n_mp, mp, sems, first):
    copies = []
    for s in range(target.shape[0] // share):
        at = pl.ds(pl.multiple_of((s * n_mp + mp) * share, share), share)
        copies.append(pltpu.make_async_copy(source.at[at], target.at[pl.ds(s * share, share)], sems.at[first + s]))
        copies[-1].start()
    return copies


def feed_up(plan, tokens, attended, params, out_w, up, up_across, down, down_across):
    dim = tokens.shape[1]
    rows, cols = attended[0].shape
    n_mp = plan.n_mp
    width = up.shape[1]
    hidden_size = n_mp * width
    share = LEN // n_mp
    seqs = rows // share
    inputs = [attended[0], out_w, up, up_across]
    shape = lambda c, t: jax.ShapeDtypeStruct((rows, c), t)
    results = [shape(dim, F32), shape(dim, BF16), shape(hidden_size, BF16), shape(hidden_size, F32)]
    n_load, n_store = len(inputs), len(results) * seqs + n_mp + 1 + seqs
    n_sems = 3 * seqs + 4

    def kernel(*refs):
        sources, (norm_ref, *sends), refs = refs[:n_load], refs[n_load : n_load + n_mp], refs[n_load + n_mp :]
        (down_in, down_across_in, tokens_in), refs = refs[:3], refs[3:]
        result_outs, att_outs, up_outs, down_outs, refs = refs[:4], refs[4 : n_mp + 3], refs[n_mp + 3 : n_mp + 5], refs[n_mp + 5 : n_mp + 7], refs[n_mp + 7 :]
        targets, bufs, att_bufs, u_bufs, refs = refs[:n_load], refs[n_load : n_load + 4], refs[n_load + 4 : n_load + n_mp + 3], refs[n_load + n_mp + 3 : n_load + n_mp + 5], refs[n_load + n_mp + 5 :]
        x_ref, load_sems, store_sems, send_sems, recv_sems = refs
        loads = Loads(sources, targets, load_sems)
        net = Sender(send_sems, recv_sems)
        x_copies = own_rows(tokens_in, x_ref, share, n_mp, net.mp, store_sems, n_store - seqs)
        net.meet([("mp", r) for r in range(1, n_mp)])
        at = lambda s: pl.ds(s * share, share)
        fetch = lambda s: [net.copy(sends[r - 1].at[at(s)], att_bufs[r - 1].at[at(s)], "mp", r) for r in range(1, n_mp)]
        rows_copies = [fetch(0)]
        up_copies = [net.copy(sources[2], u_bufs[0], "mp", 1), net.copy(sources[3], u_bufs[1], "mp", 1)]
        rows_copies += [fetch(s) for s in range(1, seqs)]
        down_copies = [net.copy(down_in, down_outs[0], "mp", 1), net.copy(down_across_in, down_outs[1], "mp", 1)]
        stores = []

        def store(src, dst):
            stores.append(pltpu.make_async_copy(src, dst, store_sems.at[len(stores)]))
            stores[-1].start()

        mid_buf, low_buf, act_buf, der_buf = bufs
        for s in range(seqs):
            here = at(s)
            att_ref, o_ref = loads[0], loads[1]
            x_copies[s].wait()
            middle = x_ref[here, :].astype(F32) + dot(att_ref[here, :], o_ref[net.mp, :, :cols], 1, 1)
            for r in range(1, n_mp):
                rows_copies[s][r - 1].wait_recv()
                middle = middle + dot(att_bufs[r - 1][here, :], o_ref[flip(net.mp, r), :, :cols], 1, 1)
            mid_buf[here, :] = middle
            normed, _ = norm_parts(middle)
            low = (normed * norm_ref[2:3, :] + norm_ref[3:4, :]).astype(BF16)
            low_buf[here, :] = low
            for c in range(n_mp):
                if c >= 2 and s == 0:
                    up_copies[c - 2].wait_recv()
                    store(u_bufs[c - 2], up_outs[c - 2])
                u_ref = loads[2 + c] if c < 2 else u_bufs[c - 2]
                columns = pl.ds(pl.multiple_of(flip(net.mp, RELATIVE[c]) * width, 128), width)
                hidden = dot(low, u_ref[...], 1, 0)
                phi = 0.5 * (1.0 + lax.erf(hidden * (0.5**0.5)))
                act_buf[here, columns] = (hidden * phi).astype(BF16)
                der_buf[here, columns] = phi + hidden * (jnp.exp(-0.5 * hidden * hidden) * 0.3989422804014327)
            for src, dst in zip(bufs, result_outs):
                store(src.at[here], dst.at[here])
        for src, dst in zip(att_bufs, att_outs):
            store(src, dst)
        for c in down_copies:
            c.wait_recv()
        net.finish()
        for c in stores:
            c.wait()

    like = lambda a: jax.ShapeDtypeStruct(a.shape, a.dtype)
    out = pl.pallas_call(
        kernel,
        in_specs=[ANY] * n_load + [pl.BlockSpec(memory_space=pltpu.VMEM)] + [ANY] * (n_mp + 2),
        out_specs=[ANY] * (n_mp + 7),
        out_shape=results + [like(a) for a in attended[1:]] + [like(up)] * 2 + [like(down)] * 2,
        scratch_shapes=[pltpu.VMEM(a.shape, a.dtype) for a in inputs + results + list(attended[1:]) + [up, up]]
        + [
            pltpu.VMEM((rows, dim), tokens.dtype),
            pltpu.SemaphoreType.DMA((n_load,)),
            pltpu.SemaphoreType.DMA((n_store,)),
            pltpu.SemaphoreType.DMA((n_sems,)),
            pltpu.SemaphoreType.DMA((n_sems,)),
        ],
        compiler_params=pltpu.CompilerParams(vmem_limit_bytes=VMEM_LIMIT, collective_id=4, has_side_effects=True),
        cost_estimate=cost(2 * rows * dim * (hidden_size + dim), rows * hidden_size * 8, rows * hidden_size * 2),
        name="feed_up",
    )(*inputs, params, *attended[1:], down, down_across, tokens)
    return out[:4], [attended[0]] + list(out[4 : n_mp + 3]), out[n_mp + 3 : n_mp + 5], out[n_mp + 5 :]


def start_all(copies):
    for c in copies:
        c.start()


def wait_all(copies):
    for c in copies:
        c.wait()


def feed_down(plan, ids, middle, active, seg_row, params, down):
    rows, dim = middle.shape
    n_mp = plan.n_mp
    hidden_size = active.shape[1]
    width = hidden_size // n_mp
    block = 256
    seqs = rows // block

    def kernel(ids_ref, mid_ref, act_ref, seg_ref, norm_ref, *refs):
        d_parts, (res_ref, block_ref, pool_ref, d_ref, sems) = refs[:4], refs[4:]
        seq = pl.program_id(0)
        copies = down_copies(plan, ids_ref, d_parts, d_ref, sems)

        @pl.when(seq == 0)
        def _():
            start_all(copies)
            wait_all(copies)

        result = mid_ref[...]
        for c in range(n_mp):
            result = result + dot(act_ref[:, c * width : (c + 1) * width], d_ref[c].reshape(dim, width), 1, 1)
        res_ref[...] = result
        block_ref[...] = result.astype(BF16)
        normed, _ = norm_parts(result)
        final = normed * norm_ref[4:5, :] + norm_ref[5:6, :]
        probe = jnp.broadcast_to(norm_ref[6:7, :], (8, dim))
        score = lax.dot_general(
            probe, final, (((1,), (1,)), ((), ())), precision=lax.Precision.HIGHEST, preferred_element_type=F32
        )[0:1]
        slot = lax.broadcasted_iota(jnp.int32, (SLOTS, block), 0)
        member = (seg_ref[0, 0:1, :] - seq * IMG_SEQ == slot) & (slot < IMG_SEQ)
        top = jnp.max(jnp.where(member, score, MASK_FILL), axis=1, keepdims=True)
        e = jnp.exp(jnp.where(member, score - top, MASK_FILL))
        e = jnp.where(member, e, 0.0)
        total = jnp.sum(e, axis=1, keepdims=True)
        low = final.astype(BF16)
        high = e.astype(BF16)
        rest = (e - high.astype(F32)).astype(BF16)
        pool_ref[:, :dim] = dot(high, low, 1, 0) + dot(rest, low, 1, 0)
        lane = lax.broadcasted_iota(jnp.int32, (SLOTS, 128), 1)
        pool_ref[:, dim:] = jnp.where(lane == 0, top, jnp.where(lane == 1, total, 0.0))

    row = lambda c: pl.BlockSpec((block, c), lambda i, *_: (i, 0))
    return pl.pallas_call(
        kernel,
        grid_spec=pltpu.PrefetchScalarGridSpec(
            num_scalar_prefetch=1,
            grid=(seqs,),
            in_specs=[row(dim), row(hidden_size), pl.BlockSpec((1, 2, block), lambda i, ids_ref: (i, 0, ids_ref[1])), whole(params.shape)] + [ANY] * 4,
            out_specs=[row(dim), row(dim), pl.BlockSpec((SLOTS, dim + 128), lambda i, *_: (i, 0))],
            scratch_shapes=[pltpu.VMEM((n_mp, plan.groups // 2, 2, plan.block, width), BF16), pltpu.SemaphoreType.DMA((8,))],
        ),
        out_shape=[
            jax.ShapeDtypeStruct((rows, dim), F32),
            jax.ShapeDtypeStruct((rows, dim), BF16),
            jax.ShapeDtypeStruct((seqs * SLOTS, dim + 128), F32),
        ],
        compiler_params=PARAMS,
        cost_estimate=cost(2 * rows * dim * hidden_size, rows * hidden_size * 4),
        name="feed_down",
    )(ids, middle, active, seg_row, params, *down)


def classify(plan, pool, labels, images, cls, cls_across, class_count):
    slots, full = pool.shape
    dim = full - 128
    n_mp = plan.n_mp
    class_cols = cls.shape[1]
    wide = n_mp * class_cols

    part = slots // 2

    def combined(mine, other, lower, ref_rows):
        first, second = jnp.where(lower, mine, other), jnp.where(lower, other, mine)
        top_a, top_b = first[:, dim : dim + 1], second[:, dim : dim + 1]
        top = jnp.maximum(top_a, top_b)
        weight_a, weight_b = jnp.exp(top_a - top), jnp.exp(top_b - top)
        total = first[:, dim + 1 : dim + 2] * weight_a + second[:, dim + 1 : dim + 2] * weight_b
        ref_rows[:, :dim] = first[:, :dim] * weight_a + second[:, :dim] * weight_b
        lane = lax.broadcasted_iota(jnp.int32, (first.shape[0], 128), 1)
        ref_rows[:, dim:] = jnp.where(lane == 0, top, jnp.where(lane == 1, total, 0.0))

    def kernel(part_ref, label_ref, images_ref, c_in, c_across, grad_ref, stat_ref, loss_ref, cls_ref, c_ref, l_ref, pool_ref, got_ref, own_sems, send_sems, recv_sems):
        net = Sender(send_sems, recv_sems)
        me, mp = net.dp // plan.merge, net.mp
        side, core = mp // 2, mp % 2
        net.meet([("mp", 1), ("mp", 2)])
        first_copy = net.copy(part_ref, got_ref.at[0], "mp", 1)
        weights = [net.copy(a, c_ref.at[flip(mp, r)], "mp", 1) for a, r in ((c_in, 0), (c_across, 2))]
        own_copies = [pltpu.make_async_copy(a, c_ref.at[flip(mp, r)], own_sems.at[r // 2]) for a, r in ((c_in, 0), (c_across, 2))]
        start_all(own_copies)
        first_copy.wait_recv()
        combined(part_ref[...], got_ref[0], core == 0, pool_ref.at[0])
        own = pl.ds(pl.multiple_of(core * part, 8), part)
        net.copy(pool_ref.at[0, own], got_ref.at[1, pl.ds(0, part)], "mp", 2).wait_recv()
        combined(pool_ref[0, own, :], got_ref[1, 0:part, :], side == 0, pool_ref.at[1, own])
        net.copy(pool_ref.at[1, own], pool_ref.at[1, own], "mp", 1).wait_recv()
        for c in weights:
            c.wait_recv()
        wait_all(own_copies)
        net.finish()
        pool_ref = pool_ref.at[1]
        top = pool_ref[:, dim : dim + 1]
        total = pool_ref[:, dim + 1 : dim + 2]
        present = jnp.where(total > 0, 1.0, 0.0)
        safe = total + (1.0 - present)
        pooled = pool_ref[:, :dim] / safe
        low = pooled.astype(BF16)
        logits = jnp.concatenate([dot(low, c_ref[c], 1, 0) for c in range(n_mp)], axis=1)
        column = lax.broadcasted_iota(jnp.int32, (slots, wide), 1)
        logits = jnp.where(column % class_cols < class_count, logits, MASK_FILL)
        row_top = jnp.max(logits, axis=1, keepdims=True)
        log_total = row_top + jnp.log(jnp.sum(jnp.exp(logits - row_top), axis=1, keepdims=True))
        chosen = jnp.where(column == label_ref[...], 1.0, 0.0)
        label_logit = jnp.sum(chosen * logits, axis=1, keepdims=True)
        loss = jnp.sum(present * (log_total - label_logit), axis=0, keepdims=True)
        loss_ref[...] = jnp.broadcast_to(loss, loss_ref.shape)
        scale = present / images_ref[0:1, 0:1]
        grad = ((jnp.exp(logits - log_total) - chosen) * scale).astype(BF16)
        l_ref[...] = grad
        row_grad = sum(dot(grad[:, c * class_cols : (c + 1) * class_cols], c_ref[c], 1, 1) for c in range(n_mp)).astype(BF16)
        grad_ref[...] = row_grad
        inner = jnp.sum(row_grad.astype(F32) * pooled, axis=1, keepdims=True)
        lane = lax.broadcasted_iota(jnp.int32, (slots, 128), 1)
        stat_ref[...] = jnp.where(lane == 0, top, jnp.where(lane == 1, 1.0 / safe, jnp.where(lane == 2, inner, 0.0)))
        own = l_ref[:, pl.ds(pl.multiple_of(mp * class_cols, 128), class_cols)]
        grad_cls = dot(low, own, 0, 0)
        for g in range(plan.groups):
            at = (g % 2 + me % 2) % 2 * (plan.groups // 2) + g // 2
            cls_ref[at] = grad_cls[g * plan.block : (g + 1) * plan.block].astype(BF16)

    vmem = pl.BlockSpec(memory_space=pltpu.VMEM)
    return pl.pallas_call(
        kernel,
        in_specs=[vmem] * 3 + [ANY] * 2,
        out_specs=[vmem] * 4,
        out_shape=[
            jax.ShapeDtypeStruct((slots, dim), BF16),
            jax.ShapeDtypeStruct((slots, 128), F32),
            jax.ShapeDtypeStruct((8, 128), F32),
            jax.ShapeDtypeStruct((plan.groups, plan.block, class_cols), BF16),
        ],
        scratch_shapes=[
            pltpu.VMEM((n_mp,) + cls.shape, BF16),
            pltpu.VMEM((slots, wide), BF16),
            pltpu.VMEM((2, slots, full), F32),
            pltpu.VMEM((2, slots, full), F32),
            pltpu.SemaphoreType.DMA((2,)),
            pltpu.SemaphoreType.DMA((5,)),
            pltpu.SemaphoreType.DMA((5,)),
        ],
        compiler_params=pltpu.CompilerParams(vmem_limit_bytes=VMEM_LIMIT, collective_id=3, has_side_effects=True),
        cost_estimate=cost(6 * slots * dim * wide, dim * wide * 2),
        name="classify",
    )(pool, labels, images, cls, cls_across)


def split_three(values):
    high = values.astype(BF16)
    rest = values - high.astype(F32)
    middle = rest.astype(BF16)
    low = (rest - middle.astype(F32)).astype(BF16)
    return high, middle, low


def feed_back(plan, ids, result, middle, slope, row_grads, stats, seg_col, params, out_w, up, down, cols):
    rows, dim = result.shape
    n_mp = plan.n_mp
    width = up[0].shape[1]
    hidden_size = n_mp * width
    block = 256

    def kernel(ids_ref, res_ref, mid_ref, der_ref, pg_ref, stat_ref, seg_ref, norm_ref, o_ref, *refs):
        u_refs, d_parts, refs = refs[:n_mp], refs[n_mp : n_mp + 4], refs[n_mp + 4 :]
        rlow_ref, hlow_ref, mlow_ref, mgrad_ref, *refs = refs
        ag_refs, (sums_ref, d_ref, sems) = refs[:n_mp], refs[n_mp:]
        mp = ids_ref[1]
        seq = pl.program_id(0)
        copies = down_copies(plan, ids_ref, d_parts, d_ref, sems)

        @pl.when(seq == 0)
        def _():
            start_all(copies)
            sums_ref[...] = jnp.zeros_like(sums_ref)

        normed, scale = norm_parts(res_ref[...])
        gain, probe = norm_ref[4:5, :], norm_ref[6:7, :]
        final = normed * gain + norm_ref[5:6, :]
        score = jnp.sum(final * probe, axis=1, keepdims=True)
        slot = lax.broadcasted_iota(jnp.int32, (block, SLOTS), 1)
        member = (seg_ref[...] - seq * IMG_SEQ == slot) & (slot < IMG_SEQ)
        held = jnp.max(jnp.where(member, 1.0, 0.0), axis=1, keepdims=True)
        one = jnp.where(member, 1.0, 0.0).astype(BF16)
        row_stat = sum(dot(one, part, 1, 0) for part in split_three(stat_ref[...]))
        top, inverse, inner = row_stat[:, 0:1], row_stat[:, 1:2], row_stat[:, 2:3]
        share = jnp.exp(jnp.where(held > 0, score - top, 0.0)) * inverse * held
        row_grad = dot(one, pg_ref[...], 1, 0)
        share_low = share.astype(BF16).astype(F32)
        share_grad = jnp.sum(row_grad * final.astype(BF16).astype(F32), axis=1, keepdims=True)
        score_grad = share * (share_grad - inner)
        final_grad = share_low * row_grad + score_grad * probe
        add = lambda slot, value: sums_ref.at[slot].__setitem__(
            ..., sums_ref[slot] + jnp.sum(value.reshape(-1, 8, dim), axis=0)
        )
        add(4, score_grad * final)
        add(2, final_grad * normed)
        add(3, final_grad)
        result_grad = norm_back(final_grad, normed, scale, gain)
        result_low = result_grad.astype(BF16)
        rlow_ref[...] = result_low
        pl.when(seq == 0)(lambda: wait_all(copies))
        second = jnp.zeros((block, dim), F32)
        for c in range(n_mp):
            other = mp ^ RELATIVE[c]
            at = pl.ds(pl.multiple_of(other * width, 128), width)
            hidden_low = (der_ref[:, at] * dot(result_low, d_ref[other].reshape(dim, width), 1, 0)).astype(BF16)
            hlow_ref[:, at] = hidden_low
            second = second + dot(hidden_low, u_refs[c][...], 1, 1)
        normed_two, scale_two = norm_parts(mid_ref[...])
        add(0, second * normed_two)
        add(1, second)
        middle_grad = result_grad + norm_back(second, normed_two, scale_two, norm_ref[2:3, :])
        mgrad_ref[...] = middle_grad
        middle_low = middle_grad.astype(BF16)
        mlow_ref[...] = middle_low
        for r in range(n_mp):
            ag_refs[r][...] = dot(middle_low, o_ref[mp ^ r, :, :cols], 1, 0).astype(BF16)

    row = lambda c: pl.BlockSpec((block, c), lambda i, *_: (i, 0))
    shape = lambda c, t: jax.ShapeDtypeStruct((rows, c), t)
    slots = lambda c: pl.BlockSpec((SLOTS, c), lambda i, *_: (i, 0))
    own_row = pl.BlockSpec((block, 1), lambda i, ids_ref: (i * n_mp + ids_ref[1], 0))
    return pl.pallas_call(
        kernel,
        grid_spec=pltpu.PrefetchScalarGridSpec(
            num_scalar_prefetch=1,
            grid=(rows // block,),
            in_specs=[row(dim), row(dim), row(hidden_size), slots(dim), slots(128), own_row, whole(params.shape), whole(out_w.shape)]
            + [whole(up[0].shape)] * n_mp
            + [ANY] * 4,
            out_specs=[row(dim), row(hidden_size), row(dim), row(dim)] + [row(cols)] * n_mp + [whole((5, 8, dim))],
            scratch_shapes=[pltpu.VMEM((n_mp, plan.groups // 2, 2, plan.block, width), BF16), pltpu.SemaphoreType.DMA((8,))],
        ),
        out_shape=[shape(dim, BF16), shape(hidden_size, BF16), shape(dim, BF16), shape(dim, F32)]
        + [shape(cols, BF16)] * n_mp
        + [jax.ShapeDtypeStruct((5, 8, dim), F32)],
        compiler_params=PARAMS,
        cost_estimate=cost(2 * rows * dim * (2 * hidden_size + dim), rows * hidden_size * 8),
        name="feed_back",
    )(ids, result, middle, slope, row_grads, stats, seg_col, params, out_w, *up, *down)


def weight_grads(plan, pairs, out_pair, cls_blocks, sends):
    dim = pairs[0][0].shape[1]
    rows = pairs[0][0].shape[0]
    n_mp, size, merge = plan.n_mp, plan.block, plan.merge
    lines = plan.groups // 2
    width = pairs[0][1].shape[1] // n_mp
    cols = out_pair[1][0].shape[1]
    out_cols = -(-cols // 128) * 128
    inputs = [a for pair in pairs for a in pair] + [out_pair[0]] + list(out_pair[1]) + [cls_blocks]
    n_load = len(inputs)
    widths = [width] * len(pairs) + [out_cols]
    n = len(widths)

    def kernel(*refs):
        sources, ag_in, refs = refs[:n_load], refs[n_load : n_load + n_mp - 1], refs[n_load + n_mp - 1 :]
        keep_out, send_out, cls_out, ag_out, refs = refs[:n], refs[n : 2 * n], refs[2 * n], refs[2 * n + 1 : 2 * n + n_mp], refs[2 * n + n_mp :]
        targets, refs = refs[:n_load], refs[n_load:]
        send_buf, got_buf, own_buf, keep_buf, low_buf = (refs[i * n : (i + 1) * n] for i in range(5))
        cls_got, load_sems, store_sems, send_sems, recv_sems = refs[5 * n :]
        loads = Loads(sources, targets, load_sems)
        net = Sender(send_sems, recv_sems)
        y = net.dp // merge % 2
        side, core = net.mp // 2, net.mp % 2
        net.meet([("mp", 1), ("mp", 2), ("mp", 3), ("dp", merge)])
        ag = [net.copy(a, b, "mp", r) for r, (a, b) in enumerate(zip(ag_in, ag_out), start=1)]
        cls_ref = loads[n_load - 1]
        cls_copy = net.copy(cls_ref.at[1], cls_got, "dp", merge)
        stores = []

        def grad(number, other_side, other_core):
            if number < len(pairs):
                left, right = loads[2 * number], loads[2 * number + 1]
                at = flip(side, other_side) * 2 + flip(core, other_core)
                return dot(left[...], right[:, pl.ds(pl.multiple_of(at * width, 128), width)], 0, 0)
            left = loads[2 * len(pairs)]
            right = loads[2 * len(pairs) + 1 + other_side * 2 + other_core]
            value = dot(left[...], right[...], 0, 0)
            return jnp.concatenate([value, jnp.zeros((dim, out_cols - cols), F32)], axis=1) if out_cols != cols else value

        split = lambda value: value.reshape(lines, 2, size, value.shape[1])
        cores = []
        for i in range(n):
            for other_side in (0, 1):
                send_buf[i][flip(side, other_side)] = split(grad(i, other_side, 1).astype(BF16))
            cores.append(net.copy(send_buf[i], got_buf[i], "mp", 1))
            for other_side in (0, 1):
                own_buf[i][flip(side, other_side)] = split(grad(i, other_side, 0))
        for i in range(n):
            cores[i].wait_recv()
            if i == 0:
                keep_buf[i][...] = own_buf[i][side] + got_buf[i][side].astype(F32)
                low_buf[i][...] = (own_buf[i][1 - side] + got_buf[i][1 - side].astype(F32)).astype(BF16)
            else:
                for x in (0, 1):
                    keep_buf[i][x] = own_buf[i][x, :, y] + got_buf[i][x, :, y].astype(F32)
                    low_buf[i][x] = (own_buf[i][x, :, 1 - y] + got_buf[i][x, :, 1 - y].astype(F32)).astype(BF16)
            for a, b in ((low_buf[i], send_out[i]), (keep_buf[i], keep_out[i])):
                stores.append(pltpu.make_async_copy(a, b, store_sems.at[len(stores)]))
                stores[-1].start()
        cls_copy.wait_recv()
        cls_out[...] = cls_ref[0].astype(F32) + cls_got[...].astype(F32)
        for c in ag:
            c.wait_recv()
        net.finish()
        for c in stores:
            c.wait()

    shape = jax.ShapeDtypeStruct
    vmem = pl.BlockSpec(memory_space=pltpu.VMEM)
    full = [(2, lines, 2, size, w) for w in widths]
    half = [(lines, 2, size, widths[0])] + [(2, lines, size, w) for w in widths[1:]]
    n_sems = n + n_mp
    out = pl.pallas_call(
        kernel,
        in_specs=[ANY] * (n_load + n_mp - 1),
        out_specs=[ANY] * (2 * n) + [vmem] + [ANY] * (n_mp - 1),
        out_shape=[shape(h, F32) for h in half]
        + [shape(h, BF16) for h in half]
        + [shape(cls_blocks.shape[1:], F32)]
        + [shape(a.shape, a.dtype) for a in sends],
        scratch_shapes=[pltpu.VMEM(a.shape, a.dtype) for a in inputs]
        + [pltpu.VMEM(f, BF16) for f in full]
        + [pltpu.VMEM(f, BF16) for f in full]
        + [pltpu.VMEM(f, F32) for f in full]
        + [pltpu.VMEM(h, F32) for h in half]
        + [pltpu.VMEM(h, BF16) for h in half]
        + [
            pltpu.VMEM(cls_blocks.shape[1:], BF16),
            pltpu.SemaphoreType.DMA((n_load,)),
            pltpu.SemaphoreType.DMA((2 * n,)),
            pltpu.SemaphoreType.DMA((n_sems,)),
            pltpu.SemaphoreType.DMA((n_sems,)),
        ],
        compiler_params=pltpu.CompilerParams(vmem_limit_bytes=60 * 1024 * 1024, collective_id=2, has_side_effects=True),
        cost_estimate=cost(2 * rows * dim * n_mp * sum(widths), rows * width * n_mp * 8),
        name="grads",
    )(*inputs, *sends)
    return out[:n], out[n : 2 * n], out[2 * n], out[2 * n + 1 :]


def assemble(plan, ids, parts, dtype, name):
    n_mp = plan.n_mp
    seqs, share, dim = parts[0].shape[-3:]
    joint = len(parts) == 1

    def kernel(ids_ref, *refs):
        part_refs, out_ref = refs[:-1], refs[-1]
        if joint:
            out_ref[...] = part_refs[0][...].astype(dtype)
            return
        for i, ref in enumerate(part_refs):

            @pl.when(pl.program_id(0) == i)
            def _():
                out_ref[...] = ref[...].astype(dtype)

    relative = lambda i: i % 2 * 2 + i // 2
    each = pl.BlockSpec((None, seqs, share, dim), lambda i, *_: (i, 0, 0, 0))
    return pl.pallas_call(
        kernel,
        grid_spec=pltpu.PrefetchScalarGridSpec(
            num_scalar_prefetch=1,
            grid=(n_mp,),
            in_specs=[each] if joint else [whole((seqs, share, dim))] * n_mp,
            out_specs=pl.BlockSpec((seqs, None, share, dim), lambda i, ids_ref: (0, ids_ref[1] ^ relative(i), 0, 0)),
        ),
        out_shape=jax.ShapeDtypeStruct((seqs, n_mp, share, dim), dtype),
        compiler_params=PARAMS,
        cost_estimate=cost(0, seqs * n_mp * share * dim * 8),
        name=name,
    )(ids, *parts).reshape(seqs * n_mp * share, dim)


def finish(plan, low, proj_grads, w, middle_grad, tokens, params, row_sums, gain_sums, loss, zx, yz, z_only):
    seqs = len(proj_grads)
    dim = low.shape[1]
    cols = w.shape[2]
    n_mp = plan.n_mp
    share = LEN // n_mp
    lines, size, merge = plan.groups // 2, plan.block, plan.merge
    dp_bits = [1 << i for i in range(plan.n_dp.bit_length() - 1)]
    far = [2 * k * merge for k in range(1, lines)]
    partners = [("mp", 1), ("mp", 2)] + [("dp", b) for b in sorted(set(dp_bits + far + [merge]))]
    stages = [("mp", 1), ("mp", 2)] + [("dp", b) for b in dp_bits]
    inputs = [w] + [g for seq in proj_grads for g in seq] + [a for pair in zx + yz for a in pair] + list(z_only)
    inputs += [low, middle_grad]
    smalls = [params, row_sums, loss] + list(gain_sums)
    n_in = len(inputs)
    n_zx, n_yz, n_z = len(zx), len(yz), len(z_only)
    n_sems = (lines - 1) * (n_zx + n_yz + n_z + 1) + n_zx + n_yz + 1 + 4 * seqs + len(stages)
    n_out = 3 + n_zx + n_yz + n_z

    def kernel(*refs):
        sources, (norm_ref, row_sum_ref, loss_ref, *gain_refs), refs = refs[:n_in], refs[n_in : n_in + 3 + seqs], refs[n_in + 3 + seqs :]
        tokens_in, refs = refs[0], refs[1:]
        rows_ref, qkv_out, total_ref, *owned = refs[:n_out]
        zx_out, yz_out, z_out = owned[:n_zx], owned[n_zx : n_zx + n_yz], owned[n_zx + n_yz :]
        scratch = list(refs[n_out:])
        take = lambda n: [scratch.pop(0) for _ in range(n)]
        targets = take(n_in)
        t_keep, t_send, t_got, t_mine, x_send, x_got, acc, q_low, q_y, q_send, q_z, got_sums, load_sems, send_sems, recv_sems, x_ref = take(16)
        zx_low, zx_got, zx_send, zx_last = take(n_zx), take(n_zx), take(n_zx), take(n_zx)
        yz_low, yz_got, yz_send, yz_last = take(n_yz), take(n_yz), take(n_yz), take(n_yz)
        z_low, z_got = take(n_z), take(n_z)
        loads = Loads(sources, targets, load_sems)
        net = Sender(send_sems, recv_sems)
        copy = net.copy
        own_copies = own_rows(tokens_in, x_ref, share, n_mp, net.mp, load_sems, n_in)
        group = net.dp // merge
        z, y = group // 2, group % 2
        side, core = net.mp // 2, net.mp % 2
        net.meet(partners)
        others = range(1, lines)
        to_z = lambda src, dst, k: copy(src, dst, "dp", 2 * k * merge)
        pair_from = 1 + 3 * seqs
        pair = lambda i: (loads[pair_from + 2 * i], loads[pair_from + 2 * i + 1])
        both = lambda a, b, *at: a[at].astype(F32) + b[at].astype(F32)
        z_from = pair_from + 2 * (n_zx + n_yz)
        y_copies, z_copies = [], []

        def over_y(i):
            a, b = pair(n_zx + i)
            for line in range(lines):
                yz_low[i][line] = both(a, b, line, 1 - y).astype(BF16)
            y_copies.append(copy(yz_low[i], yz_got[i], "dp", merge))

        def over_z(i):
            a, b = pair(i)
            for k in others:
                for s in (0, 1):
                    zx_low[i][k - 1, s] = both(a, b, s, flip(z, k)).astype(BF16)
                z_copies.append(to_z(zx_low[i].at[k - 1], zx_got[i].at[k - 1], k))

        def only_z(i):
            for k in others:
                z_low[i][k - 1] = loads[z_from + i][flip(z, k)].astype(BF16)
                z_copies.append(to_z(z_low[i].at[k - 1], z_got[i].at[k - 1], k))

        w_ref = loads[0]
        pg = [[loads.targets[1 + 3 * s + p] for p in range(3)] for s in range(seqs)]
        core_copies = []
        x_copies = []

        def over_x(s):
            core_copies[s].wait_recv()
            x_send[s] = (t_keep[s, 1].astype(F32) + t_got[s, 1].astype(F32)).astype(BF16)
            x_copies.append(copy(x_send.at[s], x_got.at[s], "mp", 2))
            t_mine[s] = t_keep[s, 0].astype(F32) + t_got[s, 0].astype(F32)

        for s in range(seqs):
            for p in range(3):
                loads[1 + 3 * s + p]

            def terms(target, i, carry):
                to_other = i // 2
                row_side = side + i % 2 * (1 - 2 * side)
                row_core = core + (1 - to_other) * (1 - 2 * core)
                at = pl.ds(pl.multiple_of((row_side * 2 + row_core) * share, share), share)
                gq, gk, gv = (ref[at, :] for ref in pg[s])
                total = dot(gq, w_ref[0], 1, 1) + dot(gk, w_ref[1], 1, 1) + dot(gv, w_ref[2], 1, 1)
                target[s, i % 2] = total.astype(BF16)
                return carry

            lax.fori_loop(0, 2, functools.partial(terms, t_send), 0)
            core_copies.append(copy(t_send.at[s], t_got.at[s], "mp", 1))
            lax.fori_loop(2, 4, functools.partial(terms, t_keep), 0)
            if s == 0:
                over_z(0)
                over_x(0)
            elif s > 1:
                over_x(s - 1)
            if s == 1:
                for i in range(n_yz):
                    over_y(i)
                for i in range(1, n_zx):
                    over_z(i)
                for i in range(n_z):
                    only_z(i)
        if seqs > 1:
            over_x(seqs - 1)

        low_ref = loads[n_in - 2]
        for s in range(seqs):
            for p in range(3):
                part = dot(low_ref[s * LEN : (s + 1) * LEN, :], pg[s][p][...], 0, 0)
                acc[p] = part if s == 0 else acc[p] + part
        for p in range(3):
            q_low[p] = acc[p].reshape(lines, 2, size, cols).astype(BF16)
        y_copy = copy(q_low.at[:, :, 1 - y], q_y, "dp", merge)

        mid_ref = loads[n_in - 1]
        for c in own_copies:
            c.wait()
        total_ref[...] = jnp.zeros_like(total_ref)
        for n in range(5):
            total_ref[2 + n : 3 + n, :] = jnp.sum(row_sum_ref[n], axis=0, keepdims=True)
        for n in range(2):
            gain_sum = sum(jnp.sum(ref[n], axis=0, keepdims=True) for ref in gain_refs)
            total_ref[8 + n : 9 + n, 0:cols] = gain_sum
        total_ref[10:11, 0:128] = loss_ref[0:1, :]
        row_copies = []
        q_copies = []
        for s in range(seqs):
            at = slice(s * share, (s + 1) * share)
            normed, scale = norm_parts(x_ref[at, :].astype(F32))
            x_copies[s].wait_recv()
            first = t_mine[s] + x_got[s].astype(F32)
            total_ref[0:1, :] += jnp.sum(first * normed, axis=0, keepdims=True)
            total_ref[1:2, :] += jnp.sum(first, axis=0, keepdims=True)
            rows_ref[0, s] = (mid_ref[at, :] + norm_back(first, normed, scale, norm_ref[0:1, :])).astype(BF16)
            row_copies.append(copy(rows_ref.at[0, s], rows_ref.at[1, s], "mp", 2))
            if s == 0:
                y_copy.wait_recv()
                for line in range(lines):
                    for p in range(3):
                        rows_at = pl.ds(pl.multiple_of((line * 2 + y) * size, 8), size)
                        q_send[line, p] = (acc[p, rows_at, :] + q_y[p, line].astype(F32)).astype(BF16)
                q_copies = [to_z(q_send.at[flip(z, k)], q_z.at[k - 1], k) for k in others]
            if s == min(1, seqs - 1):
                for i in range(n_yz):
                    a, b = pair(n_zx + i)
                    y_copies[i].wait_recv()
                    for k in others:
                        at_z = flip(z, k)
                        yz_send[i][k - 1] = (both(a, b, at_z, y) + yz_got[i][at_z].astype(F32)).astype(BF16)
                        z_copies.append(to_z(yz_send[i].at[k - 1], yz_last[i].at[k - 1], k))
        mate_copies, last_copies = [], []

        def zx_last_step(i):
            for c in z_copies[i * (lines - 1) : (i + 1) * (lines - 1)]:
                c.wait_recv()
            a, b = pair(i)
            other = both(a, b, 1 - side, z) + sum(zx_got[i][k - 1, 1 - side].astype(F32) for k in others)
            zx_send[i][...] = other.astype(BF16)
            last_copies.append(copy(zx_send[i], zx_last[i], "mp", 2))
            zx_out[i][...] = both(a, b, side, z) + sum(zx_got[i][k - 1, side].astype(F32) for k in others)

        def mate(n):
            row_copies[n].wait_recv()
            mate_copies.append(copy(rows_ref.at[pl.ds(0, 2), n], rows_ref.at[pl.ds(2, 2), n], "mp", 1))

        between = [functools.partial(zx_last_step, i) for i in range(n_zx)] + [functools.partial(mate, n) for n in range(seqs)]
        for n, (axis, bits) in enumerate(stages):
            count = 8 if axis == "mp" else 16
            stage = copy(total_ref.at[pl.ds(0, count)], got_sums.at[n, pl.ds(0, count)], axis, bits)
            net.started.pop()
            if between:
                between.pop(0)()
            stage.wait()
            total_ref[0:count, :] += got_sums[n, 0:count, :]
        for step in between:
            step()
        for c in z_copies[n_zx * (lines - 1) :]:
            c.wait_recv()
        for i in range(n_yz):
            a, b = pair(n_zx + i)
            own = both(a, b, z, y) + yz_got[i][z].astype(F32)
            yz_out[i][...] = own + sum(yz_last[i][k - 1].astype(F32) for k in others)
        for i in range(n_z):
            z_out[i][...] = loads[z_from + i][z] + sum(z_got[i][k - 1].astype(F32) for k in others)
        for c in q_copies:
            c.wait_recv()
        for p in range(3):
            rows_at = pl.ds(pl.multiple_of((z * 2 + y) * size, 8), size)
            own = acc[p, rows_at, :] + q_y[p, z].astype(F32)
            qkv_out[p] = own + sum(q_z[k - 1, p].astype(F32) for k in others)
        for i, c in enumerate(last_copies):
            c.wait_recv()
            zx_out[i][...] += zx_last[i][...].astype(F32)
        for c in mate_copies:
            c.wait_recv()
        net.finish()

    vmem = pl.BlockSpec(memory_space=pltpu.VMEM)
    shape = jax.ShapeDtypeStruct
    blk = (3, size, cols)
    piece = lambda a: a.shape[-2:]
    buf = lambda a, lead, t=BF16: pltpu.VMEM(tuple(lead) + piece(a), t)
    three = lines - 1
    scratch = [pltpu.VMEM(a.shape, a.dtype) for a in inputs]
    scratch += [
        pltpu.VMEM((seqs, 2, share, dim), BF16),
        pltpu.VMEM((seqs, 2, share, dim), BF16),
        pltpu.VMEM((seqs, 2, share, dim), BF16),
        pltpu.VMEM((seqs, share, dim), F32),
        pltpu.VMEM((seqs, share, dim), BF16),
        pltpu.VMEM((seqs, share, dim), BF16),
        pltpu.VMEM((3, dim, cols), F32),
        pltpu.VMEM((3, lines, 2, size, cols), BF16),
        pltpu.VMEM((3, lines, size, cols), BF16),
        pltpu.VMEM((lines,) + blk, BF16),
        pltpu.VMEM((three,) + blk, BF16),
        pltpu.VMEM((len(stages), 16, dim), F32),
        pltpu.SemaphoreType.DMA((n_in + seqs,)),
        pltpu.SemaphoreType.DMA((n_sems,)),
        pltpu.SemaphoreType.DMA((n_sems,)),
        pltpu.VMEM((seqs * share, dim), tokens.dtype),
    ]
    firsts, seconds = [a for a, _ in zx], [a for a, _ in yz]
    for lead in ((three, 2), (three, 2), (), ()):
        scratch += [buf(a, lead) for a in firsts]
    for lead in ((lines,), (lines,), (three,), (three,)):
        scratch += [buf(a, lead) for a in seconds]
    scratch += [buf(a, (three,)) for a in z_only] + [buf(a, (three,)) for a in z_only]
    out = pl.pallas_call(
        kernel,
        in_specs=[ANY] * n_in + [vmem] * len(smalls) + [ANY],
        out_specs=[vmem] * n_out,
        out_shape=[shape((4, seqs, share, dim), BF16), shape(blk, F32), shape((16, dim), F32)]
        + [shape(piece(a), F32) for a in firsts + seconds + list(z_only)],
        scratch_shapes=scratch,
        compiler_params=pltpu.CompilerParams(vmem_limit_bytes=60 * 1024 * 1024, collective_id=1, has_side_effects=True),
        cost_estimate=cost(12 * seqs * LEN * dim * cols, seqs * LEN * dim * 8),
        name="finish",
    )(*inputs, *smalls, tokens)
    return out[0], out[1], out[2], out[3:]


def adam_update(weight, moment_one, moment_two, gradient, step_rate, decay_rate):
    fresh_one = BETA_ONE * moment_one + (1.0 - BETA_ONE) * gradient
    fresh_two = BETA_TWO * moment_two + (1.0 - BETA_TWO) * gradient * gradient
    one_hat = fresh_one / (1.0 - BETA_ONE**STEP)
    two_hat = fresh_two / (1.0 - BETA_TWO**STEP)
    updated = weight - step_rate * (one_hat / (jnp.sqrt(two_hat) + ADAM_EPS) + decay_rate * weight)
    return (fresh_one, fresh_two, updated)


def shards(
    tokens,
    seg_ids,
    labels,
    w_qkv,
    m_qkv,
    v_qkv,
    w_out,
    m_out,
    v_out,
    w_up,
    m_up,
    v_up,
    w_down,
    m_down,
    v_down,
    w_cls,
    m_cls,
    v_cls,
    norm_params,
    m_norm,
    v_norm,
    qk_gain,
    m_qk,
    v_qk,
    *,
    n_dp,
    n_mp,
):
    dp, mp = lax.axis_index("dp"), lax.axis_index("mp")
    group_rows, dim = tokens.shape
    plan = Plan(n_dp, n_mp, dim)
    seqs = group_rows // LEN
    share = LEN // n_mp
    rows = seqs * share
    cols = w_qkv.shape[2]
    classes = w_cls.shape[1]
    class_cols = -(-classes // 128) * 128
    out_cols = -(-cols // 128) * 128
    ids = jnp.stack([dp // plan.merge, mp]).astype(jnp.int32)

    new_image = seg_ids != jnp.concatenate([jnp.full((1,), -1, jnp.int32), seg_ids[:-1]])
    count = jnp.sum((new_image & (seg_ids != PAD_ID)).astype(F32))
    dim_part, head_part = norm_params.shape[1], qk_gain.shape[2]
    pad = lambda a, r, c: jnp.pad(a, ((0, r - a.shape[0]), (0, c - a.shape[1])))
    low_param = lambda a: lax.reduce_precision(a, 8, 7)
    small = jnp.concatenate(
        [
            pad(low_param(norm_params), 8, 128),
            pad(low_param(qk_gain).reshape(2, cols // HEAD * head_part), 8, 128),
            pad(count.reshape(1, 1), 8, 128),
        ]
    )
    qkv_block = plan.merged(w_qkv.astype(BF16), 1)
    up_block = plan.merged(w_up.astype(BF16), 0)
    down_block = plan.merged(w_down.T.astype(BF16), 0)
    out_block = plan.merged(pad(w_out.T.astype(BF16), dim_part, out_cols), 0)
    cls_block = plan.merged(pad(w_cls.astype(BF16), dim_part, class_cols), 0)
    small_block = plan.merged(small[None], 0)

    tied = lambda value, tie: lax.optimization_barrier((value, tie))[0]

    head_of = jnp.arange(cols) // HEAD
    ones = jnp.where(head_of[:, None] == head_of[None, :], 1.0 / HEAD, 0.0).astype(BF16)
    starts, widths, live = key_windows(seg_ids)
    seg_col = seg_ids.reshape(group_rows, 1)
    seg_row = seg_ids.reshape(-1, LEN)
    seg_row = jnp.stack([seg_row, jnp.roll(seg_row, -ALIGN, axis=1)], axis=1)
    normed_low, pq, pk, q, k, v, w, up, down, out_w, cls, params, gains, images = gather_project(
        plan, tokens, qkv_block, up_block, down_block, out_block, cls_block, small_block, ones
    )
    w = w.reshape(3, dim, cols)
    out_w = out_w.reshape(n_mp, dim, out_cols)
    up = up.reshape(dim, up.shape[-1])
    up_across, down_across = plan.swap(up, "mp", 2), plan.group_swap(down, 1)
    cls = cls.reshape(dim, class_cols)
    cls_across = plan.swap(tied(cls, up_across), "mp", 2)
    image_total = images[0, 0]
    *attended, logs = attend(plan, ids, starts, widths, q, k, v, seg_col, seg_row)

    (middle, second_low, active, slope), attended, up_mates, down_mates = feed_up(
        plan, tokens, attended, params, out_w, up, up_across, down, down_across
    )
    up = [up, up_across, *up_mates]
    down = [down, down_across, *down_mates]
    result, block_rows, pool = feed_down(plan, ids, middle, active, seg_row, params, down)

    block_rows = block_rows.reshape(seqs, share, dim)
    slot_label = labels.reshape(seqs, IMG_SEQ)
    slot_label = slot_label // classes * class_cols + slot_label % classes
    slot_label = jnp.pad(slot_label, ((0, 0), (0, SLOTS - IMG_SEQ)), constant_values=-1).reshape(seqs * SLOTS, 1)
    row_grads, stats, loss, cls_blocks = classify(plan, pool, slot_label, images, cls, cls_across, classes)

    block_rows = lax.optimization_barrier((block_rows, stats))[0]
    block_across = plan.swap(block_rows, "mp", 2)
    block_mate, block_mate_across = plan.swap(block_rows, "mp", 1), plan.swap(block_across, "mp", 1)
    block_out = assemble(plan, ids, [block_rows, block_across, block_mate, block_mate_across], BF16, "block_out")

    result_low, hidden_low, middle_low, middle_grad, *rest = feed_back(
        plan, ids, result, middle, slope, row_grads, stats, seg_col, params, out_w, up, down, cols
    )
    attended_grads, sums = rest[:n_mp], rest[n_mp]
    cls_blocks = cls_blocks.reshape(2, plan.groups // 2, plan.block, class_cols)
    kept, sent, cls_sum, arrived = weight_grads(
        plan, [(result_low, active), (second_low, hidden_low)], (middle_low, attended), cls_blocks, attended_grads[1:]
    )
    grad_parts = [attended_grads[0]] + list(arrived)
    got = [plan.swap(sent[0], "mp", 2)] + [plan.group_swap(part, 1) for part in sent[1:]]

    proj_grads, gain_sums = [], []
    for s in range(seqs):
        *grad, gain_sum = attend_back(
            plan, s, ids, starts, widths, live, q, k, v, pq, pk, gains, ones, grad_parts, logs, seg_col, seg_row
        )
        proj_grads.append(grad)
        gain_sums.append(gain_sum)
    *got, block_out, _ = lax.optimization_barrier((*got, block_out, proj_grads[-1][0]))

    down_pair, up_pair, out_pair = zip(kept, got)
    last_rows, grad_qkv, small_grads, owned = finish(
        plan, normed_low, proj_grads, w, middle_grad, tokens, params, sums, gain_sums, loss, [up_pair, out_pair], [down_pair], [cls_sum]
    )
    mean_loss = small_grads[10, 0] / image_total
    grad_qkv = plan.unmerged(grad_qkv, 1)
    grad_up, grad_out, grad_down, grad_cls = (plan.unmerged(a, 0) for a in owned)
    grad_out, grad_down, grad_cls = grad_out[:, :cols].T, grad_down.T, grad_cls[:, :classes]
    input_grad = assemble(plan, ids, [last_rows], F32, "input_grad")
    norm_part = lax.dynamic_slice(small_grads, (0, dp * dim_part), (7, dim_part))
    qk_part = lax.dynamic_slice_in_dim(small_grads[8:10, :cols].reshape(2, cols // HEAD, HEAD), dp * head_part, head_part, 2)
    reduced = (grad_qkv, grad_out, grad_up, grad_down, grad_cls, norm_part, qk_part)
    groups = (
        (w_qkv, m_qkv, v_qkv, MATRIX_RATE, MATRIX_DECAY),
        (w_out, m_out, v_out, MATRIX_RATE, MATRIX_DECAY),
        (w_up, m_up, v_up, MATRIX_RATE, MATRIX_DECAY),
        (w_down, m_down, v_down, MATRIX_RATE, MATRIX_DECAY),
        (w_cls, m_cls, v_cls, MATRIX_RATE, MATRIX_DECAY),
        (norm_params, m_norm, v_norm, GAIN_RATE, 0.0),
        (qk_gain, m_qk, v_qk, GAIN_RATE, 0.0),
    )
    outputs = [block_out, input_grad, mean_loss]
    for number, group in enumerate(groups):
        fresh_one, fresh_two, updated = adam_update(group[0], group[1], group[2], reduced[number], group[3], group[4])
        if number == 5:
            outputs = outputs + [fresh_one, fresh_two[:6], fresh_two[6], updated]
        else:
            outputs = outputs + [fresh_one, fresh_two, updated]
    return tuple(outputs)


def solution(mesh):
    rows_cols = (P("mp", "dp"),) * 3
    cols_rows = (P("dp", "mp"),) * 3
    qkv_spec = (P(None, "dp", "mp"),) * 3
    qk_spec = (P(None, "mp", "dp"),) * 3
    norm_spec = P(None, "dp")
    in_specs = (
        (P("dp", None), P("dp"), P("dp")) + qkv_spec + rows_cols + cols_rows + rows_cols + cols_rows + (norm_spec,) * 3 + qk_spec
    )
    out_specs = (
        (P("dp", None), P("dp", None), P())
        + qkv_spec
        + rows_cols
        + cols_rows
        + rows_cols
        + cols_rows
        + (norm_spec, norm_spec, P("dp"), norm_spec)
        + qk_spec
    )
    body = functools.partial(shards, n_dp=mesh.shape["dp"], n_mp=mesh.shape["mp"])
    return jax.shard_map(body, mesh=mesh, in_specs=in_specs, out_specs=out_specs, check_vma=False)
```

```python
import functools

import jax
import jax.numpy as jnp
from jax import lax
from jax.experimental import pallas as pl
from jax.experimental.pallas import tpu as pltpu
from jax.sharding import PartitionSpec as P

LEN = 1024
STEP = 10
SEQ_DEV = 3
IMG_DEV = 180
PAD_ID = 180

NORM_EPS = 1e-06
MASK_FILL = -1000000000.0
BETA_ONE = 0.9
BETA_TWO = 0.999
ADAM_EPS = 1e-08
MATRIX_RATE = 0.1
MATRIX_DECAY = 0.1
GAIN_RATE = 0.8

HEAD = 64
QB = 256
QBLOCKS = LEN // QB
WINDOWS = (384, 512, 768, 1024)
ALIGN = 64
LANES = 128
F32 = jnp.float32
BF16 = jnp.bfloat16
VMEM_LIMIT = 56 * 1024 * 1024
IMG_SEQ = 60
SLOTS = 64
ANY = pl.BlockSpec(memory_space=pl.ANY)
PARAMS = pltpu.CompilerParams(vmem_limit_bytes=VMEM_LIMIT)


def dot(a, b, ca, cb):
    return lax.dot_general(a, b, (((ca,), (cb,)), ((), ())), preferred_element_type=F32)


def head_mean(values, ones_block):
    high = values.astype(BF16)
    rest = (values - high.astype(F32)).astype(BF16)
    return dot(high, ones_block, 1, 0) + dot(rest, ones_block, 1, 0)


def norm_parts(values):
    centre = values - jnp.mean(values, axis=-1, keepdims=True)
    spread = jnp.mean(centre * centre, axis=-1, keepdims=True)
    scale = lax.rsqrt(spread + NORM_EPS)
    return centre * scale, scale


def norm_back(grad, normed, scale, gain):
    scaled = grad * gain
    first = jnp.mean(scaled, axis=-1, keepdims=True)
    second = jnp.mean(scaled * normed, axis=-1, keepdims=True)
    return (scaled - first - normed * second) * scale


def head_parts(values, ones_block):
    centre = values - head_mean(values, ones_block)
    scale = lax.rsqrt(head_mean(centre * centre, ones_block) + NORM_EPS)
    return centre * scale, scale


def cost(flops, read, exps=0):
    return pl.CostEstimate(flops=int(flops), bytes_accessed=int(read), transcendentals=int(exps))


def whole(shape):
    return pl.BlockSpec(tuple(shape), lambda *_: (0,) * len(shape))


class Plan:
    def __init__(self, n_dp, n_mp, dim):
        self.n_dp, self.n_mp = n_dp, n_mp
        self.merge = 1 if dim // n_dp % 16 == 0 else 2
        self.groups = n_dp // self.merge
        self.block = dim // self.groups
        self.far = [2 * k for k in range(1, self.groups // 2)]

    def swap(self, value, axis, bits):
        size = self.n_dp if axis == "dp" else self.n_mp
        return lax.ppermute(value, axis, [(i, i ^ bits) for i in range(size)])

    def group_swap(self, value, bits):
        return self.swap(value, "dp", bits * self.merge)

    def merged(self, value, dim):
        if self.merge == 1:
            return value
        other = self.swap(value, "dp", 1)
        even = lax.axis_index("dp") % 2 == 0
        first, second = jnp.where(even, value, other), jnp.where(even, other, value)
        return jnp.concatenate([first, second], axis=dim)

    def unmerged(self, value, dim):
        if self.merge == 1:
            return value
        half = value.shape[dim] // 2
        me = lax.axis_index("dp") % 2
        mine = lax.dynamic_slice_in_dim(value, me * half, half, dim)
        theirs = lax.dynamic_slice_in_dim(value, (1 - me) * half, half, dim)
        return mine + self.swap(theirs, "dp", 1)

    def total(self, value, axis):
        size = self.n_dp if axis == "dp" else self.n_mp
        bits = 1
        while bits < size:
            value = value + self.swap(value, axis, bits)
            bits *= 2
        return value


MESH = pl.DeviceIdType.MESH


def flip(index, bits):
    bit = 1
    while bit <= bits:
        if bits & bit:
            index = index + bit * (1 - 2 * (index // bit % 2))
        bit *= 2
    return index


class Chain:
    def __init__(self, region, order, lines):
        self.region, self.steps = region, order
        self.copies = sum({"z": lines - 1, "c": 2}.get(step, 1) for step in order)


class Gatherer:
    def __init__(self, plan, send_sems, recv_sems):
        self.plan, self.send_sems, self.recv_sems = plan, send_sems, recv_sems
        self.dp, self.mp = lax.axis_index("dp"), lax.axis_index("mp")
        self.pair = self.dp % plan.merge
        group = self.dp // plan.merge
        self.z, self.y = group // 2, group % 2
        self.x, self.core = self.mp // 2, self.mp % 2
        self.lines = plan.groups // 2
        self.used = 0
        self.pending = []

    def device(self, z, y, x, core):
        return ((z * 2 + y) * self.plan.merge + self.pair, x * 2 + core)

    def here(self):
        return self.z, self.y, self.x, self.core

    def meet(self, barrier):
        z, y, x, core = self.here()
        others = [(z, 1 - y, x, core), (z, y, 1 - x, core), (z, y, x, 1 - core)]
        others += [(flip(z, k), y, x, core) for k in range(1, self.lines)]
        for other in others:
            pl.semaphore_signal(barrier, inc=1, device_id=self.device(*other), device_id_type=MESH)
        pl.semaphore_wait(barrier, len(others))

    def start(self, chain, number, source=None):
        step, done = chain.steps[number], chain.steps[:number]
        z, y, x, core = self.here()
        spot = dict(z=None if "z" in done else z, y=None if "y" in done else y, x=None if "x" in done else x, core=core)
        if step == "z":
            copies = [(spot, (flip(z, k), y, x, core)) for k in range(1, self.lines)]
        elif step == "c":
            copies = [({**spot, "x": side}, (z, y, x, 1 - core)) for side in (0, 1)]
        else:
            copies = [(spot, dict(y=(z, 1 - y, x, core), x=(z, y, 1 - x, core))[step])]
        started = []
        for place, other in copies:
            region = chain.region(**place)
            out = pltpu.make_async_remote_copy(
                src_ref=region if source is None else source,
                dst_ref=region,
                send_sem=self.send_sems.at[self.used],
                recv_sem=self.recv_sems.at[self.used],
                device_id=self.device(*other),
                device_id_type=MESH,
            )
            self.used += 1
            out.start()
            started.append(out)
        self.pending += started
        return started

    @staticmethod
    def arrive(copies):
        for out in copies:
            out.wait_recv()

    def finish(self):
        for out in self.pending:
            out.wait_send()


class Loads:
    def __init__(self, sources, targets, sems):
        self.targets = targets
        self.copies = [pltpu.make_async_copy(a, b, sems.at[i]) for i, (a, b) in enumerate(zip(sources, targets))]
        self.done = [False] * len(self.copies)
        for c in self.copies:
            c.start()

    def __getitem__(self, i):
        if not self.done[i]:
            self.copies[i].wait()
            self.done[i] = True
        return self.targets[i]


class Sender:
    def __init__(self, send_sems, recv_sems):
        self.dp, self.mp = lax.axis_index("dp"), lax.axis_index("mp")
        self.send_sems, self.recv_sems = send_sems, recv_sems
        self.started, self.used = [], 0

    def device(self, axis, bits):
        return (flip(self.dp, bits), self.mp) if axis == "dp" else (self.dp, flip(self.mp, bits))

    def meet(self, partners):
        barrier = pltpu.get_barrier_semaphore()
        for axis, bits in partners:
            pl.semaphore_signal(barrier, inc=1, device_id=self.device(axis, bits), device_id_type=MESH)
        pl.semaphore_wait(barrier, len(partners))

    def copy(self, src, dst, axis, bits):
        n = self.used
        self.used += 1
        c = pltpu.make_async_remote_copy(
            src_ref=src,
            dst_ref=dst,
            send_sem=self.send_sems.at[n],
            recv_sem=self.recv_sems.at[n],
            device_id=self.device(axis, bits),
            device_id_type=MESH,
        )
        self.started.append(c)
        c.start()
        return c

    def finish(self):
        for c in self.started:
            c.wait_send()


def gather_project(plan, tokens, qkv_block, up_block, down_block, out_block, cls_block, small_block, ones):
    rows, dim = tokens.shape
    cols = ones.shape[0]
    n_mp, merge, size = plan.n_mp, plan.merge, plan.block
    lines = plan.groups // 2
    width = up_block.shape[1]
    out_cols, classes = out_block.shape[1], cls_block.shape[1]
    class_cols = -(-classes // 128) * 128
    block = 512
    blocks = rows // block
    dim_part = dim // plan.n_dp
    head_part = HEAD // plan.n_dp

    orders = [("small", "zy"), ("w_qk", "zy"), ("w_v", "zy"), ("out", "zyxc"), ("cls", "zy"), ("up", "zy"), ("down", "zx")]
    sizes = {name: Chain(None, order, lines).copies for name, order in orders}
    n_sems = sum(sizes.values())

    def kernel(x_ref, qkv_wide, up_wide, down_in, out_in, cls_wide, small_in, ones_ref, *refs):
        low_ref, pq_ref, pk_ref, q_ref, k_ref, v_ref, w_ref, up_ref, down_ref, o_ref, c_ref, norm_ref, gain_ref, image_ref = refs[:14]
        w_buf, small_buf, low_buf, pq_buf, pk_buf, q_buf, k_buf, v_buf, send_sems, recv_sems, own_sems, out_sems, *lows = refs[14:]
        qkv_in, up_in, cls_in = lows
        qkv_in[...] = qkv_wide[...].astype(BF16)
        up_in[...] = up_wide[...].astype(BF16)
        cls_in[...] = jnp.concatenate([cls_wide[...].astype(BF16), jnp.zeros((size, class_cols - classes), BF16)], axis=1)
        g = Gatherer(plan, send_sems, recv_sems)
        z, y, x, core = g.here()
        everything = slice(None)

        def at(v):
            return everything if v is None else v

        def wide(ref, first, count):
            columns = pl.ds(first, count)
            return lambda z, y, x, core: ref.at[at(x), core, at(z), at(y), :, columns]

        regions = dict(
            w_qk=lambda z, y, x, core: w_buf.at[pl.ds(0, 2), at(z), at(y)],
            w_v=lambda z, y, x, core: w_buf.at[pl.ds(2, 1), at(z), at(y)],
            small=lambda z, y, x, core: small_buf.at[at(z), at(y)],
            up=lambda z, y, x, core: up_ref.at[at(z), at(y)],
            down=lambda z, y, x, core: down_ref.at[at(x), at(z)],
            out=wide(o_ref, 0, out_cols),
            cls=lambda z, y, x, core: c_ref.at[at(z), at(y)],
        )
        chains = {name: Chain(regions[name], order, lines) for name, order in orders}
        sources = dict(
            w_qk=qkv_in.at[pl.ds(0, 2)],
            w_v=qkv_in.at[pl.ds(2, 1)],
            small=small_in,
            up=up_in,
            down=down_in,
            out=out_in,
            cls=cls_in,
        )
        own = {}
        for i, (name, _) in enumerate(orders):
            own[name] = pltpu.make_async_copy(sources[name], regions[name](z, y, x, core), own_sems.at[i])
            own[name].start()
        live, reached = {}, {}

        def begin(name):
            live[name] = g.start(chains[name], 0, source=sources[name])
            reached[name] = 0

        def advance(*names):
            for name in names:
                if reached[name] == len(chains[name].steps):
                    continue
                if reached[name] == 0:
                    own[name].wait()
                g.arrive(live[name])
                reached[name] += 1
                if reached[name] < len(chains[name].steps):
                    live[name] = g.start(chains[name], reached[name])

        g.meet(pltpu.get_barrier_semaphore())
        for name in ("small", "w_qk", "w_v", "out", "cls"):
            begin(name)
        advance("small", "small")

        lane = lax.broadcasted_iota(jnp.int32, (128, dim), 0)
        column = lax.broadcasted_iota(jnp.int32, (128, dim), 1)
        head_lane = lax.broadcasted_iota(jnp.int32, (128, cols), 0)
        head_column = lax.broadcasted_iota(jnp.int32, (128, cols), 1)
        norm = jnp.zeros((8, dim), F32)
        gain = jnp.zeros((8, cols), F32)
        image = jnp.zeros((8, 128), F32)
        for d in range(plan.n_dp):
            part = small_buf[d // merge // 2, d // merge % 2, d % merge]
            spread = jnp.where((column == d * dim_part + lane) & (lane < dim_part), 1.0, 0.0).astype(BF16)
            norm = norm + dot(part[0:8].astype(BF16), spread, 1, 0)
            same = (head_column // HEAD == head_lane // head_part) & (head_column % HEAD == d * head_part + head_lane % head_part)
            gain = gain + dot(part[8:16].astype(BF16), jnp.where(same, 1.0, 0.0).astype(BF16), 1, 0)
            image = image + part[16:24]
        norm_ref[...] = norm
        gain_ref[...] = gain
        image_ref[...] = image

        def first_norm(i, carry):
            at_rows = pl.ds(pl.multiple_of(i * block, block), block)
            normed, _ = norm_parts(x_ref[at_rows, :].astype(F32))
            low_buf[at_rows, :] = (normed * norm[0:1, :] + norm[1:2, :]).astype(BF16)
            return carry

        third = blocks // 3
        lax.fori_loop(0, third, first_norm, 0)
        advance("w_qk", "w_v")
        begin("up")
        begin("down")
        lax.fori_loop(third, blocks, first_norm, 0)
        outs = [pltpu.make_async_copy(low_buf, low_ref, out_sems.at[0])]
        outs[0].start()
        advance("out", "cls", "w_qk", "w_v")
        outs.append(pltpu.make_async_copy(w_buf, w_ref, out_sems.at[1]))
        outs[1].start()

        def project(i, carry):
            at_rows = pl.ds(pl.multiple_of(i * block, block), block)
            low = low_buf[at_rows, :]
            pq = dot(low, w_buf[0].reshape(dim, cols), 1, 0)
            pk = dot(low, w_buf[1].reshape(dim, cols), 1, 0)
            pq_buf[at_rows, :] = pq
            pk_buf[at_rows, :] = pk
            v_buf[at_rows, :] = dot(low, w_buf[2].reshape(dim, cols), 1, 0).astype(BF16)
            nq, _ = head_parts(pq, ones_ref[...])
            nk, _ = head_parts(pk, ones_ref[...])
            q_buf[at_rows, :] = (nq * gain[0:1, :]).astype(BF16)
            k_buf[at_rows, :] = (nk * gain[1:2, :]).astype(BF16)
            return carry

        lax.fori_loop(0, third, project, 0)
        advance("out", "up", "down")
        lax.fori_loop(third, 2 * third, project, 0)
        lax.fori_loop(2 * third, blocks, project, 0)
        pairs = ((pq_buf, pq_ref), (pk_buf, pk_ref), (q_buf, q_ref), (k_buf, k_ref), (v_buf, v_ref))
        for i, (a, b) in enumerate(pairs):
            outs.append(pltpu.make_async_copy(a, b, out_sems.at[2 + i]))
            outs[-1].start()
        advance("out", "cls", "up", "down", "out")
        g.finish()
        for c in outs:
            c.wait()

    vmem = pl.BlockSpec(memory_space=pltpu.VMEM)
    shape = jax.ShapeDtypeStruct
    wide_shape = lambda c: (n_mp // 2, 2, lines, 2, size, c)
    n_rows = lambda c, t: shape((rows, c), t)
    return pl.pallas_call(
        kernel,
        in_specs=[vmem, vmem, vmem, ANY, ANY, vmem, ANY, vmem],
        out_specs=[ANY] * 11 + [vmem] * 3,
        out_shape=[n_rows(dim, BF16), n_rows(cols, F32), n_rows(cols, F32), n_rows(cols, BF16), n_rows(cols, BF16), n_rows(cols, BF16)]
        + [
            shape((3, lines, 2, size, cols), BF16),
            shape((lines, 2, size, width), BF16),
            shape((n_mp // 2, lines, size, width), BF16),
            shape(wide_shape(out_cols), BF16),
            shape((lines, 2, size, class_cols), BF16),
            shape((8, dim), F32),
            shape((8, cols), F32),
            shape((8, 128), F32),
        ],
        scratch_shapes=[
            pltpu.VMEM((3, lines, 2, size, cols), BF16),
            pltpu.VMEM((lines, 2, merge, 24, 128), F32),
            pltpu.VMEM((rows, dim), BF16),
            pltpu.VMEM((rows, cols), F32),
            pltpu.VMEM((rows, cols), F32),
            pltpu.VMEM((rows, cols), BF16),
            pltpu.VMEM((rows, cols), BF16),
            pltpu.VMEM((rows, cols), BF16),
            pltpu.SemaphoreType.DMA((n_sems,)),
            pltpu.SemaphoreType.DMA((n_sems,)),
            pltpu.SemaphoreType.DMA((len(orders),)),
            pltpu.SemaphoreType.DMA((7,)),
            pltpu.VMEM(qkv_block.shape, BF16),
            pltpu.VMEM(up_block.shape, BF16),
            pltpu.VMEM((size, class_cols), BF16),
        ],
        compiler_params=pltpu.CompilerParams(vmem_limit_bytes=VMEM_LIMIT, collective_id=0, has_side_effects=True),
        cost_estimate=cost(6 * rows * dim * cols, rows * dim * 8),
        name="gather_project",
    )(tokens, qkv_block, up_block, down_block, out_block, cls_block, small_block, ones)


def head_masks(cols):
    lane = lax.broadcasted_iota(jnp.int32, (1, cols), 1)
    return [(lane >= h * HEAD) & (lane < (h + 1) * HEAD) for h in range(cols // HEAD)]


def spread_heads(block, masks):
    zero = jnp.zeros_like(block)
    return jnp.concatenate([jnp.where(m, block, zero) for m in masks], axis=0)


def join_heads(stacked, masks):
    total = stacked[0:QB]
    for h in range(1, len(masks)):
        total = jnp.where(masks[h], stacked[h * QB : (h + 1) * QB], total)
    return total


def by_window(width_ref, step, body):
    width = width_ref[step]
    for number, window in enumerate(WINDOWS):
        pl.when(width == number)(functools.partial(body, window))


def key_segments(row_ref, start, window):
    at = pl.ds(pl.multiple_of(start // LANES * LANES, LANES), window)
    return jnp.where(start % LANES == 0, row_ref[0, 0:1, at], row_ref[0, 1:2, at])


def seq_specs(seq, cols):
    block = lambda c: pl.BlockSpec((QB, c), lambda b, *_: (seq * QBLOCKS + b, 0))
    all_keys = lambda c: pl.BlockSpec((LEN, c), lambda b, *_: (seq, 0))
    seg_row = pl.BlockSpec((1, 2, LEN), lambda b, *_: (seq, 0, 0))
    return block, all_keys, seg_row


def attend(plan, ids, starts, widths, q, k, v, seg_col, seg_row):
    rows, cols = q.shape
    n_mp = plan.n_mp
    share = LEN // n_mp
    per = share // QB
    seqs = rows // LEN

    def kernel(ids_ref, start_ref, width_ref, q_ref, k_ref, v_ref, col_ref, row_ref, *outs):
        out_refs, log_ref = outs[:n_mp], outs[n_mp]
        seq, block = pl.program_id(0), pl.program_id(1)
        step = seq * QBLOCKS + block
        masks = head_masks(cols)
        heads = len(masks)

        def body(window):
            start = pl.multiple_of(start_ref[step], ALIGN)
            keys = k_ref[pl.ds(start, window), :]
            values = v_ref[pl.ds(start, window), :]
            q3 = spread_heads(q_ref[...], masks)
            s = (dot(q3, keys, 1, 1) * HEAD**-0.5).reshape(heads, QB, window)
            same = col_ref[...] == key_segments(row_ref, start, window)
            s = jnp.where(same[None], s, MASK_FILL)
            top = jnp.max(s, axis=-1, keepdims=True)
            e = jnp.exp(s - top)
            total = jnp.sum(e, axis=-1, keepdims=True)
            p = (e * (1.0 / total)).astype(BF16).reshape(heads * QB, window)
            out = join_heads(dot(p, values, 1, 0), masks).astype(BF16)
            other = (block // per) ^ ids_ref[1]
            at = pl.ds(pl.multiple_of(seq * share + block % per * QB, QB), QB)
            for r in range(n_mp):

                @pl.when(other == r)
                def _():
                    out_refs[r][at, :] = out

            log = top + jnp.log(total)
            lane = lax.broadcasted_iota(jnp.int32, (QB, 128), 1)
            logs = jnp.zeros((QB, 128), F32)
            for h in range(heads):
                logs = jnp.where(lane == h, log[h], logs)
            log_ref[...] = logs

        by_window(width_ref, step, body)

    block = lambda c: pl.BlockSpec((QB, c), lambda s, b, *_: (s * QBLOCKS + b, 0))
    all_keys = lambda c: pl.BlockSpec((LEN, c), lambda s, b, *_: (s, 0))
    return pl.pallas_call(
        kernel,
        grid_spec=pltpu.PrefetchScalarGridSpec(
            num_scalar_prefetch=3,
            grid=(seqs, QBLOCKS),
            in_specs=[block(cols), all_keys(cols), all_keys(cols), block(1), pl.BlockSpec((1, 2, LEN), lambda s, b, *_: (s, 0, 0))],
            out_specs=[whole((seqs * share, cols))] * n_mp + [block(128)],
        ),
        out_shape=[jax.ShapeDtypeStruct((seqs * share, cols), BF16)] * n_mp + [jax.ShapeDtypeStruct((rows, 128), F32)],
        compiler_params=PARAMS,
        cost_estimate=cost(60 * rows * LEN * cols, rows * cols * 8, rows * LEN),
        name="attend",
    )(ids, starts, widths, q, k, v, seg_col, seg_row)


def attend_back(plan, seq, ids, starts, widths, live, q, k, v, pq, pk, gains, ones, grads, logs, seg_col, seg_row):
    rows, cols = q.shape
    n_mp = plan.n_mp
    share = LEN // n_mp
    per = share // QB

    def kernel(ids_ref, start_ref, width_ref, live_ref, q_ref, k_ref, v_ref, pq_ref, pk_ref, gain_ref, ones_ref, col_ref, row_ref, log_ref, *refs):
        grad_refs, (gq_ref, gk_ref, gv_ref, sum_ref, dk_ref, dv_ref) = refs[:n_mp], refs[n_mp:]
        block = pl.program_id(0)
        step = seq * QBLOCKS + block
        masks = head_masks(cols)
        heads = len(masks)

        @pl.when(block == 0)
        def _():
            dk_ref[...] = jnp.zeros_like(dk_ref)
            dv_ref[...] = jnp.zeros_like(dv_ref)
            sum_ref[...] = jnp.zeros_like(sum_ref)

        def back(values, grad, slot):
            ones_block = ones_ref[...]
            normed, scale = head_parts(values, ones_block)
            sum_ref[slot] += jnp.sum((grad * normed).reshape(-1, 8, cols), axis=0)
            scaled = grad * gain_ref[slot : slot + 1, :]
            first = head_mean(scaled, ones_block)
            second = head_mean(scaled * normed, ones_block)
            return ((scaled - first - normed * second) * scale).astype(BF16)

        def body(window):
            start = pl.multiple_of(start_ref[step], ALIGN)
            keys = pl.ds(start, window)
            k_win = k_ref[keys, :]
            v_win = v_ref[keys, :]
            other = (block // per) ^ ids_ref[1]
            at = pl.ds(pl.multiple_of(block % per * QB, QB), QB)
            g = grad_refs[0][at, :]
            for r in range(1, n_mp):
                g = jnp.where(other == r, grad_refs[r][at, :], g)
            q3 = spread_heads(q_ref[...], masks)
            g3 = spread_heads(g, masks)
            s = (dot(q3, k_win, 1, 1) * HEAD**-0.5).reshape(heads, QB, window)
            same = col_ref[...] == key_segments(row_ref, start, window)
            all_logs = log_ref[...]
            log = jnp.stack([all_logs[:, h : h + 1] for h in range(heads)])
            p = jnp.exp(jnp.where(same[None], s - log, MASK_FILL))
            dp = dot(g3, v_win, 1, 1).reshape(heads, QB, window)
            inner = jnp.sum(p * dp, axis=-1, keepdims=True)
            ds = (p * (dp - inner)).astype(BF16).reshape(heads * QB, window)
            p_low = p.astype(BF16).reshape(heads * QB, window)
            dv_ref[keys, :] += dot(p_low, g3, 0, 0)
            dk_ref[keys, :] += dot(ds, q3, 0, 0) * HEAD**-0.5
            dq = join_heads(dot(ds, k_win, 1, 0), masks) * HEAD**-0.5
            gq_ref[...] = back(pq_ref[...], dq, 0)

        alive = live_ref[step]

        @pl.when(alive == 0)
        def _():
            gq_ref[...] = jnp.zeros_like(gq_ref)

        @pl.when(alive != 0)
        def _():
            by_window(width_ref, step, body)

        @pl.when(block == QBLOCKS - 1)
        def _():
            gv_ref[...] = dv_ref[...].astype(BF16)

            def keys_back(i, carry):
                at = pl.ds(pl.multiple_of(i * share, share), share)
                gk_ref[at, :] = back(pk_ref[at, :], dk_ref[at, :], 1)
                return carry

            lax.fori_loop(0, n_mp, keys_back, 0)

    block, all_keys, row_spec = seq_specs(seq, cols)
    grad_spec = pl.BlockSpec((share, cols), lambda b, *_: (seq, 0))
    shape = jax.ShapeDtypeStruct((LEN, cols), BF16)
    return pl.pallas_call(
        kernel,
        grid_spec=pltpu.PrefetchScalarGridSpec(
            num_scalar_prefetch=4,
            grid=(QBLOCKS,),
            in_specs=[block(cols), all_keys(cols), all_keys(cols), block(cols), all_keys(cols), whole(gains.shape), whole(ones.shape)]
            + [block(1), row_spec, block(128)]
            + [grad_spec] * n_mp,
            out_specs=[pl.BlockSpec((QB, cols), lambda b, *_: (b, 0)), whole((LEN, cols)), whole((LEN, cols)), whole((2, 8, cols))],
            scratch_shapes=[pltpu.VMEM((LEN, cols), F32), pltpu.VMEM((LEN, cols), F32)],
        ),
        out_shape=[shape, shape, shape, jax.ShapeDtypeStruct((2, 8, cols), F32)],
        compiler_params=PARAMS,
        cost_estimate=cost(60 * LEN * LEN * cols, LEN * cols * 24, LEN * LEN),
        name="attend_back",
    )(ids, starts, widths, live, q, k, v, pq, pk, gains, ones, seg_col, seg_row, logs, *grads)


def key_windows(seg_ids):
    seg = seg_ids.reshape(-1, LEN)
    first = seg[:, ::QB]
    last = seg[:, QB - 1 :: QB]
    low = jnp.sum((seg[:, None, :] < first[:, :, None]).astype(jnp.int32), axis=2)
    high = jnp.sum((seg[:, None, :] <= last[:, :, None]).astype(jnp.int32), axis=2)
    base = low // ALIGN * ALIGN
    number = jnp.full(base.shape, len(WINDOWS) - 1, jnp.int32)
    start = jnp.zeros_like(base)
    for choice in range(len(WINDOWS) - 2, -1, -1):
        at = jnp.minimum(base, LEN - WINDOWS[choice])
        fits = high <= at + WINDOWS[choice]
        number = jnp.where(fits, choice, number)
        start = jnp.where(fits, at, start)
    live = (first != PAD_ID).astype(jnp.int32)
    return start.reshape(-1), number.reshape(-1), live.reshape(-1)


RELATIVE = (0, 2, 1, 3)


def down_copies(plan, ids_ref, parts, target, sems):
    y = ids_ref[0] % 2
    core = ids_ref[1] % 2
    copies = []
    for i, part in enumerate(parts):
        for side in range(2):
            place = target.at[side * 2 + (core ^ (i // 2)), :, y ^ (i % 2)]
            copies.append(pltpu.make_async_copy(part.at[side], place, sems.at[len(copies)]))
    return copies


def own_rows(source, target, share, n_mp, mp, sems, first):
    copies = []
    for s in range(target.shape[0] // share):
        at = pl.ds(pl.multiple_of((s * n_mp + mp) * share, share), share)
        copies.append(pltpu.make_async_copy(source.at[at], target.at[pl.ds(s * share, share)], sems.at[first + s]))
        copies[-1].start()
    return copies


def feed_up(plan, tokens, attended, params, out_w, up, up_across, down, down_across):
    dim = tokens.shape[1]
    rows, cols = attended[0].shape
    n_mp = plan.n_mp
    width = up.shape[1]
    hidden_size = n_mp * width
    share = LEN // n_mp
    seqs = rows // share
    inputs = [attended[0], out_w, up, up_across]
    shape = lambda c, t: jax.ShapeDtypeStruct((rows, c), t)
    results = [shape(dim, F32), shape(dim, BF16), shape(hidden_size, BF16), shape(hidden_size, F32)]
    n_load, n_store = len(inputs), len(results) * seqs + n_mp + 1 + seqs
    n_sems = 3 * seqs + 4

    def kernel(*refs):
        sources, (norm_ref, *sends), refs = refs[:n_load], refs[n_load : n_load + n_mp], refs[n_load + n_mp :]
        (down_in, down_across_in, tokens_in), refs = refs[:3], refs[3:]
        result_outs, att_outs, up_outs, down_outs, refs = refs[:4], refs[4 : n_mp + 3], refs[n_mp + 3 : n_mp + 5], refs[n_mp + 5 : n_mp + 7], refs[n_mp + 7 :]
        targets, bufs, att_bufs, u_bufs, refs = refs[:n_load], refs[n_load : n_load + 4], refs[n_load + 4 : n_load + n_mp + 3], refs[n_load + n_mp + 3 : n_load + n_mp + 5], refs[n_load + n_mp + 5 :]
        x_ref, load_sems, store_sems, send_sems, recv_sems = refs
        loads = Loads(sources, targets, load_sems)
        net = Sender(send_sems, recv_sems)
        x_copies = own_rows(tokens_in, x_ref, share, n_mp, net.mp, store_sems, n_store - seqs)
        net.meet([("mp", r) for r in range(1, n_mp)])
        at = lambda s: pl.ds(s * share, share)
        fetch = lambda s: [net.copy(sends[r - 1].at[at(s)], att_bufs[r - 1].at[at(s)], "mp", r) for r in range(1, n_mp)]
        rows_copies = [fetch(0)]
        up_copies = [net.copy(sources[2], u_bufs[0], "mp", 1), net.copy(sources[3], u_bufs[1], "mp", 1)]
        rows_copies += [fetch(s) for s in range(1, seqs)]
        down_copies = [net.copy(down_in, down_outs[0], "mp", 1), net.copy(down_across_in, down_outs[1], "mp", 1)]
        stores = []

        def store(src, dst):
            stores.append(pltpu.make_async_copy(src, dst, store_sems.at[len(stores)]))
            stores[-1].start()

        mid_buf, low_buf, act_buf, der_buf = bufs
        for s in range(seqs):
            here = at(s)
            att_ref, o_ref = loads[0], loads[1]
            x_copies[s].wait()
            middle = x_ref[here, :].astype(F32) + dot(att_ref[here, :], o_ref[net.mp, :, :cols], 1, 1)
            for r in range(1, n_mp):
                rows_copies[s][r - 1].wait_recv()
                middle = middle + dot(att_bufs[r - 1][here, :], o_ref[flip(net.mp, r), :, :cols], 1, 1)
            mid_buf[here, :] = middle
            normed, _ = norm_parts(middle)
            low = (normed * norm_ref[2:3, :] + norm_ref[3:4, :]).astype(BF16)
            low_buf[here, :] = low
            for c in range(n_mp):
                if c >= 2 and s == 0:
                    up_copies[c - 2].wait_recv()
                    store(u_bufs[c - 2], up_outs[c - 2])
                u_ref = loads[2 + c] if c < 2 else u_bufs[c - 2]
                columns = pl.ds(pl.multiple_of(flip(net.mp, RELATIVE[c]) * width, 128), width)
                hidden = dot(low, u_ref[...], 1, 0)
                phi = 0.5 * (1.0 + lax.erf(hidden * (0.5**0.5)))
                act_buf[here, columns] = (hidden * phi).astype(BF16)
                der_buf[here, columns] = phi + hidden * (jnp.exp(-0.5 * hidden * hidden) * 0.3989422804014327)
            for src, dst in zip(bufs, result_outs):
                store(src.at[here], dst.at[here])
        for src, dst in zip(att_bufs, att_outs):
            store(src, dst)
        for c in down_copies:
            c.wait_recv()
        net.finish()
        for c in stores:
            c.wait()

    like = lambda a: jax.ShapeDtypeStruct(a.shape, a.dtype)
    out = pl.pallas_call(
        kernel,
        in_specs=[ANY] * n_load + [pl.BlockSpec(memory_space=pltpu.VMEM)] + [ANY] * (n_mp + 2),
        out_specs=[ANY] * (n_mp + 7),
        out_shape=results + [like(a) for a in attended[1:]] + [like(up)] * 2 + [like(down)] * 2,
        scratch_shapes=[pltpu.VMEM(a.shape, a.dtype) for a in inputs + results + list(attended[1:]) + [up, up]]
        + [
            pltpu.VMEM((rows, dim), tokens.dtype),
            pltpu.SemaphoreType.DMA((n_load,)),
            pltpu.SemaphoreType.DMA((n_store,)),
            pltpu.SemaphoreType.DMA((n_sems,)),
            pltpu.SemaphoreType.DMA((n_sems,)),
        ],
        compiler_params=pltpu.CompilerParams(vmem_limit_bytes=VMEM_LIMIT, collective_id=4, has_side_effects=True),
        cost_estimate=cost(2 * rows * dim * (hidden_size + dim), rows * hidden_size * 8, rows * hidden_size * 2),
        name="feed_up",
    )(*inputs, params, *attended[1:], down, down_across, tokens)
    return out[:4], [attended[0]] + list(out[4 : n_mp + 3]), out[n_mp + 3 : n_mp + 5], out[n_mp + 5 :]


def start_all(copies):
    for c in copies:
        c.start()


def wait_all(copies):
    for c in copies:
        c.wait()


def feed_down(plan, ids, middle, active, seg_row, params, down):
    rows, dim = middle.shape
    n_mp = plan.n_mp
    hidden_size = active.shape[1]
    width = hidden_size // n_mp
    block = 256
    seqs = rows // block

    def kernel(ids_ref, mid_ref, act_ref, seg_ref, norm_ref, *refs):
        d_parts, (res_ref, block_ref, pool_ref, d_ref, sems) = refs[:4], refs[4:]
        seq = pl.program_id(0)
        copies = down_copies(plan, ids_ref, d_parts, d_ref, sems)

        @pl.when(seq == 0)
        def _():
            start_all(copies)
            wait_all(copies)

        result = mid_ref[...]
        for c in range(n_mp):
            result = result + dot(act_ref[:, c * width : (c + 1) * width], d_ref[c].reshape(dim, width), 1, 1)
        res_ref[...] = result
        block_ref[...] = result.astype(BF16)
        normed, _ = norm_parts(result)
        final = normed * norm_ref[4:5, :] + norm_ref[5:6, :]
        score = jnp.sum(final * norm_ref[6:7, :], axis=1, keepdims=True)
        score = jnp.broadcast_to(score, (block, 128)).T[0:1]
        slot = lax.broadcasted_iota(jnp.int32, (SLOTS, block), 0)
        member = (seg_ref[0, 0:1, :] - seq * IMG_SEQ == slot) & (slot < IMG_SEQ)
        top = jnp.max(jnp.where(member, score, MASK_FILL), axis=1, keepdims=True)
        e = jnp.exp(jnp.where(member, score - top, MASK_FILL))
        e = jnp.where(member, e, 0.0)
        total = jnp.sum(e, axis=1, keepdims=True)
        low = final.astype(BF16)
        high = e.astype(BF16)
        rest = (e - high.astype(F32)).astype(BF16)
        pool_ref[:, :dim] = dot(high, low, 1, 0) + dot(rest, low, 1, 0)
        lane = lax.broadcasted_iota(jnp.int32, (SLOTS, 128), 1)
        pool_ref[:, dim:] = jnp.where(lane == 0, top, jnp.where(lane == 1, total, 0.0))

    row = lambda c: pl.BlockSpec((block, c), lambda i, *_: (i, 0))
    return pl.pallas_call(
        kernel,
        grid_spec=pltpu.PrefetchScalarGridSpec(
            num_scalar_prefetch=1,
            grid=(seqs,),
            in_specs=[row(dim), row(hidden_size), pl.BlockSpec((1, 2, block), lambda i, ids_ref: (i, 0, ids_ref[1])), whole(params.shape)] + [ANY] * 4,
            out_specs=[row(dim), row(dim), pl.BlockSpec((SLOTS, dim + 128), lambda i, *_: (i, 0))],
            scratch_shapes=[pltpu.VMEM((n_mp, plan.groups // 2, 2, plan.block, width), BF16), pltpu.SemaphoreType.DMA((8,))],
        ),
        out_shape=[
            jax.ShapeDtypeStruct((rows, dim), F32),
            jax.ShapeDtypeStruct((rows, dim), BF16),
            jax.ShapeDtypeStruct((seqs * SLOTS, dim + 128), F32),
        ],
        compiler_params=PARAMS,
        cost_estimate=cost(2 * rows * dim * hidden_size, rows * hidden_size * 4),
        name="feed_down",
    )(ids, middle, active, seg_row, params, *down)


def classify(plan, pool, labels, images, cls, cls_across, class_count):
    slots, full = pool.shape
    dim = full - 128
    n_mp = plan.n_mp
    class_cols = cls.shape[1]
    wide = n_mp * class_cols

    part = slots // 2

    def combined(mine, other, lower, ref_rows):
        first, second = jnp.where(lower, mine, other), jnp.where(lower, other, mine)
        top_a, top_b = first[:, dim : dim + 1], second[:, dim : dim + 1]
        top = jnp.maximum(top_a, top_b)
        weight_a, weight_b = jnp.exp(top_a - top), jnp.exp(top_b - top)
        total = first[:, dim + 1 : dim + 2] * weight_a + second[:, dim + 1 : dim + 2] * weight_b
        ref_rows[:, :dim] = first[:, :dim] * weight_a + second[:, :dim] * weight_b
        lane = lax.broadcasted_iota(jnp.int32, (first.shape[0], 128), 1)
        ref_rows[:, dim:] = jnp.where(lane == 0, top, jnp.where(lane == 1, total, 0.0))

    def kernel(part_ref, label_ref, images_ref, c_in, c_across, grad_ref, stat_ref, loss_ref, cls_ref, c_ref, l_ref, pool_ref, got_ref, own_sems, send_sems, recv_sems):
        net = Sender(send_sems, recv_sems)
        me, mp = net.dp // plan.merge, net.mp
        side, core = mp // 2, mp % 2
        net.meet([("mp", 1), ("mp", 2)])
        first_copy = net.copy(part_ref, got_ref.at[0], "mp", 1)
        weights = [net.copy(a, c_ref.at[flip(mp, r)], "mp", 1) for a, r in ((c_in, 0), (c_across, 2))]
        own_copies = [pltpu.make_async_copy(a, c_ref.at[flip(mp, r)], own_sems.at[r // 2]) for a, r in ((c_in, 0), (c_across, 2))]
        start_all(own_copies)
        first_copy.wait_recv()
        combined(part_ref[...], got_ref[0], core == 0, pool_ref.at[0])
        own = pl.ds(pl.multiple_of(core * part, 8), part)
        net.copy(pool_ref.at[0, own], got_ref.at[1, pl.ds(0, part)], "mp", 2).wait_recv()
        combined(pool_ref[0, own, :], got_ref[1, 0:part, :], side == 0, pool_ref.at[1, own])
        net.copy(pool_ref.at[1, own], pool_ref.at[1, own], "mp", 1).wait_recv()
        for c in weights:
            c.wait_recv()
        wait_all(own_copies)
        net.finish()
        pool_ref = pool_ref.at[1]
        top = pool_ref[:, dim : dim + 1]
        total = pool_ref[:, dim + 1 : dim + 2]
        present = jnp.where(total > 0, 1.0, 0.0)
        safe = total + (1.0 - present)
        pooled = pool_ref[:, :dim] / safe
        low = pooled.astype(BF16)
        logits = jnp.concatenate([dot(low, c_ref[c], 1, 0) for c in range(n_mp)], axis=1)
        column = lax.broadcasted_iota(jnp.int32, (slots, wide), 1)
        logits = jnp.where(column % class_cols < class_count, logits, MASK_FILL)
        row_top = jnp.max(logits, axis=1, keepdims=True)
        log_total = row_top + jnp.log(jnp.sum(jnp.exp(logits - row_top), axis=1, keepdims=True))
        chosen = jnp.where(column == label_ref[...], 1.0, 0.0)
        label_logit = jnp.sum(chosen * logits, axis=1, keepdims=True)
        loss = jnp.sum(present * (log_total - label_logit), axis=0, keepdims=True)
        loss_ref[...] = jnp.broadcast_to(loss, loss_ref.shape)
        scale = present / images_ref[0:1, 0:1]
        grad = ((jnp.exp(logits - log_total) - chosen) * scale).astype(BF16)
        l_ref[...] = grad
        row_grad = sum(dot(grad[:, c * class_cols : (c + 1) * class_cols], c_ref[c], 1, 1) for c in range(n_mp)).astype(BF16)
        grad_ref[...] = row_grad
        inner = jnp.sum(row_grad.astype(F32) * pooled, axis=1, keepdims=True)
        lane = lax.broadcasted_iota(jnp.int32, (slots, 128), 1)
        stat_ref[...] = jnp.where(lane == 0, top, jnp.where(lane == 1, 1.0 / safe, jnp.where(lane == 2, inner, 0.0)))
        own = l_ref[:, pl.ds(pl.multiple_of(mp * class_cols, 128), class_cols)]
        grad_cls = dot(low, own, 0, 0)
        for g in range(plan.groups):
            at = (g % 2 + me % 2) % 2 * (plan.groups // 2) + g // 2
            cls_ref[at] = grad_cls[g * plan.block : (g + 1) * plan.block].astype(BF16)

    vmem = pl.BlockSpec(memory_space=pltpu.VMEM)
    return pl.pallas_call(
        kernel,
        in_specs=[vmem] * 3 + [ANY] * 2,
        out_specs=[vmem] * 4,
        out_shape=[
            jax.ShapeDtypeStruct((slots, dim), BF16),
            jax.ShapeDtypeStruct((slots, 128), F32),
            jax.ShapeDtypeStruct((8, 128), F32),
            jax.ShapeDtypeStruct((plan.groups, plan.block, class_cols), BF16),
        ],
        scratch_shapes=[
            pltpu.VMEM((n_mp,) + cls.shape, BF16),
            pltpu.VMEM((slots, wide), BF16),
            pltpu.VMEM((2, slots, full), F32),
            pltpu.VMEM((2, slots, full), F32),
            pltpu.SemaphoreType.DMA((2,)),
            pltpu.SemaphoreType.DMA((5,)),
            pltpu.SemaphoreType.DMA((5,)),
        ],
        compiler_params=pltpu.CompilerParams(vmem_limit_bytes=VMEM_LIMIT, collective_id=3, has_side_effects=True),
        cost_estimate=cost(6 * slots * dim * wide, dim * wide * 2),
        name="classify",
    )(pool, labels, images, cls, cls_across)


def split_three(values):
    high = values.astype(BF16)
    rest = values - high.astype(F32)
    middle = rest.astype(BF16)
    low = (rest - middle.astype(F32)).astype(BF16)
    return high, middle, low


def feed_back(plan, ids, result, middle, slope, row_grads, stats, seg_col, params, out_w, up, down, cols):
    rows, dim = result.shape
    n_mp = plan.n_mp
    width = up[0].shape[1]
    hidden_size = n_mp * width
    block = 256

    def kernel(ids_ref, res_ref, mid_ref, der_ref, pg_ref, stat_ref, seg_ref, norm_ref, o_ref, *refs):
        u_refs, d_parts, refs = refs[:n_mp], refs[n_mp : n_mp + 4], refs[n_mp + 4 :]
        rlow_ref, hlow_ref, mlow_ref, mgrad_ref, *refs = refs
        ag_refs, (sums_ref, d_ref, sems) = refs[:n_mp], refs[n_mp:]
        mp = ids_ref[1]
        seq = pl.program_id(0)
        copies = down_copies(plan, ids_ref, d_parts, d_ref, sems)

        @pl.when(seq == 0)
        def _():
            start_all(copies)
            sums_ref[...] = jnp.zeros_like(sums_ref)

        normed, scale = norm_parts(res_ref[...])
        gain, probe = norm_ref[4:5, :], norm_ref[6:7, :]
        final = normed * gain + norm_ref[5:6, :]
        score = jnp.sum(final * probe, axis=1, keepdims=True)
        slot = lax.broadcasted_iota(jnp.int32, (block, SLOTS), 1)
        member = (seg_ref[...] - seq * IMG_SEQ == slot) & (slot < IMG_SEQ)
        held = jnp.max(jnp.where(member, 1.0, 0.0), axis=1, keepdims=True)
        one = jnp.where(member, 1.0, 0.0).astype(BF16)
        row_stat = sum(dot(one, part, 1, 0) for part in split_three(stat_ref[...]))
        top, inverse, inner = row_stat[:, 0:1], row_stat[:, 1:2], row_stat[:, 2:3]
        share = jnp.exp(jnp.where(held > 0, score - top, 0.0)) * inverse * held
        row_grad = dot(one, pg_ref[...], 1, 0)
        share_low = share.astype(BF16).astype(F32)
        share_grad = jnp.sum(row_grad * final.astype(BF16).astype(F32), axis=1, keepdims=True)
        score_grad = share * (share_grad - inner)
        final_grad = share_low * row_grad + score_grad * probe
        add = lambda slot, value: sums_ref.at[slot].__setitem__(
            ..., sums_ref[slot] + jnp.sum(value.reshape(-1, 8, dim), axis=0)
        )
        add(4, score_grad * final)
        add(2, final_grad * normed)
        add(3, final_grad)
        result_grad = norm_back(final_grad, normed, scale, gain)
        result_low = result_grad.astype(BF16)
        rlow_ref[...] = result_low
        pl.when(seq == 0)(lambda: wait_all(copies))
        second = jnp.zeros((block, dim), F32)
        for c in range(n_mp):
            other = mp ^ RELATIVE[c]
            at = pl.ds(pl.multiple_of(other * width, 128), width)
            hidden_low = (der_ref[:, at] * dot(result_low, d_ref[other].reshape(dim, width), 1, 0)).astype(BF16)
            hlow_ref[:, at] = hidden_low
            second = second + dot(hidden_low, u_refs[c][...], 1, 1)
        normed_two, scale_two = norm_parts(mid_ref[...])
        add(0, second * normed_two)
        add(1, second)
        middle_grad = result_grad + norm_back(second, normed_two, scale_two, norm_ref[2:3, :])
        mgrad_ref[...] = middle_grad
        middle_low = middle_grad.astype(BF16)
        mlow_ref[...] = middle_low
        for r in range(n_mp):
            ag_refs[r][...] = dot(middle_low, o_ref[mp ^ r, :, :cols], 1, 0).astype(BF16)

    row = lambda c: pl.BlockSpec((block, c), lambda i, *_: (i, 0))
    shape = lambda c, t: jax.ShapeDtypeStruct((rows, c), t)
    slots = lambda c: pl.BlockSpec((SLOTS, c), lambda i, *_: (i, 0))
    own_row = pl.BlockSpec((block, 1), lambda i, ids_ref: (i * n_mp + ids_ref[1], 0))
    return pl.pallas_call(
        kernel,
        grid_spec=pltpu.PrefetchScalarGridSpec(
            num_scalar_prefetch=1,
            grid=(rows // block,),
            in_specs=[row(dim), row(dim), row(hidden_size), slots(dim), slots(128), own_row, whole(params.shape), whole(out_w.shape)]
            + [whole(up[0].shape)] * n_mp
            + [ANY] * 4,
            out_specs=[row(dim), row(hidden_size), row(dim), row(dim)] + [row(cols)] * n_mp + [whole((5, 8, dim))],
            scratch_shapes=[pltpu.VMEM((n_mp, plan.groups // 2, 2, plan.block, width), BF16), pltpu.SemaphoreType.DMA((8,))],
        ),
        out_shape=[shape(dim, BF16), shape(hidden_size, BF16), shape(dim, BF16), shape(dim, F32)]
        + [shape(cols, BF16)] * n_mp
        + [jax.ShapeDtypeStruct((5, 8, dim), F32)],
        compiler_params=PARAMS,
        cost_estimate=cost(2 * rows * dim * (2 * hidden_size + dim), rows * hidden_size * 8),
        name="feed_back",
    )(ids, result, middle, slope, row_grads, stats, seg_col, params, out_w, *up, *down)


def weight_grads(plan, pairs, out_pair, cls_blocks, sends, blocks):
    dim = pairs[0][0].shape[1]
    rows = pairs[0][0].shape[0]
    n_mp, size, merge = plan.n_mp, plan.block, plan.merge
    lines = plan.groups // 2
    width = pairs[0][1].shape[1] // n_mp
    cols = out_pair[1][0].shape[1]
    out_cols = -(-cols // 128) * 128
    inputs = [a for pair in pairs for a in pair] + [out_pair[0]] + list(out_pair[1]) + [cls_blocks] + list(blocks)
    n_load = len(inputs)
    widths = [width] * len(pairs) + [out_cols]
    n = len(widths)

    def kernel(*refs):
        sources, ag_in, refs = refs[:n_load], refs[n_load : n_load + n_mp - 1], refs[n_load + n_mp - 1 :]
        keep_out, send_out, cls_out, ag_out, refs = refs[:n], refs[n : 2 * n], refs[2 * n], refs[2 * n + 1 : 2 * n + n_mp], refs[2 * n + n_mp :]
        block_ref, refs = refs[0], refs[1:]
        targets, refs = refs[:n_load], refs[n_load:]
        send_buf, got_buf, own_buf, keep_buf, low_buf = (refs[i * n : (i + 1) * n] for i in range(5))
        cls_got, load_sems, store_sems, send_sems, recv_sems, block_sems = refs[5 * n :]
        loads = Loads(sources, targets, load_sems)
        net = Sender(send_sems, recv_sems)
        y = net.dp // merge % 2
        side, core = net.mp // 2, net.mp % 2
        net.meet([("mp", 1), ("mp", 2), ("mp", 3), ("dp", merge)])
        ag = [net.copy(a, b, "mp", r) for r, (a, b) in enumerate(zip(ag_in, ag_out), start=1)]
        places = [block_ref.at[:, flip(net.mp, r)] for r in (0, 2)]
        cls_ref = loads[n_load - 3]
        cls_copy = net.copy(cls_ref.at[1], cls_got, "dp", merge)
        stores = []

        def grad(number, other_side, other_core):
            if number < len(pairs):
                left, right = loads[2 * number], loads[2 * number + 1]
                at = flip(side, other_side) * 2 + flip(core, other_core)
                return dot(left[...], right[:, pl.ds(pl.multiple_of(at * width, 128), width)], 0, 0)
            left = loads[2 * len(pairs)]
            right = loads[2 * len(pairs) + 1 + other_side * 2 + other_core]
            value = dot(left[...], right[...], 0, 0)
            return jnp.concatenate([value, jnp.zeros((dim, out_cols - cols), F32)], axis=1) if out_cols != cols else value

        split = lambda value: value.reshape(lines, 2, size, value.shape[1])
        cores, block_copies, block_own = [], [], []
        for i in range(n):
            if i == 1:
                rows_in = [loads[n_load - 2], loads[n_load - 1]]
                block_copies += [net.copy(a, b, "mp", 1) for a, b in zip(rows_in, places)]
                block_own += [pltpu.make_async_copy(a, b, block_sems.at[j]) for j, (a, b) in enumerate(zip(rows_in, places))]
                start_all(block_own)
            for other_side in (0, 1):
                send_buf[i][flip(side, other_side)] = split(grad(i, other_side, 1).astype(BF16))
            cores.append(net.copy(send_buf[i], got_buf[i], "mp", 1))
            for other_side in (0, 1):
                own_buf[i][flip(side, other_side)] = split(grad(i, other_side, 0))
        for i in range(n):
            cores[i].wait_recv()
            if i == 0:
                keep_buf[i][...] = own_buf[i][side] + got_buf[i][side].astype(F32)
                low_buf[i][...] = (own_buf[i][1 - side] + got_buf[i][1 - side].astype(F32)).astype(BF16)
            else:
                for x in (0, 1):
                    keep_buf[i][x] = own_buf[i][x, :, y] + got_buf[i][x, :, y].astype(F32)
                    low_buf[i][x] = (own_buf[i][x, :, 1 - y] + got_buf[i][x, :, 1 - y].astype(F32)).astype(BF16)
            for a, b in ((low_buf[i], send_out[i]), (keep_buf[i], keep_out[i])):
                stores.append(pltpu.make_async_copy(a, b, store_sems.at[len(stores)]))
                stores[-1].start()
        cls_copy.wait_recv()
        cls_out[...] = cls_ref[0].astype(F32) + cls_got[...].astype(F32)
        for c in ag + block_copies:
            c.wait_recv()
        wait_all(block_own)
        net.finish()
        for c in stores:
            c.wait()

    shape = jax.ShapeDtypeStruct
    vmem = pl.BlockSpec(memory_space=pltpu.VMEM)
    full = [(2, lines, 2, size, w) for w in widths]
    half = [(lines, 2, size, widths[0])] + [(2, lines, size, w) for w in widths[1:]]
    n_sems = n + n_mp + 2
    seqs, share = blocks[0].shape[:2]
    out = pl.pallas_call(
        kernel,
        in_specs=[ANY] * (n_load + n_mp - 1),
        out_specs=[ANY] * (2 * n) + [vmem] + [ANY] * n_mp,
        out_shape=[shape(h, F32) for h in half]
        + [shape(h, BF16) for h in half]
        + [shape(cls_blocks.shape[1:], F32)]
        + [shape(a.shape, a.dtype) for a in sends]
        + [shape((seqs, n_mp, share, dim), BF16)],
        scratch_shapes=[pltpu.VMEM(a.shape, a.dtype) for a in inputs]
        + [pltpu.VMEM(f, BF16) for f in full]
        + [pltpu.VMEM(f, BF16) for f in full]
        + [pltpu.VMEM(f, F32) for f in full]
        + [pltpu.VMEM(h, F32) for h in half]
        + [pltpu.VMEM(h, BF16) for h in half]
        + [
            pltpu.VMEM(cls_blocks.shape[1:], BF16),
            pltpu.SemaphoreType.DMA((n_load,)),
            pltpu.SemaphoreType.DMA((2 * n,)),
            pltpu.SemaphoreType.DMA((n_sems,)),
            pltpu.SemaphoreType.DMA((n_sems,)),
            pltpu.SemaphoreType.DMA((2,)),
        ],
        compiler_params=pltpu.CompilerParams(vmem_limit_bytes=60 * 1024 * 1024, collective_id=2, has_side_effects=True),
        cost_estimate=cost(2 * rows * dim * n_mp * sum(widths), rows * width * n_mp * 8),
        name="grads",
    )(*inputs, *sends)
    return out[:n], out[n : 2 * n], out[2 * n], out[2 * n + 1 : 2 * n + n_mp], out[2 * n + n_mp].reshape(-1, dim)


def finish(plan, low, proj_grads, w, middle_grad, tokens, params, row_sums, gain_sums, loss, zx, yz, z_only):
    seqs = len(proj_grads)
    dim = low.shape[1]
    cols = w.shape[2]
    n_mp = plan.n_mp
    share = LEN // n_mp
    lines, size, merge = plan.groups // 2, plan.block, plan.merge
    dp_bits = [1 << i for i in range(plan.n_dp.bit_length() - 1)]
    far = [2 * k * merge for k in range(1, lines)]
    partners = [("mp", 1), ("mp", 2)] + [("dp", b) for b in sorted(set(dp_bits + far + [merge]))]
    stages = [("mp", 1), ("mp", 2)] + [("dp", b) for b in dp_bits]
    inputs = [w] + [g for seq in proj_grads for g in seq] + [a for pair in zx + yz for a in pair] + list(z_only)
    inputs += [low, middle_grad]
    smalls = [params, row_sums, loss] + list(gain_sums)
    n_in = len(inputs)
    n_zx, n_yz, n_z = len(zx), len(yz), len(z_only)
    n_sems = (lines - 1) * (n_zx + n_yz + n_z + 1) + n_zx + n_yz + 1 + 4 * seqs + len(stages)
    n_out = 3 + n_zx + n_yz + n_z

    def kernel(*refs):
        sources, (norm_ref, row_sum_ref, loss_ref, *gain_refs), refs = refs[:n_in], refs[n_in : n_in + 3 + seqs], refs[n_in + 3 + seqs :]
        tokens_in, refs = refs[0], refs[1:]
        rows_ref, qkv_out, total_ref, *owned = refs[:n_out]
        zx_out, yz_out, z_out = owned[:n_zx], owned[n_zx : n_zx + n_yz], owned[n_zx + n_yz :]
        scratch = list(refs[n_out:])
        take = lambda n: [scratch.pop(0) for _ in range(n)]
        targets = take(n_in)
        t_keep, t_send, t_got, t_mine, x_send, x_got, acc, q_low, q_y, q_send, q_z, got_sums, load_sems, send_sems, recv_sems, x_ref = take(16)
        zx_low, zx_got, zx_send, zx_last = take(n_zx), take(n_zx), take(n_zx), take(n_zx)
        yz_low, yz_got, yz_send, yz_last = take(n_yz), take(n_yz), take(n_yz), take(n_yz)
        z_low, z_got = take(n_z), take(n_z)
        loads = Loads(sources, targets, load_sems)
        net = Sender(send_sems, recv_sems)
        copy = net.copy
        own_copies = own_rows(tokens_in, x_ref, share, n_mp, net.mp, load_sems, n_in)
        group = net.dp // merge
        z, y = group // 2, group % 2
        side, core = net.mp // 2, net.mp % 2
        net.meet(partners)
        others = range(1, lines)
        to_z = lambda src, dst, k: copy(src, dst, "dp", 2 * k * merge)
        pair_from = 1 + 3 * seqs
        pair = lambda i: (loads[pair_from + 2 * i], loads[pair_from + 2 * i + 1])
        both = lambda a, b, *at: a[at].astype(F32) + b[at].astype(F32)
        z_from = pair_from + 2 * (n_zx + n_yz)
        y_copies, z_copies = [], []

        def over_y(i):
            a, b = pair(n_zx + i)
            for line in range(lines):
                yz_low[i][line] = both(a, b, line, 1 - y).astype(BF16)
            y_copies.append(copy(yz_low[i], yz_got[i], "dp", merge))

        def over_z(i):
            a, b = pair(i)
            for k in others:
                for s in (0, 1):
                    zx_low[i][k - 1, s] = both(a, b, s, flip(z, k)).astype(BF16)
                z_copies.append(to_z(zx_low[i].at[k - 1], zx_got[i].at[k - 1], k))

        def only_z(i):
            for k in others:
                z_low[i][k - 1] = loads[z_from + i][flip(z, k)].astype(BF16)
                z_copies.append(to_z(z_low[i].at[k - 1], z_got[i].at[k - 1], k))

        w_ref = loads[0]
        pg = [[loads.targets[1 + 3 * s + p] for p in range(3)] for s in range(seqs)]
        core_copies = []
        x_copies = []

        def over_x(s):
            core_copies[s].wait_recv()
            x_send[s] = (t_keep[s, 1].astype(F32) + t_got[s, 1].astype(F32)).astype(BF16)
            x_copies.append(copy(x_send.at[s], x_got.at[s], "mp", 2))
            t_mine[s] = t_keep[s, 0].astype(F32) + t_got[s, 0].astype(F32)

        for s in range(seqs):
            for p in range(3):
                loads[1 + 3 * s + p]

            def terms(target, i, carry):
                to_other = i // 2
                row_side = side + i % 2 * (1 - 2 * side)
                row_core = core + (1 - to_other) * (1 - 2 * core)
                at = pl.ds(pl.multiple_of((row_side * 2 + row_core) * share, share), share)
                gq, gk, gv = (ref[at, :] for ref in pg[s])
                total = dot(gq, w_ref[0], 1, 1) + dot(gk, w_ref[1], 1, 1) + dot(gv, w_ref[2], 1, 1)
                target[s, i % 2] = total.astype(BF16)
                return carry

            lax.fori_loop(0, 2, functools.partial(terms, t_send), 0)
            core_copies.append(copy(t_send.at[s], t_got.at[s], "mp", 1))
            lax.fori_loop(2, 4, functools.partial(terms, t_keep), 0)
            if s == 0:
                over_x(0)
                over_z(0)
            elif s > 1:
                over_x(s - 1)
            if s == 1:
                for i in range(n_yz):
                    over_y(i)
                for i in range(1, n_zx):
                    over_z(i)
                for i in range(n_z):
                    only_z(i)
        if seqs > 1:
            over_x(seqs - 1)

        low_ref = loads[n_in - 2]
        for s in range(seqs):
            for p in range(3):
                part = dot(low_ref[s * LEN : (s + 1) * LEN, :], pg[s][p][...], 0, 0)
                acc[p] = part if s == 0 else acc[p] + part
        for p in range(3):
            q_low[p] = acc[p].reshape(lines, 2, size, cols).astype(BF16)
        y_copy = copy(q_low.at[:, :, 1 - y], q_y, "dp", merge)

        mid_ref = loads[n_in - 1]
        for c in own_copies:
            c.wait()
        total_ref[...] = jnp.zeros_like(total_ref)
        for n in range(5):
            total_ref[2 + n : 3 + n, :] = jnp.sum(row_sum_ref[n], axis=0, keepdims=True)
        for n in range(2):
            gain_sum = sum(jnp.sum(ref[n], axis=0, keepdims=True) for ref in gain_refs)
            total_ref[8 + n : 9 + n, 0:cols] = gain_sum
        total_ref[10:11, 0:128] = loss_ref[0:1, :]
        row_copies = []
        q_copies = []
        for s in range(seqs):
            at = slice(s * share, (s + 1) * share)
            normed, scale = norm_parts(x_ref[at, :].astype(F32))
            x_copies[s].wait_recv()
            first = t_mine[s] + x_got[s].astype(F32)
            total_ref[0:1, :] += jnp.sum(first * normed, axis=0, keepdims=True)
            total_ref[1:2, :] += jnp.sum(first, axis=0, keepdims=True)
            rows_ref[0, s] = (mid_ref[at, :] + norm_back(first, normed, scale, norm_ref[0:1, :])).astype(BF16)
            row_copies.append(copy(rows_ref.at[0, s], rows_ref.at[1, s], "mp", 2))
            if s == 0:
                y_copy.wait_recv()
                for line in range(lines):
                    for p in range(3):
                        rows_at = pl.ds(pl.multiple_of((line * 2 + y) * size, 8), size)
                        q_send[line, p] = (acc[p, rows_at, :] + q_y[p, line].astype(F32)).astype(BF16)
                q_copies = [to_z(q_send.at[flip(z, k)], q_z.at[k - 1], k) for k in others]
            if s == min(1, seqs - 1):
                for i in range(n_yz):
                    a, b = pair(n_zx + i)
                    y_copies[i].wait_recv()
                    for k in others:
                        at_z = flip(z, k)
                        yz_send[i][k - 1] = (both(a, b, at_z, y) + yz_got[i][at_z].astype(F32)).astype(BF16)
                        z_copies.append(to_z(yz_send[i].at[k - 1], yz_last[i].at[k - 1], k))
        mate_copies, last_copies = [], []

        def zx_last_step(i):
            for c in z_copies[i * (lines - 1) : (i + 1) * (lines - 1)]:
                c.wait_recv()
            a, b = pair(i)
            other = both(a, b, 1 - side, z) + sum(zx_got[i][k - 1, 1 - side].astype(F32) for k in others)
            zx_send[i][...] = other.astype(BF16)
            last_copies.append(copy(zx_send[i], zx_last[i], "mp", 2))
            zx_out[i][...] = both(a, b, side, z) + sum(zx_got[i][k - 1, side].astype(F32) for k in others)

        def mate(n):
            row_copies[n].wait_recv()
            mate_copies.append(copy(rows_ref.at[pl.ds(0, 2), n], rows_ref.at[pl.ds(2, 2), n], "mp", 1))

        between = [functools.partial(zx_last_step, i) for i in range(n_zx)] + [functools.partial(mate, n) for n in range(seqs)]
        for n, (axis, bits) in enumerate(stages):
            count = 8 if axis == "mp" else 16
            stage = copy(total_ref.at[pl.ds(0, count)], got_sums.at[n, pl.ds(0, count)], axis, bits)
            net.started.pop()
            if between:
                between.pop(0)()
            stage.wait()
            total_ref[0:count, :] += got_sums[n, 0:count, :]
        for step in between:
            step()
        for c in z_copies[n_zx * (lines - 1) :]:
            c.wait_recv()
        for i in range(n_yz):
            a, b = pair(n_zx + i)
            own = both(a, b, z, y) + yz_got[i][z].astype(F32)
            yz_out[i][...] = own + sum(yz_last[i][k - 1].astype(F32) for k in others)
        for i in range(n_z):
            z_out[i][...] = loads[z_from + i][z] + sum(z_got[i][k - 1].astype(F32) for k in others)
        for c in q_copies:
            c.wait_recv()
        for p in range(3):
            rows_at = pl.ds(pl.multiple_of((z * 2 + y) * size, 8), size)
            own = acc[p, rows_at, :] + q_y[p, z].astype(F32)
            qkv_out[p] = own + sum(q_z[k - 1, p].astype(F32) for k in others)
        for i, c in enumerate(last_copies):
            c.wait_recv()
            zx_out[i][...] += zx_last[i][...].astype(F32)
        for c in mate_copies:
            c.wait_recv()
        net.finish()

    vmem = pl.BlockSpec(memory_space=pltpu.VMEM)
    shape = jax.ShapeDtypeStruct
    blk = (3, size, cols)
    piece = lambda a: a.shape[-2:]
    buf = lambda a, lead, t=BF16: pltpu.VMEM(tuple(lead) + piece(a), t)
    three = lines - 1
    scratch = [pltpu.VMEM(a.shape, a.dtype) for a in inputs]
    scratch += [
        pltpu.VMEM((seqs, 2, share, dim), BF16),
        pltpu.VMEM((seqs, 2, share, dim), BF16),
        pltpu.VMEM((seqs, 2, share, dim), BF16),
        pltpu.VMEM((seqs, share, dim), F32),
        pltpu.VMEM((seqs, share, dim), BF16),
        pltpu.VMEM((seqs, share, dim), BF16),
        pltpu.VMEM((3, dim, cols), F32),
        pltpu.VMEM((3, lines, 2, size, cols), BF16),
        pltpu.VMEM((3, lines, size, cols), BF16),
        pltpu.VMEM((lines,) + blk, BF16),
        pltpu.VMEM((three,) + blk, BF16),
        pltpu.VMEM((len(stages), 16, dim), F32),
        pltpu.SemaphoreType.DMA((n_in + seqs,)),
        pltpu.SemaphoreType.DMA((n_sems,)),
        pltpu.SemaphoreType.DMA((n_sems,)),
        pltpu.VMEM((seqs * share, dim), tokens.dtype),
    ]
    firsts, seconds = [a for a, _ in zx], [a for a, _ in yz]
    for lead in ((three, 2), (three, 2), (), ()):
        scratch += [buf(a, lead) for a in firsts]
    for lead in ((lines,), (lines,), (three,), (three,)):
        scratch += [buf(a, lead) for a in seconds]
    scratch += [buf(a, (three,)) for a in z_only] + [buf(a, (three,)) for a in z_only]
    out = pl.pallas_call(
        kernel,
        in_specs=[ANY] * n_in + [vmem] * len(smalls) + [ANY],
        out_specs=[vmem] * n_out,
        out_shape=[shape((4, seqs, share, dim), BF16), shape(blk, F32), shape((16, dim), F32)]
        + [shape(piece(a), F32) for a in firsts + seconds + list(z_only)],
        scratch_shapes=scratch,
        compiler_params=pltpu.CompilerParams(vmem_limit_bytes=60 * 1024 * 1024, collective_id=1, has_side_effects=True),
        cost_estimate=cost(12 * seqs * LEN * dim * cols, seqs * LEN * dim * 8),
        name="finish",
    )(*inputs, *smalls, tokens)
    return out[0], out[1], out[2], out[3:]


def adam_update(weight, moment_one, moment_two, gradient, step_rate, decay_rate):
    fresh_one = BETA_ONE * moment_one + (1.0 - BETA_ONE) * gradient
    fresh_two = BETA_TWO * moment_two + (1.0 - BETA_TWO) * gradient * gradient
    one_hat = fresh_one / (1.0 - BETA_ONE**STEP)
    two_hat = fresh_two / (1.0 - BETA_TWO**STEP)
    updated = weight - step_rate * (one_hat / (jnp.sqrt(two_hat) + ADAM_EPS) + decay_rate * weight)
    return (fresh_one, fresh_two, updated)


def update(plan, ids, parts, groups):
    n_mp, seqs, share, dim = parts.shape
    n = len(groups)
    arrays = [a for group in groups for a in group]

    def kernel(ids_ref, part_ref, *refs):
        sources, out_ref, results = refs[: 4 * n], refs[4 * n], refs[4 * n + 1 :]
        out_ref[...] = part_ref[...].astype(F32)

        @pl.when(pl.program_id(0) == 0)
        def _():
            for i in range(n):
                w_ref, m_ref, v_ref, g_ref = sources[4 * i : 4 * i + 4]
                columns = w_ref.shape[-1]
                grad = g_ref[...][..., :columns]
                fresh = adam_update(w_ref[...], m_ref[...], v_ref[...], grad, MATRIX_RATE, MATRIX_DECAY)
                for ref, value in zip(results[3 * i : 3 * i + 3], fresh):
                    ref[...] = value

    relative = lambda i: i % 2 * 2 + i // 2
    shapes = [jax.ShapeDtypeStruct(group[0].shape, F32) for group in groups for _ in range(3)]
    out = pl.pallas_call(
        kernel,
        grid_spec=pltpu.PrefetchScalarGridSpec(
            num_scalar_prefetch=1,
            grid=(n_mp,),
            in_specs=[pl.BlockSpec((None, seqs, share, dim), lambda i, *_: (i, 0, 0, 0))] + [whole(a.shape) for a in arrays],
            out_specs=[pl.BlockSpec((seqs, None, share, dim), lambda i, ids_ref: (0, ids_ref[1] ^ relative(i), 0, 0))]
            + [whole(a.shape) for a in shapes],
        ),
        out_shape=[jax.ShapeDtypeStruct((seqs, n_mp, share, dim), F32)] + shapes,
        compiler_params=PARAMS,
        cost_estimate=cost(0, seqs * n_mp * share * dim * 8),
        name="update",
    )(ids, parts, *arrays)
    return out[0].reshape(seqs * n_mp * share, dim), [out[1 + 3 * i : 4 + 3 * i] for i in range(n)]


def shards(
    tokens,
    seg_ids,
    labels,
    w_qkv,
    m_qkv,
    v_qkv,
    w_out,
    m_out,
    v_out,
    w_up,
    m_up,
    v_up,
    w_down,
    m_down,
    v_down,
    w_cls,
    m_cls,
    v_cls,
    norm_params,
    m_norm,
    v_norm,
    qk_gain,
    m_qk,
    v_qk,
    *,
    n_dp,
    n_mp,
):
    dp, mp = lax.axis_index("dp"), lax.axis_index("mp")
    group_rows, dim = tokens.shape
    plan = Plan(n_dp, n_mp, dim)
    seqs = group_rows // LEN
    share = LEN // n_mp
    rows = seqs * share
    cols = w_qkv.shape[2]
    classes = w_cls.shape[1]
    class_cols = -(-classes // 128) * 128
    out_cols = -(-cols // 128) * 128
    ids = jnp.stack([dp // plan.merge, mp]).astype(jnp.int32)

    new_image = seg_ids != jnp.concatenate([jnp.full((1,), -1, jnp.int32), seg_ids[:-1]])
    count = jnp.sum((new_image & (seg_ids != PAD_ID)).astype(F32))
    dim_part, head_part = norm_params.shape[1], qk_gain.shape[2]
    pad = lambda a, r, c: jnp.pad(a, ((0, r - a.shape[0]), (0, c - a.shape[1])))
    low_param = lambda a: lax.reduce_precision(a, 8, 7)
    small = jnp.concatenate(
        [
            pad(low_param(norm_params), 8, 128),
            pad(low_param(qk_gain).reshape(2, cols // HEAD * head_part), 8, 128),
            pad(count.reshape(1, 1), 8, 128),
        ]
    )
    low = lambda a: a if plan.merge == 1 else a.astype(BF16)
    qkv_block = plan.merged(low(w_qkv), 1)
    up_block = plan.merged(low(w_up), 0)
    down_block = plan.merged(w_down.T.astype(BF16), 0)
    out_block = plan.merged(pad(w_out.T.astype(BF16), dim_part, out_cols), 0)
    cls_block = plan.merged(low(w_cls), 0)
    small_block = plan.merged(small[None], 0)

    tied = lambda value, tie: lax.optimization_barrier((value, tie))[0]

    head_of = jnp.arange(cols) // HEAD
    ones = jnp.where(head_of[:, None] == head_of[None, :], 1.0 / HEAD, 0.0).astype(BF16)
    starts, widths, live = key_windows(seg_ids)
    seg_col = seg_ids.reshape(group_rows, 1)
    seg_row = seg_ids.reshape(-1, LEN)
    seg_row = jnp.stack([seg_row, jnp.roll(seg_row, -ALIGN, axis=1)], axis=1)
    normed_low, pq, pk, q, k, v, w, up, down, out_w, cls, params, gains, images = gather_project(
        plan, tokens, qkv_block, up_block, down_block, out_block, cls_block, small_block, ones
    )
    w = w.reshape(3, dim, cols)
    out_w = out_w.reshape(n_mp, dim, out_cols)
    up = up.reshape(dim, up.shape[-1])
    up_across, down_across = plan.swap(up, "mp", 2), plan.group_swap(down, 1)
    cls = cls.reshape(dim, class_cols)
    image_total = images[0, 0]
    *attended, logs = attend(plan, ids, starts, widths, q, k, v, seg_col, seg_row)

    (middle, second_low, active, slope), attended, up_mates, down_mates = feed_up(
        plan, tokens, attended, params, out_w, up, up_across, down, down_across
    )
    cls_across = plan.swap(tied(cls, middle), "mp", 2)
    up = [up, up_across, *up_mates]
    down = [down, down_across, *down_mates]
    result, block_rows, pool = feed_down(plan, ids, middle, active, seg_row, params, down)

    block_rows = block_rows.reshape(seqs, share, dim)
    slot_label = labels.reshape(seqs, IMG_SEQ)
    slot_label = slot_label // classes * class_cols + slot_label % classes
    slot_label = jnp.pad(slot_label, ((0, 0), (0, SLOTS - IMG_SEQ)), constant_values=-1).reshape(seqs * SLOTS, 1)
    row_grads, stats, loss, cls_blocks = classify(plan, pool, slot_label, images, cls, cls_across, classes)

    block_rows = lax.optimization_barrier((block_rows, stats))[0]
    block_across = plan.swap(block_rows, "mp", 2)

    result_low, hidden_low, middle_low, middle_grad, *rest = feed_back(
        plan, ids, result, middle, slope, row_grads, stats, seg_col, params, out_w, up, down, cols
    )
    attended_grads, sums = rest[:n_mp], rest[n_mp]
    cls_blocks = cls_blocks.reshape(2, plan.groups // 2, plan.block, class_cols)
    kept, sent, cls_sum, arrived, block_out = weight_grads(
        plan,
        [(result_low, active), (second_low, hidden_low)],
        (middle_low, attended),
        cls_blocks,
        attended_grads[1:],
        (block_rows, block_across),
    )
    grad_parts = [attended_grads[0]] + list(arrived)
    got = [plan.swap(sent[0], "mp", 2)] + [plan.group_swap(part, 1) for part in sent[1:]]

    proj_grads, gain_sums = [], []
    for s in range(seqs):
        *grad, gain_sum = attend_back(
            plan, s, ids, starts, widths, live, q, k, v, pq, pk, gains, ones, grad_parts, logs, seg_col, seg_row
        )
        proj_grads.append(grad)
        gain_sums.append(gain_sum)
    *got, _ = lax.optimization_barrier((*got, proj_grads[-1][0]))

    down_pair, up_pair, out_pair = zip(kept, got)
    last_rows, grad_qkv, small_grads, owned = finish(
        plan, normed_low, proj_grads, w, middle_grad, tokens, params, sums, gain_sums, loss, [up_pair, out_pair], [down_pair], [cls_sum]
    )
    mean_loss = small_grads[10, 0] / image_total
    grad_qkv = plan.unmerged(grad_qkv, 1)
    grad_up, grad_out, grad_down, grad_cls = (plan.unmerged(a, 0) for a in owned)
    matrices = [
        (w_qkv, m_qkv, v_qkv, grad_qkv),
        (w_out, m_out, v_out, grad_out[:, :cols].T),
        (w_up, m_up, v_up, grad_up),
        (w_down.T, m_down.T, v_down.T, grad_down),
        (w_cls, m_cls, v_cls, grad_cls),
    ]
    input_grad, fresh = update(plan, ids, last_rows, matrices)
    norm_part = lax.dynamic_slice(small_grads, (0, dp * dim_part), (7, dim_part))
    qk_part = lax.dynamic_slice_in_dim(small_grads[8:10, :cols].reshape(2, cols // HEAD, HEAD), dp * head_part, head_part, 2)
    fresh[3] = [a.T for a in fresh[3]]
    outputs = [block_out, input_grad, mean_loss] + [a for group in fresh for a in group]
    one, two, new = adam_update(norm_params, m_norm, v_norm, norm_part, GAIN_RATE, 0.0)
    outputs += [one, two[:6], two[6], new]
    outputs += list(adam_update(qk_gain, m_qk, v_qk, qk_part, GAIN_RATE, 0.0))
    return tuple(outputs)


def solution(mesh):
    rows_cols = (P("mp", "dp"),) * 3
    cols_rows = (P("dp", "mp"),) * 3
    qkv_spec = (P(None, "dp", "mp"),) * 3
    qk_spec = (P(None, "mp", "dp"),) * 3
    norm_spec = P(None, "dp")
    in_specs = (
        (P("dp", None), P("dp"), P("dp")) + qkv_spec + rows_cols + cols_rows + rows_cols + cols_rows + (norm_spec,) * 3 + qk_spec
    )
    out_specs = (
        (P("dp", None), P("dp", None), P())
        + qkv_spec
        + rows_cols
        + cols_rows
        + rows_cols
        + cols_rows
        + (norm_spec, norm_spec, P("dp"), norm_spec)
        + qk_spec
    )
    body = functools.partial(shards, n_dp=mesh.shape["dp"], n_mp=mesh.shape["mp"])
    return jax.shard_map(body, mesh=mesh, in_specs=in_specs, out_specs=out_specs, check_vma=False)
```

```python
import functools

import jax
import jax.numpy as jnp
from jax import lax
from jax.experimental import pallas as pl
from jax.experimental.pallas import tpu as pltpu
from jax.sharding import PartitionSpec as P

LEN = 1024
STEP = 10
SEQ_DEV = 3
IMG_DEV = 180
PAD_ID = 180

NORM_EPS = 1e-06
MASK_FILL = -1000000000.0
BETA_ONE = 0.9
BETA_TWO = 0.999
ADAM_EPS = 1e-08
MATRIX_RATE = 0.1
MATRIX_DECAY = 0.1
GAIN_RATE = 0.8

HEAD = 64
QB = 256
QBLOCKS = LEN // QB
WINDOWS = (384, 512, 768, 1024)
ALIGN = 64
LANES = 128
F32 = jnp.float32
BF16 = jnp.bfloat16
VMEM_LIMIT = 56 * 1024 * 1024
IMG_SEQ = 60
SLOTS = 64
ANY = pl.BlockSpec(memory_space=pl.ANY)
PARAMS = pltpu.CompilerParams(vmem_limit_bytes=VMEM_LIMIT)


def dot(a, b, ca, cb):
    return lax.dot_general(a, b, (((ca,), (cb,)), ((), ())), preferred_element_type=F32)


def head_mean(values, ones_block):
    high = values.astype(BF16)
    rest = (values - high.astype(F32)).astype(BF16)
    return dot(high, ones_block, 1, 0) + dot(rest, ones_block, 1, 0)


def norm_parts(values):
    centre = values - jnp.mean(values, axis=-1, keepdims=True)
    spread = jnp.mean(centre * centre, axis=-1, keepdims=True)
    scale = lax.rsqrt(spread + NORM_EPS)
    return centre * scale, scale


def norm_back(grad, normed, scale, gain):
    scaled = grad * gain
    first = jnp.mean(scaled, axis=-1, keepdims=True)
    second = jnp.mean(scaled * normed, axis=-1, keepdims=True)
    return (scaled - first - normed * second) * scale


def head_parts(values, ones_block):
    centre = values - head_mean(values, ones_block)
    scale = lax.rsqrt(head_mean(centre * centre, ones_block) + NORM_EPS)
    return centre * scale, scale


def cost(flops, read, exps=0):
    return pl.CostEstimate(flops=int(flops), bytes_accessed=int(read), transcendentals=int(exps))


def whole(shape):
    return pl.BlockSpec(tuple(shape), lambda *_: (0,) * len(shape))


class Plan:
    def __init__(self, n_dp, n_mp, dim):
        self.n_dp, self.n_mp = n_dp, n_mp
        self.merge = 1 if dim // n_dp % 16 == 0 else 2
        self.groups = n_dp // self.merge
        self.block = dim // self.groups
        self.far = [2 * k for k in range(1, self.groups // 2)]

    def swap(self, value, axis, bits):
        size = self.n_dp if axis == "dp" else self.n_mp
        return lax.ppermute(value, axis, [(i, i ^ bits) for i in range(size)])

    def group_swap(self, value, bits):
        return self.swap(value, "dp", bits * self.merge)

    def merged(self, value, dim):
        if self.merge == 1:
            return value
        other = self.swap(value, "dp", 1)
        even = lax.axis_index("dp") % 2 == 0
        first, second = jnp.where(even, value, other), jnp.where(even, other, value)
        return jnp.concatenate([first, second], axis=dim)

    def unmerged(self, value, dim):
        if self.merge == 1:
            return value
        half = value.shape[dim] // 2
        me = lax.axis_index("dp") % 2
        mine = lax.dynamic_slice_in_dim(value, me * half, half, dim)
        theirs = lax.dynamic_slice_in_dim(value, (1 - me) * half, half, dim)
        return mine + self.swap(theirs, "dp", 1)

    def total(self, value, axis):
        size = self.n_dp if axis == "dp" else self.n_mp
        bits = 1
        while bits < size:
            value = value + self.swap(value, axis, bits)
            bits *= 2
        return value


MESH = pl.DeviceIdType.MESH


def flip(index, bits):
    bit = 1
    while bit <= bits:
        if bits & bit:
            index = index + bit * (1 - 2 * (index // bit % 2))
        bit *= 2
    return index


class Chain:
    def __init__(self, region, order, lines):
        self.region, self.steps = region, order
        self.copies = sum({"z": lines - 1, "c": 2}.get(step, 1) for step in order)


class Gatherer:
    def __init__(self, plan, send_sems, recv_sems):
        self.plan, self.send_sems, self.recv_sems = plan, send_sems, recv_sems
        self.dp, self.mp = lax.axis_index("dp"), lax.axis_index("mp")
        self.pair = self.dp % plan.merge
        group = self.dp // plan.merge
        self.z, self.y = group // 2, group % 2
        self.x, self.core = self.mp // 2, self.mp % 2
        self.lines = plan.groups // 2
        self.used = 0
        self.pending = []

    def device(self, z, y, x, core):
        return ((z * 2 + y) * self.plan.merge + self.pair, x * 2 + core)

    def here(self):
        return self.z, self.y, self.x, self.core

    def meet(self, barrier):
        z, y, x, core = self.here()
        others = [(z, 1 - y, x, core), (z, y, 1 - x, core), (z, y, x, 1 - core)]
        others += [(flip(z, k), y, x, core) for k in range(1, self.lines)]
        for other in others:
            pl.semaphore_signal(barrier, inc=1, device_id=self.device(*other), device_id_type=MESH)
        pl.semaphore_wait(barrier, len(others))

    def start(self, chain, number, source=None):
        step, done = chain.steps[number], chain.steps[:number]
        z, y, x, core = self.here()
        spot = dict(z=None if "z" in done else z, y=None if "y" in done else y, x=None if "x" in done else x, core=core)
        if step == "z":
            copies = [(spot, (flip(z, k), y, x, core)) for k in range(1, self.lines)]
        elif step == "c":
            copies = [({**spot, "x": side}, (z, y, x, 1 - core)) for side in (0, 1)]
        else:
            copies = [(spot, dict(y=(z, 1 - y, x, core), x=(z, y, 1 - x, core))[step])]
        started = []
        for place, other in copies:
            region = chain.region(**place)
            out = pltpu.make_async_remote_copy(
                src_ref=region if source is None else source,
                dst_ref=region,
                send_sem=self.send_sems.at[self.used],
                recv_sem=self.recv_sems.at[self.used],
                device_id=self.device(*other),
                device_id_type=MESH,
            )
            self.used += 1
            out.start()
            started.append(out)
        self.pending += started
        return started

    @staticmethod
    def arrive(copies):
        for out in copies:
            out.wait_recv()

    def finish(self):
        for out in self.pending:
            out.wait_send()


class Loads:
    def __init__(self, sources, targets, sems):
        self.targets = targets
        self.copies = [pltpu.make_async_copy(a, b, sems.at[i]) for i, (a, b) in enumerate(zip(sources, targets))]
        self.done = [False] * len(self.copies)
        for c in self.copies:
            c.start()

    def __getitem__(self, i):
        if not self.done[i]:
            self.copies[i].wait()
            self.done[i] = True
        return self.targets[i]


class Sender:
    def __init__(self, send_sems, recv_sems):
        self.dp, self.mp = lax.axis_index("dp"), lax.axis_index("mp")
        self.send_sems, self.recv_sems = send_sems, recv_sems
        self.started, self.used = [], 0

    def device(self, axis, bits):
        return (flip(self.dp, bits), self.mp) if axis == "dp" else (self.dp, flip(self.mp, bits))

    def meet(self, partners):
        barrier = pltpu.get_barrier_semaphore()
        for axis, bits in partners:
            pl.semaphore_signal(barrier, inc=1, device_id=self.device(axis, bits), device_id_type=MESH)
        pl.semaphore_wait(barrier, len(partners))

    def copy(self, src, dst, axis, bits):
        n = self.used
        self.used += 1
        c = pltpu.make_async_remote_copy(
            src_ref=src,
            dst_ref=dst,
            send_sem=self.send_sems.at[n],
            recv_sem=self.recv_sems.at[n],
            device_id=self.device(axis, bits),
            device_id_type=MESH,
        )
        self.started.append(c)
        c.start()
        return c

    def finish(self):
        for c in self.started:
            c.wait_send()


def gather_project(plan, tokens, qkv_block, up_block, down_block, out_block, cls_block, small_block, ones):
    rows, dim = tokens.shape
    cols = ones.shape[0]
    n_mp, merge, size = plan.n_mp, plan.merge, plan.block
    lines = plan.groups // 2
    width = up_block.shape[1]
    out_cols, classes = out_block.shape[1], cls_block.shape[1]
    class_cols = -(-classes // 128) * 128
    block = 512
    blocks = rows // block
    dim_part = dim // plan.n_dp
    head_part = HEAD // plan.n_dp

    orders = [("small", "zy"), ("w_qk", "zy"), ("w_v", "zy"), ("out", "zyxc"), ("cls", "zy"), ("up", "zy"), ("down", "zx")]
    sizes = {name: Chain(None, order, lines).copies for name, order in orders}
    n_sems = sum(sizes.values())

    def kernel(x_ref, qkv_wide, up_wide, down_in, out_in, cls_wide, small_in, ones_ref, *refs):
        low_ref, pq_ref, pk_ref, q_ref, k_ref, v_ref, w_ref, up_ref, down_ref, o_ref, c_ref, norm_ref, gain_ref, image_ref = refs[:14]
        w_buf, small_buf, low_buf, pq_buf, pk_buf, q_buf, k_buf, v_buf, send_sems, recv_sems, own_sems, out_sems, *lows = refs[14:]
        qkv_in, up_in, cls_in = lows
        qkv_in[...] = qkv_wide[...].astype(BF16)
        up_in[...] = up_wide[...].astype(BF16)
        cls_in[...] = jnp.concatenate([cls_wide[...].astype(BF16), jnp.zeros((size, class_cols - classes), BF16)], axis=1)
        g = Gatherer(plan, send_sems, recv_sems)
        z, y, x, core = g.here()
        everything = slice(None)

        def at(v):
            return everything if v is None else v

        def wide(ref, first, count):
            columns = pl.ds(first, count)
            return lambda z, y, x, core: ref.at[at(x), core, at(z), at(y), :, columns]

        regions = dict(
            w_qk=lambda z, y, x, core: w_buf.at[pl.ds(0, 2), at(z), at(y)],
            w_v=lambda z, y, x, core: w_buf.at[pl.ds(2, 1), at(z), at(y)],
            small=lambda z, y, x, core: small_buf.at[at(z), at(y)],
            up=lambda z, y, x, core: up_ref.at[at(z), at(y)],
            down=lambda z, y, x, core: down_ref.at[at(x), at(z)],
            out=wide(o_ref, 0, out_cols),
            cls=lambda z, y, x, core: c_ref.at[at(z), at(y)],
        )
        chains = {name: Chain(regions[name], order, lines) for name, order in orders}
        sources = dict(
            w_qk=qkv_in.at[pl.ds(0, 2)],
            w_v=qkv_in.at[pl.ds(2, 1)],
            small=small_in,
            up=up_in,
            down=down_in,
            out=out_in,
            cls=cls_in,
        )
        own = {}
        for i, (name, _) in enumerate(orders):
            own[name] = pltpu.make_async_copy(sources[name], regions[name](z, y, x, core), own_sems.at[i])
            own[name].start()
        live, reached = {}, {}

        def begin(name):
            live[name] = g.start(chains[name], 0, source=sources[name])
            reached[name] = 0

        def advance(*names):
            for name in names:
                if reached[name] == len(chains[name].steps):
                    continue
                if reached[name] == 0:
                    own[name].wait()
                g.arrive(live[name])
                reached[name] += 1
                if reached[name] < len(chains[name].steps):
                    live[name] = g.start(chains[name], reached[name])

        g.meet(pltpu.get_barrier_semaphore())
        for name in ("small", "w_qk", "w_v", "out", "cls"):
            begin(name)
        advance("small", "small")

        lane = lax.broadcasted_iota(jnp.int32, (128, dim), 0)
        column = lax.broadcasted_iota(jnp.int32, (128, dim), 1)
        head_lane = lax.broadcasted_iota(jnp.int32, (128, cols), 0)
        head_column = lax.broadcasted_iota(jnp.int32, (128, cols), 1)
        norm = jnp.zeros((8, dim), F32)
        gain = jnp.zeros((8, cols), F32)
        image = jnp.zeros((8, 128), F32)
        for d in range(plan.n_dp):
            part = small_buf[d // merge // 2, d // merge % 2, d % merge]
            spread = jnp.where((column == d * dim_part + lane) & (lane < dim_part), 1.0, 0.0).astype(BF16)
            norm = norm + dot(part[0:8].astype(BF16), spread, 1, 0)
            same = (head_column // HEAD == head_lane // head_part) & (head_column % HEAD == d * head_part + head_lane % head_part)
            gain = gain + dot(part[8:16].astype(BF16), jnp.where(same, 1.0, 0.0).astype(BF16), 1, 0)
            image = image + part[16:24]
        norm_ref[...] = norm
        gain_ref[...] = gain
        image_ref[...] = image

        def first_norm(i, carry):
            at_rows = pl.ds(pl.multiple_of(i * block, block), block)
            normed, _ = norm_parts(x_ref[at_rows, :].astype(F32))
            low_buf[at_rows, :] = (normed * norm[0:1, :] + norm[1:2, :]).astype(BF16)
            return carry

        third = blocks // 3
        lax.fori_loop(0, third, first_norm, 0)
        advance("w_qk", "w_v")
        begin("up")
        begin("down")
        lax.fori_loop(third, blocks, first_norm, 0)
        outs = [pltpu.make_async_copy(low_buf, low_ref, out_sems.at[0])]
        outs[0].start()
        advance("out", "cls", "w_qk", "w_v")
        outs.append(pltpu.make_async_copy(w_buf, w_ref, out_sems.at[1]))
        outs[1].start()

        def project(i, carry):
            at_rows = pl.ds(pl.multiple_of(i * block, block), block)
            low = low_buf[at_rows, :]
            pq = dot(low, w_buf[0].reshape(dim, cols), 1, 0)
            pk = dot(low, w_buf[1].reshape(dim, cols), 1, 0)
            pq_buf[at_rows, :] = pq
            pk_buf[at_rows, :] = pk
            v_buf[at_rows, :] = dot(low, w_buf[2].reshape(dim, cols), 1, 0).astype(BF16)
            nq, _ = head_parts(pq, ones_ref[...])
            nk, _ = head_parts(pk, ones_ref[...])
            q_buf[at_rows, :] = (nq * gain[0:1, :]).astype(BF16)
            k_buf[at_rows, :] = (nk * gain[1:2, :]).astype(BF16)
            return carry

        lax.fori_loop(0, third, project, 0)
        advance("out", "up", "down")
        lax.fori_loop(third, 2 * third, project, 0)
        lax.fori_loop(2 * third, blocks, project, 0)
        pairs = ((pq_buf, pq_ref), (pk_buf, pk_ref), (q_buf, q_ref), (k_buf, k_ref), (v_buf, v_ref))
        for i, (a, b) in enumerate(pairs):
            outs.append(pltpu.make_async_copy(a, b, out_sems.at[2 + i]))
            outs[-1].start()
        advance("out", "cls", "up", "down", "out")
        g.finish()
        for c in outs:
            c.wait()

    vmem = pl.BlockSpec(memory_space=pltpu.VMEM)
    shape = jax.ShapeDtypeStruct
    wide_shape = lambda c: (n_mp // 2, 2, lines, 2, size, c)
    n_rows = lambda c, t: shape((rows, c), t)
    return pl.pallas_call(
        kernel,
        in_specs=[vmem, vmem, vmem, ANY, ANY, vmem, ANY, vmem],
        out_specs=[ANY] * 11 + [vmem] * 3,
        out_shape=[n_rows(dim, BF16), n_rows(cols, F32), n_rows(cols, F32), n_rows(cols, BF16), n_rows(cols, BF16), n_rows(cols, BF16)]
        + [
            shape((3, lines, 2, size, cols), BF16),
            shape((lines, 2, size, width), BF16),
            shape((n_mp // 2, lines, size, width), BF16),
            shape(wide_shape(out_cols), BF16),
            shape((lines, 2, size, class_cols), BF16),
            shape((8, dim), F32),
            shape((8, cols), F32),
            shape((8, 128), F32),
        ],
        scratch_shapes=[
            pltpu.VMEM((3, lines, 2, size, cols), BF16),
            pltpu.VMEM((lines, 2, merge, 24, 128), F32),
            pltpu.VMEM((rows, dim), BF16),
            pltpu.VMEM((rows, cols), F32),
            pltpu.VMEM((rows, cols), F32),
            pltpu.VMEM((rows, cols), BF16),
            pltpu.VMEM((rows, cols), BF16),
            pltpu.VMEM((rows, cols), BF16),
            pltpu.SemaphoreType.DMA((n_sems,)),
            pltpu.SemaphoreType.DMA((n_sems,)),
            pltpu.SemaphoreType.DMA((len(orders),)),
            pltpu.SemaphoreType.DMA((7,)),
            pltpu.VMEM(qkv_block.shape, BF16),
            pltpu.VMEM(up_block.shape, BF16),
            pltpu.VMEM((size, class_cols), BF16),
        ],
        compiler_params=pltpu.CompilerParams(vmem_limit_bytes=VMEM_LIMIT, collective_id=0, has_side_effects=True),
        cost_estimate=cost(6 * rows * dim * cols, rows * dim * 8),
        name="gather_project",
    )(tokens, qkv_block, up_block, down_block, out_block, cls_block, small_block, ones)


def head_masks(cols):
    lane = lax.broadcasted_iota(jnp.int32, (1, cols), 1)
    return [(lane >= h * HEAD) & (lane < (h + 1) * HEAD) for h in range(cols // HEAD)]


def spread_heads(block, masks):
    zero = jnp.zeros_like(block)
    return jnp.concatenate([jnp.where(m, block, zero) for m in masks], axis=0)


def join_heads(stacked, masks):
    total = stacked[0:QB]
    for h in range(1, len(masks)):
        total = jnp.where(masks[h], stacked[h * QB : (h + 1) * QB], total)
    return total


def by_window(width_ref, step, body):
    width = width_ref[step]
    for number, window in enumerate(WINDOWS):
        pl.when(width == number)(functools.partial(body, window))


def key_segments(row_ref, start, window):
    at = pl.ds(pl.multiple_of(start // LANES * LANES, LANES), window)
    return jnp.where(start % LANES == 0, row_ref[0, 0:1, at], row_ref[0, 1:2, at])


def attend(plan, ids, starts, widths, q, k, v, seg_col, seg_row):
    rows, cols = q.shape
    n_mp = plan.n_mp
    share = LEN // n_mp
    per = share // QB
    seqs = rows // LEN

    def kernel(ids_ref, start_ref, width_ref, q_ref, k_ref, v_ref, col_ref, row_ref, *outs):
        out_refs, log_ref = outs[:n_mp], outs[n_mp]
        seq, block = pl.program_id(0), pl.program_id(1)
        step = seq * QBLOCKS + block
        masks = head_masks(cols)
        heads = len(masks)

        def body(window):
            start = pl.multiple_of(start_ref[step], ALIGN)
            keys = k_ref[pl.ds(start, window), :]
            values = v_ref[pl.ds(start, window), :]
            q3 = spread_heads(q_ref[...], masks)
            s = (dot(q3, keys, 1, 1) * HEAD**-0.5).reshape(heads, QB, window)
            same = col_ref[...] == key_segments(row_ref, start, window)
            s = jnp.where(same[None], s, MASK_FILL)
            top = jnp.max(s, axis=-1, keepdims=True)
            e = jnp.exp(s - top)
            total = jnp.sum(e, axis=-1, keepdims=True)
            p = (e * (1.0 / total)).astype(BF16).reshape(heads * QB, window)
            out = join_heads(dot(p, values, 1, 0), masks).astype(BF16)
            other = (block // per) ^ ids_ref[1]
            at = pl.ds(pl.multiple_of(seq * share + block % per * QB, QB), QB)
            for r in range(n_mp):

                @pl.when(other == r)
                def _():
                    out_refs[r][at, :] = out

            log = top + jnp.log(total)
            lane = lax.broadcasted_iota(jnp.int32, (QB, 128), 1)
            logs = jnp.zeros((QB, 128), F32)
            for h in range(heads):
                logs = jnp.where(lane == h, log[h], logs)
            log_ref[...] = logs

        by_window(width_ref, step, body)

    block = lambda c: pl.BlockSpec((QB, c), lambda s, b, *_: (s * QBLOCKS + b, 0))
    all_keys = lambda c: pl.BlockSpec((LEN, c), lambda s, b, *_: (s, 0))
    return pl.pallas_call(
        kernel,
        grid_spec=pltpu.PrefetchScalarGridSpec(
            num_scalar_prefetch=3,
            grid=(seqs, QBLOCKS),
            in_specs=[block(cols), all_keys(cols), all_keys(cols), block(1), pl.BlockSpec((1, 2, LEN), lambda s, b, *_: (s, 0, 0))],
            out_specs=[whole((seqs * share, cols))] * n_mp + [block(128)],
        ),
        out_shape=[jax.ShapeDtypeStruct((seqs * share, cols), BF16)] * n_mp + [jax.ShapeDtypeStruct((rows, 128), F32)],
        compiler_params=PARAMS,
        cost_estimate=cost(60 * rows * LEN * cols, rows * cols * 8, rows * LEN),
        name="attend",
    )(ids, starts, widths, q, k, v, seg_col, seg_row)


def attend_back(plan, ids, starts, widths, live, q, k, v, pq, pk, gains, ones, grads, logs, seg_col, seg_row):
    rows, cols = q.shape
    n_mp = plan.n_mp
    share = LEN // n_mp
    per = share // QB

    def kernel(ids_ref, start_ref, width_ref, live_ref, q_ref, k_ref, v_ref, pq_ref, pk_ref, gain_ref, ones_ref, col_ref, row_ref, log_ref, *refs):
        grad_refs, (gq_ref, gk_ref, gv_ref, sum_ref, dk_ref, dv_ref) = refs[:n_mp], refs[n_mp:]
        seq, block = pl.program_id(0), pl.program_id(1)
        step = seq * QBLOCKS + block
        masks = head_masks(cols)
        heads = len(masks)

        @pl.when(block == 0)
        def _():
            dk_ref[...] = jnp.zeros_like(dk_ref)
            dv_ref[...] = jnp.zeros_like(dv_ref)

        @pl.when(step == 0)
        def _():
            sum_ref[...] = jnp.zeros_like(sum_ref)

        def back(values, grad, slot):
            ones_block = ones_ref[...]
            normed, scale = head_parts(values, ones_block)
            sum_ref[slot] += jnp.sum((grad * normed).reshape(-1, 8, cols), axis=0)
            scaled = grad * gain_ref[slot : slot + 1, :]
            first = head_mean(scaled, ones_block)
            second = head_mean(scaled * normed, ones_block)
            return ((scaled - first - normed * second) * scale).astype(BF16)

        def body(window):
            start = pl.multiple_of(start_ref[step], ALIGN)
            keys = pl.ds(start, window)
            k_win = k_ref[keys, :]
            v_win = v_ref[keys, :]
            other = (block // per) ^ ids_ref[1]
            at = pl.ds(pl.multiple_of(block % per * QB, QB), QB)
            g = grad_refs[0][at, :]
            for r in range(1, n_mp):
                g = jnp.where(other == r, grad_refs[r][at, :], g)
            q3 = spread_heads(q_ref[...], masks)
            g3 = spread_heads(g, masks)
            s = (dot(q3, k_win, 1, 1) * HEAD**-0.5).reshape(heads, QB, window)
            same = col_ref[...] == key_segments(row_ref, start, window)
            all_logs = log_ref[...]
            log = jnp.stack([all_logs[:, h : h + 1] for h in range(heads)])
            p = jnp.exp(jnp.where(same[None], s - log, MASK_FILL))
            dp = dot(g3, v_win, 1, 1).reshape(heads, QB, window)
            inner = jnp.sum(p * dp, axis=-1, keepdims=True)
            ds = (p * (dp - inner)).astype(BF16).reshape(heads * QB, window)
            p_low = p.astype(BF16).reshape(heads * QB, window)
            dv_ref[keys, :] += dot(p_low, g3, 0, 0)
            dk_ref[keys, :] += dot(ds, q3, 0, 0) * HEAD**-0.5
            dq = join_heads(dot(ds, k_win, 1, 0), masks) * HEAD**-0.5
            gq_ref[...] = back(pq_ref[...], dq, 0)

        alive = live_ref[step]

        @pl.when(alive == 0)
        def _():
            gq_ref[...] = jnp.zeros_like(gq_ref)

        @pl.when(alive != 0)
        def _():
            by_window(width_ref, step, body)

        @pl.when(block == QBLOCKS - 1)
        def _():
            gv_ref[...] = dv_ref[...].astype(BF16)

            def keys_back(i, carry):
                at = pl.ds(pl.multiple_of(i * share, share), share)
                gk_ref[at, :] = back(pk_ref[at, :], dk_ref[at, :], 1)
                return carry

            lax.fori_loop(0, n_mp, keys_back, 0)

    block = lambda c: pl.BlockSpec((QB, c), lambda s, b, *_: (s * QBLOCKS + b, 0))
    all_keys = lambda c: pl.BlockSpec((LEN, c), lambda s, b, *_: (s, 0))
    row_spec = pl.BlockSpec((1, 2, LEN), lambda s, b, *_: (s, 0, 0))
    grad_spec = pl.BlockSpec((share, cols), lambda s, b, *_: (s, 0))
    shape = jax.ShapeDtypeStruct((rows, cols), BF16)
    return pl.pallas_call(
        kernel,
        grid_spec=pltpu.PrefetchScalarGridSpec(
            num_scalar_prefetch=4,
            grid=(rows // LEN, QBLOCKS),
            in_specs=[block(cols), all_keys(cols), all_keys(cols), block(cols), all_keys(cols), whole(gains.shape), whole(ones.shape)]
            + [block(1), row_spec, block(128)]
            + [grad_spec] * n_mp,
            out_specs=[block(cols), all_keys(cols), all_keys(cols), whole((2, 8, cols))],
            scratch_shapes=[pltpu.VMEM((LEN, cols), F32), pltpu.VMEM((LEN, cols), F32)],
        ),
        out_shape=[shape, shape, shape, jax.ShapeDtypeStruct((2, 8, cols), F32)],
        compiler_params=PARAMS,
        cost_estimate=cost(60 * rows * LEN * cols, rows * cols * 24, rows * LEN),
        name="attend_back",
    )(ids, starts, widths, live, q, k, v, pq, pk, gains, ones, seg_col, seg_row, logs, *grads)


def key_windows(seg_ids):
    seg = seg_ids.reshape(-1, LEN)
    first = seg[:, ::QB]
    last = seg[:, QB - 1 :: QB]
    low = jnp.sum((seg[:, None, :] < first[:, :, None]).astype(jnp.int32), axis=2)
    high = jnp.sum((seg[:, None, :] <= last[:, :, None]).astype(jnp.int32), axis=2)
    base = low // ALIGN * ALIGN
    number = jnp.full(base.shape, len(WINDOWS) - 1, jnp.int32)
    start = jnp.zeros_like(base)
    for choice in range(len(WINDOWS) - 2, -1, -1):
        at = jnp.minimum(base, LEN - WINDOWS[choice])
        fits = high <= at + WINDOWS[choice]
        number = jnp.where(fits, choice, number)
        start = jnp.where(fits, at, start)
    live = (first != PAD_ID).astype(jnp.int32)
    return start.reshape(-1), number.reshape(-1), live.reshape(-1)


RELATIVE = (0, 2, 1, 3)


def down_copies(plan, ids_ref, parts, target, sems):
    y = ids_ref[0] % 2
    core = ids_ref[1] % 2
    copies = []
    for i, part in enumerate(parts):
        for side in range(2):
            place = target.at[side * 2 + (core ^ (i // 2)), :, y ^ (i % 2)]
            copies.append(pltpu.make_async_copy(part.at[side], place, sems.at[len(copies)]))
    return copies


def own_rows(source, target, share, n_mp, mp, sems, first):
    copies = []
    for s in range(target.shape[0] // share):
        at = pl.ds(pl.multiple_of((s * n_mp + mp) * share, share), share)
        copies.append(pltpu.make_async_copy(source.at[at], target.at[pl.ds(s * share, share)], sems.at[first + s]))
        copies[-1].start()
    return copies


def feed_up(plan, tokens, attended, params, out_w, up, up_across, down, down_across):
    dim = tokens.shape[1]
    rows, cols = attended[0].shape
    n_mp = plan.n_mp
    width = up.shape[1]
    hidden_size = n_mp * width
    share = LEN // n_mp
    seqs = rows // share
    inputs = [attended[0], out_w, up, up_across]
    shape = lambda c, t: jax.ShapeDtypeStruct((rows, c), t)
    results = [shape(dim, F32), shape(dim, BF16), shape(hidden_size, BF16), shape(hidden_size, F32)]
    n_load, n_store = len(inputs), len(results) * seqs + n_mp + 1 + seqs
    n_sems = 3 * seqs + 4

    def kernel(*refs):
        sources, (norm_ref, *sends), refs = refs[:n_load], refs[n_load : n_load + n_mp], refs[n_load + n_mp :]
        (down_in, down_across_in, tokens_in), refs = refs[:3], refs[3:]
        result_outs, att_outs, up_outs, down_outs, refs = refs[:4], refs[4 : n_mp + 3], refs[n_mp + 3 : n_mp + 5], refs[n_mp + 5 : n_mp + 7], refs[n_mp + 7 :]
        targets, bufs, att_bufs, u_bufs, refs = refs[:n_load], refs[n_load : n_load + 4], refs[n_load + 4 : n_load + n_mp + 3], refs[n_load + n_mp + 3 : n_load + n_mp + 5], refs[n_load + n_mp + 5 :]
        x_ref, load_sems, store_sems, send_sems, recv_sems = refs
        loads = Loads(sources, targets, load_sems)
        net = Sender(send_sems, recv_sems)
        x_copies = own_rows(tokens_in, x_ref, share, n_mp, net.mp, store_sems, n_store - seqs)
        net.meet([("mp", r) for r in range(1, n_mp)])
        at = lambda s: pl.ds(s * share, share)
        fetch = lambda s: [net.copy(sends[r - 1].at[at(s)], att_bufs[r - 1].at[at(s)], "mp", r) for r in range(1, n_mp)]
        rows_copies = [fetch(0)]
        up_copies = [net.copy(sources[2], u_bufs[0], "mp", 1), net.copy(sources[3], u_bufs[1], "mp", 1)]
        rows_copies += [fetch(s) for s in range(1, seqs)]
        down_copies = [net.copy(down_in, down_outs[0], "mp", 1), net.copy(down_across_in, down_outs[1], "mp", 1)]
        stores = []

        def store(src, dst):
            stores.append(pltpu.make_async_copy(src, dst, store_sems.at[len(stores)]))
            stores[-1].start()

        mid_buf, low_buf, act_buf, der_buf = bufs
        for s in range(seqs):
            here = at(s)
            att_ref, o_ref = loads[0], loads[1]
            x_copies[s].wait()
            middle = x_ref[here, :].astype(F32) + dot(att_ref[here, :], o_ref[net.mp, :, :cols], 1, 1)
            for r in range(1, n_mp):
                rows_copies[s][r - 1].wait_recv()
                middle = middle + dot(att_bufs[r - 1][here, :], o_ref[flip(net.mp, r), :, :cols], 1, 1)
            mid_buf[here, :] = middle
            normed, _ = norm_parts(middle)
            low = (normed * norm_ref[2:3, :] + norm_ref[3:4, :]).astype(BF16)
            low_buf[here, :] = low
            for c in range(n_mp):
                if c >= 2 and s == 0:
                    up_copies[c - 2].wait_recv()
                    store(u_bufs[c - 2], up_outs[c - 2])
                u_ref = loads[2 + c] if c < 2 else u_bufs[c - 2]
                columns = pl.ds(pl.multiple_of(flip(net.mp, RELATIVE[c]) * width, 128), width)
                hidden = dot(low, u_ref[...], 1, 0)
                phi = 0.5 * (1.0 + lax.erf(hidden * (0.5**0.5)))
                act_buf[here, columns] = (hidden * phi).astype(BF16)
                der_buf[here, columns] = phi + hidden * (jnp.exp(-0.5 * hidden * hidden) * 0.3989422804014327)
            for src, dst in zip(bufs, result_outs):
                store(src.at[here], dst.at[here])
        for src, dst in zip(att_bufs, att_outs):
            store(src, dst)
        for c in down_copies:
            c.wait_recv()
        net.finish()
        for c in stores:
            c.wait()

    like = lambda a: jax.ShapeDtypeStruct(a.shape, a.dtype)
    out = pl.pallas_call(
        kernel,
        in_specs=[ANY] * n_load + [pl.BlockSpec(memory_space=pltpu.VMEM)] + [ANY] * (n_mp + 2),
        out_specs=[ANY] * (n_mp + 7),
        out_shape=results + [like(a) for a in attended[1:]] + [like(up)] * 2 + [like(down)] * 2,
        scratch_shapes=[pltpu.VMEM(a.shape, a.dtype) for a in inputs + results + list(attended[1:]) + [up, up]]
        + [
            pltpu.VMEM((rows, dim), tokens.dtype),
            pltpu.SemaphoreType.DMA((n_load,)),
            pltpu.SemaphoreType.DMA((n_store,)),
            pltpu.SemaphoreType.DMA((n_sems,)),
            pltpu.SemaphoreType.DMA((n_sems,)),
        ],
        compiler_params=pltpu.CompilerParams(vmem_limit_bytes=VMEM_LIMIT, collective_id=4, has_side_effects=True),
        cost_estimate=cost(2 * rows * dim * (hidden_size + dim), rows * hidden_size * 8, rows * hidden_size * 2),
        name="feed_up",
    )(*inputs, params, *attended[1:], down, down_across, tokens)
    return out[:4], [attended[0]] + list(out[4 : n_mp + 3]), out[n_mp + 3 : n_mp + 5], out[n_mp + 5 :]


def start_all(copies):
    for c in copies:
        c.start()


def wait_all(copies):
    for c in copies:
        c.wait()


def feed_down(plan, ids, middle, active, seg_row, params, down):
    rows, dim = middle.shape
    n_mp = plan.n_mp
    hidden_size = active.shape[1]
    width = hidden_size // n_mp
    block = 256
    seqs = rows // block

    def kernel(ids_ref, mid_ref, act_ref, seg_ref, norm_ref, *refs):
        d_parts, (res_ref, block_ref, pool_ref, d_ref, sems) = refs[:4], refs[4:]
        seq = pl.program_id(0)
        copies = down_copies(plan, ids_ref, d_parts, d_ref, sems)

        @pl.when(seq == 0)
        def _():
            start_all(copies)
            wait_all(copies)

        result = mid_ref[...]
        for c in range(n_mp):
            result = result + dot(act_ref[:, c * width : (c + 1) * width], d_ref[c].reshape(dim, width), 1, 1)
        res_ref[...] = result
        block_ref[...] = result.astype(BF16)
        normed, _ = norm_parts(result)
        final = normed * norm_ref[4:5, :] + norm_ref[5:6, :]
        score = jnp.sum(final * norm_ref[6:7, :], axis=1, keepdims=True)
        score = jnp.broadcast_to(score, (block, 128)).T[0:1]
        slot = lax.broadcasted_iota(jnp.int32, (SLOTS, block), 0)
        member = (seg_ref[0, 0:1, :] - seq * IMG_SEQ == slot) & (slot < IMG_SEQ)
        top = jnp.max(jnp.where(member, score, MASK_FILL), axis=1, keepdims=True)
        e = jnp.exp(jnp.where(member, score - top, MASK_FILL))
        e = jnp.where(member, e, 0.0)
        total = jnp.sum(e, axis=1, keepdims=True)
        low = final.astype(BF16)
        high = e.astype(BF16)
        rest = (e - high.astype(F32)).astype(BF16)
        pool_ref[:, :dim] = dot(high, low, 1, 0) + dot(rest, low, 1, 0)
        lane = lax.broadcasted_iota(jnp.int32, (SLOTS, 128), 1)
        pool_ref[:, dim:] = jnp.where(lane == 0, top, jnp.where(lane == 1, total, 0.0))

    row = lambda c: pl.BlockSpec((block, c), lambda i, *_: (i, 0))
    return pl.pallas_call(
        kernel,
        grid_spec=pltpu.PrefetchScalarGridSpec(
            num_scalar_prefetch=1,
            grid=(seqs,),
            in_specs=[row(dim), row(hidden_size), pl.BlockSpec((1, 2, block), lambda i, ids_ref: (i, 0, ids_ref[1])), whole(params.shape)] + [ANY] * 4,
            out_specs=[row(dim), row(dim), pl.BlockSpec((SLOTS, dim + 128), lambda i, *_: (i, 0))],
            scratch_shapes=[pltpu.VMEM((n_mp, plan.groups // 2, 2, plan.block, width), BF16), pltpu.SemaphoreType.DMA((8,))],
        ),
        out_shape=[
            jax.ShapeDtypeStruct((rows, dim), F32),
            jax.ShapeDtypeStruct((rows, dim), BF16),
            jax.ShapeDtypeStruct((seqs * SLOTS, dim + 128), F32),
        ],
        compiler_params=PARAMS,
        cost_estimate=cost(2 * rows * dim * hidden_size, rows * hidden_size * 4),
        name="feed_down",
    )(ids, middle, active, seg_row, params, *down)


def classify(plan, pool, labels, images, cls, cls_across, class_count):
    slots, full = pool.shape
    dim = full - 128
    n_mp = plan.n_mp
    class_cols = cls.shape[1]
    wide = n_mp * class_cols

    part = slots // 2

    def combined(mine, other, lower, ref_rows):
        first, second = jnp.where(lower, mine, other), jnp.where(lower, other, mine)
        top_a, top_b = first[:, dim : dim + 1], second[:, dim : dim + 1]
        top = jnp.maximum(top_a, top_b)
        weight_a, weight_b = jnp.exp(top_a - top), jnp.exp(top_b - top)
        total = first[:, dim + 1 : dim + 2] * weight_a + second[:, dim + 1 : dim + 2] * weight_b
        ref_rows[:, :dim] = first[:, :dim] * weight_a + second[:, :dim] * weight_b
        lane = lax.broadcasted_iota(jnp.int32, (first.shape[0], 128), 1)
        ref_rows[:, dim:] = jnp.where(lane == 0, top, jnp.where(lane == 1, total, 0.0))

    def kernel(part_ref, label_ref, images_ref, c_in, c_across, grad_ref, stat_ref, loss_ref, cls_ref, c_ref, l_ref, pool_ref, got_ref, own_sems, send_sems, recv_sems):
        net = Sender(send_sems, recv_sems)
        me, mp = net.dp // plan.merge, net.mp
        side, core = mp // 2, mp % 2
        net.meet([("mp", 1), ("mp", 2)])
        first_copy = net.copy(part_ref, got_ref.at[0], "mp", 1)
        weights = [net.copy(a, c_ref.at[flip(mp, r)], "mp", 1) for a, r in ((c_in, 0), (c_across, 2))]
        own_copies = [pltpu.make_async_copy(a, c_ref.at[flip(mp, r)], own_sems.at[r // 2]) for a, r in ((c_in, 0), (c_across, 2))]
        start_all(own_copies)
        first_copy.wait_recv()
        combined(part_ref[...], got_ref[0], core == 0, pool_ref.at[0])
        own = pl.ds(pl.multiple_of(core * part, 8), part)
        net.copy(pool_ref.at[0, own], got_ref.at[1, pl.ds(0, part)], "mp", 2).wait_recv()
        combined(pool_ref[0, own, :], got_ref[1, 0:part, :], side == 0, pool_ref.at[1, own])
        net.copy(pool_ref.at[1, own], pool_ref.at[1, own], "mp", 1).wait_recv()
        for c in weights:
            c.wait_recv()
        wait_all(own_copies)
        net.finish()
        pool_ref = pool_ref.at[1]
        top = pool_ref[:, dim : dim + 1]
        total = pool_ref[:, dim + 1 : dim + 2]
        present = jnp.where(total > 0, 1.0, 0.0)
        safe = total + (1.0 - present)
        pooled = pool_ref[:, :dim] / safe
        low = pooled.astype(BF16)
        logits = jnp.concatenate([dot(low, c_ref[c], 1, 0) for c in range(n_mp)], axis=1)
        column = lax.broadcasted_iota(jnp.int32, (slots, wide), 1)
        logits = jnp.where(column % class_cols < class_count, logits, MASK_FILL)
        row_top = jnp.max(logits, axis=1, keepdims=True)
        log_total = row_top + jnp.log(jnp.sum(jnp.exp(logits - row_top), axis=1, keepdims=True))
        chosen = jnp.where(column == label_ref[...], 1.0, 0.0)
        label_logit = jnp.sum(chosen * logits, axis=1, keepdims=True)
        loss = jnp.sum(present * (log_total - label_logit), axis=0, keepdims=True)
        loss_ref[...] = jnp.broadcast_to(loss, loss_ref.shape)
        scale = present / images_ref[0:1, 0:1]
        grad = ((jnp.exp(logits - log_total) - chosen) * scale).astype(BF16)
        l_ref[...] = grad
        row_grad = sum(dot(grad[:, c * class_cols : (c + 1) * class_cols], c_ref[c], 1, 1) for c in range(n_mp)).astype(BF16)
        grad_ref[...] = row_grad
        inner = jnp.sum(row_grad.astype(F32) * pooled, axis=1, keepdims=True)
        lane = lax.broadcasted_iota(jnp.int32, (slots, 128), 1)
        stat_ref[...] = jnp.where(lane == 0, top, jnp.where(lane == 1, 1.0 / safe, jnp.where(lane == 2, inner, 0.0)))
        own = l_ref[:, pl.ds(pl.multiple_of(mp * class_cols, 128), class_cols)]
        grad_cls = dot(low, own, 0, 0)
        for g in range(plan.groups):
            at = (g % 2 + me % 2) % 2 * (plan.groups // 2) + g // 2
            cls_ref[at] = grad_cls[g * plan.block : (g + 1) * plan.block].astype(BF16)

    vmem = pl.BlockSpec(memory_space=pltpu.VMEM)
    return pl.pallas_call(
        kernel,
        in_specs=[vmem] * 3 + [ANY] * 2,
        out_specs=[vmem] * 4,
        out_shape=[
            jax.ShapeDtypeStruct((slots, dim), BF16),
            jax.ShapeDtypeStruct((slots, 128), F32),
            jax.ShapeDtypeStruct((8, 128), F32),
            jax.ShapeDtypeStruct((plan.groups, plan.block, class_cols), BF16),
        ],
        scratch_shapes=[
            pltpu.VMEM((n_mp,) + cls.shape, BF16),
            pltpu.VMEM((slots, wide), BF16),
            pltpu.VMEM((2, slots, full), F32),
            pltpu.VMEM((2, slots, full), F32),
            pltpu.SemaphoreType.DMA((2,)),
            pltpu.SemaphoreType.DMA((5,)),
            pltpu.SemaphoreType.DMA((5,)),
        ],
        compiler_params=pltpu.CompilerParams(vmem_limit_bytes=VMEM_LIMIT, collective_id=3, has_side_effects=True),
        cost_estimate=cost(6 * slots * dim * wide, dim * wide * 2),
        name="classify",
    )(pool, labels, images, cls, cls_across)


def split_three(values):
    high = values.astype(BF16)
    rest = values - high.astype(F32)
    middle = rest.astype(BF16)
    low = (rest - middle.astype(F32)).astype(BF16)
    return high, middle, low


def feed_back(plan, ids, result, middle, slope, row_grads, stats, seg_col, params, out_w, up, down, cols):
    rows, dim = result.shape
    n_mp = plan.n_mp
    width = up[0].shape[1]
    hidden_size = n_mp * width
    block = 256

    def kernel(ids_ref, res_ref, mid_ref, der_ref, pg_ref, stat_ref, seg_ref, norm_ref, o_ref, *refs):
        u_refs, d_parts, refs = refs[:n_mp], refs[n_mp : n_mp + 4], refs[n_mp + 4 :]
        rlow_ref, hlow_ref, mlow_ref, mgrad_ref, *refs = refs
        ag_refs, (sums_ref, d_ref, sems) = refs[:n_mp], refs[n_mp:]
        mp = ids_ref[1]
        seq = pl.program_id(0)
        copies = down_copies(plan, ids_ref, d_parts, d_ref, sems)

        @pl.when(seq == 0)
        def _():
            start_all(copies)
            sums_ref[...] = jnp.zeros_like(sums_ref)

        normed, scale = norm_parts(res_ref[...])
        gain, probe = norm_ref[4:5, :], norm_ref[6:7, :]
        final = normed * gain + norm_ref[5:6, :]
        score = jnp.sum(final * probe, axis=1, keepdims=True)
        slot = lax.broadcasted_iota(jnp.int32, (block, SLOTS), 1)
        member = (seg_ref[...] - seq * IMG_SEQ == slot) & (slot < IMG_SEQ)
        held = jnp.max(jnp.where(member, 1.0, 0.0), axis=1, keepdims=True)
        one = jnp.where(member, 1.0, 0.0).astype(BF16)
        row_stat = sum(dot(one, part, 1, 0) for part in split_three(stat_ref[...]))
        top, inverse, inner = row_stat[:, 0:1], row_stat[:, 1:2], row_stat[:, 2:3]
        share = jnp.exp(jnp.where(held > 0, score - top, 0.0)) * inverse * held
        row_grad = dot(one, pg_ref[...], 1, 0)
        share_low = share.astype(BF16).astype(F32)
        share_grad = jnp.sum(row_grad * final.astype(BF16).astype(F32), axis=1, keepdims=True)
        score_grad = share * (share_grad - inner)
        final_grad = share_low * row_grad + score_grad * probe
        add = lambda slot, value: sums_ref.at[slot].__setitem__(
            ..., sums_ref[slot] + jnp.sum(value.reshape(-1, 8, dim), axis=0)
        )
        add(4, score_grad * final)
        add(2, final_grad * normed)
        add(3, final_grad)
        result_grad = norm_back(final_grad, normed, scale, gain)
        result_low = result_grad.astype(BF16)
        rlow_ref[...] = result_low
        pl.when(seq == 0)(lambda: wait_all(copies))
        second = jnp.zeros((block, dim), F32)
        for c in range(n_mp):
            other = mp ^ RELATIVE[c]
            at = pl.ds(pl.multiple_of(other * width, 128), width)
            hidden_low = (der_ref[:, at] * dot(result_low, d_ref[other].reshape(dim, width), 1, 0)).astype(BF16)
            hlow_ref[:, at] = hidden_low
            second = second + dot(hidden_low, u_refs[c][...], 1, 1)
        normed_two, scale_two = norm_parts(mid_ref[...])
        add(0, second * normed_two)
        add(1, second)
        middle_grad = result_grad + norm_back(second, normed_two, scale_two, norm_ref[2:3, :])
        mgrad_ref[...] = middle_grad
        middle_low = middle_grad.astype(BF16)
        mlow_ref[...] = middle_low
        for r in range(n_mp):
            ag_refs[r][...] = dot(middle_low, o_ref[mp ^ r, :, :cols], 1, 0).astype(BF16)

    row = lambda c: pl.BlockSpec((block, c), lambda i, *_: (i, 0))
    shape = lambda c, t: jax.ShapeDtypeStruct((rows, c), t)
    slots = lambda c: pl.BlockSpec((SLOTS, c), lambda i, *_: (i, 0))
    own_row = pl.BlockSpec((block, 1), lambda i, ids_ref: (i * n_mp + ids_ref[1], 0))
    return pl.pallas_call(
        kernel,
        grid_spec=pltpu.PrefetchScalarGridSpec(
            num_scalar_prefetch=1,
            grid=(rows // block,),
            in_specs=[row(dim), row(dim), row(hidden_size), slots(dim), slots(128), own_row, whole(params.shape), whole(out_w.shape)]
            + [whole(up[0].shape)] * n_mp
            + [ANY] * 4,
            out_specs=[row(dim), row(hidden_size), row(dim), row(dim)] + [row(cols)] * n_mp + [whole((5, 8, dim))],
            scratch_shapes=[pltpu.VMEM((n_mp, plan.groups // 2, 2, plan.block, width), BF16), pltpu.SemaphoreType.DMA((8,))],
        ),
        out_shape=[shape(dim, BF16), shape(hidden_size, BF16), shape(dim, BF16), shape(dim, F32)]
        + [shape(cols, BF16)] * n_mp
        + [jax.ShapeDtypeStruct((5, 8, dim), F32)],
        compiler_params=PARAMS,
        cost_estimate=cost(2 * rows * dim * (2 * hidden_size + dim), rows * hidden_size * 8),
        name="feed_back",
    )(ids, result, middle, slope, row_grads, stats, seg_col, params, out_w, *up, *down)


def weight_grads(plan, pairs, out_pair, cls_blocks, sends, blocks):
    dim = pairs[0][0].shape[1]
    rows = pairs[0][0].shape[0]
    n_mp, size, merge = plan.n_mp, plan.block, plan.merge
    lines = plan.groups // 2
    width = pairs[0][1].shape[1] // n_mp
    cols = out_pair[1][0].shape[1]
    out_cols = -(-cols // 128) * 128
    inputs = [a for pair in pairs for a in pair] + [out_pair[0]] + list(out_pair[1]) + [cls_blocks] + list(blocks)
    n_load = len(inputs)
    widths = [width] * len(pairs) + [out_cols]
    n = len(widths)

    def kernel(*refs):
        sources, ag_in, refs = refs[:n_load], refs[n_load : n_load + n_mp - 1], refs[n_load + n_mp - 1 :]
        keep_out, send_out, cls_out, ag_out, refs = refs[:n], refs[n : 2 * n], refs[2 * n], refs[2 * n + 1 : 2 * n + n_mp], refs[2 * n + n_mp :]
        block_ref, refs = refs[0], refs[1:]
        targets, refs = refs[:n_load], refs[n_load:]
        send_buf, got_buf, own_buf, keep_buf, low_buf = (refs[i * n : (i + 1) * n] for i in range(5))
        cls_got, load_sems, store_sems, send_sems, recv_sems, block_sems = refs[5 * n :]
        loads = Loads(sources, targets, load_sems)
        net = Sender(send_sems, recv_sems)
        y = net.dp // merge % 2
        side, core = net.mp // 2, net.mp % 2
        net.meet([("mp", 1), ("mp", 2), ("mp", 3), ("dp", merge)])
        ag = [net.copy(a, b, "mp", r) for r, (a, b) in enumerate(zip(ag_in, ag_out), start=1)]
        places = [block_ref.at[:, flip(net.mp, r)] for r in (0, 2)]
        cls_ref = loads[n_load - 3]
        cls_copy = net.copy(cls_ref.at[1], cls_got, "dp", merge)
        stores = []

        def grad(number, other_side, other_core):
            if number < len(pairs):
                left, right = loads[2 * number], loads[2 * number + 1]
                at = flip(side, other_side) * 2 + flip(core, other_core)
                return dot(left[...], right[:, pl.ds(pl.multiple_of(at * width, 128), width)], 0, 0)
            left = loads[2 * len(pairs)]
            right = loads[2 * len(pairs) + 1 + other_side * 2 + other_core]
            value = dot(left[...], right[...], 0, 0)
            return jnp.concatenate([value, jnp.zeros((dim, out_cols - cols), F32)], axis=1) if out_cols != cols else value

        split = lambda value: value.reshape(lines, 2, size, value.shape[1])
        cores, block_copies, block_own = [], [], []
        for i in range(n):
            if i == 1:
                rows_in = [loads[n_load - 2], loads[n_load - 1]]
                block_copies += [net.copy(a, b, "mp", 1) for a, b in zip(rows_in, places)]
                block_own += [pltpu.make_async_copy(a, b, block_sems.at[j]) for j, (a, b) in enumerate(zip(rows_in, places))]
                start_all(block_own)
            for other_side in (0, 1):
                send_buf[i][flip(side, other_side)] = split(grad(i, other_side, 1).astype(BF16))
            cores.append(net.copy(send_buf[i], got_buf[i], "mp", 1))
            for other_side in (0, 1):
                own_buf[i][flip(side, other_side)] = split(grad(i, other_side, 0))
        for i in range(n):
            cores[i].wait_recv()
            if i == 0:
                keep_buf[i][...] = own_buf[i][side] + got_buf[i][side].astype(F32)
                low_buf[i][...] = (own_buf[i][1 - side] + got_buf[i][1 - side].astype(F32)).astype(BF16)
            else:
                for x in (0, 1):
                    keep_buf[i][x] = own_buf[i][x, :, y] + got_buf[i][x, :, y].astype(F32)
                    low_buf[i][x] = (own_buf[i][x, :, 1 - y] + got_buf[i][x, :, 1 - y].astype(F32)).astype(BF16)
            for a, b in ((low_buf[i], send_out[i]), (keep_buf[i], keep_out[i])):
                stores.append(pltpu.make_async_copy(a, b, store_sems.at[len(stores)]))
                stores[-1].start()
        cls_copy.wait_recv()
        cls_out[...] = cls_ref[0].astype(F32) + cls_got[...].astype(F32)
        for c in ag + block_copies:
            c.wait_recv()
        wait_all(block_own)
        net.finish()
        for c in stores:
            c.wait()

    shape = jax.ShapeDtypeStruct
    vmem = pl.BlockSpec(memory_space=pltpu.VMEM)
    full = [(2, lines, 2, size, w) for w in widths]
    half = [(lines, 2, size, widths[0])] + [(2, lines, size, w) for w in widths[1:]]
    n_sems = n + n_mp + 2
    seqs, share = blocks[0].shape[:2]
    out = pl.pallas_call(
        kernel,
        in_specs=[ANY] * (n_load + n_mp - 1),
        out_specs=[ANY] * (2 * n) + [vmem] + [ANY] * n_mp,
        out_shape=[shape(h, F32) for h in half]
        + [shape(h, BF16) for h in half]
        + [shape(cls_blocks.shape[1:], F32)]
        + [shape(a.shape, a.dtype) for a in sends]
        + [shape((seqs, n_mp, share, dim), BF16)],
        scratch_shapes=[pltpu.VMEM(a.shape, a.dtype) for a in inputs]
        + [pltpu.VMEM(f, BF16) for f in full]
        + [pltpu.VMEM(f, BF16) for f in full]
        + [pltpu.VMEM(f, F32) for f in full]
        + [pltpu.VMEM(h, F32) for h in half]
        + [pltpu.VMEM(h, BF16) for h in half]
        + [
            pltpu.VMEM(cls_blocks.shape[1:], BF16),
            pltpu.SemaphoreType.DMA((n_load,)),
            pltpu.SemaphoreType.DMA((2 * n,)),
            pltpu.SemaphoreType.DMA((n_sems,)),
            pltpu.SemaphoreType.DMA((n_sems,)),
            pltpu.SemaphoreType.DMA((2,)),
        ],
        compiler_params=pltpu.CompilerParams(vmem_limit_bytes=60 * 1024 * 1024, collective_id=2, has_side_effects=True),
        cost_estimate=cost(2 * rows * dim * n_mp * sum(widths), rows * width * n_mp * 8),
        name="grads",
    )(*inputs, *sends)
    return out[:n], out[n : 2 * n], out[2 * n], out[2 * n + 1 : 2 * n + n_mp], out[2 * n + n_mp].reshape(-1, dim)


def finish(plan, low, proj_grads, w, middle_grad, tokens, params, row_sums, gain_sums, loss, zx, yz, z_only):
    seqs = low.shape[0] // LEN
    dim = low.shape[1]
    cols = w.shape[2]
    n_mp = plan.n_mp
    share = LEN // n_mp
    lines, size, merge = plan.groups // 2, plan.block, plan.merge
    dp_bits = [1 << i for i in range(plan.n_dp.bit_length() - 1)]
    far = [2 * k * merge for k in range(1, lines)]
    partners = [("mp", 1), ("mp", 2)] + [("dp", b) for b in sorted(set(dp_bits + far + [merge]))]
    stages = [("mp", 1), ("mp", 2)] + [("dp", b) for b in dp_bits]
    inputs = [w] + list(proj_grads) + [a for pair in zx + yz for a in pair] + list(z_only)
    inputs += [low, middle_grad]
    smalls = [params, row_sums, loss, gain_sums]
    n_in = len(inputs)
    n_zx, n_yz, n_z = len(zx), len(yz), len(z_only)
    n_sems = (lines - 1) * (n_zx + n_yz + n_z + 1) + n_zx + n_yz + 1 + 4 * seqs + len(stages)
    n_out = 3 + n_zx + n_yz + n_z

    def kernel(*refs):
        sources, (norm_ref, row_sum_ref, loss_ref, gain_ref), refs = refs[:n_in], refs[n_in : n_in + 4], refs[n_in + 4 :]
        tokens_in, refs = refs[0], refs[1:]
        rows_ref, qkv_out, total_ref, *owned = refs[:n_out]
        zx_out, yz_out, z_out = owned[:n_zx], owned[n_zx : n_zx + n_yz], owned[n_zx + n_yz :]
        scratch = list(refs[n_out:])
        take = lambda n: [scratch.pop(0) for _ in range(n)]
        targets = take(n_in)
        t_keep, t_send, t_got, t_mine, x_send, x_got, acc, q_low, q_y, q_send, q_z, got_sums, load_sems, send_sems, recv_sems, x_ref = take(16)
        zx_low, zx_got, zx_send, zx_last = take(n_zx), take(n_zx), take(n_zx), take(n_zx)
        yz_low, yz_got, yz_send, yz_last = take(n_yz), take(n_yz), take(n_yz), take(n_yz)
        z_low, z_got = take(n_z), take(n_z)
        loads = Loads(sources, targets, load_sems)
        net = Sender(send_sems, recv_sems)
        copy = net.copy
        own_copies = own_rows(tokens_in, x_ref, share, n_mp, net.mp, load_sems, n_in)
        group = net.dp // merge
        z, y = group // 2, group % 2
        side, core = net.mp // 2, net.mp % 2
        net.meet(partners)
        others = range(1, lines)
        to_z = lambda src, dst, k: copy(src, dst, "dp", 2 * k * merge)
        pair_from = 4
        pair = lambda i: (loads[pair_from + 2 * i], loads[pair_from + 2 * i + 1])
        both = lambda a, b, *at: a[at].astype(F32) + b[at].astype(F32)
        z_from = pair_from + 2 * (n_zx + n_yz)
        y_copies, z_copies = [], []

        def over_y(i):
            a, b = pair(n_zx + i)
            for line in range(lines):
                yz_low[i][line] = both(a, b, line, 1 - y).astype(BF16)
            y_copies.append(copy(yz_low[i], yz_got[i], "dp", merge))

        def over_z(i):
            a, b = pair(i)
            for k in others:
                for s in (0, 1):
                    zx_low[i][k - 1, s] = both(a, b, s, flip(z, k)).astype(BF16)
                z_copies.append(to_z(zx_low[i].at[k - 1], zx_got[i].at[k - 1], k))

        def only_z(i):
            for k in others:
                z_low[i][k - 1] = loads[z_from + i][flip(z, k)].astype(BF16)
                z_copies.append(to_z(z_low[i].at[k - 1], z_got[i].at[k - 1], k))

        w_ref = loads[0]
        pg = [[loads[1 + p].at[pl.ds(s * LEN, LEN)] for p in range(3)] for s in range(seqs)]
        core_copies = []
        x_copies = []

        def over_x(s):
            core_copies[s].wait_recv()
            x_send[s] = (t_keep[s, 1].astype(F32) + t_got[s, 1].astype(F32)).astype(BF16)
            x_copies.append(copy(x_send.at[s], x_got.at[s], "mp", 2))
            t_mine[s] = t_keep[s, 0].astype(F32) + t_got[s, 0].astype(F32)

        for s in range(seqs):
            def terms(target, i, carry):
                to_other = i // 2
                row_side = side + i % 2 * (1 - 2 * side)
                row_core = core + (1 - to_other) * (1 - 2 * core)
                at = pl.ds(pl.multiple_of((row_side * 2 + row_core) * share, share), share)
                gq, gk, gv = (ref[at, :] for ref in pg[s])
                total = dot(gq, w_ref[0], 1, 1) + dot(gk, w_ref[1], 1, 1) + dot(gv, w_ref[2], 1, 1)
                target[s, i % 2] = total.astype(BF16)
                return carry

            lax.fori_loop(0, 2, functools.partial(terms, t_send), 0)
            core_copies.append(copy(t_send.at[s], t_got.at[s], "mp", 1))
            lax.fori_loop(2, 4, functools.partial(terms, t_keep), 0)
            if s == 0:
                over_x(0)
                over_z(0)
            elif s > 1:
                over_x(s - 1)
            if s == 1:
                for i in range(n_yz):
                    over_y(i)
                for i in range(1, n_zx):
                    over_z(i)
                for i in range(n_z):
                    only_z(i)
        if seqs > 1:
            over_x(seqs - 1)

        low_ref = loads[n_in - 2]
        for s in range(seqs):
            for p in range(3):
                part = dot(low_ref[s * LEN : (s + 1) * LEN, :], pg[s][p][...], 0, 0)
                acc[p] = part if s == 0 else acc[p] + part
        for p in range(3):
            q_low[p] = acc[p].reshape(lines, 2, size, cols).astype(BF16)
        y_copy = copy(q_low.at[:, :, 1 - y], q_y, "dp", merge)

        mid_ref = loads[n_in - 1]
        for c in own_copies:
            c.wait()
        total_ref[...] = jnp.zeros_like(total_ref)
        for n in range(5):
            total_ref[2 + n : 3 + n, :] = jnp.sum(row_sum_ref[n], axis=0, keepdims=True)
        for n in range(2):
            total_ref[8 + n : 9 + n, 0:cols] = jnp.sum(gain_ref[n], axis=0, keepdims=True)
        total_ref[10:11, 0:128] = loss_ref[0:1, :]
        row_copies = []
        q_copies = []
        for s in range(seqs):
            at = slice(s * share, (s + 1) * share)
            normed, scale = norm_parts(x_ref[at, :].astype(F32))
            x_copies[s].wait_recv()
            first = t_mine[s] + x_got[s].astype(F32)
            total_ref[0:1, :] += jnp.sum(first * normed, axis=0, keepdims=True)
            total_ref[1:2, :] += jnp.sum(first, axis=0, keepdims=True)
            rows_ref[0, s] = (mid_ref[at, :] + norm_back(first, normed, scale, norm_ref[0:1, :])).astype(BF16)
            row_copies.append(copy(rows_ref.at[0, s], rows_ref.at[1, s], "mp", 2))
            if s == 0:
                y_copy.wait_recv()
                for line in range(lines):
                    for p in range(3):
                        rows_at = pl.ds(pl.multiple_of((line * 2 + y) * size, 8), size)
                        q_send[line, p] = (acc[p, rows_at, :] + q_y[p, line].astype(F32)).astype(BF16)
                q_copies = [to_z(q_send.at[flip(z, k)], q_z.at[k - 1], k) for k in others]
            if s == min(1, seqs - 1):
                for i in range(n_yz):
                    a, b = pair(n_zx + i)
                    y_copies[i].wait_recv()
                    for k in others:
                        at_z = flip(z, k)
                        yz_send[i][k - 1] = (both(a, b, at_z, y) + yz_got[i][at_z].astype(F32)).astype(BF16)
                        z_copies.append(to_z(yz_send[i].at[k - 1], yz_last[i].at[k - 1], k))
        mate_copies, last_copies = [], []

        def zx_last_step(i):
            for c in z_copies[i * (lines - 1) : (i + 1) * (lines - 1)]:
                c.wait_recv()
            a, b = pair(i)
            other = both(a, b, 1 - side, z) + sum(zx_got[i][k - 1, 1 - side].astype(F32) for k in others)
            zx_send[i][...] = other.astype(BF16)
            last_copies.append(copy(zx_send[i], zx_last[i], "mp", 2))
            zx_out[i][...] = both(a, b, side, z) + sum(zx_got[i][k - 1, side].astype(F32) for k in others)

        def mate(n):
            row_copies[n].wait_recv()
            mate_copies.append(copy(rows_ref.at[pl.ds(0, 2), n], rows_ref.at[pl.ds(2, 2), n], "mp", 1))

        between = [functools.partial(zx_last_step, i) for i in range(n_zx)] + [functools.partial(mate, n) for n in range(seqs)]
        for n, (axis, bits) in enumerate(stages):
            count = 8 if axis == "mp" else 16
            stage = copy(total_ref.at[pl.ds(0, count)], got_sums.at[n, pl.ds(0, count)], axis, bits)
            net.started.pop()
            if between:
                between.pop(0)()
            stage.wait()
            total_ref[0:count, :] += got_sums[n, 0:count, :]
        for step in between:
            step()
        for c in z_copies[n_zx * (lines - 1) :]:
            c.wait_recv()
        for i in range(n_yz):
            a, b = pair(n_zx + i)
            own = both(a, b, z, y) + yz_got[i][z].astype(F32)
            yz_out[i][...] = own + sum(yz_last[i][k - 1].astype(F32) for k in others)
        for i in range(n_z):
            z_out[i][...] = loads[z_from + i][z] + sum(z_got[i][k - 1].astype(F32) for k in others)
        for c in q_copies:
            c.wait_recv()
        for p in range(3):
            rows_at = pl.ds(pl.multiple_of((z * 2 + y) * size, 8), size)
            own = acc[p, rows_at, :] + q_y[p, z].astype(F32)
            qkv_out[p] = own + sum(q_z[k - 1, p].astype(F32) for k in others)
        for i, c in enumerate(last_copies):
            c.wait_recv()
            zx_out[i][...] += zx_last[i][...].astype(F32)
        for c in mate_copies:
            c.wait_recv()
        net.finish()

    vmem = pl.BlockSpec(memory_space=pltpu.VMEM)
    shape = jax.ShapeDtypeStruct
    blk = (3, size, cols)
    piece = lambda a: a.shape[-2:]
    buf = lambda a, lead, t=BF16: pltpu.VMEM(tuple(lead) + piece(a), t)
    three = lines - 1
    scratch = [pltpu.VMEM(a.shape, a.dtype) for a in inputs]
    scratch += [
        pltpu.VMEM((seqs, 2, share, dim), BF16),
        pltpu.VMEM((seqs, 2, share, dim), BF16),
        pltpu.VMEM((seqs, 2, share, dim), BF16),
        pltpu.VMEM((seqs, share, dim), F32),
        pltpu.VMEM((seqs, share, dim), BF16),
        pltpu.VMEM((seqs, share, dim), BF16),
        pltpu.VMEM((3, dim, cols), F32),
        pltpu.VMEM((3, lines, 2, size, cols), BF16),
        pltpu.VMEM((3, lines, size, cols), BF16),
        pltpu.VMEM((lines,) + blk, BF16),
        pltpu.VMEM((three,) + blk, BF16),
        pltpu.VMEM((len(stages), 16, dim), F32),
        pltpu.SemaphoreType.DMA((n_in + seqs,)),
        pltpu.SemaphoreType.DMA((n_sems,)),
        pltpu.SemaphoreType.DMA((n_sems,)),
        pltpu.VMEM((seqs * share, dim), tokens.dtype),
    ]
    firsts, seconds = [a for a, _ in zx], [a for a, _ in yz]
    for lead in ((three, 2), (three, 2), (), ()):
        scratch += [buf(a, lead) for a in firsts]
    for lead in ((lines,), (lines,), (three,), (three,)):
        scratch += [buf(a, lead) for a in seconds]
    scratch += [buf(a, (three,)) for a in z_only] + [buf(a, (three,)) for a in z_only]
    out = pl.pallas_call(
        kernel,
        in_specs=[ANY] * n_in + [vmem] * len(smalls) + [ANY],
        out_specs=[vmem] * n_out,
        out_shape=[shape((4, seqs, share, dim), BF16), shape(blk, F32), shape((16, dim), F32)]
        + [shape(piece(a), F32) for a in firsts + seconds + list(z_only)],
        scratch_shapes=scratch,
        compiler_params=pltpu.CompilerParams(vmem_limit_bytes=60 * 1024 * 1024, collective_id=1, has_side_effects=True),
        cost_estimate=cost(12 * seqs * LEN * dim * cols, seqs * LEN * dim * 8),
        name="finish",
    )(*inputs, *smalls, tokens)
    return out[0], out[1], out[2], out[3:]


def adam_update(weight, moment_one, moment_two, gradient, step_rate, decay_rate):
    fresh_one = BETA_ONE * moment_one + (1.0 - BETA_ONE) * gradient
    fresh_two = BETA_TWO * moment_two + (1.0 - BETA_TWO) * gradient * gradient
    one_hat = fresh_one / (1.0 - BETA_ONE**STEP)
    two_hat = fresh_two / (1.0 - BETA_TWO**STEP)
    updated = weight - step_rate * (one_hat / (jnp.sqrt(two_hat) + ADAM_EPS) + decay_rate * weight)
    return (fresh_one, fresh_two, updated)


def update(plan, ids, parts, groups):
    n_mp, seqs, share, dim = parts.shape
    n = len(groups)
    arrays = [a for group in groups for a in group]

    def kernel(ids_ref, part_ref, *refs):
        sources, out_ref, results = refs[: 4 * n], refs[4 * n], refs[4 * n + 1 :]
        out_ref[...] = part_ref[...].astype(F32)

        @pl.when(pl.program_id(0) == 0)
        def _():
            for i in range(n):
                w_ref, m_ref, v_ref, g_ref = sources[4 * i : 4 * i + 4]
                columns = w_ref.shape[-1]
                grad = g_ref[...][..., :columns]
                fresh = adam_update(w_ref[...], m_ref[...], v_ref[...], grad, MATRIX_RATE, MATRIX_DECAY)
                for ref, value in zip(results[3 * i : 3 * i + 3], fresh):
                    ref[...] = value

    relative = lambda i: i % 2 * 2 + i // 2
    shapes = [jax.ShapeDtypeStruct(group[0].shape, F32) for group in groups for _ in range(3)]
    out = pl.pallas_call(
        kernel,
        grid_spec=pltpu.PrefetchScalarGridSpec(
            num_scalar_prefetch=1,
            grid=(n_mp,),
            in_specs=[pl.BlockSpec((None, seqs, share, dim), lambda i, *_: (i, 0, 0, 0))] + [whole(a.shape) for a in arrays],
            out_specs=[pl.BlockSpec((seqs, None, share, dim), lambda i, ids_ref: (0, ids_ref[1] ^ relative(i), 0, 0))]
            + [whole(a.shape) for a in shapes],
        ),
        out_shape=[jax.ShapeDtypeStruct((seqs, n_mp, share, dim), F32)] + shapes,
        compiler_params=PARAMS,
        cost_estimate=cost(0, seqs * n_mp * share * dim * 8),
        name="update",
    )(ids, parts, *arrays)
    return out[0].reshape(seqs * n_mp * share, dim), [out[1 + 3 * i : 4 + 3 * i] for i in range(n)]


def shards(
    tokens,
    seg_ids,
    labels,
    w_qkv,
    m_qkv,
    v_qkv,
    w_out,
    m_out,
    v_out,
    w_up,
    m_up,
    v_up,
    w_down,
    m_down,
    v_down,
    w_cls,
    m_cls,
    v_cls,
    norm_params,
    m_norm,
    v_norm,
    qk_gain,
    m_qk,
    v_qk,
    *,
    n_dp,
    n_mp,
):
    dp, mp = lax.axis_index("dp"), lax.axis_index("mp")
    group_rows, dim = tokens.shape
    plan = Plan(n_dp, n_mp, dim)
    seqs = group_rows // LEN
    share = LEN // n_mp
    rows = seqs * share
    cols = w_qkv.shape[2]
    classes = w_cls.shape[1]
    class_cols = -(-classes // 128) * 128
    out_cols = -(-cols // 128) * 128
    ids = jnp.stack([dp // plan.merge, mp]).astype(jnp.int32)

    new_image = seg_ids != jnp.concatenate([jnp.full((1,), -1, jnp.int32), seg_ids[:-1]])
    count = jnp.sum((new_image & (seg_ids != PAD_ID)).astype(F32))
    dim_part, head_part = norm_params.shape[1], qk_gain.shape[2]
    pad = lambda a, r, c: jnp.pad(a, ((0, r - a.shape[0]), (0, c - a.shape[1])))
    low_param = lambda a: lax.reduce_precision(a, 8, 7)
    small = jnp.concatenate(
        [
            pad(low_param(norm_params), 8, 128),
            pad(low_param(qk_gain).reshape(2, cols // HEAD * head_part), 8, 128),
            pad(count.reshape(1, 1), 8, 128),
        ]
    )
    low = lambda a: a if plan.merge == 1 else a.astype(BF16)
    qkv_block = plan.merged(low(w_qkv), 1)
    up_block = plan.merged(low(w_up), 0)
    down_block = plan.merged(w_down.T.astype(BF16), 0)
    out_block = plan.merged(pad(w_out.T.astype(BF16), dim_part, out_cols), 0)
    cls_block = plan.merged(low(w_cls), 0)
    small_block = plan.merged(small[None], 0)

    tied = lambda value, tie: lax.optimization_barrier((value, tie))[0]

    head_of = jnp.arange(cols) // HEAD
    ones = jnp.where(head_of[:, None] == head_of[None, :], 1.0 / HEAD, 0.0).astype(BF16)
    starts, widths, live = key_windows(seg_ids)
    seg_col = seg_ids.reshape(group_rows, 1)
    seg_row = seg_ids.reshape(-1, LEN)
    seg_row = jnp.stack([seg_row, jnp.roll(seg_row, -ALIGN, axis=1)], axis=1)
    normed_low, pq, pk, q, k, v, w, up, down, out_w, cls, params, gains, images = gather_project(
        plan, tokens, qkv_block, up_block, down_block, out_block, cls_block, small_block, ones
    )
    w = w.reshape(3, dim, cols)
    out_w = out_w.reshape(n_mp, dim, out_cols)
    up = up.reshape(dim, up.shape[-1])
    up_across, down_across = plan.swap(up, "mp", 2), plan.group_swap(down, 1)
    cls = cls.reshape(dim, class_cols)
    image_total = images[0, 0]
    *attended, logs = attend(plan, ids, starts, widths, q, k, v, seg_col, seg_row)

    (middle, second_low, active, slope), attended, up_mates, down_mates = feed_up(
        plan, tokens, attended, params, out_w, up, up_across, down, down_across
    )
    cls_across = plan.swap(tied(cls, middle), "mp", 2)
    up = [up, up_across, *up_mates]
    down = [down, down_across, *down_mates]
    result, block_rows, pool = feed_down(plan, ids, middle, active, seg_row, params, down)

    block_rows = block_rows.reshape(seqs, share, dim)
    slot_label = labels.reshape(seqs, IMG_SEQ)
    slot_label = slot_label // classes * class_cols + slot_label % classes
    slot_label = jnp.pad(slot_label, ((0, 0), (0, SLOTS - IMG_SEQ)), constant_values=-1).reshape(seqs * SLOTS, 1)
    row_grads, stats, loss, cls_blocks = classify(plan, pool, slot_label, images, cls, cls_across, classes)

    block_rows = lax.optimization_barrier((block_rows, stats))[0]
    block_across = plan.swap(block_rows, "mp", 2)

    result_low, hidden_low, middle_low, middle_grad, *rest = feed_back(
        plan, ids, result, middle, slope, row_grads, stats, seg_col, params, out_w, up, down, cols
    )
    attended_grads, sums = rest[:n_mp], rest[n_mp]
    cls_blocks = cls_blocks.reshape(2, plan.groups // 2, plan.block, class_cols)
    kept, sent, cls_sum, arrived, block_out = weight_grads(
        plan,
        [(result_low, active), (second_low, hidden_low)],
        (middle_low, attended),
        cls_blocks,
        attended_grads[1:],
        (block_rows, block_across),
    )
    grad_parts = [attended_grads[0]] + list(arrived)
    got = [plan.swap(sent[0], "mp", 2)] + [plan.group_swap(part, 1) for part in sent[1:]]

    *proj_grads, gain_sums = attend_back(
        plan, ids, starts, widths, live, q, k, v, pq, pk, gains, ones, grad_parts, logs, seg_col, seg_row
    )
    *got, _ = lax.optimization_barrier((*got, proj_grads[0]))

    down_pair, up_pair, out_pair = zip(kept, got)
    last_rows, grad_qkv, small_grads, owned = finish(
        plan, normed_low, proj_grads, w, middle_grad, tokens, params, sums, gain_sums, loss, [up_pair, out_pair], [down_pair], [cls_sum]
    )
    mean_loss = small_grads[10, 0] / image_total
    grad_qkv = plan.unmerged(grad_qkv, 1)
    grad_up, grad_out, grad_down, grad_cls = (plan.unmerged(a, 0) for a in owned)
    matrices = [
        (w_qkv, m_qkv, v_qkv, grad_qkv),
        (w_out, m_out, v_out, grad_out[:, :cols].T),
        (w_up, m_up, v_up, grad_up),
        (w_down.T, m_down.T, v_down.T, grad_down),
        (w_cls, m_cls, v_cls, grad_cls),
    ]
    input_grad, fresh = update(plan, ids, last_rows, matrices)
    norm_part = lax.dynamic_slice(small_grads, (0, dp * dim_part), (7, dim_part))
    qk_part = lax.dynamic_slice_in_dim(small_grads[8:10, :cols].reshape(2, cols // HEAD, HEAD), dp * head_part, head_part, 2)
    fresh[3] = [a.T for a in fresh[3]]
    outputs = [block_out, input_grad, mean_loss] + [a for group in fresh for a in group]
    one, two, new = adam_update(norm_params, m_norm, v_norm, norm_part, GAIN_RATE, 0.0)
    outputs += [one, two[:6], two[6], new]
    outputs += list(adam_update(qk_gain, m_qk, v_qk, qk_part, GAIN_RATE, 0.0))
    return tuple(outputs)


def solution(mesh):
    rows_cols = (P("mp", "dp"),) * 3
    cols_rows = (P("dp", "mp"),) * 3
    qkv_spec = (P(None, "dp", "mp"),) * 3
    qk_spec = (P(None, "mp", "dp"),) * 3
    norm_spec = P(None, "dp")
    in_specs = (
        (P("dp", None), P("dp"), P("dp")) + qkv_spec + rows_cols + cols_rows + rows_cols + cols_rows + (norm_spec,) * 3 + qk_spec
    )
    out_specs = (
        (P("dp", None), P("dp", None), P())
        + qkv_spec
        + rows_cols
        + cols_rows
        + rows_cols
        + cols_rows
        + (norm_spec, norm_spec, P("dp"), norm_spec)
        + qk_spec
    )
    body = functools.partial(shards, n_dp=mesh.shape["dp"], n_mp=mesh.shape["mp"])
    return jax.shard_map(body, mesh=mesh, in_specs=in_specs, out_specs=out_specs, check_vma=False)
```

```python
import functools

import jax
import jax.numpy as jnp
from jax import lax
from jax.experimental import pallas as pl
from jax.experimental.pallas import tpu as pltpu
from jax.sharding import PartitionSpec as P

LEN = 1024
STEP = 10
SEQ_DEV = 3
IMG_DEV = 180
PAD_ID = 180

NORM_EPS = 1e-06
MASK_FILL = -1000000000.0
BETA_ONE = 0.9
BETA_TWO = 0.999
ADAM_EPS = 1e-08
MATRIX_RATE = 0.1
MATRIX_DECAY = 0.1
GAIN_RATE = 0.8

HEAD = 64
QB = 256
QBLOCKS = LEN // QB
WINDOWS = (384, 512, 768, 1024)
ALIGN = 64
LANES = 128
F32 = jnp.float32
BF16 = jnp.bfloat16
VMEM_LIMIT = 56 * 1024 * 1024
IMG_SEQ = 60
SLOTS = 64
ANY = pl.BlockSpec(memory_space=pl.ANY)
PARAMS = pltpu.CompilerParams(vmem_limit_bytes=VMEM_LIMIT)


def dot(a, b, ca, cb):
    return lax.dot_general(a, b, (((ca,), (cb,)), ((), ())), preferred_element_type=F32)


def head_mean(values, ones_block):
    high = values.astype(BF16)
    rest = (values - high.astype(F32)).astype(BF16)
    return dot(high, ones_block, 1, 0) + dot(rest, ones_block, 1, 0)


def norm_parts(values):
    centre = values - jnp.mean(values, axis=-1, keepdims=True)
    spread = jnp.mean(centre * centre, axis=-1, keepdims=True)
    scale = lax.rsqrt(spread + NORM_EPS)
    return centre * scale, scale


def norm_back(grad, normed, scale, gain):
    scaled = grad * gain
    first = jnp.mean(scaled, axis=-1, keepdims=True)
    second = jnp.mean(scaled * normed, axis=-1, keepdims=True)
    return (scaled - first - normed * second) * scale


def head_parts(values, ones_block):
    centre = values - head_mean(values, ones_block)
    scale = lax.rsqrt(head_mean(centre * centre, ones_block) + NORM_EPS)
    return centre * scale, scale


def cost(flops, read, exps=0):
    return pl.CostEstimate(flops=int(flops), bytes_accessed=int(read), transcendentals=int(exps))


def whole(shape):
    return pl.BlockSpec(tuple(shape), lambda *_: (0,) * len(shape))


class Plan:
    def __init__(self, n_dp, n_mp, dim):
        self.n_dp, self.n_mp = n_dp, n_mp
        self.merge = 1 if dim // n_dp % 16 == 0 else 2
        self.groups = n_dp // self.merge
        self.block = dim // self.groups
        self.far = [2 * k for k in range(1, self.groups // 2)]

    def swap(self, value, axis, bits):
        size = self.n_dp if axis == "dp" else self.n_mp
        return lax.ppermute(value, axis, [(i, i ^ bits) for i in range(size)])

    def group_swap(self, value, bits):
        return self.swap(value, "dp", bits * self.merge)

    def merged(self, value, dim):
        if self.merge == 1:
            return value
        other = self.swap(value, "dp", 1)
        even = lax.axis_index("dp") % 2 == 0
        first, second = jnp.where(even, value, other), jnp.where(even, other, value)
        return jnp.concatenate([first, second], axis=dim)

    def unmerged(self, value, dim):
        if self.merge == 1:
            return value
        half = value.shape[dim] // 2
        me = lax.axis_index("dp") % 2
        mine = lax.dynamic_slice_in_dim(value, me * half, half, dim)
        theirs = lax.dynamic_slice_in_dim(value, (1 - me) * half, half, dim)
        return mine + self.swap(theirs, "dp", 1)

    def total(self, value, axis):
        size = self.n_dp if axis == "dp" else self.n_mp
        bits = 1
        while bits < size:
            value = value + self.swap(value, axis, bits)
            bits *= 2
        return value


MESH = pl.DeviceIdType.MESH


def flip(index, bits):
    bit = 1
    while bit <= bits:
        if bits & bit:
            index = index + bit * (1 - 2 * (index // bit % 2))
        bit *= 2
    return index


class Chain:
    def __init__(self, region, order, lines):
        self.region, self.steps = region, order
        self.copies = sum({"z": lines - 1, "c": 2}.get(step, 1) for step in order)


class Gatherer:
    def __init__(self, plan, send_sems, recv_sems):
        self.plan, self.send_sems, self.recv_sems = plan, send_sems, recv_sems
        self.dp, self.mp = lax.axis_index("dp"), lax.axis_index("mp")
        self.pair = self.dp % plan.merge
        group = self.dp // plan.merge
        self.z, self.y = group // 2, group % 2
        self.x, self.core = self.mp // 2, self.mp % 2
        self.lines = plan.groups // 2
        self.used = 0
        self.pending = []

    def device(self, z, y, x, core):
        return ((z * 2 + y) * self.plan.merge + self.pair, x * 2 + core)

    def here(self):
        return self.z, self.y, self.x, self.core

    def meet(self, barrier):
        z, y, x, core = self.here()
        others = [(z, 1 - y, x, core), (z, y, 1 - x, core), (z, y, x, 1 - core)]
        others += [(flip(z, k), y, x, core) for k in range(1, self.lines)]
        for other in others:
            pl.semaphore_signal(barrier, inc=1, device_id=self.device(*other), device_id_type=MESH)
        pl.semaphore_wait(barrier, len(others))

    def start(self, chain, number, source=None):
        step, done = chain.steps[number], chain.steps[:number]
        z, y, x, core = self.here()
        spot = dict(z=None if "z" in done else z, y=None if "y" in done else y, x=None if "x" in done else x, core=core)
        if step == "z":
            copies = [(spot, (flip(z, k), y, x, core)) for k in range(1, self.lines)]
        elif step == "c":
            copies = [({**spot, "x": side}, (z, y, x, 1 - core)) for side in (0, 1)]
        else:
            copies = [(spot, dict(y=(z, 1 - y, x, core), x=(z, y, 1 - x, core))[step])]
        started = []
        for place, other in copies:
            region = chain.region(**place)
            out = pltpu.make_async_remote_copy(
                src_ref=region if source is None else source,
                dst_ref=region,
                send_sem=self.send_sems.at[self.used],
                recv_sem=self.recv_sems.at[self.used],
                device_id=self.device(*other),
                device_id_type=MESH,
            )
            self.used += 1
            out.start()
            started.append(out)
        self.pending += started
        return started

    @staticmethod
    def arrive(copies):
        for out in copies:
            out.wait_recv()

    def finish(self):
        for out in self.pending:
            out.wait_send()


class Loads:
    def __init__(self, sources, targets, sems):
        self.targets = targets
        self.copies = [pltpu.make_async_copy(a, b, sems.at[i]) for i, (a, b) in enumerate(zip(sources, targets))]
        self.done = [False] * len(self.copies)
        for c in self.copies:
            c.start()

    def __getitem__(self, i):
        if not self.done[i]:
            self.copies[i].wait()
            self.done[i] = True
        return self.targets[i]


class Sender:
    def __init__(self, send_sems, recv_sems):
        self.dp, self.mp = lax.axis_index("dp"), lax.axis_index("mp")
        self.send_sems, self.recv_sems = send_sems, recv_sems
        self.started, self.used = [], 0

    def device(self, axis, bits):
        return (flip(self.dp, bits), self.mp) if axis == "dp" else (self.dp, flip(self.mp, bits))

    def meet(self, partners):
        barrier = pltpu.get_barrier_semaphore()
        for axis, bits in partners:
            pl.semaphore_signal(barrier, inc=1, device_id=self.device(axis, bits), device_id_type=MESH)
        pl.semaphore_wait(barrier, len(partners))

    def copy(self, src, dst, axis, bits):
        n = self.used
        self.used += 1
        c = pltpu.make_async_remote_copy(
            src_ref=src,
            dst_ref=dst,
            send_sem=self.send_sems.at[n],
            recv_sem=self.recv_sems.at[n],
            device_id=self.device(axis, bits),
            device_id_type=MESH,
        )
        self.started.append(c)
        c.start()
        return c

    def finish(self):
        for c in self.started:
            c.wait_send()


def gather_project(plan, tokens, qkv_block, up_block, down_block, out_block, cls_block, small_block, ones):
    rows, dim = tokens.shape
    cols = ones.shape[0]
    n_mp, merge, size = plan.n_mp, plan.merge, plan.block
    lines = plan.groups // 2
    width = up_block.shape[1]
    out_cols, classes = out_block.shape[1], cls_block.shape[1]
    class_cols = -(-classes // 128) * 128
    block = 512
    blocks = rows // block
    dim_part = dim // plan.n_dp
    head_part = HEAD // plan.n_dp

    orders = [("small", "zy"), ("w_qk", "zy"), ("w_v", "zy"), ("out", "zyxc"), ("cls", "zy"), ("up", "zy"), ("down", "zx")]
    sizes = {name: Chain(None, order, lines).copies for name, order in orders}
    n_sems = sum(sizes.values())

    def kernel(x_ref, qkv_wide, up_wide, down_in, out_in, cls_wide, small_in, ones_ref, *refs):
        low_ref, pq_ref, pk_ref, q_ref, k_ref, v_ref, w_ref, up_ref, down_ref, o_ref, c_ref, norm_ref, gain_ref, image_ref = refs[:14]
        w_buf, small_buf, low_buf, pq_buf, pk_buf, q_buf, k_buf, v_buf, send_sems, recv_sems, own_sems, out_sems, *lows = refs[14:]
        qkv_in, up_in, cls_in = lows
        qkv_in[...] = qkv_wide[...].astype(BF16)
        up_in[...] = up_wide[...].astype(BF16)
        cls_in[...] = jnp.concatenate([cls_wide[...].astype(BF16), jnp.zeros((size, class_cols - classes), BF16)], axis=1)
        g = Gatherer(plan, send_sems, recv_sems)
        z, y, x, core = g.here()
        everything = slice(None)

        def at(v):
            return everything if v is None else v

        def wide(ref, first, count):
            columns = pl.ds(first, count)
            return lambda z, y, x, core: ref.at[at(x), core, at(z), at(y), :, columns]

        regions = dict(
            w_qk=lambda z, y, x, core: w_buf.at[pl.ds(0, 2), at(z), at(y)],
            w_v=lambda z, y, x, core: w_buf.at[pl.ds(2, 1), at(z), at(y)],
            small=lambda z, y, x, core: small_buf.at[at(z), at(y)],
            up=lambda z, y, x, core: up_ref.at[at(z), at(y)],
            down=lambda z, y, x, core: down_ref.at[at(x), at(z)],
            out=wide(o_ref, 0, out_cols),
            cls=lambda z, y, x, core: c_ref.at[at(z), at(y)],
        )
        chains = {name: Chain(regions[name], order, lines) for name, order in orders}
        sources = dict(
            w_qk=qkv_in.at[pl.ds(0, 2)],
            w_v=qkv_in.at[pl.ds(2, 1)],
            small=small_in,
            up=up_in,
            down=down_in,
            out=out_in,
            cls=cls_in,
        )
        own = {}
        for i, (name, _) in enumerate(orders):
            own[name] = pltpu.make_async_copy(sources[name], regions[name](z, y, x, core), own_sems.at[i])
            own[name].start()
        live, reached = {}, {}

        def begin(name):
            live[name] = g.start(chains[name], 0, source=sources[name])
            reached[name] = 0

        def advance(*names):
            for name in names:
                if reached[name] == len(chains[name].steps):
                    continue
                if reached[name] == 0:
                    own[name].wait()
                g.arrive(live[name])
                reached[name] += 1
                if reached[name] < len(chains[name].steps):
                    live[name] = g.start(chains[name], reached[name])

        g.meet(pltpu.get_barrier_semaphore())
        for name in ("small", "w_qk", "w_v", "out", "cls"):
            begin(name)
        advance("small", "small")

        lane = lax.broadcasted_iota(jnp.int32, (128, dim), 0)
        column = lax.broadcasted_iota(jnp.int32, (128, dim), 1)
        head_lane = lax.broadcasted_iota(jnp.int32, (128, cols), 0)
        head_column = lax.broadcasted_iota(jnp.int32, (128, cols), 1)
        norm = jnp.zeros((8, dim), F32)
        gain = jnp.zeros((8, cols), F32)
        image = jnp.zeros((8, 128), F32)
        for d in range(plan.n_dp):
            part = small_buf[d // merge // 2, d // merge % 2, d % merge]
            spread = jnp.where((column == d * dim_part + lane) & (lane < dim_part), 1.0, 0.0).astype(BF16)
            norm = norm + dot(part[0:8].astype(BF16), spread, 1, 0)
            same = (head_column // HEAD == head_lane // head_part) & (head_column % HEAD == d * head_part + head_lane % head_part)
            gain = gain + dot(part[8:16].astype(BF16), jnp.where(same, 1.0, 0.0).astype(BF16), 1, 0)
            image = image + part[16:24]
        norm_ref[...] = norm
        gain_ref[...] = gain
        image_ref[...] = image

        def first_norm(i, carry):
            at_rows = pl.ds(pl.multiple_of(i * block, block), block)
            normed, _ = norm_parts(x_ref[at_rows, :].astype(F32))
            low_buf[at_rows, :] = (normed * norm[0:1, :] + norm[1:2, :]).astype(BF16)
            return carry

        third = blocks // 3
        lax.fori_loop(0, third, first_norm, 0)
        advance("w_qk", "w_v")
        begin("up")
        begin("down")
        lax.fori_loop(third, blocks, first_norm, 0)
        outs = [pltpu.make_async_copy(low_buf, low_ref, out_sems.at[0])]
        outs[0].start()
        advance("out", "cls", "w_qk", "w_v")
        outs.append(pltpu.make_async_copy(w_buf, w_ref, out_sems.at[1]))
        outs[1].start()

        def project(i, carry):
            at_rows = pl.ds(pl.multiple_of(i * block, block), block)
            low = low_buf[at_rows, :]
            pq = dot(low, w_buf[0].reshape(dim, cols), 1, 0)
            pk = dot(low, w_buf[1].reshape(dim, cols), 1, 0)
            pq_buf[at_rows, :] = pq
            pk_buf[at_rows, :] = pk
            v_buf[at_rows, :] = dot(low, w_buf[2].reshape(dim, cols), 1, 0).astype(BF16)
            nq, _ = head_parts(pq, ones_ref[...])
            nk, _ = head_parts(pk, ones_ref[...])
            q_buf[at_rows, :] = (nq * gain[0:1, :]).astype(BF16)
            k_buf[at_rows, :] = (nk * gain[1:2, :]).astype(BF16)
            return carry

        lax.fori_loop(0, third, project, 0)
        advance("out", "up", "down")
        lax.fori_loop(third, 2 * third, project, 0)
        lax.fori_loop(2 * third, blocks, project, 0)
        pairs = ((pq_buf, pq_ref), (pk_buf, pk_ref), (q_buf, q_ref), (k_buf, k_ref), (v_buf, v_ref))
        for i, (a, b) in enumerate(pairs):
            outs.append(pltpu.make_async_copy(a, b, out_sems.at[2 + i]))
            outs[-1].start()
        advance("out", "cls", "up", "down", "out")
        g.finish()
        for c in outs:
            c.wait()

    vmem = pl.BlockSpec(memory_space=pltpu.VMEM)
    shape = jax.ShapeDtypeStruct
    wide_shape = lambda c: (n_mp // 2, 2, lines, 2, size, c)
    n_rows = lambda c, t: shape((rows, c), t)
    return pl.pallas_call(
        kernel,
        in_specs=[vmem, vmem, vmem, ANY, ANY, vmem, ANY, vmem],
        out_specs=[ANY] * 11 + [vmem] * 3,
        out_shape=[n_rows(dim, BF16), n_rows(cols, F32), n_rows(cols, F32), n_rows(cols, BF16), n_rows(cols, BF16), n_rows(cols, BF16)]
        + [
            shape((3, lines, 2, size, cols), BF16),
            shape((lines, 2, size, width), BF16),
            shape((n_mp // 2, lines, size, width), BF16),
            shape(wide_shape(out_cols), BF16),
            shape((lines, 2, size, class_cols), BF16),
            shape((8, dim), F32),
            shape((8, cols), F32),
            shape((8, 128), F32),
        ],
        scratch_shapes=[
            pltpu.VMEM((3, lines, 2, size, cols), BF16),
            pltpu.VMEM((lines, 2, merge, 24, 128), F32),
            pltpu.VMEM((rows, dim), BF16),
            pltpu.VMEM((rows, cols), F32),
            pltpu.VMEM((rows, cols), F32),
            pltpu.VMEM((rows, cols), BF16),
            pltpu.VMEM((rows, cols), BF16),
            pltpu.VMEM((rows, cols), BF16),
            pltpu.SemaphoreType.DMA((n_sems,)),
            pltpu.SemaphoreType.DMA((n_sems,)),
            pltpu.SemaphoreType.DMA((len(orders),)),
            pltpu.SemaphoreType.DMA((7,)),
            pltpu.VMEM(qkv_block.shape, BF16),
            pltpu.VMEM(up_block.shape, BF16),
            pltpu.VMEM((size, class_cols), BF16),
        ],
        compiler_params=pltpu.CompilerParams(vmem_limit_bytes=VMEM_LIMIT, collective_id=0, has_side_effects=True),
        cost_estimate=cost(6 * rows * dim * cols, rows * dim * 8),
        name="gather_project",
    )(tokens, qkv_block, up_block, down_block, out_block, cls_block, small_block, ones)


def head_masks(cols):
    lane = lax.broadcasted_iota(jnp.int32, (1, cols), 1)
    return [(lane >= h * HEAD) & (lane < (h + 1) * HEAD) for h in range(cols // HEAD)]


def spread_heads(block, masks):
    zero = jnp.zeros_like(block)
    return jnp.concatenate([jnp.where(m, block, zero) for m in masks], axis=0)


def join_heads(stacked, masks):
    total = stacked[0:QB]
    for h in range(1, len(masks)):
        total = jnp.where(masks[h], stacked[h * QB : (h + 1) * QB], total)
    return total


def by_window(width_ref, step, body):
    width = width_ref[step]
    for number, window in enumerate(WINDOWS):
        pl.when(width == number)(functools.partial(body, window))


def key_segments(row_ref, start, window):
    at = pl.ds(pl.multiple_of(start // LANES * LANES, LANES), window)
    return jnp.where(start % LANES == 0, row_ref[0, 0:1, at], row_ref[0, 1:2, at])


def attend(plan, ids, starts, widths, q, k, v, seg_col, seg_row):
    rows, cols = q.shape
    n_mp = plan.n_mp
    share = LEN // n_mp
    per = share // QB
    seqs = rows // LEN

    def kernel(ids_ref, start_ref, width_ref, q_ref, k_ref, v_ref, col_ref, row_ref, *outs):
        out_refs, log_ref = outs[:n_mp], outs[n_mp]
        seq, block = pl.program_id(0), pl.program_id(1)
        step = seq * QBLOCKS + block
        masks = head_masks(cols)
        heads = len(masks)

        def body(window):
            start = pl.multiple_of(start_ref[step], ALIGN)
            keys = k_ref[pl.ds(start, window), :]
            values = v_ref[pl.ds(start, window), :]
            q3 = spread_heads(q_ref[...], masks)
            s = (dot(q3, keys, 1, 1) * HEAD**-0.5).reshape(heads, QB, window)
            same = col_ref[...] == key_segments(row_ref, start, window)
            s = jnp.where(same[None], s, MASK_FILL)
            top = jnp.max(s, axis=-1, keepdims=True)
            e = jnp.exp(s - top)
            total = jnp.sum(e, axis=-1, keepdims=True)
            p = (e * (1.0 / total)).astype(BF16).reshape(heads * QB, window)
            out = join_heads(dot(p, values, 1, 0), masks).astype(BF16)
            other = (block // per) ^ ids_ref[1]
            at = pl.ds(pl.multiple_of(seq * share + block % per * QB, QB), QB)
            for r in range(n_mp):

                @pl.when(other == r)
                def _():
                    out_refs[r][at, :] = out

            log = top + jnp.log(total)
            lane = lax.broadcasted_iota(jnp.int32, (QB, 128), 1)
            logs = jnp.zeros((QB, 128), F32)
            for h in range(heads):
                logs = jnp.where(lane == h, log[h], logs)
            log_ref[...] = logs

        by_window(width_ref, step, body)

    block = lambda c: pl.BlockSpec((QB, c), lambda s, b, *_: (s * QBLOCKS + b, 0))
    all_keys = lambda c: pl.BlockSpec((LEN, c), lambda s, b, *_: (s, 0))
    return pl.pallas_call(
        kernel,
        grid_spec=pltpu.PrefetchScalarGridSpec(
            num_scalar_prefetch=3,
            grid=(seqs, QBLOCKS),
            in_specs=[block(cols), all_keys(cols), all_keys(cols), block(1), pl.BlockSpec((1, 2, LEN), lambda s, b, *_: (s, 0, 0))],
            out_specs=[whole((seqs * share, cols))] * n_mp + [block(128)],
        ),
        out_shape=[jax.ShapeDtypeStruct((seqs * share, cols), BF16)] * n_mp + [jax.ShapeDtypeStruct((rows, 128), F32)],
        compiler_params=PARAMS,
        cost_estimate=cost(60 * rows * LEN * cols, rows * cols * 8, rows * LEN),
        name="attend",
    )(ids, starts, widths, q, k, v, seg_col, seg_row)


def attend_back(plan, ids, starts, widths, live, q, k, v, pq, pk, gains, ones, grads, logs, seg_col, seg_row):
    rows, cols = q.shape
    n_mp = plan.n_mp
    share = LEN // n_mp
    per = share // QB

    def kernel(ids_ref, start_ref, width_ref, live_ref, q_ref, k_ref, v_ref, pq_ref, pk_ref, gain_ref, ones_ref, col_ref, row_ref, log_ref, *refs):
        grad_refs, (gq_ref, gk_ref, gv_ref, sum_ref, dk_ref, dv_ref) = refs[:n_mp], refs[n_mp:]
        seq, block = pl.program_id(0), pl.program_id(1)
        step = seq * QBLOCKS + block
        masks = head_masks(cols)
        heads = len(masks)

        @pl.when(block == 0)
        def _():
            dk_ref[...] = jnp.zeros_like(dk_ref)
            dv_ref[...] = jnp.zeros_like(dv_ref)

        @pl.when(step == 0)
        def _():
            sum_ref[...] = jnp.zeros_like(sum_ref)

        def back(values, grad, slot):
            ones_block = ones_ref[...]
            normed, scale = head_parts(values, ones_block)
            sum_ref[slot] += jnp.sum((grad * normed).reshape(-1, 8, cols), axis=0)
            scaled = grad * gain_ref[slot : slot + 1, :]
            first = head_mean(scaled, ones_block)
            second = head_mean(scaled * normed, ones_block)
            return ((scaled - first - normed * second) * scale).astype(BF16)

        def body(window):
            start = pl.multiple_of(start_ref[step], ALIGN)
            keys = pl.ds(start, window)
            k_win = k_ref[keys, :]
            v_win = v_ref[keys, :]
            other = (block // per) ^ ids_ref[1]
            at = pl.ds(pl.multiple_of(block % per * QB, QB), QB)
            g = grad_refs[0][at, :]
            for r in range(1, n_mp):
                g = jnp.where(other == r, grad_refs[r][at, :], g)
            q3 = spread_heads(q_ref[...], masks)
            g3 = spread_heads(g, masks)
            s = (dot(q3, k_win, 1, 1) * HEAD**-0.5).reshape(heads, QB, window)
            same = col_ref[...] == key_segments(row_ref, start, window)
            all_logs = log_ref[...]
            log = jnp.stack([all_logs[:, h : h + 1] for h in range(heads)])
            p = jnp.exp(jnp.where(same[None], s - log, MASK_FILL))
            dp = dot(g3, v_win, 1, 1).reshape(heads, QB, window)
            inner = jnp.sum(p * dp, axis=-1, keepdims=True)
            ds = (p * (dp - inner)).astype(BF16).reshape(heads * QB, window)
            p_low = p.astype(BF16).reshape(heads * QB, window)
            dv_ref[keys, :] += dot(p_low, g3, 0, 0)
            dk_ref[keys, :] += dot(ds, q3, 0, 0) * HEAD**-0.5
            dq = join_heads(dot(ds, k_win, 1, 0), masks) * HEAD**-0.5
            gq_ref[...] = back(pq_ref[...], dq, 0)

        alive = live_ref[step]

        @pl.when(alive == 0)
        def _():
            gq_ref[...] = jnp.zeros_like(gq_ref)

        @pl.when(alive != 0)
        def _():
            by_window(width_ref, step, body)

        @pl.when(block == QBLOCKS - 1)
        def _():
            gv_ref[...] = dv_ref[...].astype(BF16)

            def keys_back(i, carry):
                at = pl.ds(pl.multiple_of(i * share, share), share)
                gk_ref[at, :] = back(pk_ref[at, :], dk_ref[at, :], 1)
                return carry

            lax.fori_loop(0, n_mp, keys_back, 0)

    block = lambda c: pl.BlockSpec((QB, c), lambda s, b, *_: (s * QBLOCKS + b, 0))
    all_keys = lambda c: pl.BlockSpec((LEN, c), lambda s, b, *_: (s, 0))
    row_spec = pl.BlockSpec((1, 2, LEN), lambda s, b, *_: (s, 0, 0))
    grad_spec = pl.BlockSpec((share, cols), lambda s, b, *_: (s, 0))
    shape = jax.ShapeDtypeStruct((rows, cols), BF16)
    return pl.pallas_call(
        kernel,
        grid_spec=pltpu.PrefetchScalarGridSpec(
            num_scalar_prefetch=4,
            grid=(rows // LEN, QBLOCKS),
            in_specs=[block(cols), all_keys(cols), all_keys(cols), block(cols), all_keys(cols), whole(gains.shape), whole(ones.shape)]
            + [block(1), row_spec, block(128)]
            + [grad_spec] * n_mp,
            out_specs=[block(cols), all_keys(cols), all_keys(cols), whole((2, 8, cols))],
            scratch_shapes=[pltpu.VMEM((LEN, cols), F32), pltpu.VMEM((LEN, cols), F32)],
        ),
        out_shape=[shape, shape, shape, jax.ShapeDtypeStruct((2, 8, cols), F32)],
        compiler_params=PARAMS,
        cost_estimate=cost(60 * rows * LEN * cols, rows * cols * 24, rows * LEN),
        name="attend_back",
    )(ids, starts, widths, live, q, k, v, pq, pk, gains, ones, seg_col, seg_row, logs, *grads)


def key_windows(seg_ids):
    seg = seg_ids.reshape(-1, LEN)
    first = seg[:, ::QB]
    last = seg[:, QB - 1 :: QB]
    low = jnp.sum((seg[:, None, :] < first[:, :, None]).astype(jnp.int32), axis=2)
    high = jnp.sum((seg[:, None, :] <= last[:, :, None]).astype(jnp.int32), axis=2)
    base = low // ALIGN * ALIGN
    number = jnp.full(base.shape, len(WINDOWS) - 1, jnp.int32)
    start = jnp.zeros_like(base)
    for choice in range(len(WINDOWS) - 2, -1, -1):
        at = jnp.minimum(base, LEN - WINDOWS[choice])
        fits = high <= at + WINDOWS[choice]
        number = jnp.where(fits, choice, number)
        start = jnp.where(fits, at, start)
    live = (first != PAD_ID).astype(jnp.int32)
    return start.reshape(-1), number.reshape(-1), live.reshape(-1)


RELATIVE = (0, 2, 1, 3)


def down_copies(plan, ids_ref, parts, target, sems):
    y = ids_ref[0] % 2
    core = ids_ref[1] % 2
    copies = []
    for i, part in enumerate(parts):
        for side in range(2):
            place = target.at[side * 2 + (core ^ (i // 2)), :, y ^ (i % 2)]
            copies.append(pltpu.make_async_copy(part.at[side], place, sems.at[len(copies)]))
    return copies


def own_rows(source, target, share, n_mp, mp, sems, first):
    copies = []
    for s in range(target.shape[0] // share):
        at = pl.ds(pl.multiple_of((s * n_mp + mp) * share, share), share)
        copies.append(pltpu.make_async_copy(source.at[at], target.at[pl.ds(s * share, share)], sems.at[first + s]))
        copies[-1].start()
    return copies


def feed_up(plan, tokens, attended, params, out_w, up, up_across, down, down_across):
    dim = tokens.shape[1]
    rows, cols = attended[0].shape
    n_mp = plan.n_mp
    width = up.shape[1]
    hidden_size = n_mp * width
    share = LEN // n_mp
    seqs = rows // share
    inputs = [attended[0], out_w, up, up_across]
    shape = lambda c, t: jax.ShapeDtypeStruct((rows, c), t)
    results = [shape(dim, F32), shape(dim, BF16), shape(hidden_size, BF16), shape(hidden_size, F32)]
    n_load, n_store = len(inputs), len(results) * seqs + n_mp + 1 + seqs
    n_sems = 3 * seqs + 4

    def kernel(*refs):
        sources, (norm_ref, *sends), refs = refs[:n_load], refs[n_load : n_load + n_mp], refs[n_load + n_mp :]
        (down_in, down_across_in, tokens_in), refs = refs[:3], refs[3:]
        result_outs, att_outs, up_outs, down_outs, refs = refs[:4], refs[4 : n_mp + 3], refs[n_mp + 3 : n_mp + 5], refs[n_mp + 5 : n_mp + 7], refs[n_mp + 7 :]
        targets, bufs, att_bufs, u_bufs, refs = refs[:n_load], refs[n_load : n_load + 4], refs[n_load + 4 : n_load + n_mp + 3], refs[n_load + n_mp + 3 : n_load + n_mp + 5], refs[n_load + n_mp + 5 :]
        x_ref, load_sems, store_sems, send_sems, recv_sems = refs
        loads = Loads(sources, targets, load_sems)
        net = Sender(send_sems, recv_sems)
        x_copies = own_rows(tokens_in, x_ref, share, n_mp, net.mp, store_sems, n_store - seqs)
        net.meet([("mp", r) for r in range(1, n_mp)])
        at = lambda s: pl.ds(s * share, share)
        fetch = lambda s: [net.copy(sends[r - 1].at[at(s)], att_bufs[r - 1].at[at(s)], "mp", r) for r in range(1, n_mp)]
        rows_copies = [fetch(0)]
        up_copies = [net.copy(sources[2], u_bufs[0], "mp", 1), net.copy(sources[3], u_bufs[1], "mp", 1)]
        rows_copies += [fetch(s) for s in range(1, seqs)]
        down_copies = [net.copy(down_in, down_outs[0], "mp", 1), net.copy(down_across_in, down_outs[1], "mp", 1)]
        stores = []

        def store(src, dst):
            stores.append(pltpu.make_async_copy(src, dst, store_sems.at[len(stores)]))
            stores[-1].start()

        mid_buf, low_buf, act_buf, der_buf = bufs
        for s in range(seqs):
            here = at(s)
            att_ref, o_ref = loads[0], loads[1]
            x_copies[s].wait()
            middle = x_ref[here, :].astype(F32) + dot(att_ref[here, :], o_ref[net.mp, :, :cols], 1, 1)
            for r in range(1, n_mp):
                rows_copies[s][r - 1].wait_recv()
                middle = middle + dot(att_bufs[r - 1][here, :], o_ref[flip(net.mp, r), :, :cols], 1, 1)
            mid_buf[here, :] = middle
            normed, _ = norm_parts(middle)
            low = (normed * norm_ref[2:3, :] + norm_ref[3:4, :]).astype(BF16)
            low_buf[here, :] = low
            for c in range(n_mp):
                if c >= 2 and s == 0:
                    up_copies[c - 2].wait_recv()
                    store(u_bufs[c - 2], up_outs[c - 2])
                u_ref = loads[2 + c] if c < 2 else u_bufs[c - 2]
                columns = pl.ds(pl.multiple_of(flip(net.mp, RELATIVE[c]) * width, 128), width)
                hidden = dot(low, u_ref[...], 1, 0)
                phi = 0.5 * (1.0 + lax.erf(hidden * (0.5**0.5)))
                act_buf[here, columns] = (hidden * phi).astype(BF16)
                der_buf[here, columns] = phi + hidden * (jnp.exp(-0.5 * hidden * hidden) * 0.3989422804014327)
            for src, dst in zip(bufs, result_outs):
                store(src.at[here], dst.at[here])
        for src, dst in zip(att_bufs, att_outs):
            store(src, dst)
        for c in down_copies:
            c.wait_recv()
        net.finish()
        for c in stores:
            c.wait()

    like = lambda a: jax.ShapeDtypeStruct(a.shape, a.dtype)
    out = pl.pallas_call(
        kernel,
        in_specs=[ANY] * n_load + [pl.BlockSpec(memory_space=pltpu.VMEM)] + [ANY] * (n_mp + 2),
        out_specs=[ANY] * (n_mp + 7),
        out_shape=results + [like(a) for a in attended[1:]] + [like(up)] * 2 + [like(down)] * 2,
        scratch_shapes=[pltpu.VMEM(a.shape, a.dtype) for a in inputs + results + list(attended[1:]) + [up, up]]
        + [
            pltpu.VMEM((rows, dim), tokens.dtype),
            pltpu.SemaphoreType.DMA((n_load,)),
            pltpu.SemaphoreType.DMA((n_store,)),
            pltpu.SemaphoreType.DMA((n_sems,)),
            pltpu.SemaphoreType.DMA((n_sems,)),
        ],
        compiler_params=pltpu.CompilerParams(vmem_limit_bytes=VMEM_LIMIT, collective_id=4, has_side_effects=True),
        cost_estimate=cost(2 * rows * dim * (hidden_size + dim), rows * hidden_size * 8, rows * hidden_size * 2),
        name="feed_up",
    )(*inputs, params, *attended[1:], down, down_across, tokens)
    return out[:4], [attended[0]] + list(out[4 : n_mp + 3]), out[n_mp + 3 : n_mp + 5], out[n_mp + 5 :]


def start_all(copies):
    for c in copies:
        c.start()


def wait_all(copies):
    for c in copies:
        c.wait()


def feed_down(plan, ids, middle, active, seg_row, params, down):
    rows, dim = middle.shape
    n_mp = plan.n_mp
    hidden_size = active.shape[1]
    width = hidden_size // n_mp
    block = 256
    seqs = rows // block

    def kernel(ids_ref, mid_ref, act_ref, seg_ref, norm_ref, *refs):
        d_parts, (res_ref, block_ref, pool_ref, d_ref, sems) = refs[:4], refs[4:]
        seq = pl.program_id(0)
        copies = down_copies(plan, ids_ref, d_parts, d_ref, sems)

        @pl.when(seq == 0)
        def _():
            start_all(copies)
            wait_all(copies)

        result = mid_ref[...]
        for c in range(n_mp):
            result = result + dot(act_ref[:, c * width : (c + 1) * width], d_ref[c].reshape(dim, width), 1, 1)
        res_ref[...] = result
        block_ref[...] = result.astype(BF16)
        normed, _ = norm_parts(result)
        final = normed * norm_ref[4:5, :] + norm_ref[5:6, :]
        score = jnp.sum(final * norm_ref[6:7, :], axis=1, keepdims=True)
        score = jnp.broadcast_to(score, (block, 128)).T[0:1]
        slot = lax.broadcasted_iota(jnp.int32, (SLOTS, block), 0)
        member = (seg_ref[0, 0:1, :] - seq * IMG_SEQ == slot) & (slot < IMG_SEQ)
        top = jnp.max(jnp.where(member, score, MASK_FILL), axis=1, keepdims=True)
        e = jnp.exp(jnp.where(member, score - top, MASK_FILL))
        e = jnp.where(member, e, 0.0)
        total = jnp.sum(e, axis=1, keepdims=True)
        low = final.astype(BF16)
        high = e.astype(BF16)
        rest = (e - high.astype(F32)).astype(BF16)
        pool_ref[:, :dim] = dot(high, low, 1, 0) + dot(rest, low, 1, 0)
        lane = lax.broadcasted_iota(jnp.int32, (SLOTS, 128), 1)
        pool_ref[:, dim:] = jnp.where(lane == 0, top, jnp.where(lane == 1, total, 0.0))

    row = lambda c: pl.BlockSpec((block, c), lambda i, *_: (i, 0))
    return pl.pallas_call(
        kernel,
        grid_spec=pltpu.PrefetchScalarGridSpec(
            num_scalar_prefetch=1,
            grid=(seqs,),
            in_specs=[row(dim), row(hidden_size), pl.BlockSpec((1, 2, block), lambda i, ids_ref: (i, 0, ids_ref[1])), whole(params.shape)] + [ANY] * 4,
            out_specs=[row(dim), row(dim), pl.BlockSpec((SLOTS, dim + 128), lambda i, *_: (i, 0))],
            scratch_shapes=[pltpu.VMEM((n_mp, plan.groups // 2, 2, plan.block, width), BF16), pltpu.SemaphoreType.DMA((8,))],
        ),
        out_shape=[
            jax.ShapeDtypeStruct((rows, dim), F32),
            jax.ShapeDtypeStruct((rows, dim), BF16),
            jax.ShapeDtypeStruct((seqs * SLOTS, dim + 128), F32),
        ],
        compiler_params=PARAMS,
        cost_estimate=cost(2 * rows * dim * hidden_size, rows * hidden_size * 4),
        name="feed_down",
    )(ids, middle, active, seg_row, params, *down)


def classify(plan, pool, labels, images, cls, cls_across, class_count):
    slots, full = pool.shape
    dim = full - 128
    n_mp = plan.n_mp
    class_cols = cls.shape[1]
    wide = n_mp * class_cols

    part = slots // 2

    def combined(mine, other, lower, ref_rows):
        first, second = jnp.where(lower, mine, other), jnp.where(lower, other, mine)
        top_a, top_b = first[:, dim : dim + 1], second[:, dim : dim + 1]
        top = jnp.maximum(top_a, top_b)
        weight_a, weight_b = jnp.exp(top_a - top), jnp.exp(top_b - top)
        total = first[:, dim + 1 : dim + 2] * weight_a + second[:, dim + 1 : dim + 2] * weight_b
        ref_rows[:, :dim] = first[:, :dim] * weight_a + second[:, :dim] * weight_b
        lane = lax.broadcasted_iota(jnp.int32, (first.shape[0], 128), 1)
        ref_rows[:, dim:] = jnp.where(lane == 0, top, jnp.where(lane == 1, total, 0.0))

    def kernel(part_ref, label_ref, images_ref, c_in, c_across, grad_ref, stat_ref, loss_ref, cls_ref, c_ref, l_ref, pool_ref, got_ref, own_sems, send_sems, recv_sems):
        net = Sender(send_sems, recv_sems)
        me, mp = net.dp // plan.merge, net.mp
        side, core = mp // 2, mp % 2
        net.meet([("mp", 1), ("mp", 2)])
        first_copy = net.copy(part_ref, got_ref.at[0], "mp", 1)
        weights = [net.copy(a, c_ref.at[flip(mp, r)], "mp", 1) for a, r in ((c_in, 0), (c_across, 2))]
        own_copies = [pltpu.make_async_copy(a, c_ref.at[flip(mp, r)], own_sems.at[r // 2]) for a, r in ((c_in, 0), (c_across, 2))]
        start_all(own_copies)
        first_copy.wait_recv()
        combined(part_ref[...], got_ref[0], core == 0, pool_ref.at[0])
        own = pl.ds(pl.multiple_of(core * part, 8), part)
        net.copy(pool_ref.at[0, own], got_ref.at[1, pl.ds(0, part)], "mp", 2).wait_recv()
        combined(pool_ref[0, own, :], got_ref[1, 0:part, :], side == 0, pool_ref.at[1, own])
        net.copy(pool_ref.at[1, own], pool_ref.at[1, own], "mp", 1).wait_recv()
        for c in weights:
            c.wait_recv()
        wait_all(own_copies)
        net.finish()
        pool_ref = pool_ref.at[1]
        top = pool_ref[:, dim : dim + 1]
        total = pool_ref[:, dim + 1 : dim + 2]
        present = jnp.where(total > 0, 1.0, 0.0)
        safe = total + (1.0 - present)
        pooled = pool_ref[:, :dim] / safe
        low = pooled.astype(BF16)
        logits = jnp.concatenate([dot(low, c_ref[c], 1, 0) for c in range(n_mp)], axis=1)
        column = lax.broadcasted_iota(jnp.int32, (slots, wide), 1)
        logits = jnp.where(column % class_cols < class_count, logits, MASK_FILL)
        row_top = jnp.max(logits, axis=1, keepdims=True)
        log_total = row_top + jnp.log(jnp.sum(jnp.exp(logits - row_top), axis=1, keepdims=True))
        chosen = jnp.where(column == label_ref[...], 1.0, 0.0)
        label_logit = jnp.sum(chosen * logits, axis=1, keepdims=True)
        loss = jnp.sum(present * (log_total - label_logit), axis=0, keepdims=True)
        loss_ref[...] = jnp.broadcast_to(loss, loss_ref.shape)
        scale = present / images_ref[0:1, 0:1]
        grad = ((jnp.exp(logits - log_total) - chosen) * scale).astype(BF16)
        l_ref[...] = grad
        row_grad = sum(dot(grad[:, c * class_cols : (c + 1) * class_cols], c_ref[c], 1, 1) for c in range(n_mp)).astype(BF16)
        grad_ref[...] = row_grad
        inner = jnp.sum(row_grad.astype(F32) * pooled, axis=1, keepdims=True)
        lane = lax.broadcasted_iota(jnp.int32, (slots, 128), 1)
        stat_ref[...] = jnp.where(lane == 0, top, jnp.where(lane == 1, 1.0 / safe, jnp.where(lane == 2, inner, 0.0)))
        own = l_ref[:, pl.ds(pl.multiple_of(mp * class_cols, 128), class_cols)]
        grad_cls = dot(low, own, 0, 0)
        for g in range(plan.groups):
            at = (g % 2 + me % 2) % 2 * (plan.groups // 2) + g // 2
            cls_ref[at] = grad_cls[g * plan.block : (g + 1) * plan.block].astype(BF16)

    vmem = pl.BlockSpec(memory_space=pltpu.VMEM)
    return pl.pallas_call(
        kernel,
        in_specs=[vmem] * 3 + [ANY] * 2,
        out_specs=[vmem] * 4,
        out_shape=[
            jax.ShapeDtypeStruct((slots, dim), BF16),
            jax.ShapeDtypeStruct((slots, 128), F32),
            jax.ShapeDtypeStruct((8, 128), F32),
            jax.ShapeDtypeStruct((plan.groups, plan.block, class_cols), BF16),
        ],
        scratch_shapes=[
            pltpu.VMEM((n_mp,) + cls.shape, BF16),
            pltpu.VMEM((slots, wide), BF16),
            pltpu.VMEM((2, slots, full), F32),
            pltpu.VMEM((2, slots, full), F32),
            pltpu.SemaphoreType.DMA((2,)),
            pltpu.SemaphoreType.DMA((5,)),
            pltpu.SemaphoreType.DMA((5,)),
        ],
        compiler_params=pltpu.CompilerParams(vmem_limit_bytes=VMEM_LIMIT, collective_id=3, has_side_effects=True),
        cost_estimate=cost(6 * slots * dim * wide, dim * wide * 2),
        name="classify",
    )(pool, labels, images, cls, cls_across)


def split_three(values):
    high = values.astype(BF16)
    rest = values - high.astype(F32)
    middle = rest.astype(BF16)
    low = (rest - middle.astype(F32)).astype(BF16)
    return high, middle, low


def feed_back(plan, ids, result, middle, slope, row_grads, stats, seg_col, params, out_w, up, down, cols):
    rows, dim = result.shape
    n_mp = plan.n_mp
    width = up[0].shape[1]
    hidden_size = n_mp * width
    block = 256

    def kernel(ids_ref, res_ref, mid_ref, der_ref, pg_ref, stat_ref, seg_ref, norm_ref, o_ref, *refs):
        u_refs, d_parts, refs = refs[:n_mp], refs[n_mp : n_mp + 4], refs[n_mp + 4 :]
        rlow_ref, hlow_ref, mlow_ref, mgrad_ref, *refs = refs
        ag_refs, (sums_ref, d_ref, sems) = refs[:n_mp], refs[n_mp:]
        mp = ids_ref[1]
        seq = pl.program_id(0)
        copies = down_copies(plan, ids_ref, d_parts, d_ref, sems)

        @pl.when(seq == 0)
        def _():
            start_all(copies)
            sums_ref[...] = jnp.zeros_like(sums_ref)

        normed, scale = norm_parts(res_ref[...])
        gain, probe = norm_ref[4:5, :], norm_ref[6:7, :]
        final = normed * gain + norm_ref[5:6, :]
        score = jnp.sum(final * probe, axis=1, keepdims=True)
        slot = lax.broadcasted_iota(jnp.int32, (block, SLOTS), 1)
        member = (seg_ref[...] - seq * IMG_SEQ == slot) & (slot < IMG_SEQ)
        held = jnp.max(jnp.where(member, 1.0, 0.0), axis=1, keepdims=True)
        one = jnp.where(member, 1.0, 0.0).astype(BF16)
        row_stat = sum(dot(one, part, 1, 0) for part in split_three(stat_ref[...]))
        top, inverse, inner = row_stat[:, 0:1], row_stat[:, 1:2], row_stat[:, 2:3]
        share = jnp.exp(jnp.where(held > 0, score - top, 0.0)) * inverse * held
        row_grad = dot(one, pg_ref[...], 1, 0)
        share_low = share.astype(BF16).astype(F32)
        share_grad = jnp.sum(row_grad * final.astype(BF16).astype(F32), axis=1, keepdims=True)
        score_grad = share * (share_grad - inner)
        final_grad = share_low * row_grad + score_grad * probe
        add = lambda slot, value: sums_ref.at[slot].__setitem__(
            ..., sums_ref[slot] + jnp.sum(value.reshape(-1, 8, dim), axis=0)
        )
        add(4, score_grad * final)
        add(2, final_grad * normed)
        add(3, final_grad)
        result_grad = norm_back(final_grad, normed, scale, gain)
        result_low = result_grad.astype(BF16)
        rlow_ref[...] = result_low
        pl.when(seq == 0)(lambda: wait_all(copies))
        second = jnp.zeros((block, dim), F32)
        for c in range(n_mp):
            other = mp ^ RELATIVE[c]
            at = pl.ds(pl.multiple_of(other * width, 128), width)
            hidden_low = (der_ref[:, at] * dot(result_low, d_ref[other].reshape(dim, width), 1, 0)).astype(BF16)
            hlow_ref[:, at] = hidden_low
            second = second + dot(hidden_low, u_refs[c][...], 1, 1)
        normed_two, scale_two = norm_parts(mid_ref[...])
        add(0, second * normed_two)
        add(1, second)
        middle_grad = result_grad + norm_back(second, normed_two, scale_two, norm_ref[2:3, :])
        mgrad_ref[...] = middle_grad
        middle_low = middle_grad.astype(BF16)
        mlow_ref[...] = middle_low
        for r in range(n_mp):
            ag_refs[r][...] = dot(middle_low, o_ref[mp ^ r, :, :cols], 1, 0).astype(BF16)

    row = lambda c: pl.BlockSpec((block, c), lambda i, *_: (i, 0))
    shape = lambda c, t: jax.ShapeDtypeStruct((rows, c), t)
    slots = lambda c: pl.BlockSpec((SLOTS, c), lambda i, *_: (i, 0))
    own_row = pl.BlockSpec((block, 1), lambda i, ids_ref: (i * n_mp + ids_ref[1], 0))
    return pl.pallas_call(
        kernel,
        grid_spec=pltpu.PrefetchScalarGridSpec(
            num_scalar_prefetch=1,
            grid=(rows // block,),
            in_specs=[row(dim), row(dim), row(hidden_size), slots(dim), slots(128), own_row, whole(params.shape), whole(out_w.shape)]
            + [whole(up[0].shape)] * n_mp
            + [ANY] * 4,
            out_specs=[row(dim), row(hidden_size), row(dim), row(dim)] + [row(cols)] * n_mp + [whole((5, 8, dim))],
            scratch_shapes=[pltpu.VMEM((n_mp, plan.groups // 2, 2, plan.block, width), BF16), pltpu.SemaphoreType.DMA((8,))],
        ),
        out_shape=[shape(dim, BF16), shape(hidden_size, BF16), shape(dim, BF16), shape(dim, F32)]
        + [shape(cols, BF16)] * n_mp
        + [jax.ShapeDtypeStruct((5, 8, dim), F32)],
        compiler_params=PARAMS,
        cost_estimate=cost(2 * rows * dim * (2 * hidden_size + dim), rows * hidden_size * 8),
        name="feed_back",
    )(ids, result, middle, slope, row_grads, stats, seg_col, params, out_w, *up, *down)


def weight_grads(plan, pairs, out_pair, cls_blocks, sends, blocks):
    dim = pairs[0][0].shape[1]
    rows = pairs[0][0].shape[0]
    n_mp, size, merge = plan.n_mp, plan.block, plan.merge
    lines = plan.groups // 2
    width = pairs[0][1].shape[1] // n_mp
    cols = out_pair[1][0].shape[1]
    out_cols = -(-cols // 128) * 128
    inputs = [a for pair in pairs for a in pair] + [out_pair[0]] + list(out_pair[1]) + [cls_blocks] + list(blocks)
    n_load = len(inputs)
    widths = [width] * len(pairs) + [out_cols]
    n = len(widths)

    def kernel(*refs):
        sources, ag_in, refs = refs[:n_load], refs[n_load : n_load + n_mp - 1], refs[n_load + n_mp - 1 :]
        keep_out, send_out, cls_out, ag_out, refs = refs[:n], refs[n : 2 * n], refs[2 * n], refs[2 * n + 1 : 2 * n + n_mp], refs[2 * n + n_mp :]
        block_ref, refs = refs[0], refs[1:]
        targets, refs = refs[:n_load], refs[n_load:]
        send_buf, got_buf, own_buf, keep_buf, low_buf = (refs[i * n : (i + 1) * n] for i in range(5))
        cls_got, load_sems, store_sems, send_sems, recv_sems, block_sems = refs[5 * n :]
        loads = Loads(sources, targets, load_sems)
        net = Sender(send_sems, recv_sems)
        y = net.dp // merge % 2
        side, core = net.mp // 2, net.mp % 2
        net.meet([("mp", 1), ("mp", 2), ("mp", 3), ("dp", merge)])
        ag = [net.copy(a, b, "mp", r) for r, (a, b) in enumerate(zip(ag_in, ag_out), start=1)]
        places = [block_ref.at[:, flip(net.mp, r)] for r in (0, 2)]
        cls_ref = loads[n_load - 3]
        cls_copy = net.copy(cls_ref.at[1], cls_got, "dp", merge)
        stores = []

        def grad(number, other_side, other_core):
            if number < len(pairs):
                left, right = loads[2 * number], loads[2 * number + 1]
                at = flip(side, other_side) * 2 + flip(core, other_core)
                return dot(left[...], right[:, pl.ds(pl.multiple_of(at * width, 128), width)], 0, 0)
            left = loads[2 * len(pairs)]
            right = loads[2 * len(pairs) + 1 + other_side * 2 + other_core]
            value = dot(left[...], right[...], 0, 0)
            return jnp.concatenate([value, jnp.zeros((dim, out_cols - cols), F32)], axis=1) if out_cols != cols else value

        split = lambda value: value.reshape(lines, 2, size, value.shape[1])
        cores, block_copies, block_own = [], [], []
        for i in range(n):
            if i == 1:
                rows_in = [loads[n_load - 2], loads[n_load - 1]]
                block_copies += [net.copy(a, b, "mp", 1) for a, b in zip(rows_in, places)]
                block_own += [pltpu.make_async_copy(a, b, block_sems.at[j]) for j, (a, b) in enumerate(zip(rows_in, places))]
                start_all(block_own)
            for other_side in (0, 1):
                send_buf[i][flip(side, other_side)] = split(grad(i, other_side, 1).astype(BF16))
            cores.append(net.copy(send_buf[i], got_buf[i], "mp", 1))
            for other_side in (0, 1):
                own_buf[i][flip(side, other_side)] = split(grad(i, other_side, 0))
        for i in range(n):
            cores[i].wait_recv()
            if i == 0:
                keep_buf[i][...] = own_buf[i][side] + got_buf[i][side].astype(F32)
                low_buf[i][...] = (own_buf[i][1 - side] + got_buf[i][1 - side].astype(F32)).astype(BF16)
            else:
                for x in (0, 1):
                    keep_buf[i][x] = own_buf[i][x, :, y] + got_buf[i][x, :, y].astype(F32)
                    low_buf[i][x] = (own_buf[i][x, :, 1 - y] + got_buf[i][x, :, 1 - y].astype(F32)).astype(BF16)
            for a, b in ((low_buf[i], send_out[i]), (keep_buf[i], keep_out[i])):
                stores.append(pltpu.make_async_copy(a, b, store_sems.at[len(stores)]))
                stores[-1].start()
        cls_copy.wait_recv()
        cls_out[...] = cls_ref[0].astype(F32) + cls_got[...].astype(F32)
        for c in ag + block_copies:
            c.wait_recv()
        wait_all(block_own)
        net.finish()
        for c in stores:
            c.wait()

    shape = jax.ShapeDtypeStruct
    vmem = pl.BlockSpec(memory_space=pltpu.VMEM)
    full = [(2, lines, 2, size, w) for w in widths]
    half = [(lines, 2, size, widths[0])] + [(2, lines, size, w) for w in widths[1:]]
    n_sems = n + n_mp + 2
    seqs, share = blocks[0].shape[:2]
    out = pl.pallas_call(
        kernel,
        in_specs=[ANY] * (n_load + n_mp - 1),
        out_specs=[ANY] * (2 * n) + [vmem] + [ANY] * n_mp,
        out_shape=[shape(h, F32) for h in half]
        + [shape(h, BF16) for h in half]
        + [shape(cls_blocks.shape[1:], F32)]
        + [shape(a.shape, a.dtype) for a in sends]
        + [shape((seqs, n_mp, share, dim), BF16)],
        scratch_shapes=[pltpu.VMEM(a.shape, a.dtype) for a in inputs]
        + [pltpu.VMEM(f, BF16) for f in full]
        + [pltpu.VMEM(f, BF16) for f in full]
        + [pltpu.VMEM(f, F32) for f in full]
        + [pltpu.VMEM(h, F32) for h in half]
        + [pltpu.VMEM(h, BF16) for h in half]
        + [
            pltpu.VMEM(cls_blocks.shape[1:], BF16),
            pltpu.SemaphoreType.DMA((n_load,)),
            pltpu.SemaphoreType.DMA((2 * n,)),
            pltpu.SemaphoreType.DMA((n_sems,)),
            pltpu.SemaphoreType.DMA((n_sems,)),
            pltpu.SemaphoreType.DMA((2,)),
        ],
        compiler_params=pltpu.CompilerParams(vmem_limit_bytes=60 * 1024 * 1024, collective_id=2, has_side_effects=True),
        cost_estimate=cost(2 * rows * dim * n_mp * sum(widths), rows * width * n_mp * 8),
        name="grads",
    )(*inputs, *sends)
    return out[:n], out[n : 2 * n], out[2 * n], out[2 * n + 1 : 2 * n + n_mp], out[2 * n + n_mp].reshape(-1, dim)


def finish(plan, low, proj_grads, w, middle_grad, tokens, params, row_sums, gain_sums, loss, zx, yz, z_only):
    seqs = low.shape[0] // LEN
    dim = low.shape[1]
    cols = w.shape[2]
    n_mp = plan.n_mp
    share = LEN // n_mp
    lines, size, merge = plan.groups // 2, plan.block, plan.merge
    dp_bits = [1 << i for i in range(plan.n_dp.bit_length() - 1)]
    far = [2 * k * merge for k in range(1, lines)]
    partners = [("mp", 1), ("mp", 2)] + [("dp", b) for b in sorted(set(dp_bits + far + [merge]))]
    stages = [("mp", 1), ("mp", 2)] + [("dp", b) for b in dp_bits]
    inputs = [w] + list(proj_grads) + [a for pair in zx + yz for a in pair] + list(z_only)
    inputs += [low, middle_grad]
    smalls = [params, row_sums, loss, gain_sums]
    n_in = len(inputs)
    n_zx, n_yz, n_z = len(zx), len(yz), len(z_only)
    n_sems = (lines - 1) * (n_zx + n_yz + n_z + 1) + n_zx + n_yz + 1 + 4 * seqs + len(stages)
    n_out = 3 + n_zx + n_yz + n_z

    def kernel(*refs):
        sources, (norm_ref, row_sum_ref, loss_ref, gain_ref), refs = refs[:n_in], refs[n_in : n_in + 4], refs[n_in + 4 :]
        tokens_in, refs = refs[0], refs[1:]
        rows_ref, qkv_out, total_ref, *owned = refs[:n_out]
        zx_out, yz_out, z_out = owned[:n_zx], owned[n_zx : n_zx + n_yz], owned[n_zx + n_yz :]
        scratch = list(refs[n_out:])
        take = lambda n: [scratch.pop(0) for _ in range(n)]
        targets = take(n_in)
        t_keep, t_send, t_got, t_mine, x_send, x_got, acc, q_low, q_y, q_send, q_z, got_sums, load_sems, send_sems, recv_sems, x_ref = take(16)
        zx_low, zx_got, zx_send, zx_last = take(n_zx), take(n_zx), take(n_zx), take(n_zx)
        yz_low, yz_got, yz_send, yz_last = take(n_yz), take(n_yz), take(n_yz), take(n_yz)
        z_low, z_got = take(n_z), take(n_z)
        loads = Loads(sources, targets, load_sems)
        net = Sender(send_sems, recv_sems)
        copy = net.copy
        own_copies = own_rows(tokens_in, x_ref, share, n_mp, net.mp, load_sems, n_in)
        group = net.dp // merge
        z, y = group // 2, group % 2
        side, core = net.mp // 2, net.mp % 2
        net.meet(partners)
        others = range(1, lines)
        to_z = lambda src, dst, k: copy(src, dst, "dp", 2 * k * merge)
        pair_from = 4
        pair = lambda i: (loads[pair_from + 2 * i], loads[pair_from + 2 * i + 1])
        both = lambda a, b, *at: a[at].astype(F32) + b[at].astype(F32)
        z_from = pair_from + 2 * (n_zx + n_yz)
        y_copies, z_copies = [], []

        def over_y(i):
            a, b = pair(n_zx + i)
            for line in range(lines):
                yz_low[i][line] = both(a, b, line, 1 - y).astype(BF16)
            y_copies.append(copy(yz_low[i], yz_got[i], "dp", merge))

        def over_z(i):
            a, b = pair(i)
            for k in others:
                for s in (0, 1):
                    zx_low[i][k - 1, s] = both(a, b, s, flip(z, k)).astype(BF16)
                z_copies.append(to_z(zx_low[i].at[k - 1], zx_got[i].at[k - 1], k))

        def only_z(i):
            for k in others:
                z_low[i][k - 1] = loads[z_from + i][flip(z, k)].astype(BF16)
                z_copies.append(to_z(z_low[i].at[k - 1], z_got[i].at[k - 1], k))

        w_ref = loads[0]
        pg = [[loads[1 + p].at[pl.ds(s * LEN, LEN)] for p in range(3)] for s in range(seqs)]
        core_copies = []
        x_copies = []

        def over_x(s):
            core_copies[s].wait_recv()
            x_send[s] = (t_keep[s, 1].astype(F32) + t_got[s, 1].astype(F32)).astype(BF16)
            x_copies.append(copy(x_send.at[s], x_got.at[s], "mp", 2))
            t_mine[s] = t_keep[s, 0].astype(F32) + t_got[s, 0].astype(F32)

        for s in range(seqs):
            def terms(target, i, carry):
                to_other = i // 2
                row_side = side + i % 2 * (1 - 2 * side)
                row_core = core + (1 - to_other) * (1 - 2 * core)
                at = pl.ds(pl.multiple_of((row_side * 2 + row_core) * share, share), share)
                gq, gk, gv = (ref[at, :] for ref in pg[s])
                total = dot(gq, w_ref[0], 1, 1) + dot(gk, w_ref[1], 1, 1) + dot(gv, w_ref[2], 1, 1)
                target[s, i % 2] = total.astype(BF16)
                return carry

            lax.fori_loop(0, 2, functools.partial(terms, t_send), 0)
            core_copies.append(copy(t_send.at[s], t_got.at[s], "mp", 1))
            lax.fori_loop(2, 4, functools.partial(terms, t_keep), 0)
            if s == 0:
                over_x(0)
                over_z(0)
            elif s > 1:
                over_x(s - 1)
            if s == 1:
                for i in range(n_yz):
                    over_y(i)
                for i in range(1, n_zx):
                    over_z(i)
                for i in range(n_z):
                    only_z(i)
        if seqs > 1:
            over_x(seqs - 1)

        low_ref = loads[n_in - 2]
        for s in range(seqs):
            for p in range(3):
                part = dot(low_ref[s * LEN : (s + 1) * LEN, :], pg[s][p][...], 0, 0)
                acc[p] = part if s == 0 else acc[p] + part
        for p in range(3):
            q_low[p] = acc[p].reshape(lines, 2, size, cols).astype(BF16)
        y_copy = copy(q_low.at[:, :, 1 - y], q_y, "dp", merge)

        mid_ref = loads[n_in - 1]
        for c in own_copies:
            c.wait()
        total_ref[...] = jnp.zeros_like(total_ref)
        for n in range(5):
            total_ref[2 + n : 3 + n, :] = jnp.sum(row_sum_ref[n], axis=0, keepdims=True)
        for n in range(2):
            total_ref[8 + n : 9 + n, 0:cols] = jnp.sum(gain_ref[n], axis=0, keepdims=True)
        total_ref[10:11, 0:128] = loss_ref[0:1, :]
        row_copies = []
        q_copies = []
        for s in range(seqs):
            at = slice(s * share, (s + 1) * share)
            normed, scale = norm_parts(x_ref[at, :].astype(F32))
            x_copies[s].wait_recv()
            first = t_mine[s] + x_got[s].astype(F32)
            total_ref[0:1, :] += jnp.sum(first * normed, axis=0, keepdims=True)
            total_ref[1:2, :] += jnp.sum(first, axis=0, keepdims=True)
            rows_ref[0, s] = (mid_ref[at, :] + norm_back(first, normed, scale, norm_ref[0:1, :])).astype(BF16)
            row_copies.append(copy(rows_ref.at[0, s], rows_ref.at[1, s], "mp", 2))
            if s == 0:
                y_copy.wait_recv()
                for line in range(lines):
                    for p in range(3):
                        rows_at = pl.ds(pl.multiple_of((line * 2 + y) * size, 8), size)
                        q_send[line, p] = (acc[p, rows_at, :] + q_y[p, line].astype(F32)).astype(BF16)
                q_copies = [to_z(q_send.at[flip(z, k)], q_z.at[k - 1], k) for k in others]
            if s == min(1, seqs - 1):
                for i in range(n_yz):
                    a, b = pair(n_zx + i)
                    y_copies[i].wait_recv()
                    for k in others:
                        at_z = flip(z, k)
                        yz_send[i][k - 1] = (both(a, b, at_z, y) + yz_got[i][at_z].astype(F32)).astype(BF16)
                        z_copies.append(to_z(yz_send[i].at[k - 1], yz_last[i].at[k - 1], k))
        mate_copies, last_copies = [], []

        def zx_last_step(i):
            for c in z_copies[i * (lines - 1) : (i + 1) * (lines - 1)]:
                c.wait_recv()
            a, b = pair(i)
            other = both(a, b, 1 - side, z) + sum(zx_got[i][k - 1, 1 - side].astype(F32) for k in others)
            zx_send[i][...] = other.astype(BF16)
            last_copies.append(copy(zx_send[i], zx_last[i], "mp", 2))
            zx_out[i][...] = both(a, b, side, z) + sum(zx_got[i][k - 1, side].astype(F32) for k in others)

        def mate(n):
            row_copies[n].wait_recv()
            mate_copies.append(copy(rows_ref.at[pl.ds(0, 2), n], rows_ref.at[pl.ds(2, 2), n], "mp", 1))

        between = [functools.partial(zx_last_step, i) for i in range(n_zx)] + [functools.partial(mate, n) for n in range(seqs)]
        for n, (axis, bits) in enumerate(stages):
            count = 8 if axis == "mp" else 16
            stage = copy(total_ref.at[pl.ds(0, count)], got_sums.at[n, pl.ds(0, count)], axis, bits)
            net.started.pop()
            if between:
                between.pop(0)()
            stage.wait()
            total_ref[0:count, :] += got_sums[n, 0:count, :]
        for step in between:
            step()
        for c in z_copies[n_zx * (lines - 1) :]:
            c.wait_recv()
        for i in range(n_yz):
            a, b = pair(n_zx + i)
            own = both(a, b, z, y) + yz_got[i][z].astype(F32)
            yz_out[i][...] = own + sum(yz_last[i][k - 1].astype(F32) for k in others)
        for i in range(n_z):
            z_out[i][...] = loads[z_from + i][z] + sum(z_got[i][k - 1].astype(F32) for k in others)
        for c in q_copies:
            c.wait_recv()
        for p in range(3):
            rows_at = pl.ds(pl.multiple_of((z * 2 + y) * size, 8), size)
            own = acc[p, rows_at, :] + q_y[p, z].astype(F32)
            qkv_out[p] = own + sum(q_z[k - 1, p].astype(F32) for k in others)
        for i, c in enumerate(last_copies):
            c.wait_recv()
            zx_out[i][...] += zx_last[i][...].astype(F32)
        for c in mate_copies:
            c.wait_recv()
        net.finish()

    vmem = pl.BlockSpec(memory_space=pltpu.VMEM)
    shape = jax.ShapeDtypeStruct
    blk = (3, size, cols)
    piece = lambda a: a.shape[-2:]
    buf = lambda a, lead, t=BF16: pltpu.VMEM(tuple(lead) + piece(a), t)
    three = lines - 1
    scratch = [pltpu.VMEM(a.shape, a.dtype) for a in inputs]
    scratch += [
        pltpu.VMEM((seqs, 2, share, dim), BF16),
        pltpu.VMEM((seqs, 2, share, dim), BF16),
        pltpu.VMEM((seqs, 2, share, dim), BF16),
        pltpu.VMEM((seqs, share, dim), F32),
        pltpu.VMEM((seqs, share, dim), BF16),
        pltpu.VMEM((seqs, share, dim), BF16),
        pltpu.VMEM((3, dim, cols), F32),
        pltpu.VMEM((3, lines, 2, size, cols), BF16),
        pltpu.VMEM((3, lines, size, cols), BF16),
        pltpu.VMEM((lines,) + blk, BF16),
        pltpu.VMEM((three,) + blk, BF16),
        pltpu.VMEM((len(stages), 16, dim), F32),
        pltpu.SemaphoreType.DMA((n_in + seqs,)),
        pltpu.SemaphoreType.DMA((n_sems,)),
        pltpu.SemaphoreType.DMA((n_sems,)),
        pltpu.VMEM((seqs * share, dim), tokens.dtype),
    ]
    firsts, seconds = [a for a, _ in zx], [a for a, _ in yz]
    for lead in ((three, 2), (three, 2), (), ()):
        scratch += [buf(a, lead) for a in firsts]
    for lead in ((lines,), (lines,), (three,), (three,)):
        scratch += [buf(a, lead) for a in seconds]
    scratch += [buf(a, (three,)) for a in z_only] + [buf(a, (three,)) for a in z_only]
    out = pl.pallas_call(
        kernel,
        in_specs=[ANY] * n_in + [vmem] * len(smalls) + [ANY],
        out_specs=[vmem] * n_out,
        out_shape=[shape((4, seqs, share, dim), BF16), shape(blk, F32), shape((16, dim), F32)]
        + [shape(piece(a), F32) for a in firsts + seconds + list(z_only)],
        scratch_shapes=scratch,
        compiler_params=pltpu.CompilerParams(vmem_limit_bytes=60 * 1024 * 1024, collective_id=1, has_side_effects=True),
        cost_estimate=cost(12 * seqs * LEN * dim * cols, seqs * LEN * dim * 8),
        name="finish",
    )(*inputs, *smalls, tokens)
    return out[0], out[1], out[2], out[3:]


def adam_update(weight, moment_one, moment_two, gradient, step_rate, decay_rate):
    fresh_one = BETA_ONE * moment_one + (1.0 - BETA_ONE) * gradient
    fresh_two = BETA_TWO * moment_two + (1.0 - BETA_TWO) * gradient * gradient
    one_hat = fresh_one / (1.0 - BETA_ONE**STEP)
    two_hat = fresh_two / (1.0 - BETA_TWO**STEP)
    updated = weight - step_rate * (one_hat / (jnp.sqrt(two_hat) + ADAM_EPS) + decay_rate * weight)
    return (fresh_one, fresh_two, updated)


def update(plan, ids, parts, groups):
    n_mp, seqs, share, dim = parts.shape
    n = len(groups)
    arrays = [a for group in groups for a in group]

    def kernel(ids_ref, part_ref, *refs):
        sources, out_ref, results = refs[: 4 * n], refs[4 * n], refs[4 * n + 1 :]
        out_ref[...] = part_ref[...].astype(F32)

        @pl.when(pl.program_id(0) == 0)
        def _():
            for i in range(n):
                w_ref, m_ref, v_ref, g_ref = sources[4 * i : 4 * i + 4]
                columns = w_ref.shape[-1]
                if w_ref.shape[:-1] == g_ref.shape[:-1]:
                    grad = g_ref[...][..., :columns]
                else:
                    grad = g_ref[...].T[: w_ref.shape[0], :columns]
                fresh = adam_update(w_ref[...], m_ref[...], v_ref[...], grad, MATRIX_RATE, MATRIX_DECAY)
                for ref, value in zip(results[3 * i : 3 * i + 3], fresh):
                    ref[...] = value

    relative = lambda i: i % 2 * 2 + i // 2
    shapes = [jax.ShapeDtypeStruct(group[0].shape, F32) for group in groups for _ in range(3)]
    out = pl.pallas_call(
        kernel,
        grid_spec=pltpu.PrefetchScalarGridSpec(
            num_scalar_prefetch=1,
            grid=(n_mp,),
            in_specs=[pl.BlockSpec((None, seqs, share, dim), lambda i, *_: (i, 0, 0, 0))] + [whole(a.shape) for a in arrays],
            out_specs=[pl.BlockSpec((seqs, None, share, dim), lambda i, ids_ref: (0, ids_ref[1] ^ relative(i), 0, 0))]
            + [whole(a.shape) for a in shapes],
        ),
        out_shape=[jax.ShapeDtypeStruct((seqs, n_mp, share, dim), F32)] + shapes,
        compiler_params=PARAMS,
        cost_estimate=cost(0, seqs * n_mp * share * dim * 8),
        name="update",
    )(ids, parts, *arrays)
    return out[0].reshape(seqs * n_mp * share, dim), [out[1 + 3 * i : 4 + 3 * i] for i in range(n)]


def shards(
    tokens,
    seg_ids,
    labels,
    w_qkv,
    m_qkv,
    v_qkv,
    w_out,
    m_out,
    v_out,
    w_up,
    m_up,
    v_up,
    w_down,
    m_down,
    v_down,
    w_cls,
    m_cls,
    v_cls,
    norm_params,
    m_norm,
    v_norm,
    qk_gain,
    m_qk,
    v_qk,
    *,
    n_dp,
    n_mp,
):
    dp, mp = lax.axis_index("dp"), lax.axis_index("mp")
    group_rows, dim = tokens.shape
    plan = Plan(n_dp, n_mp, dim)
    seqs = group_rows // LEN
    share = LEN // n_mp
    rows = seqs * share
    cols = w_qkv.shape[2]
    classes = w_cls.shape[1]
    class_cols = -(-classes // 128) * 128
    out_cols = -(-cols // 128) * 128
    ids = jnp.stack([dp // plan.merge, mp]).astype(jnp.int32)

    new_image = seg_ids != jnp.concatenate([jnp.full((1,), -1, jnp.int32), seg_ids[:-1]])
    count = jnp.sum((new_image & (seg_ids != PAD_ID)).astype(F32))
    dim_part, head_part = norm_params.shape[1], qk_gain.shape[2]
    pad = lambda a, r, c: jnp.pad(a, ((0, r - a.shape[0]), (0, c - a.shape[1])))
    low_param = lambda a: lax.reduce_precision(a, 8, 7)
    small = jnp.concatenate(
        [
            pad(low_param(norm_params), 8, 128),
            pad(low_param(qk_gain).reshape(2, cols // HEAD * head_part), 8, 128),
            pad(count.reshape(1, 1), 8, 128),
        ]
    )
    low = lambda a: a if plan.merge == 1 else a.astype(BF16)
    qkv_block = plan.merged(low(w_qkv), 1)
    up_block = plan.merged(low(w_up), 0)
    down_block = plan.merged(w_down.T.astype(BF16), 0)
    out_block = plan.merged(pad(w_out.T.astype(BF16), dim_part, out_cols), 0)
    cls_block = plan.merged(low(w_cls), 0)
    small_block = plan.merged(small[None], 0)

    tied = lambda value, tie: lax.optimization_barrier((value, tie))[0]

    head_of = jnp.arange(cols) // HEAD
    ones = jnp.where(head_of[:, None] == head_of[None, :], 1.0 / HEAD, 0.0).astype(BF16)
    starts, widths, live = key_windows(seg_ids)
    seg_col = seg_ids.reshape(group_rows, 1)
    seg_row = seg_ids.reshape(-1, LEN)
    seg_row = jnp.stack([seg_row, jnp.roll(seg_row, -ALIGN, axis=1)], axis=1)
    normed_low, pq, pk, q, k, v, w, up, down, out_w, cls, params, gains, images = gather_project(
        plan, tokens, qkv_block, up_block, down_block, out_block, cls_block, small_block, ones
    )
    w = w.reshape(3, dim, cols)
    out_w = out_w.reshape(n_mp, dim, out_cols)
    up = up.reshape(dim, up.shape[-1])
    up_across, down_across = plan.swap(up, "mp", 2), plan.group_swap(down, 1)
    cls = cls.reshape(dim, class_cols)
    image_total = images[0, 0]
    *attended, logs = attend(plan, ids, starts, widths, q, k, v, seg_col, seg_row)

    (middle, second_low, active, slope), attended, up_mates, down_mates = feed_up(
        plan, tokens, attended, params, out_w, up, up_across, down, down_across
    )
    cls_across = plan.swap(tied(cls, middle), "mp", 2)
    up = [up, up_across, *up_mates]
    down = [down, down_across, *down_mates]
    result, block_rows, pool = feed_down(plan, ids, middle, active, seg_row, params, down)

    block_rows = block_rows.reshape(seqs, share, dim)
    slot_label = labels.reshape(seqs, IMG_SEQ)
    slot_label = slot_label // classes * class_cols + slot_label % classes
    slot_label = jnp.pad(slot_label, ((0, 0), (0, SLOTS - IMG_SEQ)), constant_values=-1).reshape(seqs * SLOTS, 1)
    row_grads, stats, loss, cls_blocks = classify(plan, pool, slot_label, images, cls, cls_across, classes)

    block_rows = lax.optimization_barrier((block_rows, stats))[0]
    block_across = plan.swap(block_rows, "mp", 2)

    result_low, hidden_low, middle_low, middle_grad, *rest = feed_back(
        plan, ids, result, middle, slope, row_grads, stats, seg_col, params, out_w, up, down, cols
    )
    attended_grads, sums = rest[:n_mp], rest[n_mp]
    cls_blocks = cls_blocks.reshape(2, plan.groups // 2, plan.block, class_cols)
    kept, sent, cls_sum, arrived, block_out = weight_grads(
        plan,
        [(result_low, active), (second_low, hidden_low)],
        (middle_low, attended),
        cls_blocks,
        attended_grads[1:],
        (block_rows, block_across),
    )
    grad_parts = [attended_grads[0]] + list(arrived)
    got = [plan.swap(sent[0], "mp", 2)] + [plan.group_swap(part, 1) for part in sent[1:]]

    *proj_grads, gain_sums = attend_back(
        plan, ids, starts, widths, live, q, k, v, pq, pk, gains, ones, grad_parts, logs, seg_col, seg_row
    )
    *got, _ = lax.optimization_barrier((*got, proj_grads[0]))

    down_pair, up_pair, out_pair = zip(kept, got)
    last_rows, grad_qkv, small_grads, owned = finish(
        plan, normed_low, proj_grads, w, middle_grad, tokens, params, sums, gain_sums, loss, [up_pair, out_pair], [down_pair], [cls_sum]
    )
    mean_loss = small_grads[10, 0] / image_total
    grad_qkv = plan.unmerged(grad_qkv, 1)
    grad_up, grad_out, grad_down, grad_cls = (plan.unmerged(a, 0) for a in owned)
    matrices = [
        (w_qkv, m_qkv, v_qkv, grad_qkv),
        (w_out, m_out, v_out, grad_out),
        (w_up, m_up, v_up, grad_up),
        (w_down.T, m_down.T, v_down.T, grad_down),
        (w_cls, m_cls, v_cls, grad_cls),
    ]
    input_grad, fresh = update(plan, ids, last_rows, matrices)
    norm_part = lax.dynamic_slice(small_grads, (0, dp * dim_part), (7, dim_part))
    qk_part = lax.dynamic_slice_in_dim(small_grads[8:10, :cols].reshape(2, cols // HEAD, HEAD), dp * head_part, head_part, 2)
    fresh[3] = [a.T for a in fresh[3]]
    outputs = [block_out, input_grad, mean_loss] + [a for group in fresh for a in group]
    one, two, new = adam_update(norm_params, m_norm, v_norm, norm_part, GAIN_RATE, 0.0)
    outputs += [one, two[:6], two[6], new]
    outputs += list(adam_update(qk_gain, m_qk, v_qk, qk_part, GAIN_RATE, 0.0))
    return tuple(outputs)


def solution(mesh):
    rows_cols = (P("mp", "dp"),) * 3
    cols_rows = (P("dp", "mp"),) * 3
    qkv_spec = (P(None, "dp", "mp"),) * 3
    qk_spec = (P(None, "mp", "dp"),) * 3
    norm_spec = P(None, "dp")
    in_specs = (
        (P("dp", None), P("dp"), P("dp")) + qkv_spec + rows_cols + cols_rows + rows_cols + cols_rows + (norm_spec,) * 3 + qk_spec
    )
    out_specs = (
        (P("dp", None), P("dp", None), P())
        + qkv_spec
        + rows_cols
        + cols_rows
        + rows_cols
        + cols_rows
        + (norm_spec, norm_spec, P("dp"), norm_spec)
        + qk_spec
    )
    body = functools.partial(shards, n_dp=mesh.shape["dp"], n_mp=mesh.shape["mp"])
    return jax.shard_map(body, mesh=mesh, in_specs=in_specs, out_specs=out_specs, check_vma=False)
```
